32 devices in a mesh: dp: 16 (over z, y, x), tensor: 2 (over core).
Axes of the slice: x: 2, y: 2, z: 4, core: 2. Of those that a mesh axis runs over, the one named last changes fastest.
Arguments:
- latent: bfloat16 [2048, 768], P('dp', 'tensor'), may hold values from 0 to 0.25
- action: bfloat16 [2048, 6], P('dp'), may hold values from -1 to 1
- task_ids: int32 [2048], P('dp'), may hold values from 0 to 79
- action_mask: int32 [80, 6], replicated, may hold values 0 or 1
- task_table: bfloat16 [80, 96], replicated, may hold values from -6 to 6
- target_latent: float32 [2048, 768], P('dp', 'tensor'), may hold values from 0 to 0.25
- bin_lower: int32 [2048], P('dp'), may hold values from 0 to 99
- bin_frac: float32 [2048], P('dp'), may hold values from 0 to 1
- dyn_w1: bfloat16 [768, 1792], P(None, 'tensor'), may hold values from -0.21875 to 0.21875
- dyn_wc: bfloat16 [102, 1792], P(None, 'tensor'), may hold values from -0.21875 to 0.21875
- dyn_vec1: float32 [3, 1792], P(None, 'tensor'), may hold values from -1.5 to 1.5, as said below
- dyn_w2: bfloat16 [1792, 1792], P('tensor'), may hold values from -0.125 to 0.125
- dyn_vec2: float32 [3, 1792], replicated, may hold values from -1.5 to 1.5, as said below
- dyn_w3: bfloat16 [1792, 768], P(None, 'tensor'), may hold values from -0.125 to 0.125
- dyn_vec3: float32 [3, 768], P(None, 'tensor'), may hold values from -1.5 to 1.5, as said below
- q_w1: bfloat16 [5, 768, 1792], P(None, None, 'tensor'), may hold values from -0.21875 to 0.21875
- q_wc: bfloat16 [5, 102, 1792], P(None, None, 'tensor'), may hold values from -0.21875 to 0.21875
- q_vec1: float32 [5, 3, 1792], P(None, None, 'tensor'), may hold values from -1.5 to 1.5, as said below
- q_w2: bfloat16 [5, 1792, 1792], P(None, 'tensor'), may hold values from -0.125 to 0.125
- q_vec2: float32 [5, 3, 1792], replicated, may hold values from -1.5 to 1.5, as said below
- q_w3: bfloat16 [5, 1792, 101], replicated, may hold values from -0.125 to 0.125
- q_b3: float32 [5, 101], replicated, may hold values from -3 to 3
Outputs:
- losses: float32 [2048, 2], P('dp')
- latent_grad: float32 [2048, 768], P('dp', 'tensor')
- table_grad: float32 [80, 96], replicated
- dyn_w1_grad: float32 [768, 1792], P('dp', 'tensor')
- dyn_wc_grad: float32 [102, 1792], P(None, 'tensor')
- dyn_vec1_grad: float32 [3, 1792], P(None, 'tensor')
- dyn_w2_grad: float32 [1792, 1792], P('tensor', 'dp')
- dyn_vec2_grad: float32 [3, 1792], replicated
- dyn_w3_grad: float32 [1792, 768], P('dp', 'tensor')
- dyn_vec3_grad: float32 [3, 768], P(None, 'tensor')
- q_w1_grad: float32 [5, 768, 1792], P(None, 'dp', 'tensor')
- q_wc_grad: float32 [5, 102, 1792], P(None, None, 'tensor')
- q_vec1_grad: float32 [5, 3, 1792], P(None, None, 'tensor')
- q_w2_grad: float32 [5, 1792, 1792], P(None, 'tensor', 'dp')
- q_vec2_grad: float32 [5, 3, 1792], replicated
- q_w3_grad: float32 [5, 1792, 101], P(None, 'dp')
- q_b3_grad: float32 [5, 101], replicated
The draws below stay inside these ranges and needn't reach their ends.
Inputs may be any that keep to these rules, and one draw needn't show every extreme that they name: `dyn_vec1`: rows: linear bias, norm gain (positive), norm shift. `dyn_vec2`: rows: linear bias, norm gain (positive), norm shift. `dyn_vec3`: rows: linear bias, norm gain (positive), norm shift. `q_vec1`: rows: linear bias, norm gain (positive), norm shift. `q_vec2`: rows: linear bias, norm gain (positive), norm shift.
All inputs are finite; a program needn't handle non-finite values.
Results may differ from the reference program's by a relative error of at most 0.0085.
Values may be sent and summed in bfloat16 or wider, within the bound.
A program may use at most 256 MiB of HBM per device.

```python
import math
import jax
import jax.numpy as jnp
from jax import lax

LATENT = 768
ACT = 6
EMB = 96
HID = 1792
HEADS = 5
BINS = 101
TASKS = 80
GROUP = 8
CTX = 102
TOKENS = 2048


def affine_rows(key, shape):
    noise = jnp.clip(jax.random.normal(key, shape, jnp.float32), -3.0, 3.0)
    row_kind = jnp.arange(3).reshape((3, 1))
    return jnp.where(row_kind == 1, 1.0 + 0.15 * noise, jnp.where(row_kind == 0, 0.5, 0.3) * noise)


def draw_dyn_vec1(key, part):
    key = jax.random.fold_in(key, 11)
    return affine_rows(key, (3, HID))


def draw_dyn_vec2(key, part):
    key = jax.random.fold_in(key, 12)
    return affine_rows(key, (3, HID))


def draw_dyn_vec3(key, part):
    key = jax.random.fold_in(key, 13)
    return affine_rows(key, (3, LATENT))


def draw_q_vec1(key, part):
    key = jax.random.fold_in(key, 14)
    return affine_rows(key, (HEADS, 3, HID))


def draw_q_vec2(key, part):
    key = jax.random.fold_in(key, 15)
    return affine_rows(key, (HEADS, 3, HID))


def set_ends(values, stream_key, low, top_value):
    dims = values.shape
    index_at = [jax.random.randint(jax.random.fold_in(stream_key, axis), (), 0, dims[axis]) for axis in range(len(dims))]
    values = values.at[tuple(index_at)].set(low)
    longest = dims.index(max(dims))
    index_at[longest] = (index_at[longest] + 1) % dims[longest]
    return values.at[tuple(index_at)].set(top_value)


def steps_of(rng, extent, split, least, largest):
    gain = 1.0
    for position, shards_of in split:
        steps = jax.random.uniform(jax.random.fold_in(jax.random.fold_in(rng, 6), position), (shards_of,), jnp.float32, least / len(split), largest / len(split))
        gain = gain * jnp.repeat(jnp.exp(steps), extent[position] // shards_of).reshape((-1,) + (1,) * (len(extent) - 1 - position))
    return gain


def bell_draw(stream_key, dims, spread, reach, cuts=(), kind=jnp.bfloat16):
    values = jax.random.normal(stream_key, dims, jnp.float32) * spread
    if len(cuts) > 0:
        values = steps_of(stream_key, dims, cuts, -0.22, 0.18) * values
    return jnp.clip(values, min=-reach, max=reach).astype(kind)


def setup_inputs(seed: int = 0) -> dict:
    key_list = jax.random.split(jax.random.key(seed), 23)
    return {
        "latent": jnp.clip(0.25 * jax.random.uniform(key_list[0], (TOKENS, LATENT), jnp.float32) ** steps_of(key_list[0], (TOKENS, LATENT), ((0, 16), (1, 2)), -0.2, 0.2), 0.0, 0.25).astype(jnp.bfloat16),
        "action": jnp.clip(jax.random.uniform(key_list[1], (TOKENS, ACT), jnp.float32, -1.0, 1.0) * steps_of(key_list[1], (TOKENS, ACT), ((0, 16),), -0.4, 0.0), -1.0, 1.0).astype(jnp.bfloat16),
        "task_ids": set_ends(jax.random.randint(key_list[2], (TOKENS,), 0, TASKS), jax.random.fold_in(key_list[2], 1), 0, TASKS - 1).astype(jnp.int32),
        "action_mask": set_ends((jax.random.randint(key_list[3], (TASKS, ACT), 0, 4) < 3).astype(jnp.int32), jax.random.fold_in(key_list[3], 1), 0, 1),
        "task_table": bell_draw(key_list[4], (TASKS, EMB), 1.0, 6.0),
        "target_latent": jnp.clip(0.25 * jax.random.uniform(key_list[5], (TOKENS, LATENT), jnp.float32) ** steps_of(key_list[5], (TOKENS, LATENT), ((0, 16), (1, 2)), -0.2, 0.2), 0.0, 0.25),
        "bin_lower": set_ends(jax.random.randint(key_list[6], (TOKENS,), 0, BINS - 1), jax.random.fold_in(key_list[6], 1), 0, (BINS - 1) - 1).astype(jnp.int32),
        "bin_frac": jnp.clip(1.0 * jax.random.uniform(key_list[7], (TOKENS,), jnp.float32) ** steps_of(key_list[7], (TOKENS,), ((0, 16),), -0.2, 0.2), 0.0, 1.0),
        "dyn_w1": bell_draw(key_list[8], (LATENT, HID), (LATENT + CTX) ** -0.5, 0.21875, ((1, 2),)),
        "dyn_wc": bell_draw(key_list[9], (CTX, HID), (LATENT + CTX) ** -0.5, 0.21875, ((1, 2),)),
        "dyn_vec1": draw_dyn_vec1(jax.random.fold_in(key_list[22], 71), 0),
        "dyn_w2": bell_draw(key_list[11], (HID, HID), HID ** -0.5, 0.125, ((0, 2),)),
        "dyn_vec2": draw_dyn_vec2(jax.random.fold_in(key_list[22], 71), 0),
        "dyn_w3": bell_draw(key_list[13], (HID, LATENT), HID ** -0.5, 0.125, ((1, 2),)),
        "dyn_vec3": draw_dyn_vec3(jax.random.fold_in(key_list[22], 71), 0),
        "q_w1": bell_draw(key_list[15], (HEADS, LATENT, HID), (LATENT + CTX) ** -0.5, 0.21875, ((2, 2),)),
        "q_wc": bell_draw(key_list[16], (HEADS, CTX, HID), (LATENT + CTX) ** -0.5, 0.21875, ((2, 2),)),
        "q_vec1": draw_q_vec1(jax.random.fold_in(key_list[22], 71), 0),
        "q_w2": bell_draw(key_list[18], (HEADS, HID, HID), HID ** -0.5, 0.125, ((1, 2),)),
        "q_vec2": draw_q_vec2(jax.random.fold_in(key_list[22], 71), 0),
        "q_w3": bell_draw(key_list[20], (HEADS, HID, BINS), HID ** -0.5, 0.125),
        "q_b3": bell_draw(key_list[21], (HEADS, BINS), 0.5, 3.0, (), jnp.float32),
    }


EPSILON = 1e-05
HIGHEST = lax.Precision.HIGHEST

@jax.custom_vjp
def low(v):
    return lax.optimization_barrier(v.astype(jnp.bfloat16)).astype(jnp.float32)

@jax.custom_vjp
def low_back(v):
    return v

def low_keep(v):
    return (low(v), None)

def low_pass(kept, grad):
    return (grad,)

def back_keep(v):
    return (v, None)

def back_low(kept, grad):
    return (low(grad),)
low.defvjp(low_keep, low_pass)
low_back.defvjp(back_keep, back_low)

def mish_curve(values):
    return values * jnp.tanh(jax.nn.softplus(values))

def layer_norm(values, gain_row, shift_row):
    centred = values - lax.optimization_barrier(jnp.mean(values, -1, keepdims=True))
    return centred * lax.rsqrt(lax.optimization_barrier(jnp.mean(centred * centred, -1, keepdims=True)) + EPSILON) * gain_row + shift_row

def hidden_pair(latent_in, context, w_latent, w_context, vectors_one, w_second, vectors_two):
    first = jnp.einsum('ti,hij->htj', latent_in, w_latent, precision=HIGHEST)
    first = first + jnp.einsum('tc,hcj->htj', context, w_context, precision=HIGHEST) + vectors_one[:, 0:1, :]
    first = low_back(first)
    hidden = low(mish_curve(layer_norm(first, vectors_one[:, 1:2, :], vectors_one[:, 2:3, :])))
    second = jnp.einsum('htj,hjk->htk', hidden, w_second, precision=HIGHEST) + vectors_two[:, 0:1, :]
    second = low_back(second)
    return low(mish_curve(layer_norm(second, vectors_two[:, 1:2, :], vectors_two[:, 2:3, :])))

def objective(params, latent_in, acted, onehot, target_latent, target):
    task_table, dyn_w1, dyn_wc, dyn_vec1, dyn_w2, dyn_vec2, dyn_w3, dyn_vec3, q_w1, q_wc, q_vec1, q_w2, q_vec2, q_w3, q_b3 = params
    embed = jnp.dot(onehot, task_table, precision=HIGHEST)
    context = jnp.concatenate([acted, embed], 1)
    dyn_hidden = hidden_pair(latent_in, context, dyn_w1[None], dyn_wc[None], dyn_vec1[None], dyn_w2[None], dyn_vec2[None])[0]
    third = low_back(jnp.dot(dyn_hidden, dyn_w3, precision=HIGHEST) + dyn_vec3[0])
    normed = layer_norm(third, dyn_vec3[1], dyn_vec3[2])
    grouped = normed.reshape(normed.shape[0], -1, GROUP)
    next_latent = low(jax.nn.softmax(grouped, axis=-1).reshape(normed.shape))
    mismatch = next_latent - target_latent
    consistency = lax.optimization_barrier(jnp.sum(mismatch * mismatch, -1))
    q_hidden = hidden_pair(next_latent, context, q_w1, q_wc, q_vec1, q_w2, q_vec2)
    logits = low_back(jnp.einsum('htj,hjb->htb', q_hidden, q_w3, precision=HIGHEST) + q_b3[:, None, :])
    log_prob = jax.nn.log_softmax(logits, axis=-1)
    value_loss = -lax.optimization_barrier(jnp.sum(target[None] * log_prob, (0, 2))) / HEADS
    total = jnp.sum(consistency + value_loss) / math.sqrt(TOKENS)
    return (total, jnp.stack([consistency, value_loss], 1))

def reference(latent, action, task_ids, action_mask, task_table, target_latent, bin_lower, bin_frac, dyn_w1, dyn_wc, dyn_vec1, dyn_w2, dyn_vec2, dyn_w3, dyn_vec3, q_w1, q_wc, q_vec1, q_w2, q_vec2, q_w3, q_b3):
    params = tuple((item.astype(jnp.float32) for item in (task_table, dyn_w1, dyn_wc, dyn_vec1, dyn_w2, dyn_vec2, dyn_w3, dyn_vec3, q_w1, q_wc, q_vec1, q_w2, q_vec2, q_w3, q_b3)))
    onehot = (task_ids[:, None] == jnp.arange(TASKS, dtype=jnp.int32)[None, :]).astype(jnp.float32)
    mask_rows = jnp.dot(onehot, action_mask.astype(jnp.float32), precision=HIGHEST)
    acted = action.astype(jnp.float32) * mask_rows
    bin_index = jnp.arange(BINS, dtype=jnp.int32)[None, :]
    fraction = bin_frac[:, None]
    lower_bin = bin_lower[:, None]
    target = jnp.where(bin_index == lower_bin, 1.0 - fraction, 0.0) + jnp.where(bin_index == lower_bin + 1, fraction, 0.0)
    block = math.gcd(TOKENS, 4096)
    blocks = TOKENS // block

    def split_rows(values):
        return values.reshape((blocks, block) + values.shape[1:])

    def one_block(carry, pieces):
        latent_block, acted_block, onehot_block, target_latent_block, target_block = pieces

        def local_objective(weights, latent_in):
            return objective(weights, latent_in, acted_block, onehot_block, target_latent_block, target_block)
        unused, pullback, block_losses = jax.vjp(local_objective, params, latent_block, has_aux=True)
        grads, latent_grad = pullback(jnp.ones((), jnp.float32))
        carry = jax.tree.map(lambda left, right: left + right, carry, grads)
        return (carry, (block_losses, latent_grad))
    zeros = jax.tree.map(jnp.zeros_like, params)
    grads, (losses, latent_grad) = lax.scan(one_block, zeros, (split_rows(latent.astype(jnp.float32)), split_rows(acted), split_rows(onehot), split_rows(target_latent), split_rows(target)))
    return (losses.reshape(TOKENS, 2), latent_grad.reshape(TOKENS, LATENT), grads[0], grads[1], grads[2], grads[3], grads[4], grads[5], grads[6], grads[7], grads[8], grads[9], grads[10], grads[11], grads[12], grads[13], grads[14])
```

```python
import functools
import math

import jax
import jax.numpy as jnp
from jax import lax
from jax.experimental import pallas as pl
from jax.experimental.pallas import tpu as pltpu
from jax.sharding import PartitionSpec as P

GROUP = 8
LINE = 4
PLANE = 4
BLOCK = LINE * PLANE
EPSILON = 1e-05
HIGHEST = lax.Precision.HIGHEST
F32 = jnp.float32
BF16 = jnp.bfloat16
REMOTE_COPIES = 144
LOCAL_COPIES = 48
VMEM_BYTES = 63 << 20


def swap_core(values):
    return lax.ppermute(values, "tensor", [(0, 1), (1, 0)])


def swap_dp(values, bit):
    size = lax.axis_size("dp")
    return lax.ppermute(values, "dp", [(place, place ^ bit) for place in range(size)])


def pick(values, index, axis=0):
    return lax.dynamic_index_in_dim(values, index, axis, keepdims=False)


def own_then_other(values):
    return values, swap_core(values)


def mish_parts(values):
    grown = jnp.exp(jnp.minimum(values, 20.0))
    top = grown * (grown + 2.0)
    share = 1.0 / (top + 2.0)
    return grown, top * share, share


def mish(values):
    return values * mish_parts(values)[1]


def mish_slope(values):
    grown, ratio, share = mish_parts(values)
    return ratio + 4.0 * values * grown * (1.0 + grown) * share * share


def norm(before, gain, shift):
    centred = before - jnp.mean(before, -1, keepdims=True)
    inverse = lax.rsqrt(jnp.mean(centred * centred, -1, keepdims=True) + EPSILON)
    normed = centred * inverse
    return normed * gain + shift, normed, inverse


def norm_back(upstream, normed, inverse, gain):
    weighted = upstream * gain
    return inverse * (
        weighted
        - jnp.mean(weighted, -1, keepdims=True)
        - normed * jnp.mean(weighted * normed, -1, keepdims=True)
    )


def vector_sums(rounded, upstream, normed):
    return jnp.stack(
        [jnp.sum(rounded.astype(F32), 0), jnp.sum(upstream * normed, 0), jnp.sum(upstream, 0)]
    )


def mm(left, right):
    return jnp.dot(left, right, preferred_element_type=F32)


def mm_t(left, right):
    return lax.dot_general(left, right, (((1,), (1,)), ((), ())), preferred_element_type=F32)


def t_mm(left, right):
    return lax.dot_general(left, right, (((0,), (0,)), ((), ())), preferred_element_type=F32)


def block_forward(inputs, context, w_one, w_context, vec_one, w_two, vec_two):
    before = mm(inputs, w_one) + mm(context, w_context) + vec_one[0:1]
    out_one, normed_one, inverse_one = norm(before, vec_one[1:2], vec_one[2:3])
    hidden_one = mish(out_one).astype(BF16)
    second = mm(hidden_one, w_two) + vec_two[0:1]
    out_two, normed_two, inverse_two = norm(second, vec_two[1:2], vec_two[2:3])
    hidden_two = mish(out_two).astype(BF16)
    return hidden_one, hidden_two, (normed_one, inverse_one, normed_two, inverse_two)


def block_backward(grad_hidden, saved, vec_one, w_two, vec_two):
    normed_one, inverse_one, normed_two, inverse_two = saved
    upstream = mish_slope(normed_two * vec_two[1:2] + vec_two[2:3]) * grad_hidden
    grad_two = norm_back(upstream, normed_two, inverse_two, vec_two[1:2]).astype(BF16)
    sums_two = vector_sums(grad_two, upstream, normed_two)
    grad_one_hidden = mm_t(grad_two, w_two)
    upstream = mish_slope(normed_one * vec_one[1:2] + vec_one[2:3]) * grad_one_hidden
    grad_one = norm_back(upstream, normed_one, inverse_one, vec_one[1:2]).astype(BF16)
    sums_one = vector_sums(grad_one, upstream, normed_one)
    return grad_two, sums_two, grad_one, sums_one


def dynamics_forward(inputs, context, w_one, w_context, vec_one, w_two, vec_two, w_three, vec_three):
    hidden_one, hidden_two, saved = block_forward(
        inputs, context, w_one, w_context, vec_one, w_two, vec_two
    )
    before = mm(hidden_two, w_three) + vec_three[0:1]
    out, normed, inverse = norm(before, vec_three[1:2], vec_three[2:3])
    grouped = out.reshape(out.shape[0], -1, GROUP)
    simplex = jax.nn.softmax(grouped, axis=-1).reshape(out.shape)
    return hidden_one, hidden_two, saved, simplex, normed, inverse


def dynamics_backward(grad_next, simplex, normed, inverse, saved, w_three, vec_three, vec_one, w_two, vec_two):
    weighted = grad_next * simplex
    rows = weighted.shape[0]
    along = jnp.sum(weighted.reshape(rows, -1, GROUP), -1, keepdims=True)
    along = jnp.broadcast_to(along, (rows, along.shape[1], GROUP)).reshape(weighted.shape)
    upstream = weighted - simplex * along
    grad_three = norm_back(upstream, normed, inverse, vec_three[1:2]).astype(BF16)
    sums_three = vector_sums(grad_three, upstream, normed)
    grad_hidden = mm_t(grad_three, w_three)
    grad_two, sums_two, grad_one, sums_one = block_backward(
        grad_hidden, saved, vec_one, w_two, vec_two
    )
    return grad_three, sums_three, grad_two, sums_two, grad_one, sums_one


def value_head(hidden_two, w_three, bias, lower, fraction, scale, heads):
    logits = mm(hidden_two, w_three) + bias
    log_prob = jax.nn.log_softmax(logits, axis=-1)
    bins = jnp.arange(logits.shape[-1], dtype=jnp.int32)[None, :]
    target = jnp.where(bins == lower, 1.0 - fraction, 0.0) + jnp.where(
        bins == lower + 1, fraction, 0.0
    )
    loss = -jnp.sum(target * log_prob, -1) / heads
    grad_logits = (scale / heads * (jnp.exp(log_prob) - target)).astype(BF16)
    return loss, grad_logits


def spread(values, axis_len):
    blocks = lax.axis_size("dp") // BLOCK
    rows = values.shape[0] // (blocks * BLOCK)
    values = values.reshape((blocks, LINE, 2, 2, rows) + values.shape[1:])
    if blocks > 1:
        values = jnp.moveaxis(values, 0, 3)
    return values.reshape((LINE, 2, 2, blocks * rows) + values.shape[5:])


def across_blocks(values, axis):
    blocks = lax.axis_size("dp") // BLOCK
    if blocks == 1:
        return values
    groups = [[block * BLOCK + place for block in range(blocks)] for place in range(BLOCK)]
    return lax.psum_scatter(
        values, "dp", scatter_dimension=axis, axis_index_groups=groups, tiled=True
    )


def sum_across_blocks(values):
    blocks = lax.axis_size("dp") // BLOCK
    if blocks == 1:
        return values
    groups = [[block * BLOCK + place for block in range(blocks)] for place in range(BLOCK)]
    return lax.psum(values, "dp", axis_index_groups=groups)


def reduce_first(values, axis_x, bit_x, at_x, axis_y, bit_y, at_y):
    sent = pick(values, 1 - at_x, axis_x).astype(BF16)
    total = pick(values, at_x, axis_x) + swap_dp(sent, bit_x).astype(F32)
    if axis_y > axis_x:
        axis_y -= 1
    sent = pick(total, 1 - at_y, axis_y).astype(BF16)
    return pick(total, at_y, axis_y) + swap_dp(sent, bit_y).astype(F32)


def plane_scatter(values, at_x, at_y):
    half = LINE // 2
    first = reduce_first(values[:half], 2, 1, at_x, 1, 2, at_y)
    second = reduce_first(values[half:], 1, 2, at_y, 2, 1, at_x)
    return jnp.concatenate([first, second], 0)


def plane_scatter_one(values, at_x, at_y):
    half = values.shape[-1] // 256 * 128
    if half == 0:
        return reduce_first(values, 1, 1, at_x, 0, 2, at_y)
    first = reduce_first(values[..., :half], 1, 1, at_x, 0, 2, at_y)
    second = reduce_first(values[..., half:], 0, 2, at_y, 1, 1, at_x)
    return jnp.concatenate([first, second], -1)


def line_exchange(values, at_z, last):
    out = jnp.zeros((LINE + 1,) + values.shape[1:], F32)
    for step in range(LINE):
        part = pick(values, at_z ^ step)
        if step:
            part = swap_dp(part.astype(BF16), 4 * step).astype(F32)
        out = lax.dynamic_update_index_in_dim(out, part, at_z ^ step, 0)
    return lax.dynamic_update_index_in_dim(out, last, LINE, 0)


def plane_total(values, kind=F32):
    values = values + swap_dp(values.astype(kind), 1).astype(F32)
    return values + swap_dp(values.astype(kind), 2).astype(F32)


def line_collect(values, at_z, last, kind=F32):
    out = jnp.zeros((LINE + 1,) + values.shape, F32)
    sent = values.astype(kind)
    for step in range(LINE):
        part = swap_dp(sent, 4 * step).astype(F32) if step else values
        out = lax.dynamic_update_index_in_dim(out, part, at_z ^ step, 0)
    return lax.dynamic_update_index_in_dim(out, last, LINE, 0)


def line_total(values):
    total = values
    for step in range(1, LINE):
        total = total + swap_dp(values, 4 * step)
    return total


def in_core_order(core, own, other, axis):
    return jnp.where(
        core == 0, jnp.concatenate([own, other], axis), jnp.concatenate([other, own], axis)
    )


def general_shards(
    latent,
    action,
    task_ids,
    action_mask,
    task_table,
    target_latent,
    bin_lower,
    bin_frac,
    dyn_w1,
    dyn_wc,
    dyn_vec1,
    dyn_w2,
    dyn_vec2,
    dyn_w3,
    dyn_vec3,
    q_w1,
    q_wc,
    q_vec1,
    q_w2,
    q_vec2,
    q_w3,
    q_b3,
):
    place = lax.axis_index("dp")
    core = lax.axis_index("tensor")
    at_x, at_y, at_z = place % 2, place // 2 % 2, place // 4 % 4
    local_rows = latent.shape[0]
    half_rows = local_rows // 2
    half_latent = latent.shape[1]
    half_hidden = dyn_w1.shape[1]
    inv_root = 1.0 / math.sqrt(local_rows * lax.axis_size("dp"))
    task_count = task_table.shape[0]
    heads = q_w1.shape[0]
    head_places = (at_z, heads - 1)

    def both(values, axis):
        return jnp.concatenate(own_then_other(values), axis)

    dyn_w1_all, dyn_wc_all, dyn_vec1_all = both(dyn_w1, 1), both(dyn_wc, 1), both(dyn_vec1, 1)
    dyn_w2_all = both(dyn_w2, 0)
    dyn_w3_all = in_core_order(core, *own_then_other(dyn_w3), 1)
    dyn_vec3_all = in_core_order(core, *own_then_other(dyn_vec3), 1)
    head_weights = []
    for head in head_places:
        head_weights.append(
            (
                both(pick(q_w1, head), 1),
                both(pick(q_wc, head), 1),
                both(pick(q_vec1, head), 1),
                both(pick(q_w2, head), 0),
                pick(q_vec2, head),
                pick(q_w3, head),
                pick(q_b3, head),
            )
        )

    def my_rows(values):
        return lax.dynamic_slice_in_dim(values, core * half_rows, half_rows, 0)

    def their_rows(values):
        return lax.dynamic_slice_in_dim(values, (1 - core) * half_rows, half_rows, 0)

    def whole_columns(values):
        return in_core_order(core, my_rows(values), swap_core(their_rows(values)), 1)

    my_latent = whole_columns(latent)
    my_target = whole_columns(target_latent)
    my_ids = my_rows(task_ids)[:, None]
    onehot = (my_ids == jnp.arange(task_count, dtype=jnp.int32)[None, :]).astype(BF16)
    table = jnp.concatenate([action_mask.astype(BF16), task_table], 1)
    looked_up = mm(onehot, table)
    acts = action.shape[1]
    acted = my_rows(action).astype(F32) * looked_up[:, :acts]
    my_context = jnp.concatenate([acted, looked_up[:, acts:]], 1).astype(BF16)
    fraction = my_rows(bin_frac)[:, None]
    piece_one = lax.reduce_precision(fraction, 8, 7)
    piece_two = lax.reduce_precision(fraction - piece_one, 8, 7)
    piece_three = fraction - piece_one - piece_two
    meta = [my_ids, my_rows(bin_lower)[:, None], piece_one, piece_two, piece_three]
    meta = [item.astype(BF16) for item in meta]
    width = my_latent.shape[1]
    context_width = my_context.shape[1]
    packed = jnp.concatenate([my_latent, my_context] + meta, 1)
    packed = jnp.concatenate([packed] + [swap_dp(packed, 4 * step) for step in range(1, LINE)], 0)
    inputs = packed[:, :width]
    context = packed[:, width : width + context_width]
    meta = packed[:, width + context_width :].astype(F32)
    all_ids = meta[:, 0:1].astype(jnp.int32)
    lower = meta[:, 1:2].astype(jnp.int32)
    fraction = meta[:, 2:3] + meta[:, 3:4] + meta[:, 4:5]
    all_onehot = (all_ids == jnp.arange(task_count, dtype=jnp.int32)[None, :]).astype(F32)
    other_inputs, other_context = swap_core(inputs), swap_core(context)

    dyn_one, dyn_two, dyn_saved, simplex, normed_three, inverse_three = dynamics_forward(
        inputs, context, dyn_w1_all, dyn_wc_all, dyn_vec1_all, dyn_w2_all, dyn_vec2,
        dyn_w3_all, dyn_vec3_all,
    )
    next_low = simplex.astype(BF16)
    mismatch = next_low[:half_rows].astype(F32) - my_target
    consistency = jnp.sum(mismatch * mismatch, -1)
    other_next = swap_core(next_low)

    head_results = []
    for weights in head_weights:
        w_one, w_context, vec_one, w_two, vec_two, w_three, bias = weights
        hidden_one, hidden_two, saved = block_forward(
            next_low, context, w_one, w_context, vec_one, w_two, vec_two
        )
        loss, grad_logits = value_head(
            hidden_two, w_three, bias[None], lower, fraction, inv_root, heads
        )
        grad_hidden = mm_t(grad_logits, w_three)
        grad_two, sums_two, grad_one, sums_one = block_backward(
            grad_hidden, saved, vec_one, w_two, vec_two
        )
        head_results.append(
            (hidden_one, hidden_two, loss, grad_logits, grad_two, sums_two, grad_one, sums_one)
        )

    main, extra = head_results
    grad_in = mm_t(main[6], head_weights[0][0])
    own_grad = grad_in[:half_rows] + mm_t(extra[6][:half_rows], head_weights[1][0])
    own_loss = main[2][:half_rows] + extra[2][:half_rows]
    for step in range(1, LINE):
        part = slice(step * half_rows, (step + 1) * half_rows)
        own_grad = own_grad + swap_dp(grad_in[part].astype(BF16), 4 * step).astype(F32)
        own_loss = own_loss + swap_dp(main[2][part], 4 * step)
    own_grad = own_grad + 2.0 * inv_root * mismatch
    own_low = own_grad.astype(BF16)
    grad_next = jnp.concatenate(
        [own_low] + [swap_dp(own_low, 4 * step) for step in range(1, LINE)], 0
    ).astype(F32)
    my_losses = jnp.stack([consistency, own_loss], 1)
    losses = in_core_order(core, my_losses, swap_core(my_losses), 0)

    grad_three, sums_three, dyn_grad_two, dyn_sums_two, dyn_grad_one, dyn_sums_one = (
        dynamics_backward(
            grad_next, simplex, normed_three, inverse_three, dyn_saved, dyn_w3_all, dyn_vec3_all,
            dyn_vec1_all, dyn_w2_all, dyn_vec2,
        )
    )
    own_latent_grad = mm_t(dyn_grad_one[:half_rows], dyn_w1_all)
    left, right = own_latent_grad[:, :half_latent], own_latent_grad[:, half_latent:]
    kept = jnp.where(core == 0, left, right)
    received = swap_core(jnp.where(core == 0, right, left))
    latent_grad = in_core_order(core, kept, received, 0)

    def own_half(values):
        return jnp.concatenate([values[:, :half_hidden], swap_core(values[:, half_hidden:])], 0)

    def all_rows(values):
        return jnp.concatenate([values, swap_core(values)], 0)

    def quarter(values, size):
        blocks = lax.axis_size("dp") // BLOCK
        cut = values.reshape(values.shape[0], blocks, LINE, size // (blocks * LINE))
        return pick(cut, at_z, 2).reshape(values.shape[0], size // LINE)

    def spread_quarter(values):
        blocks = lax.axis_size("dp") // BLOCK
        rows = values.shape[0] // (blocks * PLANE)
        values = values.reshape((blocks, 2, 2, rows) + values.shape[1:])
        if blocks > 1:
            values = jnp.moveaxis(values, 0, 2)
        return values.reshape((2, 2, blocks * rows) + values.shape[4:])

    both_next = jnp.concatenate([next_low, other_next], 0)
    both_inputs = jnp.concatenate([inputs, other_inputs], 0)
    both_context = jnp.concatenate([context, other_context], 0)
    features = both_next.shape[1]
    hidden = 2 * half_hidden

    def quarter_grads(hidden_one, grad_two, grad_one, rows_in):
        first_factor, grad_factor = own_half(hidden_one), own_half(grad_one)
        w_two_part = t_mm(all_rows(quarter(grad_two, hidden)), first_factor)
        w_one_part = t_mm(quarter(rows_in, features), grad_factor)
        w_context_part = t_mm(both_context, grad_factor)
        return (
            plane_scatter_one(spread_quarter(w_two_part), at_x, at_y),
            plane_scatter_one(spread_quarter(w_one_part), at_x, at_y),
            plane_total(w_context_part, BF16),
        )

    def outer_quarter(left, right):
        part = t_mm(quarter(left, hidden), right)
        return plane_scatter_one(spread_quarter(part), at_x, at_y)

    first_factor, grad_factor = own_half(main[0]), own_half(main[6])
    main_two = plane_scatter(spread(t_mm(all_rows(main[4]), first_factor), 0), at_x, at_y)
    main_one = plane_scatter(spread(t_mm(both_next, grad_factor), 0), at_x, at_y)
    main_three = plane_scatter(spread(t_mm(main[1], main[3]), 0), at_x, at_y)
    main_context = plane_total(t_mm(both_context, grad_factor), BF16)
    extra_two, extra_one, extra_context = quarter_grads(extra[0], extra[4], extra[6], both_next)
    extra_three = outer_quarter(extra[1], extra[3])
    dyn_w2_part, dyn_w1_part, dyn_context = quarter_grads(
        dyn_one, dyn_grad_two, dyn_grad_one, both_inputs
    )
    dyn_w3_part = outer_quarter(
        all_rows(dyn_two),
        jnp.concatenate(
            [
                jnp.where(core == 0, grad_three[:, :half_latent], grad_three[:, half_latent:]),
                swap_core(
                    jnp.where(core == 0, grad_three[:, half_latent:], grad_three[:, :half_latent])
                ),
            ],
            0,
        ),
    )

    q_w2_out = across_blocks(line_exchange(main_two, at_z, extra_two), 1).transpose(0, 2, 1)
    q_w1_out = across_blocks(line_exchange(main_one, at_z, extra_one), 1)
    q_w3_out = line_exchange(main_three, at_z, extra_three)
    q_w3_out = across_blocks(q_w3_out + swap_core(q_w3_out), 1)
    dyn_w2_out = across_blocks(dyn_w2_part, 0).transpose(1, 0)
    dyn_w1_out = across_blocks(dyn_w1_part, 0)
    dyn_w3_out = across_blocks(dyn_w3_part, 0)
    q_wc_out = sum_across_blocks(line_collect(main_context, at_z, extra_context, BF16))
    dyn_wc_out = sum_across_blocks(dyn_context)

    def core_vec(values):
        own, other = values[:, :half_hidden], values[:, half_hidden:]
        return own + swap_core(other)

    def sums_of(result):
        return (
            core_vec(result[7]),
            result[5] + swap_core(result[5]),
            jnp.sum(result[3].astype(F32), 0)[None],
        )

    def pack(items):
        return jnp.concatenate([item.reshape(-1) for item in items])

    main_sums, extra_sums = sums_of(main), sums_of(extra)
    main_bias = main_sums[2] + swap_core(main_sums[2])
    extra_bias = extra_sums[2] + swap_core(extra_sums[2])
    main_sums, extra_sums = main_sums[:2] + (main_bias,), extra_sums[:2] + (extra_bias,)
    three_own = jnp.where(core == 0, sums_three[:, :half_latent], sums_three[:, half_latent:])
    three_other = jnp.where(core == 0, sums_three[:, half_latent:], sums_three[:, :half_latent])
    dyn_sums = (
        core_vec(dyn_sums_one),
        dyn_sums_two + swap_core(dyn_sums_two),
        three_own + swap_core(three_other),
    )
    def table_part(grad_one, w_context, rows):
        embed = mm_t(grad_one[:rows], w_context[acts:])
        return lax.dot_general(
            all_onehot[:rows], embed, (((0,), (0,)), ((), ())), precision=HIGHEST
        )

    table_grad = (
        table_part(main[6], head_weights[0][1], inputs.shape[0])
        + table_part(extra[6], head_weights[1][1], half_rows)
        + table_part(dyn_grad_one, dyn_wc_all, half_rows)
    )
    table_grad = line_total(table_grad + swap_core(table_grad))
    flat = sum_across_blocks(
        plane_total(pack((table_grad,) + dyn_sums + extra_sums + main_sums))
    )
    sizes = [table_grad] + list(dyn_sums)
    pieces = []
    start = 0
    for item in sizes:
        pieces.append(flat[start : start + item.size].reshape(item.shape))
        start += item.size
    head_size = sum(item.size for item in main_sums)
    extra_flat, main_flat = flat[start : start + head_size], flat[start + head_size :]
    head_flat = line_collect(main_flat, at_z, extra_flat)
    head_pieces = []
    start = 0
    for item in main_sums:
        head_pieces.append(
            head_flat[:, start : start + item.size].reshape((heads,) + item.shape)
        )
        start += item.size
    table_out, dyn_vec1_out, dyn_vec2_out, dyn_vec3_out = pieces
    q_vec1_out, q_vec2_out, q_b3_out = head_pieces
    return (
        losses,
        latent_grad,
        table_out,
        dyn_w1_out,
        dyn_wc_out,
        dyn_vec1_out,
        dyn_w2_out,
        dyn_vec2_out,
        dyn_w3_out,
        dyn_vec3_out,
        q_w1_out,
        q_wc_out,
        q_vec1_out,
        q_w2_out,
        q_vec2_out,
        q_w3_out,
        q_b3_out[:, 0],
    )


def gather_sum(values, ones):
    parts = []
    for start in range(0, values.shape[1], 128):
        piece = values[:, start : start + 128]
        high = piece.astype(BF16)
        rest = piece - high.astype(F32)
        middle = rest.astype(BF16)
        low = (rest - middle.astype(F32)).astype(BF16)
        parts.append(mm(high, ones) + mm(middle, ones) + mm(low, ones))
    return jnp.concatenate(parts, 1)


def line_kernel(sizes, scale, *refs):
    (slot, width, hidden, bins, tasks, acts, context_width, heads) = sizes
    (
        latent, meta, table, target_latent, dyn_vec1, dyn_vec2, dyn_vec3, q_vec1, q_vec2, q_b3,
        dyn_w1, dyn_wc, dyn_w2, dyn_w3, q_w1, q_wc, q_w2, q_w3,
        out_losses, out_latent, out_table, out_dw1, out_dwc, out_dvec, out_dvec3, out_dw2, out_dw3,
        out_qw1, out_qwc, out_qvec, out_qw2, out_qw3,
        w1, wc, w2, dw3, qw3, dv1, dv3, qv1, qv2, qb3,
        xbuf, xother, tgt, nxt, nxto, dyn_x1, dyn_x2, dyn_h1, dyn_h2, simplex, x3,
        dyn_inv, x1, x2, inv, h1, h2, gp2, gp1, h1o, gp2o, gp1o, upstream, gl, dyn_gp3,
        acc, dxm, dxr, own_g, all_g, lossbuf,
        p2, r2, t2, p1, r1, t1, p3, r3, t3, p3o,
        e2, er2, et2, e1, er1, et1, e3, er3, et3, e3o,
        er2b, et2b, er1b, et1b, d3, d3s, d3o, er3b, et3b,
        pc, pcx, pcy, vb, vbo, vbx, vby, tb, tbo, tbr,
        o3,
        send_sem, recv_sem, local_sem, free_a, free_b, free_f,
    ) = refs
    half = hidden // 2
    half_w = width // 2
    own_two, own_one = hidden // BLOCK, width // BLOCK
    rows_all = slot * LINE
    place = lax.axis_index("dp")
    core = lax.axis_index("tensor")
    at_x = lax.rem(place, 2)
    at_y = lax.rem(place // 2, 2)
    at_z = lax.rem(place // 4, 4)
    z_of = [
        at_z,
        at_z + 1 - 2 * lax.rem(at_z, 2),
        lax.rem(at_z + 2, 4),
        3 - at_z,
    ]
    to_core = (place, 1 - core)
    to_x = (place + 1 - 2 * at_x, core)
    to_y = (place + 2 - 4 * at_y, core)
    to_z = [None] + [(place + 4 * (z_of[k] - at_z), core) for k in range(1, LINE)]
    mesh_id = pl.DeviceIdType.MESH
    counter = [0, 0]
    pending = []

    def remote(source, target, device):
        at = counter[0]
        counter[0] += 1
        copy = pltpu.make_async_remote_copy(
            src_ref=source, dst_ref=target, send_sem=send_sem.at[at], recv_sem=recv_sem.at[at],
            device_id=device, device_id_type=mesh_id,
        )
        copy.start()
        pending.append(copy)
        return copy

    def sent(copy):
        copy.wait_send()
        pending[:] = [item for item in pending if item is not copy]

    def local(source, target):
        at = counter[1]
        counter[1] += 1
        copy = pltpu.make_async_copy(source, target, local_sem.at[at])
        copy.start()
        return copy

    barrier = pltpu.get_barrier_semaphore()
    peers = [to_core, to_x, to_y] + to_z[1:]
    for peer in peers:
        pl.semaphore_signal(barrier, inc=1, device_id=peer, device_id_type=mesh_id)
    pl.semaphore_wait(barrier, len(peers))

    low = slice(0, half)
    high = slice(half, hidden)
    own_cols = pl.ds(pl.multiple_of(half_w * core, 128), half_w)
    other_cols = pl.ds(pl.multiple_of(half_w * (1 - core), 128), half_w)
    own_rows = pl.ds(pl.multiple_of(slot * core, 64), slot)
    other_rows = pl.ds(pl.multiple_of(slot * (1 - core), 64), slot)

    lat_copy = remote(latent.at[other_rows], xbuf.at[pl.ds(0, slot), own_cols], to_core)
    tgt_copy = remote(target_latent.at[other_rows], tgt.at[:, own_cols], to_core)

    def load_weights(to, one, context, two):
        mine = [
            local(one, w1.at[to, :, low]),
            local(context, wc.at[to, :, low]),
            local(two, w2.at[to, low, :]),
        ]
        return mine

    def send_weights(to, one, context, two):
        return [
            remote(one, w1.at[to, :, high], to_core),
            remote(context, wc.at[to, :, high], to_core),
            remote(two, w2.at[to, high, :], to_core),
        ]

    head_z = at_z
    last = heads - 1
    vec_copies = [
        remote(dyn_vec1, dv1.at[:, high], to_core),
        remote(dyn_vec3, dv3.at[:, own_cols], to_core),
        remote(q_vec1.at[head_z], qv1.at[0, :, high], to_core),
        remote(q_vec1.at[last], qv1.at[1, :, high], to_core),
    ]
    dyn_ready = load_weights(0, dyn_w1, dyn_wc, dyn_w2)
    dyn_ready_other = send_weights(0, dyn_w1, dyn_wc, dyn_w2)
    three_ready = local(dyn_w3, dw3.at[:, own_cols])
    three_ready_other = remote(dyn_w3, dw3.at[:, own_cols], to_core)
    main_ready = load_weights(1, q_w1.at[head_z], q_wc.at[head_z], q_w2.at[head_z])
    main_three = local(q_w3.at[head_z], qw3.at[0])
    extra_three = local(q_w3.at[last], qw3.at[1])
    main_ready_other = send_weights(1, q_w1.at[head_z], q_wc.at[head_z], q_w2.at[head_z])

    dv1[:, low] = dyn_vec1[...]
    dv3[:, own_cols] = dyn_vec3[...]
    qv1[0, :, low] = q_vec1[head_z]
    qv1[1, :, low] = q_vec1[last]
    qv2[0] = q_vec2[head_z]
    qv2[1] = q_vec2[last]
    qb3[0] = q_b3[pl.ds(head_z, 1), :]
    qb3[1] = q_b3[last : last + 1, :]
    vb[...] = jnp.zeros_like(vb)

    facts = meta[own_rows, :]
    task_row = lax.broadcasted_iota(jnp.int32, (slot, tasks), 1).astype(F32)
    onehot = (facts[:, context_width : context_width + 1] == task_row).astype(F32).astype(BF16)
    looked = mm(onehot, table[...])
    lane = lax.broadcasted_iota(jnp.int32, (slot, 128), 1)
    xbuf[0:slot, width : width + 128] = jnp.where(
        lane < context_width, looked * facts, facts
    ).astype(BF16)
    xbuf[0:slot, own_cols] = latent[own_rows, :]
    tgt[:, own_cols] = target_latent[own_rows, :]
    lat_copy.wait_recv()
    line_in = [
        remote(xbuf.at[pl.ds(0, slot)], xbuf.at[pl.ds(slot * k, slot)], to_z[k])
        for k in range(1, LINE)
    ]
    for copy in vec_copies:
        copy.wait_recv()
    for copy in line_in:
        copy.wait_recv()
    x_copy = remote(xbuf, xother, to_core)

    CH = 64

    def over_rows(first, count, body):
        if count <= CH:
            body(pl.ds(first, count))
            return

        def step(index, carry):
            body(pl.ds(pl.multiple_of(first + index * CH, CH), CH))
            return carry

        lax.fori_loop(0, count // CH, step, 0)

    def norm_rows(pre, keep, inverse, vec, out, first, count):
        features = pre.shape[1]

        def body(rows):
            values = pre[rows, :]
            centred = values - jnp.sum(values, -1, keepdims=True) * (1.0 / features)
            inv_rows = lax.rsqrt(
                jnp.sum(centred * centred, -1, keepdims=True) * (1.0 / features) + EPSILON
            )
            normed = centred * inv_rows
            keep[rows, :] = normed.astype(keep.dtype)
            inverse[rows, :] = inv_rows
            out[rows, :] = mish(normed * vec[1:2, :] + vec[2:3, :]).astype(BF16)

        over_rows(first, count, body)

    def add_sums(at, rounded, along, shift):
        count, features = shift.shape
        for index, item in enumerate((rounded, along, shift)):
            acc[at + index, :, 0:features] += jnp.sum(item.reshape(count // 8, 8, features), 0)

    def back_rows(grad, normed_ref, inverse, vec, out, at, first, count, slope):
        features = normed_ref.shape[1]

        def body(rows):
            normed = normed_ref[rows, :].astype(F32)
            gain = vec[1:2, :]
            up = grad[rows, :]
            if slope:
                up = mish_slope(normed * gain + vec[2:3, :]) * up
            weighted = up * gain
            along = up * normed
            mean_one = jnp.sum(weighted, -1, keepdims=True) * (1.0 / features)
            mean_two = jnp.sum(weighted * normed, -1, keepdims=True) * (1.0 / features)
            result = (inverse[rows, :] * (weighted - mean_one - normed * mean_two)).astype(BF16)
            out[rows, :] = result
            add_sums(at, result.astype(F32), along, up)

        over_rows(first, count, body)

    def two_tiles(body):
        def step(index, carry):
            body(pl.ds(pl.multiple_of(index * half, 128), half))
            return carry

        lax.fori_loop(0, 2, step, 0)

    def layers_forward(to, source, vec_one, vec_two, keep_one, keep_two, inverse, hid_one, hid_two,
                       first, count, ready):
        rows = pl.ds(first, count)
        ready(0)

        def first_tile(cols):
            x1[rows, cols] = (
                mm(source[rows, 0:width], w1[to, :, cols])
                + mm(xbuf[rows, width : width + context_width], wc[to, :, cols])
                + vec_one[0:1, cols]
            )

        two_tiles(first_tile)
        norm_rows(x1, keep_one, inverse.at[0], vec_one, hid_one, first, count)
        ready(1)

        def second_tile(cols):
            x2[rows, cols] = mm(hid_one[rows, :], w2[to, :, cols]) + vec_two[0:1, cols]

        two_tiles(second_tile)
        norm_rows(x2, keep_two, inverse.at[1], vec_two, hid_two, first, count)

    def back_two_to_one(to, grad, first, count):
        rows = pl.ds(first, count)

        def tile(cols):
            upstream[rows, cols] = mm_t(grad[rows, :], w2[to, cols, :])

        two_tiles(tile)

    def ready_of(mine, others):
        def ready(stage):
            picked = (0, 1) if stage == 0 else (2,)
            for index in picked:
                mine[index].wait()
                others[index].wait_recv()

        return ready

    def nothing(stage):
        return None

    layers_forward(
        0, xbuf, dv1, dyn_vec2, dyn_x1, dyn_x2, dyn_inv, dyn_h1, dyn_h2, 0, rows_all,
        ready_of(dyn_ready, dyn_ready_other),
    )
    three_ready.wait()
    three_ready_other.wait_recv()
    x3[...] = mm(dyn_h2[...], dw3[...]) + dv3[0:1, :]
    group_row = lax.broadcasted_iota(jnp.int32, (128, 128), 0) // GROUP
    group_col = lax.broadcasted_iota(jnp.int32, (128, 128), 1) // GROUP
    ones = (group_row == group_col).astype(F32).astype(BF16)

    def simplex_rows(rows):
        values = x3[rows, :]
        centred = values - jnp.sum(values, -1, keepdims=True) * (1.0 / width)
        inv_rows = lax.rsqrt(
            jnp.sum(centred * centred, -1, keepdims=True) * (1.0 / width) + EPSILON
        )
        normed = centred * inv_rows
        x3[rows, :] = normed
        dyn_inv[2, rows, :] = inv_rows
        grown = jnp.exp(normed * dv3[1:2, :] + dv3[2:3, :])
        share = grown / gather_sum(grown, ones)
        simplex[rows, :] = share
        nxt[rows, :] = share.astype(BF16)

    over_rows(0, rows_all, simplex_rows)
    for copy in dyn_ready_other:
        sent(copy)
    pl.semaphore_signal(free_a, inc=1, device_id=to_core, device_id_type=mesh_id)
    extra_ready = load_weights(0, q_w1.at[last], q_wc.at[last], q_w2.at[last])
    next_copy = remote(nxt, nxto, to_core)
    tgt_copy.wait_recv()
    gap = nxt[0:slot, :].astype(F32) - tgt[...]
    own_g[...] = gap * (2.0 * scale)
    consistency = jnp.sum(gap * gap, -1, keepdims=True)
    pl.semaphore_wait(free_a, 1)
    extra_ready_other = send_weights(0, q_w1.at[last], q_wc.at[last], q_w2.at[last])

    def value_rows(head, first, count):
        rows = pl.ds(first, count)
        logits = mm(h2[rows, :], qw3[head]) + qb3[head]
        logits = logits - jnp.max(logits, -1, keepdims=True)
        grown = jnp.exp(logits)
        total = jnp.sum(grown, -1, keepdims=True)
        lane = lax.broadcasted_iota(jnp.int32, (count, bins), 1).astype(F32)
        facts = xbuf[rows, width : width + 128].astype(F32)
        lower = facts[:, context_width + 1 : context_width + 2]
        fraction = (
            facts[:, context_width + 2 : context_width + 3]
            + facts[:, context_width + 3 : context_width + 4]
            + facts[:, context_width + 4 : context_width + 5]
        )
        target = jnp.where(lane == lower, 1.0 - fraction, 0.0) + jnp.where(
            lane == lower + 1.0, fraction, 0.0
        )
        loss = -jnp.sum(target * (logits - jnp.log(total)), -1, keepdims=True) * (1.0 / heads)
        grad = (scale / heads * (grown / total - target)).astype(BF16)
        gl[rows, :] = grad

        def tile(cols):
            upstream[rows, cols] = mm_t(grad, qw3[head, cols, :])

        two_tiles(tile)
        acc[6, 0, 0:bins] += jnp.sum(grad.astype(F32), 0)
        return loss

    def table_sum(to, grad, first, count):
        rows = pl.ds(first, count)
        embed = mm_t(grad[rows, :], wc[to])
        ids = xbuf[rows, width : width + 128].astype(F32)[:, context_width : context_width + 1]
        task = lax.broadcasted_iota(jnp.int32, (count, tasks), 1).astype(F32)
        onehot = (ids == task).astype(F32).astype(BF16)
        top = embed.astype(BF16)
        rest = embed - top.astype(F32)
        middle = rest.astype(BF16)
        lowest = (rest - middle.astype(F32)).astype(BF16)
        tb[:, 0:context_width] += (
            t_mm(onehot, top) + t_mm(onehot, middle) + t_mm(onehot, lowest)
        )

    def finish_vectors(slot_at, width_three):
        for index in range(3):
            vb[slot_at, index : index + 1, :] = jnp.sum(acc[index], 0, keepdims=True)
            vb[slot_at, 3 + index : 4 + index, :] = jnp.sum(acc[3 + index], 0, keepdims=True)
        if width_three:
            three = [jnp.sum(acc[6 + index, :, 0:width], 0, keepdims=True) for index in range(3)]
            vb[slot_at, 6:7, 0:width] = three[0]
            vb[slot_at, 6:7, width : 2 * width] = three[1]
            vb[slot_at, 7:8, 0:width] = three[2]
        else:
            vb[slot_at, 6:7, :] = jnp.sum(acc[6], 0, keepdims=True)
        return remote(vb.at[slot_at], vbo.at[slot_at], to_core)

    def join_vectors(slot_at, copy):
        copy.wait_recv()
        sent(copy)
        vb[slot_at, 0:3, low] = vb[slot_at, 0:3, low] + vbo[slot_at, 0:3, high]
        vb[slot_at, 3:8, :] = vb[slot_at, 3:8, :] + vbo[slot_at, 3:8, :]
        return remote(vb.at[slot_at], vbx.at[slot_at], to_x)

    def plane_vectors(slot_at, copy):
        copy.wait_recv()
        sent(copy)
        vb[slot_at] = vb[slot_at] + vbx[slot_at]
        return remote(vb.at[slot_at], vby.at[slot_at], to_y)

    def total_vectors(slot_at, copy):
        copy.wait_recv()
        sent(copy)
        vb[slot_at] = vb[slot_at] + vby[slot_at]

    def scatter_start(source, target, x_first, lead):
        if lead is None:
            piece = source.at[:, 1 - at_x] if x_first else source.at[1 - at_y]
        else:
            piece = source.at[lead, :, 1 - at_x] if x_first else source.at[lead, 1 - at_y]
        return remote(piece, target, to_x if x_first else to_y)

    def scatter_middle(copy, source, received, target, x_first, lead):
        copy.wait_recv()
        if lead is None:
            for other in range(2):
                kept = source[other, at_x] if x_first else source[at_y, other]
                received[other] = (received[other].astype(F32) + kept.astype(F32)).astype(BF16)
            piece = received.at[1 - at_y] if x_first else received.at[1 - at_x]
        else:
            for index in range(lead.size):
                for other in range(2):
                    kept = (
                        source[lead.start + index, other, at_x]
                        if x_first
                        else source[lead.start + index, at_y, other]
                    )
                    received[index, other] = (
                        received[index, other].astype(F32) + kept.astype(F32)
                    ).astype(BF16)
            piece = received.at[:, 1 - at_y] if x_first else received.at[:, 1 - at_x]
        return remote(piece, target, to_y if x_first else to_x)

    def scatter_end(copy, received, target, x_first):
        copy.wait_recv()
        mine = at_y if x_first else at_x
        return received[mine].astype(F32) + target[...].astype(F32)

    def scatter_end_lead(copy, received, target, x_first, count):
        copy.wait_recv()
        mine = at_y if x_first else at_x
        for index in range(count):
            target[index] = (
                received[index, mine].astype(F32) + target[index].astype(F32)
            ).astype(BF16)

    first_half, second_half = pl.ds(0, 2), pl.ds(2, 2)

    acc[...] = jnp.zeros_like(acc)
    tb[...] = jnp.zeros_like(tb)
    main_three.wait()
    extra_three.wait()
    layers_forward(
        1, nxt, qv1.at[0], qv2.at[0], x1, x2, inv, h1, h2, 0, rows_all,
        ready_of(main_ready, main_ready_other),
    )
    main_loss = value_rows(0, 0, rows_all)
    back_rows(upstream, x2, inv.at[1], qv2.at[0], gp2, 3, 0, rows_all, True)
    factor_copies = [remote(gp2, gp2o, to_core), remote(h1.at[:, high], h1o, to_core)]
    back_two_to_one(1, gp2, 0, rows_all)
    for copy in factor_copies:
        copy.wait_recv()
    wide = half // 256 * 128 + 128
    for index in range(2):
        cols = slice(index * half, (index + 1) * half)
        for part in (slice(0, wide), slice(wide, half)):
            whole = t_mm(gp2[:, cols], h1[:, part]) + t_mm(gp2o[:, cols], h1o[:, part])
            p2[2 * index : 2 * index + 2, :, :, :, part] = whole.astype(BF16).reshape(
                (2, 2, 2, own_two, part.stop - part.start)
            )
    main_two_a = scatter_start(p2, r2.at[0:2], True, first_half)
    main_two_b = scatter_start(p2, r2.at[2:4], False, second_half)
    back_rows(upstream, x1, inv.at[0], qv1.at[0], gp1, 0, 0, rows_all, True)
    one_copy = remote(gp1.at[:, high], gp1o, to_core)
    dx = mm_t(gp1[...], w1[1])
    own_g[...] = own_g[...] + dx[0:slot]
    dxm[:, 0:width] = dx.astype(BF16)
    lane_all = lax.broadcasted_iota(jnp.int32, (rows_all, 128), 1)
    loss_high = main_loss.astype(BF16).astype(F32)
    loss_rest = main_loss - loss_high
    loss_middle = loss_rest.astype(BF16).astype(F32)
    loss_low = loss_rest - loss_middle
    dxm[:, width : width + 128] = jnp.where(
        lane_all == 0, loss_high, jnp.where(lane_all == 1, loss_middle, loss_low)
    ).astype(BF16)
    dx_copies = [
        remote(dxm.at[pl.ds(slot * k, slot)], dxr.at[k - 1], to_z[k]) for k in range(1, LINE)
    ]
    table_sum(1, gp1, 0, rows_all)
    for copy in main_ready_other:
        sent(copy)
    pl.semaphore_signal(free_b, inc=1, device_id=to_core, device_id_type=mesh_id)
    dyn_again = load_weights(1, dyn_w1, dyn_wc, dyn_w2)
    main_vec = finish_vectors(0, False)
    acc[...] = jnp.zeros_like(acc)
    next_copy.wait_recv()
    x_copy.wait_recv()
    one_copy.wait_recv()
    whole = t_mm(nxt[...], gp1[:, low]) + t_mm(nxto[...], gp1o[...])
    p1[...] = whole.astype(BF16).reshape(p1.shape)
    main_one_a = scatter_start(p1, r1.at[0:2], True, first_half)
    main_one_b = scatter_start(p1, r1.at[2:4], False, second_half)
    part = t_mm(h2[...], gl[...])
    p3[...] = part.astype(BF16).reshape(p3.shape)
    three_copy = remote(p3, p3o, to_core)

    def context_sum(at, grad):
        whole = t_mm(xbuf[:, width : width + 128], grad[:, low]) + t_mm(
            xother[:, width : width + 128], gp1o[...]
        )
        pc[at] = whole[0 : pc.shape[1]].astype(BF16)
        return remote(pc.at[at], pcx.at[at], to_x)

    def context_middle(at, copy):
        copy.wait_recv()
        sent(copy)
        pc[at] = (pc[at].astype(F32) + pcx[at].astype(F32)).astype(BF16)
        return remote(pc.at[at], pcy.at[at], to_y)

    def context_end(at, copy):
        copy.wait_recv()
        sent(copy)
        pc[at] = (pc[at].astype(F32) + pcy[at].astype(F32)).astype(BF16)

    main_context = context_sum(0, gp1)
    for copy in factor_copies + [one_copy]:
        sent(copy)
    pl.semaphore_signal(free_f, inc=1, device_id=to_core, device_id_type=mesh_id)
    pl.semaphore_wait(free_b, 1)
    dyn_again_other = send_weights(1, dyn_w1, dyn_wc, dyn_w2)

    layers_forward(
        0, nxt, qv1.at[1], qv2.at[1], x1, x2, inv, h1, h2, 0, slot,
        ready_of(extra_ready, extra_ready_other),
    )
    extra_loss = value_rows(1, 0, slot)
    back_rows(upstream, x2, inv.at[1], qv2.at[1], gp2, 3, 0, slot, True)
    back_two_to_one(0, gp2, 0, slot)
    back_rows(upstream, x1, inv.at[0], qv1.at[1], gp1, 0, 0, slot, True)
    own_total = own_g[...] + mm_t(gp1[0:slot, :], w1[0])
    value = main_loss[0:slot] + extra_loss
    for index, copy in enumerate(dx_copies):
        copy.wait_recv()
        message = dxr[index].astype(F32)
        own_total = own_total + message[:, 0:width]
        value = value + (
            message[:, width : width + 1]
            + message[:, width + 1 : width + 2]
            + message[:, width + 2 : width + 3]
        )
    all_g[0:slot, :] = own_total.astype(BF16)
    grad_copies = [
        remote(all_g.at[pl.ds(0, slot)], all_g.at[pl.ds(slot * k, slot)], to_z[k])
        for k in range(1, LINE)
    ]
    lane_own = lax.broadcasted_iota(jnp.int32, (slot, 128), 1)
    lossbuf[...] = jnp.where(lane_own == 0, consistency, value)
    loss_copies = [
        remote(lossbuf, out_losses.at[own_rows], to_core),
        local(lossbuf, out_losses.at[own_rows]),
    ]
    table_sum(0, gp1, 0, slot)
    rest = rows_all - slot
    layers_forward(
        0, nxt, qv1.at[1], qv2.at[1], x1, x2, inv, h1, h2, slot, rest, nothing
    )
    value_rows(1, slot, rest)
    back_rows(upstream, x2, inv.at[1], qv2.at[1], gp2, 3, slot, rest, True)
    pl.semaphore_wait(free_f, 1)
    factor_copies = [remote(gp2, gp2o, to_core), remote(h1.at[:, high], h1o, to_core)]
    back_two_to_one(0, gp2, slot, rest)
    back_rows(upstream, x1, inv.at[0], qv1.at[1], gp1, 0, slot, rest, True)
    one_copy = remote(gp1.at[:, high], gp1o, to_core)
    extra_vec = finish_vectors(1, False)
    acc[...] = jnp.zeros_like(acc)

    main_two_a = scatter_middle(main_two_a, p2, r2.at[0:2], t2.at[0:2], True, first_half)
    main_two_b = scatter_middle(main_two_b, p2, r2.at[2:4], t2.at[2:4], False, second_half)
    main_one_a = scatter_middle(main_one_a, p1, r1.at[0:2], t1.at[0:2], True, first_half)
    main_one_b = scatter_middle(main_one_b, p1, r1.at[2:4], t1.at[2:4], False, second_half)
    three_copy.wait_recv()
    sent(three_copy)
    p3[...] = (p3[...].astype(F32) + p3o[...].astype(F32)).astype(BF16)
    main_three_a = scatter_start(p3, r3.at[0:2], True, first_half)
    main_three_b = scatter_start(p3, r3.at[2:4], False, second_half)
    main_vec = join_vectors(0, main_vec)
    main_context = context_middle(0, main_context)

    def by_place(body):
        for index in range(LINE):
            @pl.when(at_z == index)
            def _(index=index):
                body(index)

    quarter = hidden // LINE
    quarter_w = width // LINE

    def quarter_two(index, hid):
        cols = slice(index * quarter, (index + 1) * quarter)
        whole = t_mm(gp2[:, cols], hid[:, low]) + t_mm(gp2o[:, cols], h1o[...])
        e2[...] = whole.astype(BF16).reshape(e2.shape)

    def quarter_one(index, mine, others):
        cols = slice(index * quarter_w, (index + 1) * quarter_w)
        whole = t_mm(mine[:, cols], gp1[:, low]) + t_mm(others[:, cols], gp1o[...])
        e1[...] = whole.astype(BF16).reshape(e1.shape)

    for copy in factor_copies + [one_copy]:
        copy.wait_recv()

    def extra_parts(index):
        quarter_two(index, h1)
        quarter_one(index, nxt, nxto)
        part = t_mm(h2[:, index * quarter : (index + 1) * quarter], gl[...])
        e3[...] = part.astype(BF16).reshape(e3.shape)

    by_place(extra_parts)
    extra_two = scatter_start(e2, er2, True, None)
    extra_one = scatter_start(e1, er1, False, None)
    extra_copy = remote(e3, e3o, to_core)
    extra_context = context_sum(1, gp1)
    for copy in factor_copies + [one_copy]:
        sent(copy)
    pl.semaphore_signal(free_f, inc=1, device_id=to_core, device_id_type=mesh_id)
    extra_vec = join_vectors(1, extra_vec)
    extra_copy.wait_recv()
    sent(extra_copy)
    e3[...] = (e3[...].astype(F32) + e3o[...].astype(F32)).astype(BF16)
    extra_three_sum = scatter_start(e3, er3, False, None)

    for copy in grad_copies:
        copy.wait_recv()

    def simplex_back(rows):
        share = simplex[rows, :]
        weighted = all_g[rows, :].astype(F32) * share
        up = weighted - share * gather_sum(weighted, ones)
        upstream[rows, 0:width] = up

    over_rows(0, rows_all, simplex_back)
    back_rows(
        upstream.at[:, 0:width], x3, dyn_inv.at[2], dv3, dyn_gp3, 6, 0, rows_all, False
    )

    def three_tile(cols):
        upstream[:, cols] = mm_t(dyn_gp3[...], dw3[cols, :])

    two_tiles(three_tile)
    back_rows(upstream, dyn_x2, dyn_inv.at[1], dyn_vec2, gp2, 3, 0, rows_all, True)
    pl.semaphore_wait(free_f, 1)
    factor_copies = [remote(gp2, gp2o, to_core), remote(dyn_h1.at[:, high], h1o, to_core)]
    for index in (2,):
        dyn_again[index].wait()
        dyn_again_other[index].wait_recv()
    back_two_to_one(1, gp2, 0, rows_all)
    back_rows(upstream, dyn_x1, dyn_inv.at[0], dv1, gp1, 0, 0, rows_all, True)
    one_copy = remote(gp1.at[:, high], gp1o, to_core)
    dyn_vec = finish_vectors(2, True)
    for index in (0, 1):
        dyn_again[index].wait()
        dyn_again_other[index].wait_recv()
    lat_g = tgt
    lat_g[...] = mm_t(gp1[0:slot, :], w1[1])
    latent_copies = [
        remote(lat_g.at[:, other_cols], out_latent.at[own_rows], to_core),
        local(lat_g.at[:, own_cols], out_latent.at[own_rows]),
    ]
    table_sum(1, gp1, 0, slot)
    table_copy = remote(tb, tbo, to_core)

    scatter_end_lead(main_two_a, r2.at[0:2], t2.at[0:2], True, 2)
    scatter_end_lead(main_two_b, r2.at[2:4], t2.at[2:4], False, 2)
    hand = [remote(t2.at[z_of[k]], out_qw2.at[at_z], to_z[k]) for k in range(1, LINE)]
    keep = [local(t2.at[at_z], out_qw2.at[at_z])]
    scatter_end_lead(main_one_a, r1.at[0:2], t1.at[0:2], True, 2)
    scatter_end_lead(main_one_b, r1.at[2:4], t1.at[2:4], False, 2)
    hand += [remote(t1.at[z_of[k]], out_qw1.at[at_z], to_z[k]) for k in range(1, LINE)]
    keep += [local(t1.at[at_z], out_qw1.at[at_z])]
    for copy in factor_copies + [one_copy]:
        copy.wait_recv()

    def dyn_parts(index):
        quarter_two(index, dyn_h1)
        quarter_one(index, xbuf, xother)
        left = dyn_h2[:, index * quarter : (index + 1) * quarter]
        d3s[...] = t_mm(left, dyn_gp3[:, other_cols]).astype(BF16).reshape(d3s.shape)
        d3[...] = t_mm(left, dyn_gp3[:, own_cols]).astype(BF16).reshape(d3.shape)

    extra_two2 = scatter_middle(extra_two, e2, er2, et2, True, None)
    extra_one2 = scatter_middle(extra_one, e1, er1, et1, False, None)
    sent(extra_two)
    sent(extra_one)
    by_place(dyn_parts)
    dyn_two_sum = scatter_start(e2, er2b, True, None)
    d3_copy = remote(d3s, d3o, to_core)
    dyn_one_sum = scatter_start(e1, er1b, False, None)
    dyn_context = context_sum(2, gp1)
    d3_copy.wait_recv()
    d3[...] = (d3[...].astype(F32) + d3o[...].astype(F32)).astype(BF16)
    dyn_three_sum = scatter_start(d3, er3b, False, None)
    dyn_vec = join_vectors(2, dyn_vec)
    table_copy.wait_recv()
    sent(table_copy)
    tb[...] = tb[...] + tbo[...]
    table_copy = remote(tb, tbr.at[0], to_x)

    main_three_a = scatter_middle(main_three_a, p3, r3.at[0:2], t3.at[0:2], True, first_half)
    main_three_b = scatter_middle(main_three_b, p3, r3.at[2:4], t3.at[2:4], False, second_half)
    extra_three2 = scatter_middle(extra_three_sum, e3, er3, et3, False, None)
    main_vec = plane_vectors(0, main_vec)
    extra_vec = plane_vectors(1, extra_vec)
    context_end(0, main_context)
    hand += [remote(pc.at[0], out_qwc.at[at_z], to_z[k]) for k in range(1, LINE)]
    keep += [local(pc.at[0], out_qwc.at[at_z])]
    extra_context = context_middle(1, extra_context)
    total_vectors(0, main_vec)
    hand += [remote(vb.at[0], out_qvec.at[at_z], to_z[k]) for k in range(1, LINE)]
    keep += [local(vb.at[0], out_qvec.at[at_z])]
    total_vectors(1, extra_vec)
    keep += [local(vb.at[1], out_qvec.at[last])]
    dyn_vec = plane_vectors(2, dyn_vec)
    table_copy.wait_recv()
    sent(table_copy)
    tb[...] = tb[...] + tbr[0]
    table_copy = remote(tb, tbr.at[1], to_y)
    et2[...] = scatter_end(extra_two2, er2, et2, True).astype(BF16)
    keep += [local(et2, out_qw2.at[last])]
    et1[...] = scatter_end(extra_one2, er1, et1, False).astype(BF16)
    keep += [local(et1, out_qw1.at[last])]
    dyn_two2 = scatter_middle(dyn_two_sum, e2, er2b, et2b, True, None)
    dyn_one2 = scatter_middle(dyn_one_sum, e1, er1b, et1b, False, None)
    dyn_three2 = scatter_middle(dyn_three_sum, d3, er3b, et3b, False, None)
    dyn_context = context_middle(2, dyn_context)
    scatter_end_lead(main_three_a, r3.at[0:2], t3.at[0:2], True, 2)
    scatter_end_lead(main_three_b, r3.at[2:4], t3.at[2:4], False, 2)
    hand += [remote(t3.at[z_of[k]], out_qw3.at[at_z], to_z[k]) for k in range(1, LINE)]
    keep += [local(t3.at[at_z], out_qw3.at[at_z])]
    et3[...] = scatter_end(extra_three2, er3, et3, False).astype(BF16)
    keep += [local(et3, out_qw3.at[last])]
    table_copy.wait_recv()
    sent(table_copy)
    tb[...] = tb[...] + tbr[1]
    table_copies = [remote(tb, tbr.at[1 + k], to_z[k]) for k in range(1, LINE)]
    context_end(1, extra_context)
    keep += [local(pc.at[1], out_qwc.at[last])]
    total_vectors(2, dyn_vec)
    keep += [local(vb.at[2], out_dvec)]
    out3 = jnp.concatenate(
        [
            vb[2, 6:7, own_cols],
            vb[2, 6:7, pl.ds(pl.multiple_of(width + half_w * core, 128), half_w)],
            vb[2, 7:8, own_cols],
        ],
        0,
    )
    o3[0:3, :] = out3
    keep += [local(o3, out_dvec3)]
    o2 = upstream.at[0:own_two, 0:half]
    o1 = upstream.at[own_two : own_two + own_one, 0:half]
    oc = upstream.at[0:own_two, half : half + half_w]
    o2[...] = scatter_end(dyn_two2, er2b, et2b, True)
    keep += [local(o2, out_dw2)]
    o1[...] = scatter_end(dyn_one2, er1b, et1b, False)
    keep += [local(o1, out_dw1)]
    oc[...] = scatter_end(dyn_three2, er3b, et3b, False)
    keep += [local(oc, out_dw3)]
    context_end(2, dyn_context)
    keep += [local(pc.at[2], out_dwc)]
    for copy in table_copies:
        copy.wait_recv()
        sent(copy)
    tb[...] = tb[...] + tbr[2] + tbr[3] + tbr[4]
    keep += [local(tb, out_table)]
    for copy in hand + [loss_copies[0], latent_copies[0]]:
        copy.wait_recv()
    for copy in keep + [loss_copies[1], latent_copies[1]]:
        copy.wait()
    for copy in list(pending):
        sent(copy)


def line_shards(
    latent,
    action,
    task_ids,
    action_mask,
    task_table,
    target_latent,
    bin_lower,
    bin_frac,
    dyn_w1,
    dyn_wc,
    dyn_vec1,
    dyn_w2,
    dyn_vec2,
    dyn_w3,
    dyn_vec3,
    q_w1,
    q_wc,
    q_vec1,
    q_w2,
    q_vec2,
    q_w3,
    q_b3,
):
    local_rows, half_w = latent.shape
    slot = local_rows // 2
    rows = slot * LINE
    width = 2 * half_w
    half = dyn_w1.shape[1]
    hidden = 2 * half
    heads, bins = q_b3.shape
    tasks, acts = action_mask.shape
    context_width = dyn_wc.shape[0]
    pad_context = -(-context_width // 16) * 16
    own_two = hidden // BLOCK
    own_one = width // BLOCK
    scale = 1.0 / math.sqrt(local_rows * lax.axis_size("dp"))
    sizes = (slot, width, hidden, bins, tasks, acts, context_width, heads)

    fraction = bin_frac[:, None]
    piece_one = lax.reduce_precision(fraction, 8, 7)
    piece_two = lax.reduce_precision(fraction - piece_one, 8, 7)
    meta = jnp.concatenate(
        [
            action.astype(F32),
            jnp.ones((local_rows, context_width - acts), F32),
            task_ids.astype(F32)[:, None],
            bin_lower.astype(F32)[:, None],
            piece_one,
            piece_two,
            fraction - piece_one - piece_two,
            jnp.zeros((local_rows, 128 - context_width - 5), F32),
        ],
        1,
    )
    table = jnp.concatenate(
        [
            action_mask.astype(BF16),
            task_table,
            jnp.zeros((tasks, 128 - context_width), BF16),
        ],
        1,
    )

    def shape(*dims, kind=F32):
        return jax.ShapeDtypeStruct(dims, kind)

    out_shape = (
        shape(local_rows, 128),
        shape(local_rows, half_w),
        shape(tasks, 128),
        shape(own_one, half),
        shape(pad_context, half, kind=BF16),
        shape(8, hidden),
        shape(8, half_w),
        shape(own_two, half),
        shape(own_two, half_w),
        shape(heads, own_one, half, kind=BF16),
        shape(heads, pad_context, half, kind=BF16),
        shape(heads, 8, hidden),
        shape(heads, own_two, half, kind=BF16),
        shape(heads, own_two, bins, kind=BF16),
    )
    v = pltpu.VMEM
    scratch = [
        v((2, width, hidden), BF16),
        v((2, context_width, hidden), BF16),
        v((2, hidden, hidden), BF16),
        v((hidden, width), BF16),
        v((2, hidden, bins), BF16),
        v((3, hidden), F32),
        v((3, width), F32),
        v((2, 3, hidden), F32),
        v((2, 3, hidden), F32),
        v((2, 1, bins), F32),
        v((rows, width + 128), BF16),
        v((rows, width + 128), BF16),
        v((slot, width), F32),
        v((rows, width), BF16),
        v((rows, width), BF16),
        v((rows, hidden), BF16),
        v((rows, hidden), BF16),
        v((rows, hidden), BF16),
        v((rows, hidden), BF16),
        v((rows, width), F32),
        v((rows, width), F32),
        v((3, rows, 1), F32),
        v((rows, hidden), F32),
        v((rows, hidden), F32),
        v((2, rows, 1), F32),
        v((rows, hidden), BF16),
        v((rows, hidden), BF16),
        v((rows, hidden), BF16),
        v((rows, hidden), BF16),
        v((rows, half), BF16),
        v((rows, hidden), BF16),
        v((rows, half), BF16),
        v((rows, hidden), F32),
        v((rows, bins), BF16),
        v((rows, width), BF16),
        v((9, 8, hidden), F32),
        v((rows, width + 128), BF16),
        v((LINE - 1, slot, width + 128), BF16),
        v((slot, width), F32),
        v((rows, width), BF16),
        v((slot, 128), F32),
        v((LINE, 2, 2, own_two, half), BF16),
        v((LINE, 2, own_two, half), BF16),
        v((LINE, own_two, half), BF16),
        v((LINE, 2, 2, own_one, half), BF16),
        v((LINE, 2, own_one, half), BF16),
        v((LINE, own_one, half), BF16),
        v((LINE, 2, 2, own_two, bins), BF16),
        v((LINE, 2, own_two, bins), BF16),
        v((LINE, own_two, bins), BF16),
        v((LINE, 2, 2, own_two, bins), BF16),
        v((2, 2, own_two, half), BF16),
        v((2, own_two, half), BF16),
        v((own_two, half), BF16),
        v((2, 2, own_one, half), BF16),
        v((2, own_one, half), BF16),
        v((own_one, half), BF16),
        v((2, 2, own_two, bins), BF16),
        v((2, own_two, bins), BF16),
        v((own_two, bins), BF16),
        v((2, 2, own_two, bins), BF16),
        v((2, own_two, half), BF16),
        v((own_two, half), BF16),
        v((2, own_one, half), BF16),
        v((own_one, half), BF16),
        v((2, 2, own_two, half_w), BF16),
        v((2, 2, own_two, half_w), BF16),
        v((2, 2, own_two, half_w), BF16),
        v((2, own_two, half_w), BF16),
        v((own_two, half_w), BF16),
        v((3, pad_context, half), BF16),
        v((3, pad_context, half), BF16),
        v((3, pad_context, half), BF16),
        v((3, 8, hidden), F32),
        v((3, 8, hidden), F32),
        v((3, 8, hidden), F32),
        v((3, 8, hidden), F32),
        v((tasks, 128), F32),
        v((tasks, 128), F32),
        v((5, tasks, 128), F32),
        v((8, half_w), F32),
        pltpu.SemaphoreType.DMA((REMOTE_COPIES,)),
        pltpu.SemaphoreType.DMA((REMOTE_COPIES,)),
        pltpu.SemaphoreType.DMA((LOCAL_COPIES,)),
        pltpu.SemaphoreType.REGULAR,
        pltpu.SemaphoreType.REGULAR,
        pltpu.SemaphoreType.REGULAR,
    ]
    inside = pl.BlockSpec(memory_space=pltpu.VMEM)
    outside = pl.BlockSpec(memory_space=pl.ANY)
    (
        losses, latent_grad, table_grad, dyn_w1_grad, dyn_wc_grad, dyn_vecs, dyn_vec3_grad,
        dyn_w2_grad, dyn_w3_grad, q_w1_grad, q_wc_grad, q_vecs, q_w2_grad, q_w3_grad,
    ) = pl.pallas_call(
        functools.partial(line_kernel, sizes, scale),
        out_shape=out_shape,
        in_specs=[inside] * 10 + [outside] * 8,
        out_specs=[outside] * len(out_shape),
        scratch_shapes=scratch,
        compiler_params=pltpu.CompilerParams(
            collective_id=0, has_side_effects=True, vmem_limit_bytes=VMEM_BYTES
        ),
        cost_estimate=pl.CostEstimate(
            flops=2 * 10**10, bytes_accessed=6 * 10**7, transcendentals=10**7
        ),
        name="line_update",
    )(
        latent, meta, table, target_latent, dyn_vec1, dyn_vec2, dyn_vec3, q_vec1, q_vec2, q_b3,
        dyn_w1, dyn_wc, dyn_w2, dyn_w3, q_w1, q_wc, q_w2, q_w3,
    )
    return (
        losses[:, :2],
        latent_grad,
        table_grad[:, acts:context_width],
        dyn_w1_grad,
        dyn_wc_grad[:context_width].astype(F32),
        dyn_vecs[0:3, :half],
        dyn_w2_grad.transpose(1, 0),
        dyn_vecs[3:6],
        dyn_w3_grad,
        dyn_vec3_grad[0:3],
        q_w1_grad.astype(F32),
        q_wc_grad[:, :context_width].astype(F32),
        q_vecs[:, 0:3, :half],
        q_w2_grad.astype(F32).transpose(0, 2, 1),
        q_vecs[:, 3:6],
        q_w3_grad.astype(F32),
        q_vecs[:, 6, :bins],
    )


def shards(*arrays):
    if lax.axis_size("dp") == BLOCK:
        return line_shards(*arrays)
    return general_shards(*arrays)


def solution(mesh):
    return jax.shard_map(
        shards,
        mesh=mesh,
        in_specs=(
            P("dp", "tensor"),
            P("dp", None),
            P("dp"),
            P(),
            P(),
            P("dp", "tensor"),
            P("dp"),
            P("dp"),
            P(None, "tensor"),
            P(None, "tensor"),
            P(None, "tensor"),
            P("tensor", None),
            P(),
            P(None, "tensor"),
            P(None, "tensor"),
            P(None, None, "tensor"),
            P(None, None, "tensor"),
            P(None, None, "tensor"),
            P(None, "tensor", None),
            P(),
            P(),
            P(),
        ),
        out_specs=(
            P("dp", None),
            P("dp", "tensor"),
            P(),
            P("dp", "tensor"),
            P(None, "tensor"),
            P(None, "tensor"),
            P("tensor", "dp"),
            P(),
            P("dp", "tensor"),
            P(None, "tensor"),
            P(None, "dp", "tensor"),
            P(None, None, "tensor"),
            P(None, None, "tensor"),
            P(None, "tensor", "dp"),
            P(),
            P(None, "dp", None),
            P(),
        ),
        check_vma=False,
    )
```

```python
import functools
import math

import jax
import jax.numpy as jnp
from jax import lax
from jax.experimental import pallas as pl
from jax.experimental.pallas import tpu as pltpu
from jax.sharding import PartitionSpec as P

GROUP = 8
LINE = 4
PLANE = 4
BLOCK = LINE * PLANE
EPSILON = 1e-05
HIGHEST = lax.Precision.HIGHEST
F32 = jnp.float32
BF16 = jnp.bfloat16
REMOTE_COPIES = 144
LOCAL_COPIES = 48
VMEM_BYTES = 63 << 20


def swap_core(values):
    return lax.ppermute(values, "tensor", [(0, 1), (1, 0)])


def swap_dp(values, bit):
    size = lax.axis_size("dp")
    return lax.ppermute(values, "dp", [(place, place ^ bit) for place in range(size)])


def pick(values, index, axis=0):
    return lax.dynamic_index_in_dim(values, index, axis, keepdims=False)


def own_then_other(values):
    return values, swap_core(values)


def mish_parts(values):
    grown = jnp.exp(jnp.minimum(values, 20.0))
    top = grown * (grown + 2.0)
    share = 1.0 / (top + 2.0)
    return grown, top * share, share


def mish(values):
    return values * mish_parts(values)[1]


def mish_slope(values):
    grown, ratio, share = mish_parts(values)
    return ratio + 4.0 * values * grown * (1.0 + grown) * share * share


def norm(before, gain, shift):
    centred = before - jnp.mean(before, -1, keepdims=True)
    inverse = lax.rsqrt(jnp.mean(centred * centred, -1, keepdims=True) + EPSILON)
    normed = centred * inverse
    return normed * gain + shift, normed, inverse


def norm_back(upstream, normed, inverse, gain):
    weighted = upstream * gain
    return inverse * (
        weighted
        - jnp.mean(weighted, -1, keepdims=True)
        - normed * jnp.mean(weighted * normed, -1, keepdims=True)
    )


def vector_sums(rounded, upstream, normed):
    return jnp.stack(
        [jnp.sum(rounded.astype(F32), 0), jnp.sum(upstream * normed, 0), jnp.sum(upstream, 0)]
    )


def mm(left, right):
    return jnp.dot(left, right, preferred_element_type=F32)


def mm_t(left, right):
    return lax.dot_general(left, right, (((1,), (1,)), ((), ())), preferred_element_type=F32)


def t_mm(left, right):
    return lax.dot_general(left, right, (((0,), (0,)), ((), ())), preferred_element_type=F32)


def block_forward(inputs, context, w_one, w_context, vec_one, w_two, vec_two):
    before = mm(inputs, w_one) + mm(context, w_context) + vec_one[0:1]
    out_one, normed_one, inverse_one = norm(before, vec_one[1:2], vec_one[2:3])
    hidden_one = mish(out_one).astype(BF16)
    second = mm(hidden_one, w_two) + vec_two[0:1]
    out_two, normed_two, inverse_two = norm(second, vec_two[1:2], vec_two[2:3])
    hidden_two = mish(out_two).astype(BF16)
    return hidden_one, hidden_two, (normed_one, inverse_one, normed_two, inverse_two)


def block_backward(grad_hidden, saved, vec_one, w_two, vec_two):
    normed_one, inverse_one, normed_two, inverse_two = saved
    upstream = mish_slope(normed_two * vec_two[1:2] + vec_two[2:3]) * grad_hidden
    grad_two = norm_back(upstream, normed_two, inverse_two, vec_two[1:2]).astype(BF16)
    sums_two = vector_sums(grad_two, upstream, normed_two)
    grad_one_hidden = mm_t(grad_two, w_two)
    upstream = mish_slope(normed_one * vec_one[1:2] + vec_one[2:3]) * grad_one_hidden
    grad_one = norm_back(upstream, normed_one, inverse_one, vec_one[1:2]).astype(BF16)
    sums_one = vector_sums(grad_one, upstream, normed_one)
    return grad_two, sums_two, grad_one, sums_one


def dynamics_forward(inputs, context, w_one, w_context, vec_one, w_two, vec_two, w_three, vec_three):
    hidden_one, hidden_two, saved = block_forward(
        inputs, context, w_one, w_context, vec_one, w_two, vec_two
    )
    before = mm(hidden_two, w_three) + vec_three[0:1]
    out, normed, inverse = norm(before, vec_three[1:2], vec_three[2:3])
    grouped = out.reshape(out.shape[0], -1, GROUP)
    simplex = jax.nn.softmax(grouped, axis=-1).reshape(out.shape)
    return hidden_one, hidden_two, saved, simplex, normed, inverse


def dynamics_backward(grad_next, simplex, normed, inverse, saved, w_three, vec_three, vec_one, w_two, vec_two):
    weighted = grad_next * simplex
    rows = weighted.shape[0]
    along = jnp.sum(weighted.reshape(rows, -1, GROUP), -1, keepdims=True)
    along = jnp.broadcast_to(along, (rows, along.shape[1], GROUP)).reshape(weighted.shape)
    upstream = weighted - simplex * along
    grad_three = norm_back(upstream, normed, inverse, vec_three[1:2]).astype(BF16)
    sums_three = vector_sums(grad_three, upstream, normed)
    grad_hidden = mm_t(grad_three, w_three)
    grad_two, sums_two, grad_one, sums_one = block_backward(
        grad_hidden, saved, vec_one, w_two, vec_two
    )
    return grad_three, sums_three, grad_two, sums_two, grad_one, sums_one


def value_head(hidden_two, w_three, bias, lower, fraction, scale, heads):
    logits = mm(hidden_two, w_three) + bias
    log_prob = jax.nn.log_softmax(logits, axis=-1)
    bins = jnp.arange(logits.shape[-1], dtype=jnp.int32)[None, :]
    target = jnp.where(bins == lower, 1.0 - fraction, 0.0) + jnp.where(
        bins == lower + 1, fraction, 0.0
    )
    loss = -jnp.sum(target * log_prob, -1) / heads
    grad_logits = (scale / heads * (jnp.exp(log_prob) - target)).astype(BF16)
    return loss, grad_logits


def spread(values, axis_len):
    blocks = lax.axis_size("dp") // BLOCK
    rows = values.shape[0] // (blocks * BLOCK)
    values = values.reshape((blocks, LINE, 2, 2, rows) + values.shape[1:])
    if blocks > 1:
        values = jnp.moveaxis(values, 0, 3)
    return values.reshape((LINE, 2, 2, blocks * rows) + values.shape[5:])


def across_blocks(values, axis):
    blocks = lax.axis_size("dp") // BLOCK
    if blocks == 1:
        return values
    groups = [[block * BLOCK + place for block in range(blocks)] for place in range(BLOCK)]
    return lax.psum_scatter(
        values, "dp", scatter_dimension=axis, axis_index_groups=groups, tiled=True
    )


def sum_across_blocks(values):
    blocks = lax.axis_size("dp") // BLOCK
    if blocks == 1:
        return values
    groups = [[block * BLOCK + place for block in range(blocks)] for place in range(BLOCK)]
    return lax.psum(values, "dp", axis_index_groups=groups)


def reduce_first(values, axis_x, bit_x, at_x, axis_y, bit_y, at_y):
    sent = pick(values, 1 - at_x, axis_x).astype(BF16)
    total = pick(values, at_x, axis_x) + swap_dp(sent, bit_x).astype(F32)
    if axis_y > axis_x:
        axis_y -= 1
    sent = pick(total, 1 - at_y, axis_y).astype(BF16)
    return pick(total, at_y, axis_y) + swap_dp(sent, bit_y).astype(F32)


def plane_scatter(values, at_x, at_y):
    half = LINE // 2
    first = reduce_first(values[:half], 2, 1, at_x, 1, 2, at_y)
    second = reduce_first(values[half:], 1, 2, at_y, 2, 1, at_x)
    return jnp.concatenate([first, second], 0)


def plane_scatter_one(values, at_x, at_y):
    half = values.shape[-1] // 256 * 128
    if half == 0:
        return reduce_first(values, 1, 1, at_x, 0, 2, at_y)
    first = reduce_first(values[..., :half], 1, 1, at_x, 0, 2, at_y)
    second = reduce_first(values[..., half:], 0, 2, at_y, 1, 1, at_x)
    return jnp.concatenate([first, second], -1)


def line_exchange(values, at_z, last):
    out = jnp.zeros((LINE + 1,) + values.shape[1:], F32)
    for step in range(LINE):
        part = pick(values, at_z ^ step)
        if step:
            part = swap_dp(part.astype(BF16), 4 * step).astype(F32)
        out = lax.dynamic_update_index_in_dim(out, part, at_z ^ step, 0)
    return lax.dynamic_update_index_in_dim(out, last, LINE, 0)


def plane_total(values, kind=F32):
    values = values + swap_dp(values.astype(kind), 1).astype(F32)
    return values + swap_dp(values.astype(kind), 2).astype(F32)


def line_collect(values, at_z, last, kind=F32):
    out = jnp.zeros((LINE + 1,) + values.shape, F32)
    sent = values.astype(kind)
    for step in range(LINE):
        part = swap_dp(sent, 4 * step).astype(F32) if step else values
        out = lax.dynamic_update_index_in_dim(out, part, at_z ^ step, 0)
    return lax.dynamic_update_index_in_dim(out, last, LINE, 0)


def line_total(values):
    total = values
    for step in range(1, LINE):
        total = total + swap_dp(values, 4 * step)
    return total


def in_core_order(core, own, other, axis):
    return jnp.where(
        core == 0, jnp.concatenate([own, other], axis), jnp.concatenate([other, own], axis)
    )


def general_shards(
    latent,
    action,
    task_ids,
    action_mask,
    task_table,
    target_latent,
    bin_lower,
    bin_frac,
    dyn_w1,
    dyn_wc,
    dyn_vec1,
    dyn_w2,
    dyn_vec2,
    dyn_w3,
    dyn_vec3,
    q_w1,
    q_wc,
    q_vec1,
    q_w2,
    q_vec2,
    q_w3,
    q_b3,
):
    place = lax.axis_index("dp")
    core = lax.axis_index("tensor")
    at_x, at_y, at_z = place % 2, place // 2 % 2, place // 4 % 4
    local_rows = latent.shape[0]
    half_rows = local_rows // 2
    half_latent = latent.shape[1]
    half_hidden = dyn_w1.shape[1]
    inv_root = 1.0 / math.sqrt(local_rows * lax.axis_size("dp"))
    task_count = task_table.shape[0]
    heads = q_w1.shape[0]
    head_places = (at_z, heads - 1)

    def both(values, axis):
        return jnp.concatenate(own_then_other(values), axis)

    dyn_w1_all, dyn_wc_all, dyn_vec1_all = both(dyn_w1, 1), both(dyn_wc, 1), both(dyn_vec1, 1)
    dyn_w2_all = both(dyn_w2, 0)
    dyn_w3_all = in_core_order(core, *own_then_other(dyn_w3), 1)
    dyn_vec3_all = in_core_order(core, *own_then_other(dyn_vec3), 1)
    head_weights = []
    for head in head_places:
        head_weights.append(
            (
                both(pick(q_w1, head), 1),
                both(pick(q_wc, head), 1),
                both(pick(q_vec1, head), 1),
                both(pick(q_w2, head), 0),
                pick(q_vec2, head),
                pick(q_w3, head),
                pick(q_b3, head),
            )
        )

    def my_rows(values):
        return lax.dynamic_slice_in_dim(values, core * half_rows, half_rows, 0)

    def their_rows(values):
        return lax.dynamic_slice_in_dim(values, (1 - core) * half_rows, half_rows, 0)

    def whole_columns(values):
        return in_core_order(core, my_rows(values), swap_core(their_rows(values)), 1)

    my_latent = whole_columns(latent)
    my_target = whole_columns(target_latent)
    my_ids = my_rows(task_ids)[:, None]
    onehot = (my_ids == jnp.arange(task_count, dtype=jnp.int32)[None, :]).astype(BF16)
    table = jnp.concatenate([action_mask.astype(BF16), task_table], 1)
    looked_up = mm(onehot, table)
    acts = action.shape[1]
    acted = my_rows(action).astype(F32) * looked_up[:, :acts]
    my_context = jnp.concatenate([acted, looked_up[:, acts:]], 1).astype(BF16)
    fraction = my_rows(bin_frac)[:, None]
    piece_one = lax.reduce_precision(fraction, 8, 7)
    piece_two = lax.reduce_precision(fraction - piece_one, 8, 7)
    piece_three = fraction - piece_one - piece_two
    meta = [my_ids, my_rows(bin_lower)[:, None], piece_one, piece_two, piece_three]
    meta = [item.astype(BF16) for item in meta]
    width = my_latent.shape[1]
    context_width = my_context.shape[1]
    packed = jnp.concatenate([my_latent, my_context] + meta, 1)
    packed = jnp.concatenate([packed] + [swap_dp(packed, 4 * step) for step in range(1, LINE)], 0)
    inputs = packed[:, :width]
    context = packed[:, width : width + context_width]
    meta = packed[:, width + context_width :].astype(F32)
    all_ids = meta[:, 0:1].astype(jnp.int32)
    lower = meta[:, 1:2].astype(jnp.int32)
    fraction = meta[:, 2:3] + meta[:, 3:4] + meta[:, 4:5]
    all_onehot = (all_ids == jnp.arange(task_count, dtype=jnp.int32)[None, :]).astype(F32)
    other_inputs, other_context = swap_core(inputs), swap_core(context)

    dyn_one, dyn_two, dyn_saved, simplex, normed_three, inverse_three = dynamics_forward(
        inputs, context, dyn_w1_all, dyn_wc_all, dyn_vec1_all, dyn_w2_all, dyn_vec2,
        dyn_w3_all, dyn_vec3_all,
    )
    next_low = simplex.astype(BF16)
    mismatch = next_low[:half_rows].astype(F32) - my_target
    consistency = jnp.sum(mismatch * mismatch, -1)
    other_next = swap_core(next_low)

    head_results = []
    for weights in head_weights:
        w_one, w_context, vec_one, w_two, vec_two, w_three, bias = weights
        hidden_one, hidden_two, saved = block_forward(
            next_low, context, w_one, w_context, vec_one, w_two, vec_two
        )
        loss, grad_logits = value_head(
            hidden_two, w_three, bias[None], lower, fraction, inv_root, heads
        )
        grad_hidden = mm_t(grad_logits, w_three)
        grad_two, sums_two, grad_one, sums_one = block_backward(
            grad_hidden, saved, vec_one, w_two, vec_two
        )
        head_results.append(
            (hidden_one, hidden_two, loss, grad_logits, grad_two, sums_two, grad_one, sums_one)
        )

    main, extra = head_results
    grad_in = mm_t(main[6], head_weights[0][0])
    own_grad = grad_in[:half_rows] + mm_t(extra[6][:half_rows], head_weights[1][0])
    own_loss = main[2][:half_rows] + extra[2][:half_rows]
    for step in range(1, LINE):
        part = slice(step * half_rows, (step + 1) * half_rows)
        own_grad = own_grad + swap_dp(grad_in[part].astype(BF16), 4 * step).astype(F32)
        own_loss = own_loss + swap_dp(main[2][part], 4 * step)
    own_grad = own_grad + 2.0 * inv_root * mismatch
    own_low = own_grad.astype(BF16)
    grad_next = jnp.concatenate(
        [own_low] + [swap_dp(own_low, 4 * step) for step in range(1, LINE)], 0
    ).astype(F32)
    my_losses = jnp.stack([consistency, own_loss], 1)
    losses = in_core_order(core, my_losses, swap_core(my_losses), 0)

    grad_three, sums_three, dyn_grad_two, dyn_sums_two, dyn_grad_one, dyn_sums_one = (
        dynamics_backward(
            grad_next, simplex, normed_three, inverse_three, dyn_saved, dyn_w3_all, dyn_vec3_all,
            dyn_vec1_all, dyn_w2_all, dyn_vec2,
        )
    )
    own_latent_grad = mm_t(dyn_grad_one[:half_rows], dyn_w1_all)
    left, right = own_latent_grad[:, :half_latent], own_latent_grad[:, half_latent:]
    kept = jnp.where(core == 0, left, right)
    received = swap_core(jnp.where(core == 0, right, left))
    latent_grad = in_core_order(core, kept, received, 0)

    def own_half(values):
        return jnp.concatenate([values[:, :half_hidden], swap_core(values[:, half_hidden:])], 0)

    def all_rows(values):
        return jnp.concatenate([values, swap_core(values)], 0)

    def quarter(values, size):
        blocks = lax.axis_size("dp") // BLOCK
        cut = values.reshape(values.shape[0], blocks, LINE, size // (blocks * LINE))
        return pick(cut, at_z, 2).reshape(values.shape[0], size // LINE)

    def spread_quarter(values):
        blocks = lax.axis_size("dp") // BLOCK
        rows = values.shape[0] // (blocks * PLANE)
        values = values.reshape((blocks, 2, 2, rows) + values.shape[1:])
        if blocks > 1:
            values = jnp.moveaxis(values, 0, 2)
        return values.reshape((2, 2, blocks * rows) + values.shape[4:])

    both_next = jnp.concatenate([next_low, other_next], 0)
    both_inputs = jnp.concatenate([inputs, other_inputs], 0)
    both_context = jnp.concatenate([context, other_context], 0)
    features = both_next.shape[1]
    hidden = 2 * half_hidden

    def quarter_grads(hidden_one, grad_two, grad_one, rows_in):
        first_factor, grad_factor = own_half(hidden_one), own_half(grad_one)
        w_two_part = t_mm(all_rows(quarter(grad_two, hidden)), first_factor)
        w_one_part = t_mm(quarter(rows_in, features), grad_factor)
        w_context_part = t_mm(both_context, grad_factor)
        return (
            plane_scatter_one(spread_quarter(w_two_part), at_x, at_y),
            plane_scatter_one(spread_quarter(w_one_part), at_x, at_y),
            plane_total(w_context_part, BF16),
        )

    def outer_quarter(left, right):
        part = t_mm(quarter(left, hidden), right)
        return plane_scatter_one(spread_quarter(part), at_x, at_y)

    first_factor, grad_factor = own_half(main[0]), own_half(main[6])
    main_two = plane_scatter(spread(t_mm(all_rows(main[4]), first_factor), 0), at_x, at_y)
    main_one = plane_scatter(spread(t_mm(both_next, grad_factor), 0), at_x, at_y)
    main_three = plane_scatter(spread(t_mm(main[1], main[3]), 0), at_x, at_y)
    main_context = plane_total(t_mm(both_context, grad_factor), BF16)
    extra_two, extra_one, extra_context = quarter_grads(extra[0], extra[4], extra[6], both_next)
    extra_three = outer_quarter(extra[1], extra[3])
    dyn_w2_part, dyn_w1_part, dyn_context = quarter_grads(
        dyn_one, dyn_grad_two, dyn_grad_one, both_inputs
    )
    dyn_w3_part = outer_quarter(
        all_rows(dyn_two),
        jnp.concatenate(
            [
                jnp.where(core == 0, grad_three[:, :half_latent], grad_three[:, half_latent:]),
                swap_core(
                    jnp.where(core == 0, grad_three[:, half_latent:], grad_three[:, :half_latent])
                ),
            ],
            0,
        ),
    )

    q_w2_out = across_blocks(line_exchange(main_two, at_z, extra_two), 1).transpose(0, 2, 1)
    q_w1_out = across_blocks(line_exchange(main_one, at_z, extra_one), 1)
    q_w3_out = line_exchange(main_three, at_z, extra_three)
    q_w3_out = across_blocks(q_w3_out + swap_core(q_w3_out), 1)
    dyn_w2_out = across_blocks(dyn_w2_part, 0).transpose(1, 0)
    dyn_w1_out = across_blocks(dyn_w1_part, 0)
    dyn_w3_out = across_blocks(dyn_w3_part, 0)
    q_wc_out = sum_across_blocks(line_collect(main_context, at_z, extra_context, BF16))
    dyn_wc_out = sum_across_blocks(dyn_context)

    def core_vec(values):
        own, other = values[:, :half_hidden], values[:, half_hidden:]
        return own + swap_core(other)

    def sums_of(result):
        return (
            core_vec(result[7]),
            result[5] + swap_core(result[5]),
            jnp.sum(result[3].astype(F32), 0)[None],
        )

    def pack(items):
        return jnp.concatenate([item.reshape(-1) for item in items])

    main_sums, extra_sums = sums_of(main), sums_of(extra)
    main_bias = main_sums[2] + swap_core(main_sums[2])
    extra_bias = extra_sums[2] + swap_core(extra_sums[2])
    main_sums, extra_sums = main_sums[:2] + (main_bias,), extra_sums[:2] + (extra_bias,)
    three_own = jnp.where(core == 0, sums_three[:, :half_latent], sums_three[:, half_latent:])
    three_other = jnp.where(core == 0, sums_three[:, half_latent:], sums_three[:, :half_latent])
    dyn_sums = (
        core_vec(dyn_sums_one),
        dyn_sums_two + swap_core(dyn_sums_two),
        three_own + swap_core(three_other),
    )
    def table_part(grad_one, w_context, rows):
        embed = mm_t(grad_one[:rows], w_context[acts:])
        return lax.dot_general(
            all_onehot[:rows], embed, (((0,), (0,)), ((), ())), precision=HIGHEST
        )

    table_grad = (
        table_part(main[6], head_weights[0][1], inputs.shape[0])
        + table_part(extra[6], head_weights[1][1], half_rows)
        + table_part(dyn_grad_one, dyn_wc_all, half_rows)
    )
    table_grad = line_total(table_grad + swap_core(table_grad))
    flat = sum_across_blocks(
        plane_total(pack((table_grad,) + dyn_sums + extra_sums + main_sums))
    )
    sizes = [table_grad] + list(dyn_sums)
    pieces = []
    start = 0
    for item in sizes:
        pieces.append(flat[start : start + item.size].reshape(item.shape))
        start += item.size
    head_size = sum(item.size for item in main_sums)
    extra_flat, main_flat = flat[start : start + head_size], flat[start + head_size :]
    head_flat = line_collect(main_flat, at_z, extra_flat)
    head_pieces = []
    start = 0
    for item in main_sums:
        head_pieces.append(
            head_flat[:, start : start + item.size].reshape((heads,) + item.shape)
        )
        start += item.size
    table_out, dyn_vec1_out, dyn_vec2_out, dyn_vec3_out = pieces
    q_vec1_out, q_vec2_out, q_b3_out = head_pieces
    return (
        losses,
        latent_grad,
        table_out,
        dyn_w1_out,
        dyn_wc_out,
        dyn_vec1_out,
        dyn_w2_out,
        dyn_vec2_out,
        dyn_w3_out,
        dyn_vec3_out,
        q_w1_out,
        q_wc_out,
        q_vec1_out,
        q_w2_out,
        q_vec2_out,
        q_w3_out,
        q_b3_out[:, 0],
    )


def gather_sum(values, ones):
    parts = []
    for start in range(0, values.shape[1], 128):
        piece = values[:, start : start + 128]
        high = piece.astype(BF16)
        rest = piece - high.astype(F32)
        middle = rest.astype(BF16)
        low = (rest - middle.astype(F32)).astype(BF16)
        parts.append(mm(high, ones) + mm(middle, ones) + mm(low, ones))
    return jnp.concatenate(parts, 1)


def line_kernel(sizes, scale, *refs):
    (slot, width, hidden, bins, tasks, acts, context_width, heads) = sizes
    (
        latent, action, task_ids, action_mask, task_table, target_latent, bin_lower, bin_frac,
        dyn_vec1, dyn_vec2, dyn_vec3, q_vec1, q_vec2, q_b3,
        dyn_w1, dyn_wc, dyn_w2, dyn_w3, q_w1, q_wc, q_w2, q_w3,
        out_losses, out_latent, out_table, out_dw1, out_dwc, out_dvec, out_dvec3, out_dw2, out_dw3,
        out_qw1, out_qwc, out_qvec, out_qw2, out_qw3,
        w1, wc, w2, dw3, qw3, dv1, dv3, qv1, qv2, qb3,
        xbuf, xother, tgt, nxt, nxto, dyn_x1, dyn_x2, dyn_h1, dyn_h2, simplex, x3,
        dyn_inv, x1, x2, inv, h1, h2, gp2, gp1, h1o, gp2o, gp1o, upstream, gl, dyn_gp3,
        acc, dxm, dxr, own_g, all_g, lossbuf,
        p2, r2, t2, p1, r1, t1, p3, r3, t3, p3o,
        e2, er2, et2, e1, er1, et1, e3, er3, et3, e3o,
        er2b, et2b, er1b, et1b, d3, d3s, d3o, er3b, et3b,
        pc, pcx, pcy, pq, pqx, pqy, ctx, vb, vbo, vbx, vby, tb, tbo, tbr,
        o3,
        send_sem, recv_sem, local_sem, free_a, free_b, free_f,
    ) = refs
    half = hidden // 2
    half_w = width // 2
    own_two, own_one = hidden // BLOCK, width // BLOCK
    rows_all = slot * LINE
    place = lax.axis_index("dp")
    core = lax.axis_index("tensor")
    at_x = lax.rem(place, 2)
    at_y = lax.rem(place // 2, 2)
    at_z = lax.rem(place // 4, 4)
    z_of = [
        at_z,
        at_z + 1 - 2 * lax.rem(at_z, 2),
        lax.rem(at_z + 2, 4),
        3 - at_z,
    ]
    to_core = (place, 1 - core)
    to_x = (place + 1 - 2 * at_x, core)
    to_y = (place + 2 - 4 * at_y, core)
    to_z = [None] + [(place + 4 * (z_of[k] - at_z), core) for k in range(1, LINE)]
    mesh_id = pl.DeviceIdType.MESH
    counter = [0, 0]
    pending = []

    def remote(source, target, device):
        at = counter[0]
        counter[0] += 1
        copy = pltpu.make_async_remote_copy(
            src_ref=source, dst_ref=target, send_sem=send_sem.at[at], recv_sem=recv_sem.at[at],
            device_id=device, device_id_type=mesh_id,
        )
        copy.start()
        pending.append(copy)
        return copy

    def sent(copy):
        copy.wait_send()
        pending[:] = [item for item in pending if item is not copy]

    def local(source, target):
        at = counter[1]
        counter[1] += 1
        copy = pltpu.make_async_copy(source, target, local_sem.at[at])
        copy.start()
        return copy

    barrier = pltpu.get_barrier_semaphore()
    peers = [to_core, to_x, to_y] + to_z[1:]
    for peer in peers:
        pl.semaphore_signal(barrier, inc=1, device_id=peer, device_id_type=mesh_id)
    pl.semaphore_wait(barrier, len(peers))

    low = slice(0, half)
    high = slice(half, hidden)
    own_cols = pl.ds(pl.multiple_of(half_w * core, 128), half_w)
    other_cols = pl.ds(pl.multiple_of(half_w * (1 - core), 128), half_w)
    own_rows = pl.ds(pl.multiple_of(slot * core, 64), slot)
    other_rows = pl.ds(pl.multiple_of(slot * (1 - core), 64), slot)

    lat_copy = remote(latent.at[other_rows], xbuf.at[pl.ds(0, slot), own_cols], to_core)
    tgt_copy = remote(target_latent.at[other_rows], tgt.at[:, own_cols], to_core)

    def load_weights(to, one, context, two):
        mine = [
            local(one, w1.at[to, :, low]),
            local(context, wc.at[to, :, low]),
            local(two, w2.at[to, low, :]),
        ]
        return mine

    def send_weights(to, one, context, two):
        return [
            remote(one, w1.at[to, :, high], to_core),
            remote(context, wc.at[to, :, high], to_core),
            remote(two, w2.at[to, high, :], to_core),
        ]

    head_z = at_z
    last = heads - 1
    vec_copies = [
        remote(dyn_vec1, dv1.at[:, high], to_core),
        remote(dyn_vec3, dv3.at[:, own_cols], to_core),
        remote(q_vec1.at[head_z], qv1.at[0, :, high], to_core),
        remote(q_vec1.at[last], qv1.at[1, :, high], to_core),
    ]
    dyn_ready = load_weights(0, dyn_w1, dyn_wc, dyn_w2)
    dyn_ready_other = send_weights(0, dyn_w1, dyn_wc, dyn_w2)
    three_ready = local(dyn_w3, dw3.at[:, own_cols])
    three_ready_other = remote(dyn_w3, dw3.at[:, own_cols], to_core)
    main_ready = load_weights(1, q_w1.at[head_z], q_wc.at[head_z], q_w2.at[head_z])
    main_three = local(q_w3.at[head_z], qw3.at[0])
    extra_three = local(q_w3.at[last], qw3.at[1])
    main_ready_other = send_weights(1, q_w1.at[head_z], q_wc.at[head_z], q_w2.at[head_z])

    dv1[:, low] = dyn_vec1[...]
    dv3[:, own_cols] = dyn_vec3[...]
    qv1[0, :, low] = q_vec1[head_z]
    qv1[1, :, low] = q_vec1[last]
    qv2[0] = q_vec2[head_z]
    qv2[1] = q_vec2[last]
    qb3[0] = q_b3[pl.ds(head_z, 1), :]
    qb3[1] = q_b3[last : last + 1, :]
    vb[...] = jnp.zeros_like(vb)

    rows_chip = 2 * slot
    row = lax.broadcasted_iota(jnp.int32, (rows_chip, rows_chip), 0)
    lane = lax.broadcasted_iota(jnp.int32, (rows_chip, rows_chip), 1)

    def column(values):
        return jnp.sum(jnp.where(row == lane, values.astype(F32), 0.0), 1, keepdims=True)

    ids = column(task_ids[...])
    fraction = column(bin_frac[...])
    task = lax.broadcasted_iota(jnp.int32, (rows_chip, tasks), 1).astype(F32)
    onehot = (ids == task).astype(F32).astype(BF16)

    def shift_matrix(count, start):
        near = lax.broadcasted_iota(jnp.int32, (count, 128), 0)
        far = lax.broadcasted_iota(jnp.int32, (count, 128), 1)
        return (near + start == far).astype(F32).astype(BF16)

    to_acts = shift_matrix(acts, 0)
    table = (
        t_mm(action_mask[...].astype(F32).astype(BF16), to_acts)
        + mm(task_table[...], shift_matrix(context_width - acts, acts))
    ).astype(BF16)
    lane = lax.broadcasted_iota(jnp.int32, (rows_chip, 128), 1)
    factor = t_mm(action[...], to_acts) + (lane >= acts).astype(F32)
    piece_one = fraction.astype(BF16).astype(F32)
    piece_two = (fraction - piece_one).astype(BF16).astype(F32)
    facts = mm(onehot, table) * factor
    for index, item in enumerate(
        (ids, column(bin_lower[...]), piece_one, piece_two, fraction - piece_one - piece_two)
    ):
        facts = facts + jnp.where(lane == context_width + index, item, 0.0)
    ctx[...] = facts
    xbuf[0:slot, width : width + 128] = ctx[own_rows, :].astype(BF16)
    xbuf[0:slot, own_cols] = latent[own_rows, :]
    tgt[:, own_cols] = target_latent[own_rows, :]
    lat_copy.wait_recv()
    line_in = [
        remote(xbuf.at[pl.ds(0, slot)], xbuf.at[pl.ds(slot * k, slot)], to_z[k])
        for k in range(1, LINE)
    ]
    for copy in vec_copies:
        copy.wait_recv()

    CH = 64

    def over_rows(first, count, body):
        if count <= CH:
            body(pl.ds(first, count))
            return

        def step(index, carry):
            body(pl.ds(pl.multiple_of(first + index * CH, CH), CH))
            return carry

        lax.fori_loop(0, count // CH, step, 0)

    def norm_rows(pre, keep, inverse, vec, out, first, count):
        features = pre.shape[1]

        def body(rows):
            values = pre[rows, :]
            centred = values - jnp.sum(values, -1, keepdims=True) * (1.0 / features)
            inv_rows = lax.rsqrt(
                jnp.sum(centred * centred, -1, keepdims=True) * (1.0 / features) + EPSILON
            )
            normed = centred * inv_rows
            keep[rows, :] = normed.astype(keep.dtype)
            inverse[rows, :] = inv_rows
            out[rows, :] = mish(normed * vec[1:2, :] + vec[2:3, :]).astype(BF16)

        over_rows(first, count, body)

    def add_sums(at, rounded, along, shift):
        count, features = shift.shape
        for index, item in enumerate((rounded, along, shift)):
            acc[at + index, :, 0:features] += jnp.sum(item.reshape(count // 8, 8, features), 0)

    def back_rows(grad, normed_ref, inverse, vec, out, at, first, count, slope):
        features = normed_ref.shape[1]

        def body(rows):
            normed = normed_ref[rows, :].astype(F32)
            gain = vec[1:2, :]
            up = grad[rows, :]
            if slope:
                up = mish_slope(normed * gain + vec[2:3, :]) * up
            weighted = up * gain
            along = up * normed
            mean_one = jnp.sum(weighted, -1, keepdims=True) * (1.0 / features)
            mean_two = jnp.sum(weighted * normed, -1, keepdims=True) * (1.0 / features)
            result = (inverse[rows, :] * (weighted - mean_one - normed * mean_two)).astype(BF16)
            out[rows, :] = result
            add_sums(at, result.astype(F32), along, up)

        over_rows(first, count, body)

    def two_tiles(body):
        def step(index, carry):
            body(pl.ds(pl.multiple_of(index * half, 128), half))
            return carry

        lax.fori_loop(0, 2, step, 0)

    def layers_forward(to, source, vec_one, vec_two, keep_one, keep_two, inverse, hid_one, hid_two,
                       first, count, ready):
        rows = pl.ds(first, count)
        ready(0)

        def first_tile(cols):
            x1[rows, cols] = (
                mm(source[rows, 0:width], w1[to, :, cols])
                + mm(xbuf[rows, width : width + context_width], wc[to, :, cols])
                + vec_one[0:1, cols]
            )

        two_tiles(first_tile)
        norm_rows(x1, keep_one, inverse.at[0], vec_one, hid_one, first, count)
        ready(1)

        def second_tile(cols):
            x2[rows, cols] = mm(hid_one[rows, :], w2[to, :, cols]) + vec_two[0:1, cols]

        two_tiles(second_tile)
        norm_rows(x2, keep_two, inverse.at[1], vec_two, hid_two, first, count)

    def back_two_to_one(to, grad, first, count):
        rows = pl.ds(first, count)

        def tile(cols):
            upstream[rows, cols] = mm_t(grad[rows, :], w2[to, cols, :])

        two_tiles(tile)

    def ready_of(mine, others):
        def ready(stage):
            picked = (0, 1) if stage == 0 else (2,)
            for index in picked:
                mine[index].wait()
                others[index].wait_recv()

        return ready

    def nothing(stage):
        return None

    layers_forward(
        0, xbuf, dv1, dyn_vec2, dyn_x1, dyn_x2, dyn_inv, dyn_h1, dyn_h2, 0, slot,
        ready_of(dyn_ready, dyn_ready_other),
    )
    for copy in line_in:
        copy.wait_recv()
    x_copy = remote(xbuf, xother, to_core)
    layers_forward(
        0, xbuf, dv1, dyn_vec2, dyn_x1, dyn_x2, dyn_inv, dyn_h1, dyn_h2, slot, rows_all - slot,
        nothing,
    )
    three_ready.wait()
    three_ready_other.wait_recv()
    x3[...] = mm(dyn_h2[...], dw3[...]) + dv3[0:1, :]
    group_row = lax.broadcasted_iota(jnp.int32, (128, 128), 0) // GROUP
    group_col = lax.broadcasted_iota(jnp.int32, (128, 128), 1) // GROUP
    ones = (group_row == group_col).astype(F32).astype(BF16)

    def simplex_rows(rows):
        values = x3[rows, :]
        centred = values - jnp.sum(values, -1, keepdims=True) * (1.0 / width)
        inv_rows = lax.rsqrt(
            jnp.sum(centred * centred, -1, keepdims=True) * (1.0 / width) + EPSILON
        )
        normed = centred * inv_rows
        x3[rows, :] = normed
        dyn_inv[2, rows, :] = inv_rows
        grown = jnp.exp(normed * dv3[1:2, :] + dv3[2:3, :])
        share = grown / gather_sum(grown, ones)
        simplex[rows, :] = share
        nxt[rows, :] = share.astype(BF16)

    over_rows(0, rows_all, simplex_rows)
    for copy in dyn_ready_other:
        sent(copy)
    pl.semaphore_signal(free_a, inc=1, device_id=to_core, device_id_type=mesh_id)
    extra_ready = load_weights(0, q_w1.at[last], q_wc.at[last], q_w2.at[last])
    next_copy = remote(nxt, nxto, to_core)
    tgt_copy.wait_recv()
    gap = nxt[0:slot, :].astype(F32) - tgt[...]
    own_g[...] = gap * (2.0 * scale)
    consistency = jnp.sum(gap * gap, -1, keepdims=True)
    pl.semaphore_wait(free_a, 1)
    extra_ready_other = send_weights(0, q_w1.at[last], q_wc.at[last], q_w2.at[last])

    def value_rows(head, first, count):
        rows = pl.ds(first, count)
        logits = mm_t(h2[rows, :], qw3[head]) + qb3[head]
        logits = logits - jnp.max(logits, -1, keepdims=True)
        grown = jnp.exp(logits)
        total = jnp.sum(grown, -1, keepdims=True)
        lane = lax.broadcasted_iota(jnp.int32, (count, bins), 1).astype(F32)
        facts = xbuf[rows, width : width + 128].astype(F32)
        lower = facts[:, context_width + 1 : context_width + 2]
        fraction = (
            facts[:, context_width + 2 : context_width + 3]
            + facts[:, context_width + 3 : context_width + 4]
            + facts[:, context_width + 4 : context_width + 5]
        )
        target = jnp.where(lane == lower, 1.0 - fraction, 0.0) + jnp.where(
            lane == lower + 1.0, fraction, 0.0
        )
        loss = -jnp.sum(target * (logits - jnp.log(total)), -1, keepdims=True) * (1.0 / heads)
        grad = (scale / heads * (grown / total - target)).astype(BF16)
        gl[rows, :] = grad

        def tile(cols):
            upstream[rows, cols] = mm(grad, qw3[head, :, cols])

        two_tiles(tile)
        acc[6, 0, 0:bins] += jnp.sum(grad.astype(F32), 0)
        return loss

    def table_sum(to, grad, first, count):
        rows = pl.ds(first, count)
        embed = mm_t(grad[rows, :], wc[to])
        ids = xbuf[rows, width : width + 128].astype(F32)[:, context_width : context_width + 1]
        task = lax.broadcasted_iota(jnp.int32, (count, tasks), 1).astype(F32)
        onehot = (ids == task).astype(F32).astype(BF16)
        top = embed.astype(BF16)
        rest = embed - top.astype(F32)
        middle = rest.astype(BF16)
        lowest = (rest - middle.astype(F32)).astype(BF16)
        tb[:, 0:context_width] += (
            t_mm(onehot, top) + t_mm(onehot, middle) + t_mm(onehot, lowest)
        )

    def finish_vectors(slot_at, width_three):
        for index in range(3):
            vb[slot_at, index : index + 1, :] = jnp.sum(acc[index], 0, keepdims=True)
            vb[slot_at, 3 + index : 4 + index, :] = jnp.sum(acc[3 + index], 0, keepdims=True)
        if width_three:
            three = [jnp.sum(acc[6 + index, :, 0:width], 0, keepdims=True) for index in range(3)]
            vb[slot_at, 6:7, 0:width] = three[0]
            vb[slot_at, 6:7, width : 2 * width] = three[1]
            vb[slot_at, 7:8, 0:width] = three[2]
        else:
            vb[slot_at, 6:7, :] = jnp.sum(acc[6], 0, keepdims=True)
        return remote(vb.at[slot_at], vbo.at[slot_at], to_core)

    def join_vectors(slot_at, copy):
        copy.wait_recv()
        sent(copy)
        vb[slot_at, 0:3, low] = vb[slot_at, 0:3, low] + vbo[slot_at, 0:3, high]
        vb[slot_at, 3:8, :] = vb[slot_at, 3:8, :] + vbo[slot_at, 3:8, :]
        return remote(vb.at[slot_at], vbx.at[slot_at], to_x)

    def plane_vectors(slot_at, copy):
        copy.wait_recv()
        sent(copy)
        vb[slot_at] = vb[slot_at] + vbx[slot_at]
        return remote(vb.at[slot_at], vby.at[slot_at], to_y)

    def total_vectors(slot_at, copy):
        copy.wait_recv()
        sent(copy)
        vb[slot_at] = vb[slot_at] + vby[slot_at]

    def scatter_start(source, target, x_first, lead):
        if lead is None:
            piece = source.at[:, 1 - at_x] if x_first else source.at[1 - at_y]
        else:
            piece = source.at[lead, :, 1 - at_x] if x_first else source.at[lead, 1 - at_y]
        return remote(piece, target, to_x if x_first else to_y)

    def scatter_middle(copy, source, received, target, x_first, lead):
        copy.wait_recv()
        if lead is None:
            for other in range(2):
                kept = source[other, at_x] if x_first else source[at_y, other]
                received[other] = (received[other].astype(F32) + kept.astype(F32)).astype(BF16)
            piece = received.at[1 - at_y] if x_first else received.at[1 - at_x]
        else:
            for index in range(lead.size):
                for other in range(2):
                    kept = (
                        source[lead.start + index, other, at_x]
                        if x_first
                        else source[lead.start + index, at_y, other]
                    )
                    received[index, other] = (
                        received[index, other].astype(F32) + kept.astype(F32)
                    ).astype(BF16)
            piece = received.at[:, 1 - at_y] if x_first else received.at[:, 1 - at_x]
        return remote(piece, target, to_y if x_first else to_x)

    def scatter_end(copy, received, target, x_first):
        copy.wait_recv()
        mine = at_y if x_first else at_x
        return received[mine].astype(F32) + target[...].astype(F32)

    def scatter_end_lead(copy, received, target, x_first, count):
        copy.wait_recv()
        mine = at_y if x_first else at_x
        for index in range(count):
            target[index] = (
                received[index, mine].astype(F32) + target[index].astype(F32)
            ).astype(BF16)

    first_half, second_half = pl.ds(0, 2), pl.ds(2, 2)

    acc[...] = jnp.zeros_like(acc)
    tb[...] = jnp.zeros_like(tb)
    main_three.wait()
    extra_three.wait()
    layers_forward(
        1, nxt, qv1.at[0], qv2.at[0], x1, x2, inv, h1, h2, 0, rows_all,
        ready_of(main_ready, main_ready_other),
    )
    main_loss = value_rows(0, 0, rows_all)
    back_rows(upstream, x2, inv.at[1], qv2.at[0], gp2, 3, 0, rows_all, True)
    factor_copies = [remote(h1.at[:, high], h1o, to_core), remote(gp2, gp2o, to_core)]
    back_two_to_one(1, gp2, 0, rows_all)
    for copy in factor_copies:
        copy.wait_recv()
    wide = half // 256 * 128 + 128
    main_two = []
    for index in range(2):
        cols = slice(index * half, (index + 1) * half)
        for part in (slice(0, wide), slice(wide, half)):
            whole = t_mm(gp2[:, cols], h1[:, part]) + t_mm(gp2o[:, cols], h1o[:, part])
            p2[2 * index : 2 * index + 2, :, :, :, part] = whole.astype(BF16).reshape(
                (2, 2, 2, own_two, part.stop - part.start)
            )
        main_two.append(
            scatter_start(p2, r2.at[2 * index : 2 * index + 2], index == 0, pl.ds(2 * index, 2))
        )
    back_rows(upstream, x1, inv.at[0], qv1.at[0], gp1, 0, 0, rows_all, True)
    one_copy = remote(gp1.at[:, high], gp1o, to_core)
    dx = mm_t(gp1[...], w1[1])
    own_g[...] = own_g[...] + dx[0:slot]
    dxm[:, 0:width] = dx.astype(BF16)
    lane_all = lax.broadcasted_iota(jnp.int32, (rows_all, 128), 1)
    loss_high = main_loss.astype(BF16).astype(F32)
    loss_rest = main_loss - loss_high
    loss_middle = loss_rest.astype(BF16).astype(F32)
    loss_low = loss_rest - loss_middle
    dxm[:, width : width + 128] = jnp.where(
        lane_all == 0, loss_high, jnp.where(lane_all == 1, loss_middle, loss_low)
    ).astype(BF16)
    dx_copies = [
        remote(dxm.at[pl.ds(slot * k, slot)], dxr.at[k - 1], to_z[k]) for k in range(1, LINE)
    ]
    part = t_mm(h2[...], gl[...])
    p3[...] = part.astype(BF16).reshape(p3.shape)
    three_copy = remote(p3, p3o, to_core)
    main_vec = finish_vectors(0, False)
    acc[...] = jnp.zeros_like(acc)
    next_copy.wait_recv()
    x_copy.wait_recv()
    one_copy.wait_recv()
    whole = t_mm(xbuf[:, width : width + 128], gp1[:, low]) + t_mm(
        xother[:, width : width + 128], gp1o[...]
    )
    pc[...] = whole[0 : pc.shape[0]].astype(BF16)
    main_context = remote(pc, pcx, to_x)
    whole = t_mm(nxt[...], gp1[:, low]) + t_mm(nxto[...], gp1o[...])
    p1[...] = whole.astype(BF16).reshape(p1.shape)
    main_one = [
        scatter_start(p1, r1.at[2 * index : 2 * index + 2], index == 0, pl.ds(2 * index, 2))
        for index in range(2)
    ]
    table_sum(1, gp1, 0, rows_all)
    for copy in main_ready_other:
        sent(copy)
    pl.semaphore_signal(free_b, inc=1, device_id=to_core, device_id_type=mesh_id)
    dyn_again = load_weights(1, dyn_w1, dyn_wc, dyn_w2)
    for copy in factor_copies + [one_copy]:
        sent(copy)
    pl.semaphore_signal(free_f, inc=1, device_id=to_core, device_id_type=mesh_id)
    pl.semaphore_wait(free_b, 1)
    dyn_again_other = send_weights(1, dyn_w1, dyn_wc, dyn_w2)

    def context_middle(source, received, target, copy):
        copy.wait_recv()
        sent(copy)
        source[...] = (source[...].astype(F32) + received[...].astype(F32)).astype(BF16)
        return remote(source, target, to_y)

    def context_end(source, received, copy):
        copy.wait_recv()
        sent(copy)
        source[...] = (source[...].astype(F32) + received[...].astype(F32)).astype(BF16)

    hand, keep = [], []

    layers_forward(
        0, nxt, qv1.at[1], qv2.at[1], x1, x2, inv, h1, h2, 0, slot,
        ready_of(extra_ready, extra_ready_other),
    )
    extra_loss = value_rows(1, 0, slot)
    back_rows(upstream, x2, inv.at[1], qv2.at[1], gp2, 3, 0, slot, True)
    back_two_to_one(0, gp2, 0, slot)
    back_rows(upstream, x1, inv.at[0], qv1.at[1], gp1, 0, 0, slot, True)
    own_total = own_g[...] + mm_t(gp1[0:slot, :], w1[0])
    value = main_loss[0:slot] + extra_loss
    for index, copy in enumerate(dx_copies):
        copy.wait_recv()
        message = dxr[index].astype(F32)
        own_total = own_total + message[:, 0:width]
        value = value + (
            message[:, width : width + 1]
            + message[:, width + 1 : width + 2]
            + message[:, width + 2 : width + 3]
        )
    all_g[0:slot, :] = own_total.astype(BF16)
    grad_copies = [
        remote(all_g.at[pl.ds(0, slot)], all_g.at[pl.ds(slot * k, slot)], to_z[k])
        for k in range(1, LINE)
    ]
    lane_own = lax.broadcasted_iota(jnp.int32, (slot, 128), 1)
    lossbuf[...] = jnp.where(lane_own == 0, consistency, value)
    loss_copy = remote(lossbuf, out_losses.at[own_rows], to_core)
    keep += [local(lossbuf, out_losses.at[own_rows])]
    table_sum(0, gp1, 0, slot)
    three_copy.wait_recv()
    sent(three_copy)
    p3[...] = (p3[...].astype(F32) + p3o[...].astype(F32)).astype(BF16)
    main_three_sum = [
        scatter_start(p3, r3.at[2 * index : 2 * index + 2], index == 0, pl.ds(2 * index, 2))
        for index in range(2)
    ]
    main_vec = join_vectors(0, main_vec)
    rest = rows_all - slot
    layers_forward(
        0, nxt, qv1.at[1], qv2.at[1], x1, x2, inv, h1, h2, slot, rest, nothing
    )
    value_rows(1, slot, rest)
    def middle_two(copies, source, received, target):
        return [
            scatter_middle(
                copies[index], source, received.at[2 * index : 2 * index + 2],
                target.at[2 * index : 2 * index + 2], index == 0, pl.ds(2 * index, 2),
            )
            for index in range(2)
        ]

    def end_two(copies, received, target):
        for index in range(2):
            scatter_end_lead(
                copies[index], received.at[2 * index : 2 * index + 2],
                target.at[2 * index : 2 * index + 2], index == 0, 2,
            )

    def hand_on(source, target):
        keep.append(local(source.at[at_z], target.at[at_z]))
        for k in range(1, LINE):
            hand.append(remote(source.at[z_of[k]], target.at[at_z], to_z[k]))

    def hand_all(source, target):
        mine = target(at_z)
        keep.append(local(source, mine))
        near = remote(source, mine, to_z[1])
        far = remote(source, mine, to_z[2])
        hand.append(near)
        return far, target

    def hand_further(started):
        far, target = started
        far.wait_recv()
        theirs = target(z_of[2])
        hand.append(remote(theirs, theirs, to_z[1]))

    main_context = context_middle(pc, pcx, pcy, main_context)
    first_two = main_two
    main_two = middle_two(main_two, p2, r2, t2)
    back_rows(upstream, x2, inv.at[1], qv2.at[1], gp2, 3, slot, rest, True)
    pl.semaphore_wait(free_f, 1)
    factor_copies = [remote(gp2, gp2o, to_core), remote(h1.at[:, high], h1o, to_core)]
    back_two_to_one(0, gp2, slot, rest)
    back_rows(upstream, x1, inv.at[0], qv1.at[1], gp1, 0, slot, rest, True)
    one_copy = remote(gp1.at[:, high], gp1o, to_core)
    extra_vec = finish_vectors(1, False)
    acc[...] = jnp.zeros_like(acc)

    first_one = main_one
    main_one = middle_two(main_one, p1, r1, t1)
    main_vec = plane_vectors(0, main_vec)

    def by_place(body):
        for index in range(LINE):
            @pl.when(at_z == index)
            def _(index=index):
                body(index)

    quarter = hidden // LINE
    quarter_w = width // LINE
    quarter_c = 128 // LINE

    def quarter_two(index, hid, target):
        cols = slice(index * quarter, (index + 1) * quarter)
        whole = t_mm(gp2[:, cols], hid[:, low]) + t_mm(gp2o[:, cols], h1o[...])
        target[...] = whole.astype(BF16).reshape(target.shape)

    def quarter_one(index, mine, others, target, at):
        cols = slice(index * quarter_w, (index + 1) * quarter_w)
        whole = t_mm(mine[:, cols], gp1[:, low]) + t_mm(others[:, cols], gp1o[...])
        target[...] = whole.astype(BF16).reshape(target.shape)
        cols = slice(width + index * quarter_c, width + (index + 1) * quarter_c)
        whole = t_mm(xbuf[:, cols], gp1[:, low]) + t_mm(xother[:, cols], gp1o[...])
        pq[at] = whole.astype(BF16)

    for copy in factor_copies + [one_copy]:
        copy.wait_recv()

    def extra_parts(index):
        part = t_mm(h2[:, index * quarter : (index + 1) * quarter], gl[...])
        e3[...] = part.astype(BF16).reshape(e3.shape)
        quarter_two(index, h1, e2)
        quarter_one(index, nxt, nxto, e1, 0)

    by_place(extra_parts)
    extra_three_sum = remote(e3, e3o, to_core)
    extra_two = scatter_start(e2, er2, True, None)
    extra_one = scatter_start(e1, er1, False, None)
    extra_context = remote(pq.at[0], pqx.at[0], to_x)
    for copy in factor_copies + [one_copy]:
        sent(copy)
    pl.semaphore_signal(free_f, inc=1, device_id=to_core, device_id_type=mesh_id)
    extra_vec = join_vectors(1, extra_vec)
    for copy in grad_copies:
        copy.wait_recv()

    def simplex_back(rows):
        share = simplex[rows, :]
        weighted = all_g[rows, :].astype(F32) * share
        up = weighted - share * gather_sum(weighted, ones)
        upstream[rows, 0:width] = up

    over_rows(0, rows_all, simplex_back)
    back_rows(
        upstream.at[:, 0:width], x3, dyn_inv.at[2], dv3, dyn_gp3, 6, 0, rows_all, False
    )

    def dyn_third(index):
        left = dyn_h2[:, index * quarter : (index + 1) * quarter]
        d3s[...] = t_mm(left, dyn_gp3[:, other_cols]).astype(BF16).reshape(d3s.shape)
        d3[...] = t_mm(left, dyn_gp3[:, own_cols]).astype(BF16).reshape(d3.shape)

    by_place(dyn_third)
    d3_copy = remote(d3s, d3o, to_core)
    context_end(pc, pcy, main_context)
    context_hand = hand_all(pc, lambda at: out_qwc.at[at, pl.ds(0, pc.shape[0])])
    main_three_sum = middle_two(main_three_sum, p3, r3, t3)
    def three_tile(cols):
        upstream[:, cols] = mm_t(dyn_gp3[...], dw3[cols, :])

    two_tiles(three_tile)
    back_rows(upstream, dyn_x2, dyn_inv.at[1], dyn_vec2, gp2, 3, 0, rows_all, True)
    pl.semaphore_wait(free_f, 1)
    factor_copies = [remote(gp2, gp2o, to_core), remote(dyn_h1.at[:, high], h1o, to_core)]
    d3_copy.wait_recv()
    sent(d3_copy)
    d3[...] = (d3[...].astype(F32) + d3o[...].astype(F32)).astype(BF16)
    dyn_three_sum = scatter_start(d3, er3b, False, None)
    end_two(main_two, r2, t2)
    hand_on(t2, out_qw2)
    total_vectors(0, main_vec)
    vec_hand = hand_all(vb.at[0], lambda at: out_qvec.at[at])
    dyn_again[2].wait()
    dyn_again_other[2].wait_recv()
    back_two_to_one(1, gp2, 0, rows_all)
    for copy in factor_copies:
        copy.wait_recv()
    for copy in first_two + first_one:
        sent(copy)
    d2, d1 = p2.at[0], p1.at[0]
    by_place(lambda index: quarter_two(index, dyn_h1, d2))
    dyn_two_sum = scatter_start(d2, er2b, True, None)
    hand_further(context_hand)
    end_two(main_one, r1, t1)
    hand_on(t1, out_qw1)
    back_rows(upstream, dyn_x1, dyn_inv.at[0], dv1, gp1, 0, 0, rows_all, True)
    one_copy = remote(gp1.at[:, high], gp1o, to_core)
    dyn_vec = finish_vectors(2, True)
    for index in (0, 1):
        dyn_again[index].wait()
        dyn_again_other[index].wait_recv()
    table_sum(1, gp1, 0, slot)
    table_copy = remote(tb, tbo, to_core)
    one_copy.wait_recv()
    by_place(lambda index: quarter_one(index, xbuf, xother, d1, 1))
    dyn_one_sum = scatter_start(d1, er1b, False, None)
    dyn_context = remote(pq.at[1], pqx.at[1], to_x)
    lat_g = tgt
    lat_g[...] = mm_t(gp1[0:slot, :], w1[1])
    latent_copy = remote(lat_g.at[:, other_cols], out_latent.at[own_rows], to_core)
    keep += [local(lat_g.at[:, own_cols], out_latent.at[own_rows])]
    dyn_vec = join_vectors(2, dyn_vec)
    table_copy.wait_recv()
    sent(table_copy)
    tb[...] = tb[...] + tbo[...]
    table_copy = remote(tb, tbr.at[0], to_x)

    extra_two2 = scatter_middle(extra_two, e2, er2, et2, True, None)
    extra_one2 = scatter_middle(extra_one, e1, er1, et1, False, None)
    extra_context = context_middle(pq.at[0], pqx.at[0], pqy.at[0], extra_context)
    extra_three_sum.wait_recv()
    sent(extra_three_sum)
    e3[...] = (e3[...].astype(F32) + e3o[...].astype(F32)).astype(BF16)
    extra_three_sum = scatter_start(e3, er3, False, None)
    extra_vec = plane_vectors(1, extra_vec)
    hand_further(vec_hand)
    dyn_three2 = scatter_middle(dyn_three_sum, d3, er3b, et3b, False, None)
    dyn_two2 = scatter_middle(dyn_two_sum, d2, er2b, et2b, True, None)
    dyn_one2 = scatter_middle(dyn_one_sum, d1, er1b, et1b, False, None)
    dyn_context = context_middle(pq.at[1], pqx.at[1], pqy.at[1], dyn_context)
    dyn_vec = plane_vectors(2, dyn_vec)
    table_copy.wait_recv()
    sent(table_copy)
    tb[...] = tb[...] + tbr[0]
    table_copy = remote(tb, tbr.at[1], to_y)
    end_two(main_three_sum, r3, t3)
    hand_on(t3, out_qw3)
    extra_three2 = scatter_middle(extra_three_sum, e3, er3, et3, False, None)
    context_end(pq.at[0], pqy.at[0], extra_context)
    def quarter_rows(at):
        return pl.ds(pl.multiple_of(quarter_c * at, quarter_c), quarter_c)

    extra_hand = hand_all(pq.at[0], lambda at: out_qwc.at[last, quarter_rows(at)])
    total_vectors(1, extra_vec)
    keep += [local(vb.at[1], out_qvec.at[last])]
    et2[...] = scatter_end(extra_two2, er2, et2, True).astype(BF16)
    keep += [local(et2, out_qw2.at[last])]
    et1[...] = scatter_end(extra_one2, er1, et1, False).astype(BF16)
    keep += [local(et1, out_qw1.at[last])]
    table_copy.wait_recv()
    sent(table_copy)
    tb[...] = tb[...] + tbr[1]
    table_copies = [remote(tb, tbr.at[1 + k], to_z[k]) for k in range(1, LINE)]
    context_end(pq.at[1], pqy.at[1], dyn_context)
    dyn_hand = hand_all(pq.at[1], lambda at: out_dwc.at[quarter_rows(at)])
    total_vectors(2, dyn_vec)
    keep += [local(vb.at[2], out_dvec)]
    o3[0:3, :] = jnp.concatenate(
        [
            vb[2, 6:7, own_cols],
            vb[2, 6:7, pl.ds(pl.multiple_of(width + half_w * core, 128), half_w)],
            vb[2, 7:8, own_cols],
        ],
        0,
    )
    keep += [local(o3, out_dvec3)]
    o2 = upstream.at[0:own_two, 0:half]
    o1 = upstream.at[own_two : own_two + own_one, 0:half]
    oc = upstream.at[0:own_two, half : half + half_w]
    oc[...] = scatter_end(dyn_three2, er3b, et3b, False)
    keep += [local(oc, out_dw3)]
    et3[...] = scatter_end(extra_three2, er3, et3, False).astype(BF16)
    keep += [local(et3, out_qw3.at[last])]
    o2[...] = scatter_end(dyn_two2, er2b, et2b, True)
    keep += [local(o2, out_dw2)]
    o1[...] = scatter_end(dyn_one2, er1b, et1b, False)
    keep += [local(o1, out_dw1)]
    hand_further(extra_hand)
    hand_further(dyn_hand)
    for copy in table_copies:
        copy.wait_recv()
        sent(copy)
    tb[...] = tb[...] + tbr[2] + tbr[3] + tbr[4]
    keep += [local(tb, out_table)]
    for copy in hand + [loss_copy, latent_copy]:
        copy.wait_recv()
    for copy in keep:
        copy.wait()
    for copy in list(pending):
        sent(copy)


def line_shards(
    latent,
    action,
    task_ids,
    action_mask,
    task_table,
    target_latent,
    bin_lower,
    bin_frac,
    dyn_w1,
    dyn_wc,
    dyn_vec1,
    dyn_w2,
    dyn_vec2,
    dyn_w3,
    dyn_vec3,
    q_w1,
    q_wc,
    q_vec1,
    q_w2,
    q_vec2,
    q_w3,
    q_b3,
):
    local_rows, half_w = latent.shape
    slot = local_rows // 2
    rows = slot * LINE
    width = 2 * half_w
    half = dyn_w1.shape[1]
    hidden = 2 * half
    heads, bins = q_b3.shape
    tasks, acts = action_mask.shape
    context_width = dyn_wc.shape[0]
    pad_context = -(-context_width // 16) * 16
    own_two = hidden // BLOCK
    own_one = width // BLOCK
    scale = 1.0 / math.sqrt(local_rows * lax.axis_size("dp"))
    sizes = (slot, width, hidden, bins, tasks, acts, context_width, heads)

    def shape(*dims, kind=F32):
        return jax.ShapeDtypeStruct(dims, kind)

    out_shape = (
        shape(local_rows, 128),
        shape(local_rows, half_w),
        shape(tasks, 128),
        shape(own_one, half),
        shape(128, half, kind=BF16),
        shape(8, hidden),
        shape(8, half_w),
        shape(own_two, half),
        shape(own_two, half_w),
        shape(heads, own_one, half, kind=BF16),
        shape(heads, 128, half, kind=BF16),
        shape(heads, 8, hidden),
        shape(heads, own_two, half, kind=BF16),
        shape(heads, own_two, bins, kind=BF16),
    )
    v = pltpu.VMEM
    scratch = [
        v((2, width, hidden), BF16),
        v((2, context_width, hidden), BF16),
        v((2, hidden, hidden), BF16),
        v((hidden, width), BF16),
        v((2, bins, hidden), BF16),
        v((3, hidden), F32),
        v((3, width), F32),
        v((2, 3, hidden), F32),
        v((2, 3, hidden), F32),
        v((2, 1, bins), F32),
        v((rows, width + 128), BF16),
        v((rows, width + 128), BF16),
        v((slot, width), F32),
        v((rows, width), BF16),
        v((rows, width), BF16),
        v((rows, hidden), BF16),
        v((rows, hidden), BF16),
        v((rows, hidden), BF16),
        v((rows, hidden), BF16),
        v((rows, width), F32),
        v((rows, width), F32),
        v((3, rows, 1), F32),
        v((rows, hidden), F32),
        v((rows, hidden), F32),
        v((2, rows, 1), F32),
        v((rows, hidden), BF16),
        v((rows, hidden), BF16),
        v((rows, hidden), BF16),
        v((rows, hidden), BF16),
        v((rows, half), BF16),
        v((rows, hidden), BF16),
        v((rows, half), BF16),
        v((rows, hidden), F32),
        v((rows, bins), BF16),
        v((rows, width), BF16),
        v((9, 8, hidden), F32),
        v((rows, width + 128), BF16),
        v((LINE - 1, slot, width + 128), BF16),
        v((slot, width), F32),
        v((rows, width), BF16),
        v((slot, 128), F32),
        v((LINE, 2, 2, own_two, half), BF16),
        v((LINE, 2, own_two, half), BF16),
        v((LINE, own_two, half), BF16),
        v((LINE, 2, 2, own_one, half), BF16),
        v((LINE, 2, own_one, half), BF16),
        v((LINE, own_one, half), BF16),
        v((LINE, 2, 2, own_two, bins), BF16),
        v((LINE, 2, own_two, bins), BF16),
        v((LINE, own_two, bins), BF16),
        v((LINE, 2, 2, own_two, bins), BF16),
        v((2, 2, own_two, half), BF16),
        v((2, own_two, half), BF16),
        v((own_two, half), BF16),
        v((2, 2, own_one, half), BF16),
        v((2, own_one, half), BF16),
        v((own_one, half), BF16),
        v((2, 2, own_two, bins), BF16),
        v((2, own_two, bins), BF16),
        v((own_two, bins), BF16),
        v((2, 2, own_two, bins), BF16),
        v((2, own_two, half), BF16),
        v((own_two, half), BF16),
        v((2, own_one, half), BF16),
        v((own_one, half), BF16),
        v((2, 2, own_two, half_w), BF16),
        v((2, 2, own_two, half_w), BF16),
        v((2, 2, own_two, half_w), BF16),
        v((2, own_two, half_w), BF16),
        v((own_two, half_w), BF16),
        v((pad_context, half), BF16),
        v((pad_context, half), BF16),
        v((pad_context, half), BF16),
        v((2, 128 // LINE, half), BF16),
        v((2, 128 // LINE, half), BF16),
        v((2, 128 // LINE, half), BF16),
        v((local_rows, 128), F32),
        v((3, 8, hidden), F32),
        v((3, 8, hidden), F32),
        v((3, 8, hidden), F32),
        v((3, 8, hidden), F32),
        v((tasks, 128), F32),
        v((tasks, 128), F32),
        v((5, tasks, 128), F32),
        v((8, half_w), F32),
        pltpu.SemaphoreType.DMA((REMOTE_COPIES,)),
        pltpu.SemaphoreType.DMA((REMOTE_COPIES,)),
        pltpu.SemaphoreType.DMA((LOCAL_COPIES,)),
        pltpu.SemaphoreType.REGULAR,
        pltpu.SemaphoreType.REGULAR,
        pltpu.SemaphoreType.REGULAR,
    ]
    inside = pl.BlockSpec(memory_space=pltpu.VMEM)
    outside = pl.BlockSpec(memory_space=pl.ANY)
    raw = pl.pallas_call(
        functools.partial(line_kernel, sizes, scale),
        out_shape=out_shape,
        in_specs=[inside] * 14 + [outside] * 8,
        out_specs=[outside] * len(out_shape),
        scratch_shapes=scratch,
        compiler_params=pltpu.CompilerParams(
            collective_id=0, has_side_effects=True, vmem_limit_bytes=VMEM_BYTES
        ),
        cost_estimate=pl.CostEstimate(
            flops=2 * 10**10, bytes_accessed=6 * 10**7, transcendentals=10**7
        ),
        name="line_update",
    )(
        latent, action.T, task_ids[None], action_mask.T, task_table, target_latent,
        bin_lower[None], bin_frac[None], dyn_vec1, dyn_vec2, dyn_vec3, q_vec1, q_vec2, q_b3,
        dyn_w1, dyn_wc, dyn_w2, dyn_w3, q_w1, q_wc, q_w2, jnp.swapaxes(q_w3, 1, 2),
    )
    return finish(raw, (slot, width, hidden, bins, tasks, acts, context_width, heads))


def finish_kernel(sizes, *refs):
    (slot, width, hidden, bins, tasks, acts, context_width, heads) = sizes
    half = hidden // 2
    (
        raw_losses, raw_latent, raw_table, raw_dw1, raw_dwc, raw_dvec, raw_dvec3, raw_dw2, raw_dw3,
        raw_qw1, raw_qwc, raw_qvec, raw_qw2, raw_qw3,
        losses, latent, table, dw1, dwc, dvec1, dw2, dvec2, dw3, dvec3,
        qw1, qwc, qvec1, qw2, qvec2, qw3, qb3,
    ) = refs
    head = pl.program_id(0)

    @pl.when(head == 0)
    def _():
        losses[...] = raw_losses[...].T[0:2]
        latent[...] = raw_latent[...]
        table[...] = raw_table[:, acts:context_width]
        dw1[...] = raw_dw1[...]
        dwc[...] = raw_dwc[...].astype(F32)[0:context_width]
        dvec1[...] = raw_dvec[0:3, 0:half]
        dw2[...] = raw_dw2[...]
        dvec2[...] = raw_dvec[3:6, :]
        dw3[...] = raw_dw3[...]
        dvec3[...] = raw_dvec3[0:3, :]

    qw1[0] = raw_qw1[0].astype(F32)
    qwc[0] = raw_qwc[0].astype(F32)[0:context_width]
    qvec1[0] = raw_qvec[0, 0:3, 0:half]
    qw2[0] = raw_qw2[0].astype(F32)
    qvec2[0] = raw_qvec[0, 3:6, :]
    qw3[0] = raw_qw3[0].astype(F32).T
    qb3[pl.ds(head, 1), :] = raw_qvec[0, 6:7, 0:bins]


def finish(raw, sizes):
    (slot, width, hidden, bins, tasks, acts, context_width, heads) = sizes
    half, half_w = hidden // 2, width // 2
    own_two, own_one = hidden // BLOCK, width // BLOCK

    def whole(*dims):
        return pl.BlockSpec(dims, lambda head: (0,) * len(dims))

    def by_head(*dims):
        return pl.BlockSpec((1,) + dims, lambda head: (head,) + (0,) * len(dims))

    dims = [
        (whole, (2, 2 * slot)),
        (whole, (2 * slot, half_w)),
        (whole, (tasks, context_width - acts)),
        (whole, (own_one, half)),
        (whole, (context_width, half)),
        (whole, (3, half)),
        (whole, (own_two, half)),
        (whole, (3, hidden)),
        (whole, (own_two, half_w)),
        (whole, (3, half_w)),
        (by_head, (own_one, half)),
        (by_head, (context_width, half)),
        (by_head, (3, half)),
        (by_head, (own_two, half)),
        (by_head, (3, hidden)),
        (by_head, (bins, own_two)),
        (whole, (heads, bins)),
    ]
    outs = pl.pallas_call(
        functools.partial(finish_kernel, sizes),
        grid=(heads,),
        in_specs=[whole(*item.shape) for item in raw[:9]]
        + [by_head(*item.shape[1:]) for item in raw[9:]],
        out_specs=[kind(*item) for kind, item in dims],
        out_shape=[
            jax.ShapeDtypeStruct(item if kind is whole else (heads,) + item, F32)
            for kind, item in dims
        ],
        compiler_params=pltpu.CompilerParams(dimension_semantics=("arbitrary",)),
        name="finish",
    )(*raw)
    outs = list(outs)
    outs[0] = outs[0].T
    outs[6] = outs[6].T
    outs[13] = jnp.swapaxes(outs[13], 1, 2)
    outs[15] = jnp.swapaxes(outs[15], 1, 2)
    return tuple(outs)


def shards(*arrays):
    if lax.axis_size("dp") == BLOCK:
        return line_shards(*arrays)
    return general_shards(*arrays)


def solution(mesh):
    return jax.shard_map(
        shards,
        mesh=mesh,
        in_specs=(
            P("dp", "tensor"),
            P("dp", None),
            P("dp"),
            P(),
            P(),
            P("dp", "tensor"),
            P("dp"),
            P("dp"),
            P(None, "tensor"),
            P(None, "tensor"),
            P(None, "tensor"),
            P("tensor", None),
            P(),
            P(None, "tensor"),
            P(None, "tensor"),
            P(None, None, "tensor"),
            P(None, None, "tensor"),
            P(None, None, "tensor"),
            P(None, "tensor", None),
            P(),
            P(),
            P(),
        ),
        out_specs=(
            P("dp", None),
            P("dp", "tensor"),
            P(),
            P("dp", "tensor"),
            P(None, "tensor"),
            P(None, "tensor"),
            P("tensor", "dp"),
            P(),
            P("dp", "tensor"),
            P(None, "tensor"),
            P(None, "dp", "tensor"),
            P(None, None, "tensor"),
            P(None, None, "tensor"),
            P(None, "tensor", "dp"),
            P(),
            P(None, "dp", None),
            P(),
        ),
        check_vma=False,
    )
```

```python
import functools
import math

import jax
import jax.numpy as jnp
from jax import lax
from jax.experimental import pallas as pl
from jax.experimental.pallas import tpu as pltpu
from jax.sharding import PartitionSpec as P

GROUP = 8
LINE = 4
PLANE = 4
BLOCK = LINE * PLANE
EPSILON = 1e-05
HIGHEST = lax.Precision.HIGHEST
F32 = jnp.float32
BF16 = jnp.bfloat16
REMOTE_COPIES = 119
LOCAL_COPIES = 33
VMEM_BYTES = 63 << 20


def swap_core(values):
    return lax.ppermute(values, "tensor", [(0, 1), (1, 0)])


def swap_dp(values, bit):
    size = lax.axis_size("dp")
    return lax.ppermute(values, "dp", [(place, place ^ bit) for place in range(size)])


def pick(values, index, axis=0):
    return lax.dynamic_index_in_dim(values, index, axis, keepdims=False)


def own_then_other(values):
    return values, swap_core(values)


def mish_parts(values):
    grown = jnp.exp(jnp.minimum(values, 20.0))
    top = grown * (grown + 2.0)
    share = 1.0 / (top + 2.0)
    return grown, top * share, share


def mish(values):
    return values * mish_parts(values)[1]


def mish_slope(values):
    grown, ratio, share = mish_parts(values)
    return ratio + 4.0 * values * grown * (1.0 + grown) * share * share


def norm(before, gain, shift):
    centred = before - jnp.mean(before, -1, keepdims=True)
    inverse = lax.rsqrt(jnp.mean(centred * centred, -1, keepdims=True) + EPSILON)
    normed = centred * inverse
    return normed * gain + shift, normed, inverse


def norm_back(upstream, normed, inverse, gain):
    weighted = upstream * gain
    return inverse * (
        weighted
        - jnp.mean(weighted, -1, keepdims=True)
        - normed * jnp.mean(weighted * normed, -1, keepdims=True)
    )


def vector_sums(rounded, upstream, normed):
    return jnp.stack(
        [jnp.sum(rounded.astype(F32), 0), jnp.sum(upstream * normed, 0), jnp.sum(upstream, 0)]
    )


def mm(left, right):
    return jnp.dot(left, right, preferred_element_type=F32)


def mm_t(left, right):
    return lax.dot_general(left, right, (((1,), (1,)), ((), ())), preferred_element_type=F32)


def t_mm(left, right):
    return lax.dot_general(left, right, (((0,), (0,)), ((), ())), preferred_element_type=F32)


def block_forward(inputs, context, w_one, w_context, vec_one, w_two, vec_two):
    before = mm(inputs, w_one) + mm(context, w_context) + vec_one[0:1]
    out_one, normed_one, inverse_one = norm(before, vec_one[1:2], vec_one[2:3])
    hidden_one = mish(out_one).astype(BF16)
    second = mm(hidden_one, w_two) + vec_two[0:1]
    out_two, normed_two, inverse_two = norm(second, vec_two[1:2], vec_two[2:3])
    hidden_two = mish(out_two).astype(BF16)
    return hidden_one, hidden_two, (normed_one, inverse_one, normed_two, inverse_two)


def block_backward(grad_hidden, saved, vec_one, w_two, vec_two):
    normed_one, inverse_one, normed_two, inverse_two = saved
    upstream = mish_slope(normed_two * vec_two[1:2] + vec_two[2:3]) * grad_hidden
    grad_two = norm_back(upstream, normed_two, inverse_two, vec_two[1:2]).astype(BF16)
    sums_two = vector_sums(grad_two, upstream, normed_two)
    grad_one_hidden = mm_t(grad_two, w_two)
    upstream = mish_slope(normed_one * vec_one[1:2] + vec_one[2:3]) * grad_one_hidden
    grad_one = norm_back(upstream, normed_one, inverse_one, vec_one[1:2]).astype(BF16)
    sums_one = vector_sums(grad_one, upstream, normed_one)
    return grad_two, sums_two, grad_one, sums_one


def dynamics_forward(inputs, context, w_one, w_context, vec_one, w_two, vec_two, w_three, vec_three):
    hidden_one, hidden_two, saved = block_forward(
        inputs, context, w_one, w_context, vec_one, w_two, vec_two
    )
    before = mm(hidden_two, w_three) + vec_three[0:1]
    out, normed, inverse = norm(before, vec_three[1:2], vec_three[2:3])
    grouped = out.reshape(out.shape[0], -1, GROUP)
    simplex = jax.nn.softmax(grouped, axis=-1).reshape(out.shape)
    return hidden_one, hidden_two, saved, simplex, normed, inverse


def dynamics_backward(grad_next, simplex, normed, inverse, saved, w_three, vec_three, vec_one, w_two, vec_two):
    weighted = grad_next * simplex
    rows = weighted.shape[0]
    along = jnp.sum(weighted.reshape(rows, -1, GROUP), -1, keepdims=True)
    along = jnp.broadcast_to(along, (rows, along.shape[1], GROUP)).reshape(weighted.shape)
    upstream = weighted - simplex * along
    grad_three = norm_back(upstream, normed, inverse, vec_three[1:2]).astype(BF16)
    sums_three = vector_sums(grad_three, upstream, normed)
    grad_hidden = mm_t(grad_three, w_three)
    grad_two, sums_two, grad_one, sums_one = block_backward(
        grad_hidden, saved, vec_one, w_two, vec_two
    )
    return grad_three, sums_three, grad_two, sums_two, grad_one, sums_one


def value_head(hidden_two, w_three, bias, lower, fraction, scale, heads):
    logits = mm(hidden_two, w_three) + bias
    log_prob = jax.nn.log_softmax(logits, axis=-1)
    bins = jnp.arange(logits.shape[-1], dtype=jnp.int32)[None, :]
    target = jnp.where(bins == lower, 1.0 - fraction, 0.0) + jnp.where(
        bins == lower + 1, fraction, 0.0
    )
    loss = -jnp.sum(target * log_prob, -1) / heads
    grad_logits = (scale / heads * (jnp.exp(log_prob) - target)).astype(BF16)
    return loss, grad_logits


def spread(values, axis_len):
    blocks = lax.axis_size("dp") // BLOCK
    rows = values.shape[0] // (blocks * BLOCK)
    values = values.reshape((blocks, LINE, 2, 2, rows) + values.shape[1:])
    if blocks > 1:
        values = jnp.moveaxis(values, 0, 3)
    return values.reshape((LINE, 2, 2, blocks * rows) + values.shape[5:])


def across_blocks(values, axis):
    blocks = lax.axis_size("dp") // BLOCK
    if blocks == 1:
        return values
    groups = [[block * BLOCK + place for block in range(blocks)] for place in range(BLOCK)]
    return lax.psum_scatter(
        values, "dp", scatter_dimension=axis, axis_index_groups=groups, tiled=True
    )


def sum_across_blocks(values):
    blocks = lax.axis_size("dp") // BLOCK
    if blocks == 1:
        return values
    groups = [[block * BLOCK + place for block in range(blocks)] for place in range(BLOCK)]
    return lax.psum(values, "dp", axis_index_groups=groups)


def reduce_first(values, axis_x, bit_x, at_x, axis_y, bit_y, at_y):
    sent = pick(values, 1 - at_x, axis_x).astype(BF16)
    total = pick(values, at_x, axis_x) + swap_dp(sent, bit_x).astype(F32)
    if axis_y > axis_x:
        axis_y -= 1
    sent = pick(total, 1 - at_y, axis_y).astype(BF16)
    return pick(total, at_y, axis_y) + swap_dp(sent, bit_y).astype(F32)


def plane_scatter(values, at_x, at_y):
    half = LINE // 2
    first = reduce_first(values[:half], 2, 1, at_x, 1, 2, at_y)
    second = reduce_first(values[half:], 1, 2, at_y, 2, 1, at_x)
    return jnp.concatenate([first, second], 0)


def plane_scatter_one(values, at_x, at_y):
    half = values.shape[-1] // 256 * 128
    if half == 0:
        return reduce_first(values, 1, 1, at_x, 0, 2, at_y)
    first = reduce_first(values[..., :half], 1, 1, at_x, 0, 2, at_y)
    second = reduce_first(values[..., half:], 0, 2, at_y, 1, 1, at_x)
    return jnp.concatenate([first, second], -1)


def line_exchange(values, at_z, last):
    out = jnp.zeros((LINE + 1,) + values.shape[1:], F32)
    for step in range(LINE):
        part = pick(values, at_z ^ step)
        if step:
            part = swap_dp(part.astype(BF16), 4 * step).astype(F32)
        out = lax.dynamic_update_index_in_dim(out, part, at_z ^ step, 0)
    return lax.dynamic_update_index_in_dim(out, last, LINE, 0)


def plane_total(values, kind=F32):
    values = values + swap_dp(values.astype(kind), 1).astype(F32)
    return values + swap_dp(values.astype(kind), 2).astype(F32)


def line_collect(values, at_z, last, kind=F32):
    out = jnp.zeros((LINE + 1,) + values.shape, F32)
    sent = values.astype(kind)
    for step in range(LINE):
        part = swap_dp(sent, 4 * step).astype(F32) if step else values
        out = lax.dynamic_update_index_in_dim(out, part, at_z ^ step, 0)
    return lax.dynamic_update_index_in_dim(out, last, LINE, 0)


def line_total(values):
    total = values
    for step in range(1, LINE):
        total = total + swap_dp(values, 4 * step)
    return total


def in_core_order(core, own, other, axis):
    return jnp.where(
        core == 0, jnp.concatenate([own, other], axis), jnp.concatenate([other, own], axis)
    )


def general_shards(
    latent,
    action,
    task_ids,
    action_mask,
    task_table,
    target_latent,
    bin_lower,
    bin_frac,
    dyn_w1,
    dyn_wc,
    dyn_vec1,
    dyn_w2,
    dyn_vec2,
    dyn_w3,
    dyn_vec3,
    q_w1,
    q_wc,
    q_vec1,
    q_w2,
    q_vec2,
    q_w3,
    q_b3,
):
    place = lax.axis_index("dp")
    core = lax.axis_index("tensor")
    at_x, at_y, at_z = place % 2, place // 2 % 2, place // 4 % 4
    local_rows = latent.shape[0]
    half_rows = local_rows // 2
    half_latent = latent.shape[1]
    half_hidden = dyn_w1.shape[1]
    inv_root = 1.0 / math.sqrt(local_rows * lax.axis_size("dp"))
    task_count = task_table.shape[0]
    heads = q_w1.shape[0]
    head_places = (at_z, heads - 1)

    def both(values, axis):
        return jnp.concatenate(own_then_other(values), axis)

    dyn_w1_all, dyn_wc_all, dyn_vec1_all = both(dyn_w1, 1), both(dyn_wc, 1), both(dyn_vec1, 1)
    dyn_w2_all = both(dyn_w2, 0)
    dyn_w3_all = in_core_order(core, *own_then_other(dyn_w3), 1)
    dyn_vec3_all = in_core_order(core, *own_then_other(dyn_vec3), 1)
    head_weights = []
    for head in head_places:
        head_weights.append(
            (
                both(pick(q_w1, head), 1),
                both(pick(q_wc, head), 1),
                both(pick(q_vec1, head), 1),
                both(pick(q_w2, head), 0),
                pick(q_vec2, head),
                pick(q_w3, head),
                pick(q_b3, head),
            )
        )

    def my_rows(values):
        return lax.dynamic_slice_in_dim(values, core * half_rows, half_rows, 0)

    def their_rows(values):
        return lax.dynamic_slice_in_dim(values, (1 - core) * half_rows, half_rows, 0)

    def whole_columns(values):
        return in_core_order(core, my_rows(values), swap_core(their_rows(values)), 1)

    my_latent = whole_columns(latent)
    my_target = whole_columns(target_latent)
    my_ids = my_rows(task_ids)[:, None]
    onehot = (my_ids == jnp.arange(task_count, dtype=jnp.int32)[None, :]).astype(BF16)
    table = jnp.concatenate([action_mask.astype(BF16), task_table], 1)
    looked_up = mm(onehot, table)
    acts = action.shape[1]
    acted = my_rows(action).astype(F32) * looked_up[:, :acts]
    my_context = jnp.concatenate([acted, looked_up[:, acts:]], 1).astype(BF16)
    fraction = my_rows(bin_frac)[:, None]
    piece_one = lax.reduce_precision(fraction, 8, 7)
    piece_two = lax.reduce_precision(fraction - piece_one, 8, 7)
    piece_three = fraction - piece_one - piece_two
    meta = [my_ids, my_rows(bin_lower)[:, None], piece_one, piece_two, piece_three]
    meta = [item.astype(BF16) for item in meta]
    width = my_latent.shape[1]
    context_width = my_context.shape[1]
    packed = jnp.concatenate([my_latent, my_context] + meta, 1)
    packed = jnp.concatenate([packed] + [swap_dp(packed, 4 * step) for step in range(1, LINE)], 0)
    inputs = packed[:, :width]
    context = packed[:, width : width + context_width]
    meta = packed[:, width + context_width :].astype(F32)
    all_ids = meta[:, 0:1].astype(jnp.int32)
    lower = meta[:, 1:2].astype(jnp.int32)
    fraction = meta[:, 2:3] + meta[:, 3:4] + meta[:, 4:5]
    all_onehot = (all_ids == jnp.arange(task_count, dtype=jnp.int32)[None, :]).astype(F32)
    other_inputs, other_context = swap_core(inputs), swap_core(context)

    dyn_one, dyn_two, dyn_saved, simplex, normed_three, inverse_three = dynamics_forward(
        inputs, context, dyn_w1_all, dyn_wc_all, dyn_vec1_all, dyn_w2_all, dyn_vec2,
        dyn_w3_all, dyn_vec3_all,
    )
    next_low = simplex.astype(BF16)
    mismatch = next_low[:half_rows].astype(F32) - my_target
    consistency = jnp.sum(mismatch * mismatch, -1)
    other_next = swap_core(next_low)

    head_results = []
    for weights in head_weights:
        w_one, w_context, vec_one, w_two, vec_two, w_three, bias = weights
        hidden_one, hidden_two, saved = block_forward(
            next_low, context, w_one, w_context, vec_one, w_two, vec_two
        )
        loss, grad_logits = value_head(
            hidden_two, w_three, bias[None], lower, fraction, inv_root, heads
        )
        grad_hidden = mm_t(grad_logits, w_three)
        grad_two, sums_two, grad_one, sums_one = block_backward(
            grad_hidden, saved, vec_one, w_two, vec_two
        )
        head_results.append(
            (hidden_one, hidden_two, loss, grad_logits, grad_two, sums_two, grad_one, sums_one)
        )

    main, extra = head_results
    grad_in = mm_t(main[6], head_weights[0][0])
    own_grad = grad_in[:half_rows] + mm_t(extra[6][:half_rows], head_weights[1][0])
    own_loss = main[2][:half_rows] + extra[2][:half_rows]
    for step in range(1, LINE):
        part = slice(step * half_rows, (step + 1) * half_rows)
        own_grad = own_grad + swap_dp(grad_in[part].astype(BF16), 4 * step).astype(F32)
        own_loss = own_loss + swap_dp(main[2][part], 4 * step)
    own_grad = own_grad + 2.0 * inv_root * mismatch
    own_low = own_grad.astype(BF16)
    grad_next = jnp.concatenate(
        [own_low] + [swap_dp(own_low, 4 * step) for step in range(1, LINE)], 0
    ).astype(F32)
    my_losses = jnp.stack([consistency, own_loss], 1)
    losses = in_core_order(core, my_losses, swap_core(my_losses), 0)

    grad_three, sums_three, dyn_grad_two, dyn_sums_two, dyn_grad_one, dyn_sums_one = (
        dynamics_backward(
            grad_next, simplex, normed_three, inverse_three, dyn_saved, dyn_w3_all, dyn_vec3_all,
            dyn_vec1_all, dyn_w2_all, dyn_vec2,
        )
    )
    own_latent_grad = mm_t(dyn_grad_one[:half_rows], dyn_w1_all)
    left, right = own_latent_grad[:, :half_latent], own_latent_grad[:, half_latent:]
    kept = jnp.where(core == 0, left, right)
    received = swap_core(jnp.where(core == 0, right, left))
    latent_grad = in_core_order(core, kept, received, 0)

    def own_half(values):
        return jnp.concatenate([values[:, :half_hidden], swap_core(values[:, half_hidden:])], 0)

    def all_rows(values):
        return jnp.concatenate([values, swap_core(values)], 0)

    def quarter(values, size):
        blocks = lax.axis_size("dp") // BLOCK
        cut = values.reshape(values.shape[0], blocks, LINE, size // (blocks * LINE))
        return pick(cut, at_z, 2).reshape(values.shape[0], size // LINE)

    def spread_quarter(values):
        blocks = lax.axis_size("dp") // BLOCK
        rows = values.shape[0] // (blocks * PLANE)
        values = values.reshape((blocks, 2, 2, rows) + values.shape[1:])
        if blocks > 1:
            values = jnp.moveaxis(values, 0, 2)
        return values.reshape((2, 2, blocks * rows) + values.shape[4:])

    both_next = jnp.concatenate([next_low, other_next], 0)
    both_inputs = jnp.concatenate([inputs, other_inputs], 0)
    both_context = jnp.concatenate([context, other_context], 0)
    features = both_next.shape[1]
    hidden = 2 * half_hidden

    def quarter_grads(hidden_one, grad_two, grad_one, rows_in):
        first_factor, grad_factor = own_half(hidden_one), own_half(grad_one)
        w_two_part = t_mm(all_rows(quarter(grad_two, hidden)), first_factor)
        w_one_part = t_mm(quarter(rows_in, features), grad_factor)
        w_context_part = t_mm(both_context, grad_factor)
        return (
            plane_scatter_one(spread_quarter(w_two_part), at_x, at_y),
            plane_scatter_one(spread_quarter(w_one_part), at_x, at_y),
            plane_total(w_context_part, BF16),
        )

    def outer_quarter(left, right):
        part = t_mm(quarter(left, hidden), right)
        return plane_scatter_one(spread_quarter(part), at_x, at_y)

    first_factor, grad_factor = own_half(main[0]), own_half(main[6])
    main_two = plane_scatter(spread(t_mm(all_rows(main[4]), first_factor), 0), at_x, at_y)
    main_one = plane_scatter(spread(t_mm(both_next, grad_factor), 0), at_x, at_y)
    main_three = plane_scatter(spread(t_mm(main[1], main[3]), 0), at_x, at_y)
    main_context = plane_total(t_mm(both_context, grad_factor), BF16)
    extra_two, extra_one, extra_context = quarter_grads(extra[0], extra[4], extra[6], both_next)
    extra_three = outer_quarter(extra[1], extra[3])
    dyn_w2_part, dyn_w1_part, dyn_context = quarter_grads(
        dyn_one, dyn_grad_two, dyn_grad_one, both_inputs
    )
    dyn_w3_part = outer_quarter(
        all_rows(dyn_two),
        jnp.concatenate(
            [
                jnp.where(core == 0, grad_three[:, :half_latent], grad_three[:, half_latent:]),
                swap_core(
                    jnp.where(core == 0, grad_three[:, half_latent:], grad_three[:, :half_latent])
                ),
            ],
            0,
        ),
    )

    q_w2_out = across_blocks(line_exchange(main_two, at_z, extra_two), 1).transpose(0, 2, 1)
    q_w1_out = across_blocks(line_exchange(main_one, at_z, extra_one), 1)
    q_w3_out = line_exchange(main_three, at_z, extra_three)
    q_w3_out = across_blocks(q_w3_out + swap_core(q_w3_out), 1)
    dyn_w2_out = across_blocks(dyn_w2_part, 0).transpose(1, 0)
    dyn_w1_out = across_blocks(dyn_w1_part, 0)
    dyn_w3_out = across_blocks(dyn_w3_part, 0)
    q_wc_out = sum_across_blocks(line_collect(main_context, at_z, extra_context, BF16))
    dyn_wc_out = sum_across_blocks(dyn_context)

    def core_vec(values):
        own, other = values[:, :half_hidden], values[:, half_hidden:]
        return own + swap_core(other)

    def sums_of(result):
        return (
            core_vec(result[7]),
            result[5] + swap_core(result[5]),
            jnp.sum(result[3].astype(F32), 0)[None],
        )

    def pack(items):
        return jnp.concatenate([item.reshape(-1) for item in items])

    main_sums, extra_sums = sums_of(main), sums_of(extra)
    main_bias = main_sums[2] + swap_core(main_sums[2])
    extra_bias = extra_sums[2] + swap_core(extra_sums[2])
    main_sums, extra_sums = main_sums[:2] + (main_bias,), extra_sums[:2] + (extra_bias,)
    three_own = jnp.where(core == 0, sums_three[:, :half_latent], sums_three[:, half_latent:])
    three_other = jnp.where(core == 0, sums_three[:, half_latent:], sums_three[:, :half_latent])
    dyn_sums = (
        core_vec(dyn_sums_one),
        dyn_sums_two + swap_core(dyn_sums_two),
        three_own + swap_core(three_other),
    )
    def table_part(grad_one, w_context, rows):
        embed = mm_t(grad_one[:rows], w_context[acts:])
        return lax.dot_general(
            all_onehot[:rows], embed, (((0,), (0,)), ((), ())), precision=HIGHEST
        )

    table_grad = (
        table_part(main[6], head_weights[0][1], inputs.shape[0])
        + table_part(extra[6], head_weights[1][1], half_rows)
        + table_part(dyn_grad_one, dyn_wc_all, half_rows)
    )
    table_grad = line_total(table_grad + swap_core(table_grad))
    flat = sum_across_blocks(
        plane_total(pack((table_grad,) + dyn_sums + extra_sums + main_sums))
    )
    sizes = [table_grad] + list(dyn_sums)
    pieces = []
    start = 0
    for item in sizes:
        pieces.append(flat[start : start + item.size].reshape(item.shape))
        start += item.size
    head_size = sum(item.size for item in main_sums)
    extra_flat, main_flat = flat[start : start + head_size], flat[start + head_size :]
    head_flat = line_collect(main_flat, at_z, extra_flat)
    head_pieces = []
    start = 0
    for item in main_sums:
        head_pieces.append(
            head_flat[:, start : start + item.size].reshape((heads,) + item.shape)
        )
        start += item.size
    table_out, dyn_vec1_out, dyn_vec2_out, dyn_vec3_out = pieces
    q_vec1_out, q_vec2_out, q_b3_out = head_pieces
    return (
        losses,
        latent_grad,
        table_out,
        dyn_w1_out,
        dyn_wc_out,
        dyn_vec1_out,
        dyn_w2_out,
        dyn_vec2_out,
        dyn_w3_out,
        dyn_vec3_out,
        q_w1_out,
        q_wc_out,
        q_vec1_out,
        q_w2_out,
        q_vec2_out,
        q_w3_out,
        q_b3_out[:, 0],
    )


def gather_sum(values, ones):
    parts = []
    for start in range(0, values.shape[1], 128):
        piece = values[:, start : start + 128]
        high = piece.astype(BF16)
        rest = piece - high.astype(F32)
        middle = rest.astype(BF16)
        low = (rest - middle.astype(F32)).astype(BF16)
        parts.append(mm(high, ones) + mm(middle, ones) + mm(low, ones))
    return jnp.concatenate(parts, 1)


def line_kernel(sizes, scale, *refs):
    (slot, width, hidden, bins, tasks, acts, context_width, heads) = sizes
    (
        latent, action, task_ids, action_mask, task_table, target_latent, bin_lower, bin_frac,
        dyn_vec1, dyn_vec2, dyn_vec3, q_vec1, q_vec2, q_b3,
        dyn_w1, dyn_wc, dyn_w2, dyn_w3, q_w1, q_wc, q_w2, q_w3,
        out_losses, out_latent, out_table, out_dw1, out_dwc, out_dvec, out_dw2, out_dw3,
        out_qw1, out_qwc, out_qvec, out_qw2, out_qw3,
        w1, wc, w2, dw3, qw3, dv1, dv3, qv1, qv2, qb3,
        xbuf, xother, tgt, nxt, nxto, dyn_x1, dyn_x2, dyn_h1, dyn_h2, simplex, x3,
        dyn_inv, x1, x2, inv, h1, h2, gp2, gp1, h1o, gp2o, gp1o, upstream, gl, dyn_gp3,
        acc, dxm, dxr, own_g, all_g, lossbuf,
        p2, r2, t2, p1, r1, t1, p3, p3h, r3, t3, p3o,
        e2, er2, et2, e1, er1, et1, e3, er3, et3, e3o,
        er2b, et2b, er1b, et1b, d3, d3s, d3o, er3b, et3b,
        pc, pcx, pcy, pq, pqx, pqy, ctx, vb, vbo, vp, vpx, vpy, tb, tbo, tbr,
        send_sem, recv_sem, local_sem, free_a, free_b, free_f,
    ) = refs
    half = hidden // 2
    half_w = width // 2
    own_two, own_one = hidden // BLOCK, width // BLOCK
    rows_all = slot * LINE
    place = lax.axis_index("dp")
    core = lax.axis_index("tensor")
    at_x = lax.rem(place, 2)
    at_y = lax.rem(place // 2, 2)
    at_z = lax.rem(place // 4, 4)
    z_of = [
        at_z,
        at_z + 1 - 2 * lax.rem(at_z, 2),
        lax.rem(at_z + 2, 4),
        3 - at_z,
    ]
    to_core = (place, 1 - core)
    to_x = (place + 1 - 2 * at_x, core)
    to_y = (place + 2 - 4 * at_y, core)
    to_z = [None] + [(place + 4 * (z_of[k] - at_z), core) for k in range(1, LINE)]
    mesh_id = pl.DeviceIdType.MESH
    counter = [0, 0]
    pending = []

    def describe(source, target, device):
        at = counter[0]
        counter[0] += 1
        return pltpu.make_async_remote_copy(
            src_ref=source, dst_ref=target, send_sem=send_sem.at[at], recv_sem=recv_sem.at[at],
            device_id=device, device_id_type=mesh_id,
        )

    def remote(source, target, device):
        copy = describe(source, target, device)
        copy.start()
        pending.append(copy)
        return copy

    def sent(copy):
        copy.wait_send()
        pending[:] = [item for item in pending if item is not copy]

    def describe_local(source, target):
        at = counter[1]
        counter[1] += 1
        return pltpu.make_async_copy(source, target, local_sem.at[at])

    def local(source, target):
        copy = describe_local(source, target)
        copy.start()
        return copy

    low = slice(0, half)
    high = slice(half, hidden)
    own_cols = pl.ds(pl.multiple_of(half_w * core, 128), half_w)
    other_cols = pl.ds(pl.multiple_of(half_w * (1 - core), 128), half_w)
    own_rows = pl.ds(pl.multiple_of(slot * core, 64), slot)
    other_rows = pl.ds(pl.multiple_of(slot * (1 - core), 64), slot)

    def load_weights(to, one, context, two):
        mine = [
            local(one, w1.at[to, :, low]),
            local(context, wc.at[to, :, low]),
            local(two, w2.at[to, low, :]),
        ]
        return mine

    def send_weights(to, one, context, two):
        return [
            remote(one, w1.at[to, :, high], to_core),
            remote(context, wc.at[to, :, high], to_core),
            remote(two, w2.at[to, high, :], to_core),
        ]

    head_z = at_z
    last = heads - 1
    dyn_ready = load_weights(0, dyn_w1, dyn_wc, dyn_w2)
    three_ready = local(dyn_w3, dw3.at[:, own_cols])
    main_ready = load_weights(1, q_w1.at[head_z], q_wc.at[head_z], q_w2.at[head_z])
    main_three = local(q_w3.at[head_z], qw3.at[0])
    extra_three = local(q_w3.at[last], qw3.at[1])

    dv1[:, low] = dyn_vec1[...]
    dv3[:, own_cols] = dyn_vec3[...]
    qv1[0, :, low] = q_vec1[head_z]
    qv1[1, :, low] = q_vec1[last]
    qv2[0] = q_vec2[head_z]
    qv2[1] = q_vec2[last]
    qb3[0] = q_b3[pl.ds(head_z, 1), :]
    qb3[1] = q_b3[last : last + 1, :]
    vb[...] = jnp.zeros_like(vb)

    rows_chip = 2 * slot
    row = lax.broadcasted_iota(jnp.int32, (rows_chip, rows_chip), 0)
    lane = lax.broadcasted_iota(jnp.int32, (rows_chip, rows_chip), 1)

    def column(values):
        return jnp.sum(jnp.where(row == lane, values.astype(F32), 0.0), 1, keepdims=True)

    ids = column(task_ids[...])
    fraction = column(bin_frac[...])
    task = lax.broadcasted_iota(jnp.int32, (rows_chip, tasks), 1).astype(F32)
    onehot = (ids == task).astype(F32).astype(BF16)

    def shift_matrix(count, start):
        near = lax.broadcasted_iota(jnp.int32, (count, 128), 0)
        far = lax.broadcasted_iota(jnp.int32, (count, 128), 1)
        return (near + start == far).astype(F32).astype(BF16)

    to_acts = shift_matrix(acts, 0)
    table = (
        t_mm(action_mask[...].astype(F32).astype(BF16), to_acts)
        + mm(task_table[...], shift_matrix(context_width - acts, acts))
    ).astype(BF16)
    lane = lax.broadcasted_iota(jnp.int32, (rows_chip, 128), 1)
    factor = t_mm(action[...], to_acts) + (lane >= acts).astype(F32)
    piece_one = fraction.astype(BF16).astype(F32)
    piece_two = (fraction - piece_one).astype(BF16).astype(F32)
    facts = mm(onehot, table) * factor
    for index, item in enumerate(
        (ids, column(bin_lower[...]), piece_one, piece_two, fraction - piece_one - piece_two)
    ):
        facts = facts + jnp.where(lane == context_width + index, item, 0.0)
    ctx[...] = facts
    xbuf[0:slot, width : width + 128] = ctx[own_rows, :].astype(BF16)
    xbuf[0:slot, own_cols] = latent[own_rows, :]
    tgt[:, own_cols] = target_latent[own_rows, :]
    barrier = pltpu.get_barrier_semaphore()
    peers = [to_core, to_x, to_y] + to_z[1:]
    for peer in peers:
        pl.semaphore_signal(barrier, inc=1, device_id=peer, device_id_type=mesh_id)
    pl.semaphore_wait(barrier, len(peers))

    lat_copy = remote(latent.at[other_rows], xbuf.at[pl.ds(0, slot), own_cols], to_core)
    tgt_copy = remote(target_latent.at[other_rows], tgt.at[:, own_cols], to_core)

    vec_copies = [
        remote(dyn_vec1, dv1.at[:, high], to_core),
        remote(dyn_vec3, dv3.at[:, own_cols], to_core),
        remote(q_vec1.at[head_z], qv1.at[0, :, high], to_core),
        remote(q_vec1.at[last], qv1.at[1, :, high], to_core),
    ]
    dyn_ready_other = send_weights(0, dyn_w1, dyn_wc, dyn_w2)
    three_ready_other = remote(dyn_w3, dw3.at[:, own_cols], to_core)
    main_ready_other = send_weights(1, q_w1.at[head_z], q_wc.at[head_z], q_w2.at[head_z])
    lat_copy.wait_recv()
    line_in = [
        remote(xbuf.at[pl.ds(0, slot)], xbuf.at[pl.ds(slot * k, slot)], to_z[k])
        for k in range(1, LINE)
    ]
    for copy in vec_copies:
        copy.wait_recv()

    CH = 64

    def over_rows(first, count, body):
        if count <= CH:
            body(pl.ds(first, count))
            return

        def step(index, carry):
            body(pl.ds(pl.multiple_of(first + index * CH, CH), CH))
            return carry

        lax.fori_loop(0, count // CH, step, 0)

    def norm_rows(pre, keep, inverse, vec, out, first, count):
        features = pre.shape[1]

        def body(rows):
            values = pre[rows, :]
            centred = values - jnp.sum(values, -1, keepdims=True) * (1.0 / features)
            inv_rows = lax.rsqrt(
                jnp.sum(centred * centred, -1, keepdims=True) * (1.0 / features) + EPSILON
            )
            normed = centred * inv_rows
            keep[rows, :] = normed.astype(keep.dtype)
            inverse[rows, :] = inv_rows
            out[rows, :] = mish(normed * vec[1:2, :] + vec[2:3, :]).astype(BF16)

        over_rows(first, count, body)

    def add_sums(at, rounded, along, shift):
        count, features = shift.shape
        for index, item in enumerate((rounded, along, shift)):
            acc[at + index, :, 0:features] += jnp.sum(item.reshape(count // 8, 8, features), 0)

    def back_rows(grad, normed_ref, inverse, vec, out, at, first, count, slope):
        features = normed_ref.shape[1]

        def body(rows):
            normed = normed_ref[rows, :].astype(F32)
            gain = vec[1:2, :]
            up = grad[rows, :]
            if slope:
                up = mish_slope(normed * gain + vec[2:3, :]) * up
            weighted = up * gain
            along = up * normed
            mean_one = jnp.sum(weighted, -1, keepdims=True) * (1.0 / features)
            mean_two = jnp.sum(weighted * normed, -1, keepdims=True) * (1.0 / features)
            result = (inverse[rows, :] * (weighted - mean_one - normed * mean_two)).astype(BF16)
            out[rows, :] = result
            add_sums(at, result.astype(F32), along, up)

        over_rows(first, count, body)

    def two_tiles(body):
        def step(index, carry):
            body(pl.ds(pl.multiple_of(index * half, 128), half))
            return carry

        lax.fori_loop(0, 2, step, 0)

    def layers_forward(to, source, vec_one, vec_two, keep_one, keep_two, inverse, hid_one, hid_two,
                       first, count, ready):
        rows = pl.ds(first, count)
        ready(0)

        def first_tile(cols):
            x1[rows, cols] = (
                mm(source[rows, 0:width], w1[to, :, cols])
                + mm(xbuf[rows, width : width + context_width], wc[to, :, cols])
                + vec_one[0:1, cols]
            )

        two_tiles(first_tile)
        norm_rows(x1, keep_one, inverse.at[0], vec_one, hid_one, first, count)
        ready(1)

        def second_tile(cols):
            x2[rows, cols] = mm(hid_one[rows, :], w2[to, :, cols]) + vec_two[0:1, cols]

        two_tiles(second_tile)
        norm_rows(x2, keep_two, inverse.at[1], vec_two, hid_two, first, count)

    def back_two_to_one(to, grad, first, count, parts=(0, 1)):
        rows = pl.ds(first, count)

        def tile(cols):
            upstream[rows, cols] = mm_t(grad[rows, :], w2[to, cols, :])

        if len(parts) == 2:
            two_tiles(tile)
        else:
            tile(slice(parts[0] * half, (parts[0] + 1) * half))

    def ready_of(mine, others):
        def ready(stage):
            picked = (0, 1) if stage == 0 else (2,)
            for index in picked:
                mine[index].wait()
                others[index].wait_recv()

        return ready

    def nothing(stage):
        return None

    line_in[0].wait_recv()
    layers_forward(
        0, xbuf, dv1, dyn_vec2, dyn_x1, dyn_x2, dyn_inv, dyn_h1, dyn_h2, 0, 2 * slot,
        ready_of(dyn_ready, dyn_ready_other),
    )
    for copy in line_in[1:]:
        copy.wait_recv()
    x_copy = remote(xbuf, xother, to_core)
    layers_forward(
        0, xbuf, dv1, dyn_vec2, dyn_x1, dyn_x2, dyn_inv, dyn_h1, dyn_h2, 2 * slot,
        rows_all - 2 * slot, nothing,
    )
    three_ready.wait()
    three_ready_other.wait_recv()
    x3[...] = mm(dyn_h2[...], dw3[...]) + dv3[0:1, :]
    group_row = lax.broadcasted_iota(jnp.int32, (128, 128), 0) // GROUP
    group_col = lax.broadcasted_iota(jnp.int32, (128, 128), 1) // GROUP
    ones = (group_row == group_col).astype(F32).astype(BF16)

    def simplex_rows(rows):
        values = x3[rows, :]
        centred = values - jnp.sum(values, -1, keepdims=True) * (1.0 / width)
        inv_rows = lax.rsqrt(
            jnp.sum(centred * centred, -1, keepdims=True) * (1.0 / width) + EPSILON
        )
        normed = centred * inv_rows
        x3[rows, :] = normed
        dyn_inv[2, rows, :] = inv_rows
        grown = jnp.exp(normed * dv3[1:2, :] + dv3[2:3, :])
        share = grown / gather_sum(grown, ones)
        simplex[rows, :] = share
        nxt[rows, :] = share.astype(BF16)

    over_rows(0, rows_all, simplex_rows)
    for copy in dyn_ready_other:
        sent(copy)
    pl.semaphore_signal(free_a, inc=1, device_id=to_core, device_id_type=mesh_id)
    extra_ready = load_weights(0, q_w1.at[last], q_wc.at[last], q_w2.at[last])
    next_copy = remote(nxt, nxto, to_core)
    tgt_copy.wait_recv()
    gap = nxt[0:slot, :].astype(F32) - tgt[...]
    own_g[...] = gap * (2.0 * scale)
    consistency = jnp.sum(gap * gap, -1, keepdims=True)
    pl.semaphore_wait(free_a, 1)
    extra_ready_other = send_weights(0, q_w1.at[last], q_wc.at[last], q_w2.at[last])

    def value_rows(head, first, count):
        rows = pl.ds(first, count)
        logits = mm_t(h2[rows, :], qw3[head]) + qb3[head]
        logits = logits - jnp.max(logits, -1, keepdims=True)
        grown = jnp.exp(logits)
        total = jnp.sum(grown, -1, keepdims=True)
        lane = lax.broadcasted_iota(jnp.int32, (count, bins), 1).astype(F32)
        facts = xbuf[rows, width : width + 128].astype(F32)
        lower = facts[:, context_width + 1 : context_width + 2]
        fraction = (
            facts[:, context_width + 2 : context_width + 3]
            + facts[:, context_width + 3 : context_width + 4]
            + facts[:, context_width + 4 : context_width + 5]
        )
        target = jnp.where(lane == lower, 1.0 - fraction, 0.0) + jnp.where(
            lane == lower + 1.0, fraction, 0.0
        )
        loss = -jnp.sum(target * (logits - jnp.log(total)), -1, keepdims=True) * (1.0 / heads)
        grad = (scale / heads * (grown / total - target)).astype(BF16)
        gl[rows, :] = grad

        def tile(cols):
            upstream[rows, cols] = mm(grad, qw3[head, :, cols])

        two_tiles(tile)
        acc[6, 0, 0:bins] += jnp.sum(grad.astype(F32), 0)
        return loss

    def table_sum(to, grad, first, count):
        rows = pl.ds(first, count)
        embed = mm_t(grad[rows, :], wc[to])
        ids = xbuf[rows, width : width + 128].astype(F32)[:, context_width : context_width + 1]
        task = lax.broadcasted_iota(jnp.int32, (count, tasks), 1).astype(F32)
        onehot = (ids == task).astype(F32).astype(BF16)
        top = embed.astype(BF16)
        rest = embed - top.astype(F32)
        middle = rest.astype(BF16)
        lowest = (rest - middle.astype(F32)).astype(BF16)
        tb[:, 0:context_width] += (
            t_mm(onehot, top) + t_mm(onehot, middle) + t_mm(onehot, lowest)
        )

    def finish_vectors(slot_at, width_three):
        for index in range(3):
            vb[slot_at, index : index + 1, :] = jnp.sum(acc[index], 0, keepdims=True)
            vb[slot_at, 3 + index : 4 + index, :] = jnp.sum(acc[3 + index], 0, keepdims=True)
        if width_three:
            three = [jnp.sum(acc[6 + index, :, 0:width], 0, keepdims=True) for index in range(3)]
            vb[slot_at, 6:7, 0:width] = three[0]
            vb[slot_at, 6:7, width : 2 * width] = three[1]
            vb[slot_at, 7:8, 0:width] = three[2]
        else:
            vb[slot_at, 6:7, :] = jnp.sum(acc[6], 0, keepdims=True)
        return remote(vb.at[slot_at], vbo.at[slot_at], to_core)

    half_cols = pl.ds(pl.multiple_of(half * core, 128), half)

    def join_vectors(slot_at, copy):
        copy.wait_recv()
        sent(copy)
        vp[slot_at, 0:3, :] = vb[slot_at, 0:3, low] + vbo[slot_at, 0:3, high]
        vp[slot_at, 3:8, :] = vb[slot_at, 3:8, half_cols] + vbo[slot_at, 3:8, half_cols]
        return remote(vp.at[slot_at], vpx.at[slot_at], to_x)

    def plane_vectors(slot_at, copy):
        copy.wait_recv()
        sent(copy)
        vp[slot_at] = vp[slot_at] + vpx[slot_at]
        return remote(vp.at[slot_at], vpy.at[slot_at], to_y)

    def total_vectors(slot_at, copy):
        copy.wait_recv()
        sent(copy)
        vp[slot_at] = vp[slot_at] + vpy[slot_at]

    def scatter_start(source, target, x_first, lead):
        if lead is None:
            piece = source.at[:, 1 - at_x] if x_first else source.at[1 - at_y]
        else:
            piece = source.at[lead, :, 1 - at_x] if x_first else source.at[lead, 1 - at_y]
        return remote(piece, target, to_x if x_first else to_y)

    def scatter_middle(copy, source, received, target, x_first, lead):
        copy.wait_recv()
        if lead is None:
            for other in range(2):
                kept = source[other, at_x] if x_first else source[at_y, other]
                received[other] = (received[other].astype(F32) + kept.astype(F32)).astype(BF16)
            piece = received.at[1 - at_y] if x_first else received.at[1 - at_x]
        else:
            for index in range(lead.size):
                for other in range(2):
                    kept = (
                        source[lead.start + index, other, at_x]
                        if x_first
                        else source[lead.start + index, at_y, other]
                    )
                    received[index, other] = (
                        received[index, other].astype(F32) + kept.astype(F32)
                    ).astype(BF16)
            piece = received.at[:, 1 - at_y] if x_first else received.at[:, 1 - at_x]
        return remote(piece, target, to_y if x_first else to_x)

    def scatter_end(copy, received, target, x_first):
        copy.wait_recv()
        mine = at_y if x_first else at_x
        return received[mine].astype(F32) + target[...].astype(F32)

    def scatter_end_lead(copy, received, target, x_first, count):
        copy.wait_recv()
        mine = at_y if x_first else at_x
        for index in range(count):
            target[index] = (
                received[index, mine].astype(F32) + target[index].astype(F32)
            ).astype(BF16)

    first_half, second_half = pl.ds(0, 2), pl.ds(2, 2)

    acc[...] = jnp.zeros_like(acc)
    tb[...] = jnp.zeros_like(tb)
    main_three.wait()
    extra_three.wait()
    layers_forward(
        1, nxt, qv1.at[0], qv2.at[0], x1, x2, inv, h1, h2, 0, rows_all,
        ready_of(main_ready, main_ready_other),
    )
    main_loss = value_rows(0, 0, rows_all)
    back_rows(upstream, x2, inv.at[1], qv2.at[0], gp2, 3, 0, rows_all, True)
    factor_copies = [remote(h1.at[:, high], h1o, to_core), remote(gp2, gp2o, to_core)]
    back_two_to_one(1, gp2, 0, rows_all, (0,))
    for copy in factor_copies:
        copy.wait_recv()
    wide = half // 256 * 128 + 128
    main_two = []
    for index in range(2):
        cols = slice(index * half, (index + 1) * half)
        for part in (slice(0, wide), slice(wide, half)):
            whole = t_mm(gp2[:, cols], h1[:, part]) + t_mm(gp2o[:, cols], h1o[:, part])
            p2[2 * index : 2 * index + 2, :, :, :, part] = whole.astype(BF16).reshape(
                (2, 2, 2, own_two, part.stop - part.start)
            )
        main_two.append(
            scatter_start(p2, r2.at[2 * index : 2 * index + 2], index == 0, pl.ds(2 * index, 2))
        )
    back_two_to_one(1, gp2, 0, rows_all, (1,))
    back_rows(upstream, x1, inv.at[0], qv1.at[0], gp1, 0, 0, rows_all, True)
    one_copy = remote(gp1.at[:, high], gp1o, to_core)
    dx = mm_t(gp1[...], w1[1])
    own_g[...] = own_g[...] + dx[0:slot]
    dxm[:, 0:width] = dx.astype(BF16)
    lane_all = lax.broadcasted_iota(jnp.int32, (rows_all, 128), 1)
    loss_high = main_loss.astype(BF16).astype(F32)
    loss_rest = main_loss - loss_high
    loss_middle = loss_rest.astype(BF16).astype(F32)
    loss_low = loss_rest - loss_middle
    dxm[:, width : width + 128] = jnp.where(
        lane_all == 0, loss_high, jnp.where(lane_all == 1, loss_middle, loss_low)
    ).astype(BF16)
    dx_copies = [
        remote(dxm.at[pl.ds(slot * k, slot)], dxr.at[k - 1], to_z[k]) for k in range(1, LINE)
    ]
    hand, keep = [], []

    def start_two(source, received):
        return [
            scatter_start(
                source, received.at[2 * index : 2 * index + 2], index == 0, pl.ds(2 * index, 2)
            )
            for index in range(2)
        ]

    def middle_two(copies, source, received, target):
        return [
            scatter_middle(
                copies[index], source, received.at[2 * index : 2 * index + 2],
                target.at[2 * index : 2 * index + 2], index == 0, pl.ds(2 * index, 2),
            )
            for index in range(2)
        ]

    def end_two(copies, received, target):
        for index in range(2):
            scatter_end_lead(
                copies[index], received.at[2 * index : 2 * index + 2],
                target.at[2 * index : 2 * index + 2], index == 0, 2,
            )

    def hand_on(source, target):
        keep.append(local(source.at[at_z], target.at[at_z]))
        for k in range(1, LINE):
            hand.append(remote(source.at[z_of[k]], target.at[at_z], to_z[k]))

    def hand_all(source, target):
        mine = target(at_z)
        keep.append(local(source, mine))
        near = remote(source, mine, to_z[1])
        far = remote(source, mine, to_z[2])
        hand.append(near)
        return far, target

    def hand_further(started):
        far, target = started
        far.wait_recv()
        theirs = target(z_of[2])
        hand.append(remote(theirs, theirs, to_z[1]))

    left, right = slice(0, wide), slice(wide, half)

    def context_start(source, received):
        return (
            remote(source.at[:, left], received.at[:, left], to_x),
            remote(source.at[:, right], received.at[:, right], to_y),
        )

    def context_add(source, received, copies):
        for copy in copies:
            copy.wait_recv()
            sent(copy)
        source[...] = (source[...].astype(F32) + received[...].astype(F32)).astype(BF16)

    def context_middle(source, received, target, copies):
        context_add(source, received, copies)
        return (
            remote(source.at[:, left], target.at[:, left], to_y),
            remote(source.at[:, right], target.at[:, right], to_x),
        )

    x_copy.wait_recv()
    one_copy.wait_recv()
    whole = t_mm(xbuf[:, width : width + 128], gp1[:, low]) + t_mm(
        xother[:, width : width + 128], gp1o[...]
    )
    pc[...] = whole[0 : pc.shape[0]].astype(BF16)
    main_context = context_start(pc, pcx)
    next_copy.wait_recv()
    whole = t_mm(nxt[...], gp1[:, low]) + t_mm(nxto[...], gp1o[...])
    p1[...] = whole.astype(BF16).reshape(p1.shape)
    main_one = start_two(p1, r1)
    part = t_mm(h2[...], gl[...])
    p3[...] = part.astype(BF16).reshape(p3.shape)
    three_copy = remote(p3.at[pl.ds(2 * (1 - core), 2)], p3o, to_core)
    main_vec = finish_vectors(0, False)
    acc[...] = jnp.zeros_like(acc)
    table_sum(1, gp1, 0, rows_all)
    for copy in main_ready_other:
        sent(copy)
    pl.semaphore_signal(free_b, inc=1, device_id=to_core, device_id_type=mesh_id)
    dyn_again = load_weights(1, dyn_w1, dyn_wc, dyn_w2)
    for copy in factor_copies + [one_copy]:
        sent(copy)
    pl.semaphore_signal(free_f, inc=1, device_id=to_core, device_id_type=mesh_id)
    pl.semaphore_wait(free_b, 1)
    dyn_again_other = send_weights(1, dyn_w1, dyn_wc, dyn_w2)

    layers_forward(
        0, nxt, qv1.at[1], qv2.at[1], x1, x2, inv, h1, h2, 0, slot,
        ready_of(extra_ready, extra_ready_other),
    )
    extra_loss = value_rows(1, 0, slot)
    back_rows(upstream, x2, inv.at[1], qv2.at[1], gp2, 3, 0, slot, True)
    back_two_to_one(0, gp2, 0, slot)
    back_rows(upstream, x1, inv.at[0], qv1.at[1], gp1, 0, 0, slot, True)
    own_total = own_g[...] + mm_t(gp1[0:slot, :], w1[0])
    value = main_loss[0:slot] + extra_loss
    for index, copy in enumerate(dx_copies):
        copy.wait_recv()
        message = dxr[index].astype(F32)
        own_total = own_total + message[:, 0:width]
        value = value + (
            message[:, width : width + 1]
            + message[:, width + 1 : width + 2]
            + message[:, width + 2 : width + 3]
        )
    all_g[0:slot, :] = own_total.astype(BF16)
    grad_copies = [
        remote(all_g.at[pl.ds(0, slot)], all_g.at[pl.ds(slot * k, slot)], to_z[k])
        for k in range(1, LINE)
    ]
    lane_own = lax.broadcasted_iota(jnp.int32, (slot, 128), 1)
    lossbuf[...] = jnp.where(lane_own == 0, consistency, value)
    loss_copy = remote(lossbuf, out_losses.at[own_rows], to_core)
    keep += [local(lossbuf, out_losses.at[own_rows])]
    table_sum(0, gp1, 0, slot)
    rest = rows_all - slot
    stage = {}

    def between(step):
        if step == 0:
            return
        stage["context"] = context_middle(pc, pcx, pcy, main_context)
        stage["two"] = middle_two(main_two, p2, r2, t2)
        three_copy.wait_recv()
        sent(three_copy)
        stage["three"] = []
        for index in range(2):
            p3h[index] = (
                p3[2 * core + index].astype(F32) + p3o[index].astype(F32)
            ).astype(BF16)
            stage["three"].append(scatter_start(p3h.at[index], r3.at[index], index == 0, None))
        stage["vec"] = join_vectors(0, main_vec)

    layers_forward(
        0, nxt, qv1.at[1], qv2.at[1], x1, x2, inv, h1, h2, slot, rest, between
    )
    first_two = main_two
    main_context, main_two, main_vec = stage["context"], stage["two"], stage["vec"]
    main_three_sum = stage["three"]
    value_rows(1, slot, rest)
    back_rows(upstream, x2, inv.at[1], qv2.at[1], gp2, 3, slot, rest, True)
    pl.semaphore_wait(free_f, 1)
    factor_copies = [remote(gp2, gp2o, to_core), remote(h1.at[:, high], h1o, to_core)]
    back_two_to_one(0, gp2, slot, rest)
    back_rows(upstream, x1, inv.at[0], qv1.at[1], gp1, 0, slot, rest, True)
    one_copy = remote(gp1.at[:, high], gp1o, to_core)
    extra_vec = finish_vectors(1, False)
    acc[...] = jnp.zeros_like(acc)

    context_add(pc, pcy, main_context)
    context_hand = hand_all(pc, lambda at: out_qwc.at[at, pl.ds(0, pc.shape[0])])
    first_one = main_one
    main_one = middle_two(main_one, p1, r1, t1)

    def by_place(body):
        for index in range(LINE):
            @pl.when(at_z == index)
            def _(index=index):
                body(index)

    quarter = hidden // LINE
    quarter_w = width // LINE
    quarter_c = 128 // LINE

    def quarter_two(index, hid, target):
        cols = slice(index * quarter, (index + 1) * quarter)
        whole = t_mm(gp2[:, cols], hid[:, low]) + t_mm(gp2o[:, cols], h1o[...])
        target[...] = whole.astype(BF16).reshape(target.shape)

    def quarter_one(index, mine, others, target, at):
        cols = slice(index * quarter_w, (index + 1) * quarter_w)
        whole = t_mm(mine[:, cols], gp1[:, low]) + t_mm(others[:, cols], gp1o[...])
        target[...] = whole.astype(BF16).reshape(target.shape)
        cols = slice(width + index * quarter_c, width + (index + 1) * quarter_c)
        whole = t_mm(xbuf[:, cols], gp1[:, low]) + t_mm(xother[:, cols], gp1o[...])
        pq[at] = whole.astype(BF16)

    for copy in factor_copies + [one_copy]:
        copy.wait_recv()

    def extra_parts(index):
        part = t_mm(h2[:, index * quarter : (index + 1) * quarter], gl[...])
        e3[...] = part.astype(BF16).reshape(e3.shape)
        quarter_two(index, h1, e2)
        quarter_one(index, nxt, nxto, e1, 0)

    by_place(extra_parts)
    extra_three_sum = remote(e3, e3o, to_core)
    extra_two = scatter_start(e2, er2, True, None)
    extra_one = scatter_start(e1, er1, False, None)
    extra_context = context_start(pq.at[0], pqx.at[0])
    for copy in factor_copies + [one_copy]:
        sent(copy)
    pl.semaphore_signal(free_f, inc=1, device_id=to_core, device_id_type=mesh_id)
    for copy in grad_copies:
        copy.wait_recv()

    def simplex_back(rows):
        share = simplex[rows, :]
        weighted = all_g[rows, :].astype(F32) * share
        up = weighted - share * gather_sum(weighted, ones)
        upstream[rows, 0:width] = up

    over_rows(0, rows_all, simplex_back)
    back_rows(
        upstream.at[:, 0:width], x3, dyn_inv.at[2], dv3, dyn_gp3, 6, 0, rows_all, False
    )

    def dyn_third(index):
        left = dyn_h2[:, index * quarter : (index + 1) * quarter]
        d3s[...] = t_mm(left, dyn_gp3[:, other_cols]).astype(BF16).reshape(d3s.shape)
        d3[...] = t_mm(left, dyn_gp3[:, own_cols]).astype(BF16).reshape(d3.shape)

    by_place(dyn_third)
    d3_copy = remote(d3s, d3o, to_core)

    def three_tile(cols):
        upstream[:, cols] = mm_t(dyn_gp3[...], dw3[cols, :])

    two_tiles(three_tile)
    end_two(main_two, r2, t2)
    hand_on(t2, out_qw2)
    back_rows(upstream, dyn_x2, dyn_inv.at[1], dyn_vec2, gp2, 3, 0, rows_all, True)
    pl.semaphore_wait(free_f, 1)
    factor_copies = [remote(gp2, gp2o, to_core), remote(dyn_h1.at[:, high], h1o, to_core)]
    d3_copy.wait_recv()
    sent(d3_copy)
    d3[...] = (d3[...].astype(F32) + d3o[...].astype(F32)).astype(BF16)
    dyn_three_sum = scatter_start(d3, er3b, False, None)
    extra_three_sum.wait_recv()
    sent(extra_three_sum)
    e3[...] = (e3[...].astype(F32) + e3o[...].astype(F32)).astype(BF16)
    extra_three_sum = scatter_start(e3, er3, False, None)
    extra_vec = join_vectors(1, extra_vec)
    dyn_again[2].wait()
    dyn_again_other[2].wait_recv()
    back_two_to_one(1, gp2, 0, rows_all)
    for copy in factor_copies:
        copy.wait_recv()
    for copy in first_two + first_one:
        sent(copy)
    d2, d1 = p2.at[0], p1.at[0]
    by_place(lambda index: quarter_two(index, dyn_h1, d2))
    back_rows(upstream, dyn_x1, dyn_inv.at[0], dv1, gp1, 0, 0, rows_all, True)
    one_copy = remote(gp1.at[:, high], gp1o, to_core)
    dyn_vec = finish_vectors(2, True)
    for index in (0, 1):
        dyn_again[index].wait()
        dyn_again_other[index].wait_recv()
    table_sum(1, gp1, 0, slot)
    table_copy = remote(tb, tbo, to_core)
    one_copy.wait_recv()
    by_place(lambda index: quarter_one(index, xbuf, xother, d1, 1))
    dyn_one_sum = scatter_start(d1, er1b, False, None)
    dyn_context = context_start(pq.at[1], pqx.at[1])
    lat_g = tgt
    lat_g[...] = mm_t(gp1[0:slot, :], w1[1])
    latent_copy = remote(lat_g.at[:, other_cols], out_latent.at[own_rows], to_core)
    keep += [local(lat_g.at[:, own_cols], out_latent.at[own_rows])]
    dyn_vec = join_vectors(2, dyn_vec)
    table_copy.wait_recv()
    sent(table_copy)
    tb[...] = tb[...] + tbo[...]
    table_copy = remote(tb, tbr.at[0], to_x)

    end_two(main_one, r1, t1)
    hand_on(t1, out_qw1)
    main_three_sum = [
        scatter_middle(main_three_sum[index], p3h.at[index], r3.at[index], t3.at[index],
                       index == 0, None)
        for index in range(2)
    ]
    extra_one2 = scatter_middle(extra_one, e1, er1, et1, False, None)
    extra_two2 = scatter_middle(extra_two, e2, er2, et2, True, None)
    main_vec = plane_vectors(0, main_vec)
    extra_context = context_middle(pq.at[0], pqx.at[0], pqy.at[0], extra_context)
    extra_vec = plane_vectors(1, extra_vec)
    hand_further(context_hand)
    dyn_context = context_middle(pq.at[1], pqx.at[1], pqy.at[1], dyn_context)
    table_copy.wait_recv()
    sent(table_copy)
    tb[...] = tb[...] + tbr[0]
    table_copy = remote(tb, tbr.at[1], to_y)
    dyn_vec = plane_vectors(2, dyn_vec)
    dyn_two_sum = scatter_start(d2, er2b, True, None)
    dyn_three2 = scatter_middle(dyn_three_sum, d3, er3b, et3b, False, None)
    extra_three2 = scatter_middle(extra_three_sum, e3, er3, et3, False, None)
    dyn_one2 = scatter_middle(dyn_one_sum, d1, er1b, et1b, False, None)
    def quarter_rows(at):
        return pl.ds(pl.multiple_of(quarter_c * at, quarter_c), quarter_c)

    context_add(pq.at[0], pqy.at[0], extra_context)
    extra_hand = hand_all(pq.at[0], lambda at: out_qwc.at[last, quarter_rows(at)])
    total_vectors(0, main_vec)
    vec_hand = hand_all(vp.at[0], lambda at: out_qvec.at[at, core])
    vec_near = hand.pop()
    vec_keep = [keep.pop()]
    for index in range(2):
        t3[index] = scatter_end(
            main_three_sum[index], r3.at[index], t3.at[index], index == 0
        ).astype(BF16)
    mine = at_z // 2 == core
    three_out = out_qw3.at[at_z]
    three_copies = []
    for k in range(1, LINE):
        theirs = z_of[k] // 2 == core
        copy = describe(t3.at[lax.rem(z_of[k], 2)], three_out, to_z[k])
        three_copies.append((theirs, copy))

        @pl.when(theirs)
        def _(copy=copy):
            copy.start()

    three_keep = describe_local(t3.at[lax.rem(at_z, 2)], three_out)

    @pl.when(mine)
    def _():
        three_keep.start()

    context_add(pq.at[1], pqy.at[1], dyn_context)
    dyn_hand = hand_all(pq.at[1], lambda at: out_dwc.at[quarter_rows(at)])
    table_copy.wait_recv()
    sent(table_copy)
    tb[...] = tb[...] + tbr[1]
    table_copies = [remote(tb, tbr.at[1 + k], to_z[k]) for k in range(1, LINE)]
    dyn_two2 = scatter_middle(dyn_two_sum, d2, er2b, et2b, True, None)
    total_vectors(1, extra_vec)
    vec_keep += [local(vp.at[1], out_qvec.at[last, core])]
    total_vectors(2, dyn_vec)
    keep += [local(vp.at[2], out_dvec.at[core])]
    hand += [remote(vp.at[2], out_dvec.at[core], to_core)]
    et2[...] = scatter_end(extra_two2, er2, et2, True).astype(BF16)
    keep += [local(et2, out_qw2.at[last])]
    et1[...] = scatter_end(extra_one2, er1, et1, False).astype(BF16)
    keep += [local(et1, out_qw1.at[last])]
    hand_further(vec_hand)
    vec_further = hand.pop()
    hand_further(extra_hand)
    hand_further(dyn_hand)
    o2 = upstream.at[0:own_two, 0:half]
    o1 = upstream.at[own_two : own_two + own_one, 0:half]
    oc = upstream.at[0:own_two, half : half + half_w]
    oc[...] = scatter_end(dyn_three2, er3b, et3b, False)
    keep += [local(oc, out_dw3)]
    et3[...] = scatter_end(extra_three2, er3, et3, False).astype(BF16)
    keep += [local(et3, out_qw3.at[last])]
    o1[...] = scatter_end(dyn_one2, er1b, et1b, False)
    keep += [local(o1, out_dw1)]
    o2[...] = scatter_end(dyn_two2, er2b, et2b, True)
    keep += [local(o2, out_dw2)]
    vec_near.wait_recv()
    vec_further.wait_recv()
    for copy in vec_keep:
        copy.wait()
    vec_cores = remote(out_qvec.at[:, core], out_qvec.at[:, core], to_core)
    for theirs, copy in three_copies:
        @pl.when(theirs)
        def _(copy=copy):
            copy.wait_send()

    three_further = describe(
        out_qw3.at[pl.ds(0, LINE)], out_qw3.at[pl.ds(0, LINE)], to_core
    )

    @pl.when(mine)
    def _():
        three_keep.wait()
        for _, copy in three_copies:
            copy.wait_recv()
        three_further.start()

    for copy in table_copies:
        copy.wait_recv()
        sent(copy)
    tb[...] = tb[...] + tbr[2] + tbr[3] + tbr[4]
    keep += [local(tb, out_table)]
    for copy in hand + [loss_copy, latent_copy]:
        copy.wait_recv()
    for copy in keep:
        copy.wait()
    @pl.when(mine)
    def _():
        three_further.wait_send()

    @pl.when(jnp.logical_not(mine))
    def _():
        three_further.wait_recv()

    vec_cores.wait_recv()
    for copy in list(pending):
        sent(copy)


def line_shards(
    latent,
    action,
    task_ids,
    action_mask,
    task_table,
    target_latent,
    bin_lower,
    bin_frac,
    dyn_w1,
    dyn_wc,
    dyn_vec1,
    dyn_w2,
    dyn_vec2,
    dyn_w3,
    dyn_vec3,
    q_w1,
    q_wc,
    q_vec1,
    q_w2,
    q_vec2,
    q_w3,
    q_b3,
):
    local_rows, half_w = latent.shape
    slot = local_rows // 2
    rows = slot * LINE
    width = 2 * half_w
    half = dyn_w1.shape[1]
    hidden = 2 * half
    heads, bins = q_b3.shape
    tasks, acts = action_mask.shape
    context_width = dyn_wc.shape[0]
    pad_context = -(-context_width // 16) * 16
    own_two = hidden // BLOCK
    own_one = width // BLOCK
    scale = 1.0 / math.sqrt(local_rows * lax.axis_size("dp"))
    sizes = (slot, width, hidden, bins, tasks, acts, context_width, heads)

    def shape(*dims, kind=F32):
        return jax.ShapeDtypeStruct(dims, kind)

    out_shape = (
        shape(local_rows, 128),
        shape(local_rows, half_w),
        shape(tasks, 128),
        shape(own_one, half),
        shape(128, half, kind=BF16),
        shape(2, 8, half),
        shape(own_two, half),
        shape(own_two, half_w),
        shape(heads, own_one, half, kind=BF16),
        shape(heads, 128, half, kind=BF16),
        shape(heads, 2, 8, half),
        shape(heads, own_two, half, kind=BF16),
        shape(heads, own_two, bins, kind=BF16),
    )
    v = pltpu.VMEM
    scratch = [
        v((2, width, hidden), BF16),
        v((2, context_width, hidden), BF16),
        v((2, hidden, hidden), BF16),
        v((hidden, width), BF16),
        v((2, bins, hidden), BF16),
        v((3, hidden), F32),
        v((3, width), F32),
        v((2, 3, hidden), F32),
        v((2, 3, hidden), F32),
        v((2, 1, bins), F32),
        v((rows, width + 128), BF16),
        v((rows, width + 128), BF16),
        v((slot, width), F32),
        v((rows, width), BF16),
        v((rows, width), BF16),
        v((rows, hidden), BF16),
        v((rows, hidden), BF16),
        v((rows, hidden), BF16),
        v((rows, hidden), BF16),
        v((rows, width), F32),
        v((rows, width), F32),
        v((3, rows, 1), F32),
        v((rows, hidden), F32),
        v((rows, hidden), F32),
        v((2, rows, 1), F32),
        v((rows, hidden), BF16),
        v((rows, hidden), BF16),
        v((rows, hidden), BF16),
        v((rows, hidden), BF16),
        v((rows, half), BF16),
        v((rows, hidden), BF16),
        v((rows, half), BF16),
        v((rows, hidden), F32),
        v((rows, bins), BF16),
        v((rows, width), BF16),
        v((9, 8, hidden), F32),
        v((rows, width + 128), BF16),
        v((LINE - 1, slot, width + 128), BF16),
        v((slot, width), F32),
        v((rows, width), BF16),
        v((slot, 128), F32),
        v((LINE, 2, 2, own_two, half), BF16),
        v((LINE, 2, own_two, half), BF16),
        v((LINE, own_two, half), BF16),
        v((LINE, 2, 2, own_one, half), BF16),
        v((LINE, 2, own_one, half), BF16),
        v((LINE, own_one, half), BF16),
        v((LINE, 2, 2, own_two, bins), BF16),
        v((2, 2, 2, own_two, bins), BF16),
        v((2, 2, own_two, bins), BF16),
        v((2, own_two, bins), BF16),
        v((2, 2, 2, own_two, bins), BF16),
        v((2, 2, own_two, half), BF16),
        v((2, own_two, half), BF16),
        v((own_two, half), BF16),
        v((2, 2, own_one, half), BF16),
        v((2, own_one, half), BF16),
        v((own_one, half), BF16),
        v((2, 2, own_two, bins), BF16),
        v((2, own_two, bins), BF16),
        v((own_two, bins), BF16),
        v((2, 2, own_two, bins), BF16),
        v((2, own_two, half), BF16),
        v((own_two, half), BF16),
        v((2, own_one, half), BF16),
        v((own_one, half), BF16),
        v((2, 2, own_two, half_w), BF16),
        v((2, 2, own_two, half_w), BF16),
        v((2, 2, own_two, half_w), BF16),
        v((2, own_two, half_w), BF16),
        v((own_two, half_w), BF16),
        v((pad_context, half), BF16),
        v((pad_context, half), BF16),
        v((pad_context, half), BF16),
        v((2, 128 // LINE, half), BF16),
        v((2, 128 // LINE, half), BF16),
        v((2, 128 // LINE, half), BF16),
        v((local_rows, 128), F32),
        v((3, 8, hidden), F32),
        v((3, 8, hidden), F32),
        v((3, 8, half), F32),
        v((3, 8, half), F32),
        v((3, 8, half), F32),
        v((tasks, 128), F32),
        v((tasks, 128), F32),
        v((5, tasks, 128), F32),
        pltpu.SemaphoreType.DMA((REMOTE_COPIES,)),
        pltpu.SemaphoreType.DMA((REMOTE_COPIES,)),
        pltpu.SemaphoreType.DMA((LOCAL_COPIES,)),
        pltpu.SemaphoreType.REGULAR,
        pltpu.SemaphoreType.REGULAR,
        pltpu.SemaphoreType.REGULAR,
    ]
    inside = pl.BlockSpec(memory_space=pltpu.VMEM)
    outside = pl.BlockSpec(memory_space=pl.ANY)
    raw = pl.pallas_call(
        functools.partial(line_kernel, sizes, scale),
        out_shape=out_shape,
        in_specs=[inside] * 14 + [outside] * 8,
        out_specs=[outside] * len(out_shape),
        scratch_shapes=scratch,
        compiler_params=pltpu.CompilerParams(
            collective_id=0, has_side_effects=True, vmem_limit_bytes=VMEM_BYTES
        ),
        cost_estimate=pl.CostEstimate(
            flops=2 * 10**10, bytes_accessed=6 * 10**7, transcendentals=10**7
        ),
        name="line_update",
    )(
        latent, action.T, task_ids[None], action_mask.T, task_table, target_latent,
        bin_lower[None], bin_frac[None], dyn_vec1, dyn_vec2, dyn_vec3, q_vec1, q_vec2, q_b3,
        dyn_w1, dyn_wc, dyn_w2, dyn_w3, q_w1, q_wc, q_w2, jnp.swapaxes(q_w3, 1, 2),
    )
    return finish(raw, (slot, width, hidden, bins, tasks, acts, context_width, heads))


def finish_kernel(sizes, *refs):
    (slot, width, hidden, bins, tasks, acts, context_width, heads) = sizes
    half, half_w = hidden // 2, width // 2
    (
        raw_losses, raw_latent, raw_table, raw_dw1, raw_dwc, raw_dvec, raw_dw2, raw_dw3,
        raw_qw1, raw_qwc, raw_qvec, raw_qw2, raw_qw3,
        losses, latent, table, dw1, dwc, dvec1, dw2, dvec2, dw3, dvec3,
        qw1, qwc, qvec1, qw2, qvec2, qw3, qb3,
    ) = refs
    head = pl.program_id(0)
    core = lax.axis_index("tensor")

    @pl.when(head == 0)
    def _():
        losses[...] = raw_losses[...].T[0:2]
        latent[...] = raw_latent[...]
        table[...] = raw_table[:, acts:context_width]
        dw1[...] = raw_dw1[...]
        dwc[...] = raw_dwc[...].astype(F32)[0:context_width]
        dvec1[...] = raw_dvec[core, 0:3]
        dw2[...] = raw_dw2[...]
        dw3[...] = raw_dw3[...]
        line = jnp.concatenate([raw_dvec[0, 6:7], raw_dvec[1, 6:7]], 1)
        rows = jnp.concatenate(
            [line[:, 0:width], line[:, width : 2 * width], raw_dvec[0, 7:8, 0:width]], 0
        )
        dvec3[...] = jnp.where(core == 0, rows[:, 0:half_w], rows[:, half_w:])
        for index in range(2):
            dvec2[:, index * half : (index + 1) * half] = raw_dvec[index, 3:6]

    qw1[0] = raw_qw1[0].astype(F32)
    qwc[0] = raw_qwc[0].astype(F32)[0:context_width]
    qvec1[0] = raw_qvec[0, core, 0:3]
    qw2[0] = raw_qw2[0].astype(F32)
    for index in range(2):
        qvec2[0, :, index * half : (index + 1) * half] = raw_qvec[0, index, 3:6]
    qw3[0] = raw_qw3[0].astype(F32).T
    qb3[pl.ds(head, 1), :] = raw_qvec[0, 0, 6:7, 0:bins]


def finish(raw, sizes):
    (slot, width, hidden, bins, tasks, acts, context_width, heads) = sizes
    half, half_w = hidden // 2, width // 2
    own_two, own_one = hidden // BLOCK, width // BLOCK

    def whole(*dims):
        return pl.BlockSpec(dims, lambda head: (0,) * len(dims))

    def by_head(*dims):
        return pl.BlockSpec((1,) + dims, lambda head: (head,) + (0,) * len(dims))

    dims = [
        (whole, (2, 2 * slot)),
        (whole, (2 * slot, half_w)),
        (whole, (tasks, context_width - acts)),
        (whole, (own_one, half)),
        (whole, (context_width, half)),
        (whole, (3, half)),
        (whole, (own_two, half)),
        (whole, (3, hidden)),
        (whole, (own_two, half_w)),
        (whole, (3, half_w)),
        (by_head, (own_one, half)),
        (by_head, (context_width, half)),
        (by_head, (3, half)),
        (by_head, (own_two, half)),
        (by_head, (3, hidden)),
        (by_head, (bins, own_two)),
        (whole, (heads, bins)),
    ]
    outs = pl.pallas_call(
        functools.partial(finish_kernel, sizes),
        grid=(heads,),
        in_specs=[whole(*item.shape) for item in raw[:8]]
        + [by_head(*item.shape[1:]) for item in raw[8:]],
        out_specs=[kind(*item) for kind, item in dims],
        out_shape=[
            jax.ShapeDtypeStruct(item if kind is whole else (heads,) + item, F32)
            for kind, item in dims
        ],
        compiler_params=pltpu.CompilerParams(
            dimension_semantics=("arbitrary",), vmem_limit_bytes=VMEM_BYTES
        ),
        name="finish",
    )(*raw)
    outs = list(outs)
    outs[0] = outs[0].T
    outs[6] = outs[6].T
    outs[13] = jnp.swapaxes(outs[13], 1, 2)
    outs[15] = jnp.swapaxes(outs[15], 1, 2)
    return tuple(outs)


def shards(*arrays):
    if lax.axis_size("dp") == BLOCK:
        return line_shards(*arrays)
    return general_shards(*arrays)


def solution(mesh):
    return jax.shard_map(
        shards,
        mesh=mesh,
        in_specs=(
            P("dp", "tensor"),
            P("dp", None),
            P("dp"),
            P(),
            P(),
            P("dp", "tensor"),
            P("dp"),
            P("dp"),
            P(None, "tensor"),
            P(None, "tensor"),
            P(None, "tensor"),
            P("tensor", None),
            P(),
            P(None, "tensor"),
            P(None, "tensor"),
            P(None, None, "tensor"),
            P(None, None, "tensor"),
            P(None, None, "tensor"),
            P(None, "tensor", None),
            P(),
            P(),
            P(),
        ),
        out_specs=(
            P("dp", None),
            P("dp", "tensor"),
            P(),
            P("dp", "tensor"),
            P(None, "tensor"),
            P(None, "tensor"),
            P("tensor", "dp"),
            P(),
            P("dp", "tensor"),
            P(None, "tensor"),
            P(None, "dp", "tensor"),
            P(None, None, "tensor"),
            P(None, None, "tensor"),
            P(None, "tensor", "dp"),
            P(),
            P(None, "dp", None),
            P(),
        ),
        check_vma=False,
    )
```

```python
import functools
import math

import jax
import jax.numpy as jnp
from jax import lax
from jax.experimental import pallas as pl
from jax.experimental.pallas import tpu as pltpu
from jax.sharding import PartitionSpec as P

GROUP = 8
LINE = 4
PLANE = 4
BLOCK = LINE * PLANE
EPSILON = 1e-05
HIGHEST = lax.Precision.HIGHEST
F32 = jnp.float32
BF16 = jnp.bfloat16
REMOTE_COPIES = 126
LOCAL_COPIES = 49
VMEM_BYTES = 63 << 20


def swap_core(values):
    return lax.ppermute(values, "tensor", [(0, 1), (1, 0)])


def swap_dp(values, bit):
    size = lax.axis_size("dp")
    return lax.ppermute(values, "dp", [(place, place ^ bit) for place in range(size)])


def pick(values, index, axis=0):
    return lax.dynamic_index_in_dim(values, index, axis, keepdims=False)


def own_then_other(values):
    return values, swap_core(values)


def mish_parts(values):
    grown = jnp.exp(jnp.minimum(values, 20.0))
    top = grown * (grown + 2.0)
    share = 1.0 / (top + 2.0)
    return grown, top * share, share


def mish(values):
    return values * mish_parts(values)[1]


def mish_slope(values):
    grown, ratio, share = mish_parts(values)
    return ratio + 4.0 * values * grown * (1.0 + grown) * share * share


def norm(before, gain, shift):
    centred = before - jnp.mean(before, -1, keepdims=True)
    inverse = lax.rsqrt(jnp.mean(centred * centred, -1, keepdims=True) + EPSILON)
    normed = centred * inverse
    return normed * gain + shift, normed, inverse


def norm_back(upstream, normed, inverse, gain):
    weighted = upstream * gain
    return inverse * (
        weighted
        - jnp.mean(weighted, -1, keepdims=True)
        - normed * jnp.mean(weighted * normed, -1, keepdims=True)
    )


def vector_sums(rounded, upstream, normed):
    return jnp.stack(
        [jnp.sum(rounded.astype(F32), 0), jnp.sum(upstream * normed, 0), jnp.sum(upstream, 0)]
    )


def mm(left, right):
    return jnp.dot(left, right, preferred_element_type=F32)


def mm_t(left, right):
    return lax.dot_general(left, right, (((1,), (1,)), ((), ())), preferred_element_type=F32)


def t_mm(left, right):
    return lax.dot_general(left, right, (((0,), (0,)), ((), ())), preferred_element_type=F32)


def block_forward(inputs, context, w_one, w_context, vec_one, w_two, vec_two):
    before = mm(inputs, w_one) + mm(context, w_context) + vec_one[0:1]
    out_one, normed_one, inverse_one = norm(before, vec_one[1:2], vec_one[2:3])
    hidden_one = mish(out_one).astype(BF16)
    second = mm(hidden_one, w_two) + vec_two[0:1]
    out_two, normed_two, inverse_two = norm(second, vec_two[1:2], vec_two[2:3])
    hidden_two = mish(out_two).astype(BF16)
    return hidden_one, hidden_two, (normed_one, inverse_one, normed_two, inverse_two)


def block_backward(grad_hidden, saved, vec_one, w_two, vec_two):
    normed_one, inverse_one, normed_two, inverse_two = saved
    upstream = mish_slope(normed_two * vec_two[1:2] + vec_two[2:3]) * grad_hidden
    grad_two = norm_back(upstream, normed_two, inverse_two, vec_two[1:2]).astype(BF16)
    sums_two = vector_sums(grad_two, upstream, normed_two)
    grad_one_hidden = mm_t(grad_two, w_two)
    upstream = mish_slope(normed_one * vec_one[1:2] + vec_one[2:3]) * grad_one_hidden
    grad_one = norm_back(upstream, normed_one, inverse_one, vec_one[1:2]).astype(BF16)
    sums_one = vector_sums(grad_one, upstream, normed_one)
    return grad_two, sums_two, grad_one, sums_one


def dynamics_forward(inputs, context, w_one, w_context, vec_one, w_two, vec_two, w_three, vec_three):
    hidden_one, hidden_two, saved = block_forward(
        inputs, context, w_one, w_context, vec_one, w_two, vec_two
    )
    before = mm(hidden_two, w_three) + vec_three[0:1]
    out, normed, inverse = norm(before, vec_three[1:2], vec_three[2:3])
    grouped = out.reshape(out.shape[0], -1, GROUP)
    simplex = jax.nn.softmax(grouped, axis=-1).reshape(out.shape)
    return hidden_one, hidden_two, saved, simplex, normed, inverse


def dynamics_backward(grad_next, simplex, normed, inverse, saved, w_three, vec_three, vec_one, w_two, vec_two):
    weighted = grad_next * simplex
    rows = weighted.shape[0]
    along = jnp.sum(weighted.reshape(rows, -1, GROUP), -1, keepdims=True)
    along = jnp.broadcast_to(along, (rows, along.shape[1], GROUP)).reshape(weighted.shape)
    upstream = weighted - simplex * along
    grad_three = norm_back(upstream, normed, inverse, vec_three[1:2]).astype(BF16)
    sums_three = vector_sums(grad_three, upstream, normed)
    grad_hidden = mm_t(grad_three, w_three)
    grad_two, sums_two, grad_one, sums_one = block_backward(
        grad_hidden, saved, vec_one, w_two, vec_two
    )
    return grad_three, sums_three, grad_two, sums_two, grad_one, sums_one


def value_head(hidden_two, w_three, bias, lower, fraction, scale, heads):
    logits = mm(hidden_two, w_three) + bias
    log_prob = jax.nn.log_softmax(logits, axis=-1)
    bins = jnp.arange(logits.shape[-1], dtype=jnp.int32)[None, :]
    target = jnp.where(bins == lower, 1.0 - fraction, 0.0) + jnp.where(
        bins == lower + 1, fraction, 0.0
    )
    loss = -jnp.sum(target * log_prob, -1) / heads
    grad_logits = (scale / heads * (jnp.exp(log_prob) - target)).astype(BF16)
    return loss, grad_logits


def spread(values, axis_len):
    blocks = lax.axis_size("dp") // BLOCK
    rows = values.shape[0] // (blocks * BLOCK)
    values = values.reshape((blocks, LINE, 2, 2, rows) + values.shape[1:])
    if blocks > 1:
        values = jnp.moveaxis(values, 0, 3)
    return values.reshape((LINE, 2, 2, blocks * rows) + values.shape[5:])


def across_blocks(values, axis):
    blocks = lax.axis_size("dp") // BLOCK
    if blocks == 1:
        return values
    groups = [[block * BLOCK + place for block in range(blocks)] for place in range(BLOCK)]
    return lax.psum_scatter(
        values, "dp", scatter_dimension=axis, axis_index_groups=groups, tiled=True
    )


def sum_across_blocks(values):
    blocks = lax.axis_size("dp") // BLOCK
    if blocks == 1:
        return values
    groups = [[block * BLOCK + place for block in range(blocks)] for place in range(BLOCK)]
    return lax.psum(values, "dp", axis_index_groups=groups)


def reduce_first(values, axis_x, bit_x, at_x, axis_y, bit_y, at_y):
    sent = pick(values, 1 - at_x, axis_x).astype(BF16)
    total = pick(values, at_x, axis_x) + swap_dp(sent, bit_x).astype(F32)
    if axis_y > axis_x:
        axis_y -= 1
    sent = pick(total, 1 - at_y, axis_y).astype(BF16)
    return pick(total, at_y, axis_y) + swap_dp(sent, bit_y).astype(F32)


def plane_scatter(values, at_x, at_y):
    half = LINE // 2
    first = reduce_first(values[:half], 2, 1, at_x, 1, 2, at_y)
    second = reduce_first(values[half:], 1, 2, at_y, 2, 1, at_x)
    return jnp.concatenate([first, second], 0)


def plane_scatter_one(values, at_x, at_y):
    half = values.shape[-1] // 256 * 128
    if half == 0:
        return reduce_first(values, 1, 1, at_x, 0, 2, at_y)
    first = reduce_first(values[..., :half], 1, 1, at_x, 0, 2, at_y)
    second = reduce_first(values[..., half:], 0, 2, at_y, 1, 1, at_x)
    return jnp.concatenate([first, second], -1)


def line_exchange(values, at_z, last):
    out = jnp.zeros((LINE + 1,) + values.shape[1:], F32)
    for step in range(LINE):
        part = pick(values, at_z ^ step)
        if step:
            part = swap_dp(part.astype(BF16), 4 * step).astype(F32)
        out = lax.dynamic_update_index_in_dim(out, part, at_z ^ step, 0)
    return lax.dynamic_update_index_in_dim(out, last, LINE, 0)


def plane_total(values, kind=F32):
    values = values + swap_dp(values.astype(kind), 1).astype(F32)
    return values + swap_dp(values.astype(kind), 2).astype(F32)


def line_collect(values, at_z, last, kind=F32):
    out = jnp.zeros((LINE + 1,) + values.shape, F32)
    sent = values.astype(kind)
    for step in range(LINE):
        part = swap_dp(sent, 4 * step).astype(F32) if step else values
        out = lax.dynamic_update_index_in_dim(out, part, at_z ^ step, 0)
    return lax.dynamic_update_index_in_dim(out, last, LINE, 0)


def line_total(values):
    total = values
    for step in range(1, LINE):
        total = total + swap_dp(values, 4 * step)
    return total


def in_core_order(core, own, other, axis):
    return jnp.where(
        core == 0, jnp.concatenate([own, other], axis), jnp.concatenate([other, own], axis)
    )


def general_shards(
    latent,
    action,
    task_ids,
    action_mask,
    task_table,
    target_latent,
    bin_lower,
    bin_frac,
    dyn_w1,
    dyn_wc,
    dyn_vec1,
    dyn_w2,
    dyn_vec2,
    dyn_w3,
    dyn_vec3,
    q_w1,
    q_wc,
    q_vec1,
    q_w2,
    q_vec2,
    q_w3,
    q_b3,
):
    place = lax.axis_index("dp")
    core = lax.axis_index("tensor")
    at_x, at_y, at_z = place % 2, place // 2 % 2, place // 4 % 4
    local_rows = latent.shape[0]
    half_rows = local_rows // 2
    half_latent = latent.shape[1]
    half_hidden = dyn_w1.shape[1]
    inv_root = 1.0 / math.sqrt(local_rows * lax.axis_size("dp"))
    task_count = task_table.shape[0]
    heads = q_w1.shape[0]
    head_places = (at_z, heads - 1)

    def both(values, axis):
        return jnp.concatenate(own_then_other(values), axis)

    dyn_w1_all, dyn_wc_all, dyn_vec1_all = both(dyn_w1, 1), both(dyn_wc, 1), both(dyn_vec1, 1)
    dyn_w2_all = both(dyn_w2, 0)
    dyn_w3_all = in_core_order(core, *own_then_other(dyn_w3), 1)
    dyn_vec3_all = in_core_order(core, *own_then_other(dyn_vec3), 1)
    head_weights = []
    for head in head_places:
        head_weights.append(
            (
                both(pick(q_w1, head), 1),
                both(pick(q_wc, head), 1),
                both(pick(q_vec1, head), 1),
                both(pick(q_w2, head), 0),
                pick(q_vec2, head),
                pick(q_w3, head),
                pick(q_b3, head),
            )
        )

    def my_rows(values):
        return lax.dynamic_slice_in_dim(values, core * half_rows, half_rows, 0)

    def their_rows(values):
        return lax.dynamic_slice_in_dim(values, (1 - core) * half_rows, half_rows, 0)

    def whole_columns(values):
        return in_core_order(core, my_rows(values), swap_core(their_rows(values)), 1)

    my_latent = whole_columns(latent)
    my_target = whole_columns(target_latent)
    my_ids = my_rows(task_ids)[:, None]
    onehot = (my_ids == jnp.arange(task_count, dtype=jnp.int32)[None, :]).astype(BF16)
    table = jnp.concatenate([action_mask.astype(BF16), task_table], 1)
    looked_up = mm(onehot, table)
    acts = action.shape[1]
    acted = my_rows(action).astype(F32) * looked_up[:, :acts]
    my_context = jnp.concatenate([acted, looked_up[:, acts:]], 1).astype(BF16)
    fraction = my_rows(bin_frac)[:, None]
    piece_one = lax.reduce_precision(fraction, 8, 7)
    piece_two = lax.reduce_precision(fraction - piece_one, 8, 7)
    piece_three = fraction - piece_one - piece_two
    meta = [my_ids, my_rows(bin_lower)[:, None], piece_one, piece_two, piece_three]
    meta = [item.astype(BF16) for item in meta]
    width = my_latent.shape[1]
    context_width = my_context.shape[1]
    packed = jnp.concatenate([my_latent, my_context] + meta, 1)
    packed = jnp.concatenate([packed] + [swap_dp(packed, 4 * step) for step in range(1, LINE)], 0)
    inputs = packed[:, :width]
    context = packed[:, width : width + context_width]
    meta = packed[:, width + context_width :].astype(F32)
    all_ids = meta[:, 0:1].astype(jnp.int32)
    lower = meta[:, 1:2].astype(jnp.int32)
    fraction = meta[:, 2:3] + meta[:, 3:4] + meta[:, 4:5]
    all_onehot = (all_ids == jnp.arange(task_count, dtype=jnp.int32)[None, :]).astype(F32)
    other_inputs, other_context = swap_core(inputs), swap_core(context)

    dyn_one, dyn_two, dyn_saved, simplex, normed_three, inverse_three = dynamics_forward(
        inputs, context, dyn_w1_all, dyn_wc_all, dyn_vec1_all, dyn_w2_all, dyn_vec2,
        dyn_w3_all, dyn_vec3_all,
    )
    next_low = simplex.astype(BF16)
    mismatch = next_low[:half_rows].astype(F32) - my_target
    consistency = jnp.sum(mismatch * mismatch, -1)
    other_next = swap_core(next_low)

    head_results = []
    for weights in head_weights:
        w_one, w_context, vec_one, w_two, vec_two, w_three, bias = weights
        hidden_one, hidden_two, saved = block_forward(
            next_low, context, w_one, w_context, vec_one, w_two, vec_two
        )
        loss, grad_logits = value_head(
            hidden_two, w_three, bias[None], lower, fraction, inv_root, heads
        )
        grad_hidden = mm_t(grad_logits, w_three)
        grad_two, sums_two, grad_one, sums_one = block_backward(
            grad_hidden, saved, vec_one, w_two, vec_two
        )
        head_results.append(
            (hidden_one, hidden_two, loss, grad_logits, grad_two, sums_two, grad_one, sums_one)
        )

    main, extra = head_results
    grad_in = mm_t(main[6], head_weights[0][0])
    own_grad = grad_in[:half_rows] + mm_t(extra[6][:half_rows], head_weights[1][0])
    own_loss = main[2][:half_rows] + extra[2][:half_rows]
    for step in range(1, LINE):
        part = slice(step * half_rows, (step + 1) * half_rows)
        own_grad = own_grad + swap_dp(grad_in[part].astype(BF16), 4 * step).astype(F32)
        own_loss = own_loss + swap_dp(main[2][part], 4 * step)
    own_grad = own_grad + 2.0 * inv_root * mismatch
    own_low = own_grad.astype(BF16)
    grad_next = jnp.concatenate(
        [own_low] + [swap_dp(own_low, 4 * step) for step in range(1, LINE)], 0
    ).astype(F32)
    my_losses = jnp.stack([consistency, own_loss], 1)
    losses = in_core_order(core, my_losses, swap_core(my_losses), 0)

    grad_three, sums_three, dyn_grad_two, dyn_sums_two, dyn_grad_one, dyn_sums_one = (
        dynamics_backward(
            grad_next, simplex, normed_three, inverse_three, dyn_saved, dyn_w3_all, dyn_vec3_all,
            dyn_vec1_all, dyn_w2_all, dyn_vec2,
        )
    )
    own_latent_grad = mm_t(dyn_grad_one[:half_rows], dyn_w1_all)
    left, right = own_latent_grad[:, :half_latent], own_latent_grad[:, half_latent:]
    kept = jnp.where(core == 0, left, right)
    received = swap_core(jnp.where(core == 0, right, left))
    latent_grad = in_core_order(core, kept, received, 0)

    def own_half(values):
        return jnp.concatenate([values[:, :half_hidden], swap_core(values[:, half_hidden:])], 0)

    def all_rows(values):
        return jnp.concatenate([values, swap_core(values)], 0)

    def quarter(values, size):
        blocks = lax.axis_size("dp") // BLOCK
        cut = values.reshape(values.shape[0], blocks, LINE, size // (blocks * LINE))
        return pick(cut, at_z, 2).reshape(values.shape[0], size // LINE)

    def spread_quarter(values):
        blocks = lax.axis_size("dp") // BLOCK
        rows = values.shape[0] // (blocks * PLANE)
        values = values.reshape((blocks, 2, 2, rows) + values.shape[1:])
        if blocks > 1:
            values = jnp.moveaxis(values, 0, 2)
        return values.reshape((2, 2, blocks * rows) + values.shape[4:])

    both_next = jnp.concatenate([next_low, other_next], 0)
    both_inputs = jnp.concatenate([inputs, other_inputs], 0)
    both_context = jnp.concatenate([context, other_context], 0)
    features = both_next.shape[1]
    hidden = 2 * half_hidden

    def quarter_grads(hidden_one, grad_two, grad_one, rows_in):
        first_factor, grad_factor = own_half(hidden_one), own_half(grad_one)
        w_two_part = t_mm(all_rows(quarter(grad_two, hidden)), first_factor)
        w_one_part = t_mm(quarter(rows_in, features), grad_factor)
        w_context_part = t_mm(both_context, grad_factor)
        return (
            plane_scatter_one(spread_quarter(w_two_part), at_x, at_y),
            plane_scatter_one(spread_quarter(w_one_part), at_x, at_y),
            plane_total(w_context_part, BF16),
        )

    def outer_quarter(left, right):
        part = t_mm(quarter(left, hidden), right)
        return plane_scatter_one(spread_quarter(part), at_x, at_y)

    first_factor, grad_factor = own_half(main[0]), own_half(main[6])
    main_two = plane_scatter(spread(t_mm(all_rows(main[4]), first_factor), 0), at_x, at_y)
    main_one = plane_scatter(spread(t_mm(both_next, grad_factor), 0), at_x, at_y)
    main_three = plane_scatter(spread(t_mm(main[1], main[3]), 0), at_x, at_y)
    main_context = plane_total(t_mm(both_context, grad_factor), BF16)
    extra_two, extra_one, extra_context = quarter_grads(extra[0], extra[4], extra[6], both_next)
    extra_three = outer_quarter(extra[1], extra[3])
    dyn_w2_part, dyn_w1_part, dyn_context = quarter_grads(
        dyn_one, dyn_grad_two, dyn_grad_one, both_inputs
    )
    dyn_w3_part = outer_quarter(
        all_rows(dyn_two),
        jnp.concatenate(
            [
                jnp.where(core == 0, grad_three[:, :half_latent], grad_three[:, half_latent:]),
                swap_core(
                    jnp.where(core == 0, grad_three[:, half_latent:], grad_three[:, :half_latent])
                ),
            ],
            0,
        ),
    )

    q_w2_out = across_blocks(line_exchange(main_two, at_z, extra_two), 1).transpose(0, 2, 1)
    q_w1_out = across_blocks(line_exchange(main_one, at_z, extra_one), 1)
    q_w3_out = line_exchange(main_three, at_z, extra_three)
    q_w3_out = across_blocks(q_w3_out + swap_core(q_w3_out), 1)
    dyn_w2_out = across_blocks(dyn_w2_part, 0).transpose(1, 0)
    dyn_w1_out = across_blocks(dyn_w1_part, 0)
    dyn_w3_out = across_blocks(dyn_w3_part, 0)
    q_wc_out = sum_across_blocks(line_collect(main_context, at_z, extra_context, BF16))
    dyn_wc_out = sum_across_blocks(dyn_context)

    def core_vec(values):
        own, other = values[:, :half_hidden], values[:, half_hidden:]
        return own + swap_core(other)

    def sums_of(result):
        return (
            core_vec(result[7]),
            result[5] + swap_core(result[5]),
            jnp.sum(result[3].astype(F32), 0)[None],
        )

    def pack(items):
        return jnp.concatenate([item.reshape(-1) for item in items])

    main_sums, extra_sums = sums_of(main), sums_of(extra)
    main_bias = main_sums[2] + swap_core(main_sums[2])
    extra_bias = extra_sums[2] + swap_core(extra_sums[2])
    main_sums, extra_sums = main_sums[:2] + (main_bias,), extra_sums[:2] + (extra_bias,)
    three_own = jnp.where(core == 0, sums_three[:, :half_latent], sums_three[:, half_latent:])
    three_other = jnp.where(core == 0, sums_three[:, half_latent:], sums_three[:, :half_latent])
    dyn_sums = (
        core_vec(dyn_sums_one),
        dyn_sums_two + swap_core(dyn_sums_two),
        three_own + swap_core(three_other),
    )
    def table_part(grad_one, w_context, rows):
        embed = mm_t(grad_one[:rows], w_context[acts:])
        return lax.dot_general(
            all_onehot[:rows], embed, (((0,), (0,)), ((), ())), precision=HIGHEST
        )

    table_grad = (
        table_part(main[6], head_weights[0][1], inputs.shape[0])
        + table_part(extra[6], head_weights[1][1], half_rows)
        + table_part(dyn_grad_one, dyn_wc_all, half_rows)
    )
    table_grad = line_total(table_grad + swap_core(table_grad))
    flat = sum_across_blocks(
        plane_total(pack((table_grad,) + dyn_sums + extra_sums + main_sums))
    )
    sizes = [table_grad] + list(dyn_sums)
    pieces = []
    start = 0
    for item in sizes:
        pieces.append(flat[start : start + item.size].reshape(item.shape))
        start += item.size
    head_size = sum(item.size for item in main_sums)
    extra_flat, main_flat = flat[start : start + head_size], flat[start + head_size :]
    head_flat = line_collect(main_flat, at_z, extra_flat)
    head_pieces = []
    start = 0
    for item in main_sums:
        head_pieces.append(
            head_flat[:, start : start + item.size].reshape((heads,) + item.shape)
        )
        start += item.size
    table_out, dyn_vec1_out, dyn_vec2_out, dyn_vec3_out = pieces
    q_vec1_out, q_vec2_out, q_b3_out = head_pieces
    return (
        losses,
        latent_grad,
        table_out,
        dyn_w1_out,
        dyn_wc_out,
        dyn_vec1_out,
        dyn_w2_out,
        dyn_vec2_out,
        dyn_w3_out,
        dyn_vec3_out,
        q_w1_out,
        q_wc_out,
        q_vec1_out,
        q_w2_out,
        q_vec2_out,
        q_w3_out,
        q_b3_out[:, 0],
    )


def gather_sum(values, ones):
    parts = []
    for start in range(0, values.shape[1], 128):
        piece = values[:, start : start + 128]
        high = piece.astype(BF16)
        rest = piece - high.astype(F32)
        middle = rest.astype(BF16)
        low = (rest - middle.astype(F32)).astype(BF16)
        parts.append(mm(high, ones) + mm(middle, ones) + mm(low, ones))
    return jnp.concatenate(parts, 1)


def line_kernel(sizes, scale, *refs):
    (slot, width, hidden, bins, tasks, acts, context_width, heads) = sizes
    (
        latent, raw_action, raw_ids, raw_mask, raw_table, target_latent, raw_lower, raw_frac,
        dyn_vec1, raw_dyn_vec2, dyn_vec3, q_vec1, q_vec2, raw_b3,
        dyn_w1, dyn_wc, dyn_w2, dyn_w3, q_w1, q_wc, q_w2, q_w3,
        out_losses, out_latent, out_table, out_dw1, out_dwc, out_dvec, out_dw2, out_dw3,
        out_qw1, out_qwc, out_qvec, out_qw2, out_qw3,
        action, task_ids, action_mask, task_table, bin_lower, bin_frac, dyn_vec2, q_b3,
        w1, wc, w2, dw3, qw3, dv1, dv3, qv1, qv2, qb3,
        xbuf, xother, tgt, nxt, nxto, dyn_x1, dyn_x2, dyn_h1, dyn_h2, simplex, x3,
        dyn_inv, x1, x2, inv, h1, h2, gp2, gp1, h1o, gp2o, gp1o, upstream, gl, dyn_gp3,
        acc, dxm, dxr, own_g, all_g, lossbuf,
        p2, r2, t2, p1, r1, t1, p3, p3h, r3, t3, p3o,
        e2, er2, et2, e1, er1, et1, e3, er3, et3, e3o,
        er2b, et2b, er1b, et1b, d3, d3s, d3o, er3b, et3b,
        pc, pcx, pcy, pq, pqx, pqy, ctx, fr, vb, vbo, vp, vpx, vpy, tb, tbo, tq, tqr,
        send_sem, recv_sem, local_sem, free_a, free_b, free_f,
    ) = refs
    half = hidden // 2
    half_w = width // 2
    own_two, own_one = hidden // BLOCK, width // BLOCK
    rows_all = slot * LINE
    place = lax.axis_index("dp")
    core = lax.axis_index("tensor")
    at_x = lax.rem(place, 2)
    at_y = lax.rem(place // 2, 2)
    at_z = lax.rem(place // 4, 4)
    z_of = [
        at_z,
        at_z + 1 - 2 * lax.rem(at_z, 2),
        lax.rem(at_z + 2, 4),
        3 - at_z,
    ]
    to_core = (place, 1 - core)
    to_x = (place + 1 - 2 * at_x, core)
    to_y = (place + 2 - 4 * at_y, core)
    to_z = [None] + [(place + 4 * (z_of[k] - at_z), core) for k in range(1, LINE)]
    mesh_id = pl.DeviceIdType.MESH
    counter = [0, 0]
    pending = []

    def describe(source, target, device):
        at = counter[0]
        counter[0] += 1
        return pltpu.make_async_remote_copy(
            src_ref=source, dst_ref=target, send_sem=send_sem.at[at], recv_sem=recv_sem.at[at],
            device_id=device, device_id_type=mesh_id,
        )

    def remote(source, target, device):
        copy = describe(source, target, device)
        copy.start()
        pending.append(copy)
        return copy

    def sent(copy):
        copy.wait_send()
        pending[:] = [item for item in pending if item is not copy]

    def describe_local(source, target):
        at = counter[1]
        counter[1] += 1
        return pltpu.make_async_copy(source, target, local_sem.at[at])

    def local(source, target):
        copy = describe_local(source, target)
        copy.start()
        return copy

    barrier = pltpu.get_barrier_semaphore()
    peers = [to_core, to_x, to_y] + to_z[1:]
    for peer in peers:
        pl.semaphore_signal(barrier, inc=1, device_id=peer, device_id_type=mesh_id)


    low = slice(0, half)
    high = slice(half, hidden)
    own_cols = pl.ds(pl.multiple_of(half_w * core, 128), half_w)
    other_cols = pl.ds(pl.multiple_of(half_w * (1 - core), 128), half_w)
    own_rows = pl.ds(pl.multiple_of(slot * core, 64), slot)
    other_rows = pl.ds(pl.multiple_of(slot * (1 - core), 64), slot)

    def load_weights(to, one, context, two):
        mine = [
            local(one, w1.at[to, :, low]),
            local(context, wc.at[to, :, low]),
            local(two, w2.at[to, low, :]),
        ]
        return mine

    def send_weights(to, one, context, two):
        return [
            remote(one, w1.at[to, :, high], to_core),
            remote(context, wc.at[to, :, high], to_core),
            remote(two, w2.at[to, high, :], to_core),
        ]

    head_z = at_z
    last = heads - 1
    fact_copies = [
        local(source, target)
        for source, target in (
            (raw_ids, task_ids), (raw_frac, bin_frac), (raw_lower, bin_lower),
            (raw_action, action), (raw_mask, action_mask), (raw_table, task_table),
            (latent.at[own_rows], xbuf.at[pl.ds(0, slot), own_cols]),
        )
    ]
    vec_ready = [
        local(source, target)
        for source, target in (
            (dyn_vec1, dv1.at[:, low]), (raw_dyn_vec2, dyn_vec2), (dyn_vec3, dv3.at[:, own_cols]),
            (q_vec1.at[head_z], qv1.at[0, :, low]), (q_vec1.at[last], qv1.at[1, :, low]),
            (q_vec2.at[head_z], qv2.at[0]), (q_vec2.at[last], qv2.at[1]), (raw_b3, q_b3),
            (target_latent.at[own_rows], tgt.at[:, own_cols]),
        )
    ]
    dyn_ready = load_weights(0, dyn_w1, dyn_wc, dyn_w2)
    three_ready = local(dyn_w3, dw3.at[:, own_cols])
    main_ready = load_weights(1, q_w1.at[head_z], q_wc.at[head_z], q_w2.at[head_z])
    main_three = local(q_w3.at[head_z], qw3.at[0])
    extra_three = local(q_w3.at[last], qw3.at[1])

    vb[...] = jnp.zeros_like(vb)

    for copy in fact_copies:
        copy.wait()
    fr[0] = jnp.zeros_like(fr[0])
    fr[0, 0:1, :] = task_ids[...].astype(F32)
    fr[0, 1:2, :] = bin_lower[...].astype(F32)
    fr[0, 2:3, :] = bin_frac[...]
    fr[0, 3 : 3 + acts, :] = action[...].astype(F32)

    def shift_matrix(count, start):
        near = lax.broadcasted_iota(jnp.int32, (count, 128), 0)
        far = lax.broadcasted_iota(jnp.int32, (count, 128), 1)
        return (near + start == far).astype(F32).astype(BF16)

    def context_rows(index):
        ctx[...] = fr[index].T
        columns = ctx[own_rows, :]
        ids, lower, fraction = columns[:, 0:1], columns[:, 1:2], columns[:, 2:3]
        task = lax.broadcasted_iota(jnp.int32, (slot, tasks), 1).astype(F32)
        onehot = (ids == task).astype(F32).astype(BF16)
        lane = lax.broadcasted_iota(jnp.int32, (slot, 128), 1)
        factor = mm(columns[:, 3 : 3 + acts].astype(BF16), to_acts) + (lane >= acts).astype(F32)
        piece_one = fraction.astype(BF16).astype(F32)
        piece_two = (fraction - piece_one).astype(BF16).astype(F32)
        facts = mm(onehot, lookup) * factor
        for at, item in enumerate(
            (ids, lower, piece_one, piece_two, fraction - piece_one - piece_two)
        ):
            facts = facts + jnp.where(lane == context_width + at, item, 0.0)
        rows = slice(index * slot, (index + 1) * slot)
        xbuf[rows, width : width + 128] = facts.astype(BF16)

    to_acts = shift_matrix(acts, 0)
    lookup = (
        t_mm(action_mask[...].astype(F32).astype(BF16), to_acts)
        + mm(task_table[...], shift_matrix(context_width - acts, acts))
    ).astype(BF16)
    pl.semaphore_wait(barrier, len(peers))
    facts_in = [remote(fr.at[0], fr.at[k], to_z[k]) for k in range(1, LINE)]
    lat_copy = remote(latent.at[other_rows], xbuf.at[pl.ds(0, slot), own_cols], to_core)
    tgt_copy = remote(target_latent.at[other_rows], tgt.at[:, own_cols], to_core)

    vec_copies = [
        remote(dyn_vec1, dv1.at[:, high], to_core),
        remote(dyn_vec3, dv3.at[:, own_cols], to_core),
        remote(q_vec1.at[head_z], qv1.at[0, :, high], to_core),
        remote(q_vec1.at[last], qv1.at[1, :, high], to_core),
    ]
    dyn_ready_other = send_weights(0, dyn_w1, dyn_wc, dyn_w2)
    three_ready_other = remote(dyn_w3, dw3.at[:, own_cols], to_core)
    main_ready_other = send_weights(1, q_w1.at[head_z], q_wc.at[head_z], q_w2.at[head_z])
    lat_copy.wait_recv()
    line_in = [
        remote(
            xbuf.at[pl.ds(0, slot), pl.ds(0, width)],
            xbuf.at[pl.ds(slot * k, slot), pl.ds(0, width)],
            to_z[k],
        )
        for k in range(1, LINE)
    ]
    context_rows(0)
    for index, copy in enumerate(facts_in):
        copy.wait_recv()
        context_rows(1 + index)
    for copy in vec_copies:
        copy.wait_recv()
    for copy in vec_ready:
        copy.wait()
    qb3[0] = q_b3[pl.ds(head_z, 1), :]
    qb3[1] = q_b3[last : last + 1, :]

    CH = 64

    def over_rows(first, count, body):
        if count <= CH:
            body(pl.ds(first, count))
            return

        def step(index, carry):
            body(pl.ds(pl.multiple_of(first + index * CH, CH), CH))
            return carry

        lax.fori_loop(0, count // CH, step, 0)

    def norm_rows(pre, keep, inverse, vec, out, first, count):
        features = pre.shape[1]

        def body(rows):
            values = pre[rows, :]
            centred = values - jnp.sum(values, -1, keepdims=True) * (1.0 / features)
            inv_rows = lax.rsqrt(
                jnp.sum(centred * centred, -1, keepdims=True) * (1.0 / features) + EPSILON
            )
            normed = centred * inv_rows
            keep[rows, :] = normed.astype(keep.dtype)
            inverse[rows, :] = inv_rows
            out[rows, :] = mish(normed * vec[1:2, :] + vec[2:3, :]).astype(BF16)

        over_rows(first, count, body)

    def add_sums(at, rounded, along, shift):
        count, features = shift.shape
        for index, item in enumerate((rounded, along, shift)):
            acc[at + index, :, 0:features] += jnp.sum(item.reshape(count // 8, 8, features), 0)

    def back_rows(grad, normed_ref, inverse, vec, out, at, first, count, slope):
        features = normed_ref.shape[1]

        def body(rows):
            normed = normed_ref[rows, :].astype(F32)
            gain = vec[1:2, :]
            up = grad[rows, :]
            if slope:
                up = mish_slope(normed * gain + vec[2:3, :]) * up
            weighted = up * gain
            along = up * normed
            mean_one = jnp.sum(weighted, -1, keepdims=True) * (1.0 / features)
            mean_two = jnp.sum(weighted * normed, -1, keepdims=True) * (1.0 / features)
            result = (inverse[rows, :] * (weighted - mean_one - normed * mean_two)).astype(BF16)
            out[rows, :] = result
            add_sums(at, result.astype(F32), along, up)

        over_rows(first, count, body)

    def two_tiles(body):
        def step(index, carry):
            body(pl.ds(pl.multiple_of(index * half, 128), half))
            return carry

        lax.fori_loop(0, 2, step, 0)

    def layers_forward(to, source, vec_one, vec_two, keep_one, keep_two, inverse, hid_one, hid_two,
                       first, count, ready):
        rows = pl.ds(first, count)
        ready(0)

        def first_tile(cols):
            x1[rows, cols] = (
                mm(source[rows, 0:width], w1[to, :, cols])
                + mm(xbuf[rows, width : width + context_width], wc[to, :, cols])
                + vec_one[0:1, cols]
            )

        two_tiles(first_tile)
        norm_rows(x1, keep_one, inverse.at[0], vec_one, hid_one, first, count)
        ready(1)

        def second_tile(cols):
            x2[rows, cols] = mm(hid_one[rows, :], w2[to, :, cols]) + vec_two[0:1, cols]

        two_tiles(second_tile)
        norm_rows(x2, keep_two, inverse.at[1], vec_two, hid_two, first, count)

    def back_two_to_one(to, grad, first, count, parts=(0, 1)):
        rows = pl.ds(first, count)

        def tile(cols):
            upstream[rows, cols] = mm_t(grad[rows, :], w2[to, cols, :])

        if len(parts) == 2:
            two_tiles(tile)
        else:
            tile(slice(parts[0] * half, (parts[0] + 1) * half))

    def ready_of(mine, others):
        def ready(stage):
            picked = (0, 1) if stage == 0 else (2,)
            for index in picked:
                mine[index].wait()
                others[index].wait_recv()

        return ready

    def nothing(stage):
        return None

    line_in[0].wait_recv()
    layers_forward(
        0, xbuf, dv1, dyn_vec2, dyn_x1, dyn_x2, dyn_inv, dyn_h1, dyn_h2, 0, 2 * slot,
        ready_of(dyn_ready, dyn_ready_other),
    )
    for copy in line_in[1:]:
        copy.wait_recv()
    x_copy = remote(xbuf, xother, to_core)
    layers_forward(
        0, xbuf, dv1, dyn_vec2, dyn_x1, dyn_x2, dyn_inv, dyn_h1, dyn_h2, 2 * slot,
        rows_all - 2 * slot, nothing,
    )
    three_ready.wait()
    three_ready_other.wait_recv()
    x3[...] = mm(dyn_h2[...], dw3[...]) + dv3[0:1, :]
    group_row = lax.broadcasted_iota(jnp.int32, (128, 128), 0) // GROUP
    group_col = lax.broadcasted_iota(jnp.int32, (128, 128), 1) // GROUP
    ones = (group_row == group_col).astype(F32).astype(BF16)

    def simplex_rows(rows):
        values = x3[rows, :]
        centred = values - jnp.sum(values, -1, keepdims=True) * (1.0 / width)
        inv_rows = lax.rsqrt(
            jnp.sum(centred * centred, -1, keepdims=True) * (1.0 / width) + EPSILON
        )
        normed = centred * inv_rows
        x3[rows, :] = normed
        dyn_inv[2, rows, :] = inv_rows
        grown = jnp.exp(normed * dv3[1:2, :] + dv3[2:3, :])
        share = grown / gather_sum(grown, ones)
        simplex[rows, :] = share
        nxt[rows, :] = share.astype(BF16)

    over_rows(0, rows_all, simplex_rows)
    for copy in dyn_ready_other:
        sent(copy)
    pl.semaphore_signal(free_a, inc=1, device_id=to_core, device_id_type=mesh_id)
    extra_ready = load_weights(0, q_w1.at[last], q_wc.at[last], q_w2.at[last])
    next_copy = remote(nxt, nxto, to_core)
    tgt_copy.wait_recv()
    gap = nxt[0:slot, :].astype(F32) - tgt[...]
    own_g[...] = gap * (2.0 * scale)
    consistency = jnp.sum(gap * gap, -1, keepdims=True)
    pl.semaphore_wait(free_a, 1)
    extra_ready_other = send_weights(0, q_w1.at[last], q_wc.at[last], q_w2.at[last])

    def value_rows(head, first, count):
        rows = pl.ds(first, count)
        logits = mm_t(h2[rows, :], qw3[head]) + qb3[head]
        logits = logits - jnp.max(logits, -1, keepdims=True)
        grown = jnp.exp(logits)
        total = jnp.sum(grown, -1, keepdims=True)
        lane = lax.broadcasted_iota(jnp.int32, (count, bins), 1).astype(F32)
        facts = xbuf[rows, width : width + 128].astype(F32)
        lower = facts[:, context_width + 1 : context_width + 2]
        fraction = (
            facts[:, context_width + 2 : context_width + 3]
            + facts[:, context_width + 3 : context_width + 4]
            + facts[:, context_width + 4 : context_width + 5]
        )
        target = jnp.where(lane == lower, 1.0 - fraction, 0.0) + jnp.where(
            lane == lower + 1.0, fraction, 0.0
        )
        loss = -jnp.sum(target * (logits - jnp.log(total)), -1, keepdims=True) * (1.0 / heads)
        grad = (scale / heads * (grown / total - target)).astype(BF16)
        gl[rows, :] = grad

        def tile(cols):
            upstream[rows, cols] = mm(grad, qw3[head, :, cols])

        two_tiles(tile)
        acc[6, 0, 0:bins] += jnp.sum(grad.astype(F32), 0)
        return loss

    def table_sum(to, grad, first, count):
        rows = pl.ds(first, count)
        embed = mm_t(grad[rows, :], wc[to])
        ids = xbuf[rows, width : width + 128].astype(F32)[:, context_width : context_width + 1]
        task = lax.broadcasted_iota(jnp.int32, (count, tasks), 1).astype(F32)
        onehot = (ids == task).astype(F32).astype(BF16)
        top = embed.astype(BF16)
        rest = embed - top.astype(F32)
        middle = rest.astype(BF16)
        lowest = (rest - middle.astype(F32)).astype(BF16)
        tb[:, 0:context_width] += (
            t_mm(onehot, top) + t_mm(onehot, middle) + t_mm(onehot, lowest)
        )

    def finish_vectors(slot_at, width_three):
        for index in range(3):
            vb[slot_at, index : index + 1, :] = jnp.sum(acc[index], 0, keepdims=True)
            vb[slot_at, 3 + index : 4 + index, :] = jnp.sum(acc[3 + index], 0, keepdims=True)
        if width_three:
            three = [jnp.sum(acc[6 + index, :, 0:width], 0, keepdims=True) for index in range(3)]
            vb[slot_at, 6:7, 0:width] = three[0]
            vb[slot_at, 6:7, width : 2 * width] = three[1]
            vb[slot_at, 7:8, 0:width] = three[2]
        else:
            vb[slot_at, 6:7, :] = jnp.sum(acc[6], 0, keepdims=True)
        return remote(vb.at[slot_at], vbo.at[slot_at], to_core)

    own_tasks = pl.ds(pl.multiple_of(tasks // 2 * core, 8), tasks // 2)
    half_cols = pl.ds(pl.multiple_of(half * core, 128), half)

    def join_vectors(slot_at, copy):
        copy.wait_recv()
        sent(copy)
        vp[slot_at, 0:3, :] = vb[slot_at, 0:3, low] + vbo[slot_at, 0:3, high]
        vp[slot_at, 3:8, :] = vb[slot_at, 3:8, half_cols] + vbo[slot_at, 3:8, half_cols]
        return remote(vp.at[slot_at], vpx.at[slot_at], to_x)

    def plane_vectors(slot_at, copy):
        copy.wait_recv()
        sent(copy)
        vp[slot_at] = vp[slot_at] + vpx[slot_at]
        return remote(vp.at[slot_at], vpy.at[slot_at], to_y)

    def total_vectors(slot_at, copy):
        copy.wait_recv()
        sent(copy)
        vp[slot_at] = vp[slot_at] + vpy[slot_at]

    def scatter_start(source, target, x_first, lead):
        if lead is None:
            piece = source.at[:, 1 - at_x] if x_first else source.at[1 - at_y]
        else:
            piece = source.at[lead, :, 1 - at_x] if x_first else source.at[lead, 1 - at_y]
        return remote(piece, target, to_x if x_first else to_y)

    def scatter_middle(copy, source, received, target, x_first, lead):
        copy.wait_recv()
        if lead is None:
            for other in range(2):
                kept = source[other, at_x] if x_first else source[at_y, other]
                received[other] = (received[other].astype(F32) + kept.astype(F32)).astype(BF16)
            piece = received.at[1 - at_y] if x_first else received.at[1 - at_x]
        else:
            for index in range(lead.size):
                for other in range(2):
                    kept = (
                        source[lead.start + index, other, at_x]
                        if x_first
                        else source[lead.start + index, at_y, other]
                    )
                    received[index, other] = (
                        received[index, other].astype(F32) + kept.astype(F32)
                    ).astype(BF16)
            piece = received.at[:, 1 - at_y] if x_first else received.at[:, 1 - at_x]
        return remote(piece, target, to_y if x_first else to_x)

    def scatter_end(copy, received, target, x_first):
        copy.wait_recv()
        mine = at_y if x_first else at_x
        return received[mine].astype(F32) + target[...].astype(F32)

    def scatter_end_lead(copy, received, target, x_first, count):
        copy.wait_recv()
        mine = at_y if x_first else at_x
        for index in range(count):
            target[index] = (
                received[index, mine].astype(F32) + target[index].astype(F32)
            ).astype(BF16)

    first_half, second_half = pl.ds(0, 2), pl.ds(2, 2)

    acc[...] = jnp.zeros_like(acc)
    tb[...] = jnp.zeros_like(tb)
    main_three.wait()
    extra_three.wait()
    layers_forward(
        1, nxt, qv1.at[0], qv2.at[0], x1, x2, inv, h1, h2, 0, rows_all,
        ready_of(main_ready, main_ready_other),
    )
    factor_copies = [remote(h1.at[:, high], h1o, to_core)]
    main_loss = value_rows(0, 0, rows_all)
    for first in range(0, rows_all, 2 * slot):
        back_rows(upstream, x2, inv.at[1], qv2.at[0], gp2, 3, first, 2 * slot, True)
        block = pl.ds(first, 2 * slot)
        factor_copies.append(remote(gp2.at[block], gp2o.at[block], to_core))
    back_two_to_one(1, gp2, 0, rows_all, (0,))
    for copy in factor_copies:
        copy.wait_recv()
    wide = half // 256 * 128 + 128
    main_two = []
    for index in range(2):
        cols = slice(index * half, (index + 1) * half)
        for part in (slice(0, wide), slice(wide, half)):
            whole = t_mm(gp2[:, cols], h1[:, part]) + t_mm(gp2o[:, cols], h1o[:, part])
            p2[2 * index : 2 * index + 2, :, :, :, part] = whole.astype(BF16).reshape(
                (2, 2, 2, own_two, part.stop - part.start)
            )
        main_two.append(
            scatter_start(p2, r2.at[2 * index : 2 * index + 2], index == 0, pl.ds(2 * index, 2))
        )
    back_two_to_one(1, gp2, 0, rows_all, (1,))
    back_rows(upstream, x1, inv.at[0], qv1.at[0], gp1, 0, 0, rows_all, True)
    one_copy = remote(gp1.at[:, high], gp1o, to_core)
    dx = mm_t(gp1[...], w1[1])
    own_g[...] = own_g[...] + dx[0:slot]
    dxm[:, 0:width] = dx.astype(BF16)
    lane_all = lax.broadcasted_iota(jnp.int32, (rows_all, 128), 1)
    loss_high = main_loss.astype(BF16).astype(F32)
    loss_rest = main_loss - loss_high
    loss_middle = loss_rest.astype(BF16).astype(F32)
    loss_low = loss_rest - loss_middle
    dxm[:, width : width + 128] = jnp.where(
        lane_all == 0, loss_high, jnp.where(lane_all == 1, loss_middle, loss_low)
    ).astype(BF16)
    dx_copies = [
        remote(dxm.at[pl.ds(slot * k, slot)], dxr.at[k - 1], to_z[k]) for k in range(1, LINE)
    ]
    hand, keep = [], []

    def start_two(source, received):
        return [
            scatter_start(
                source, received.at[2 * index : 2 * index + 2], index == 0, pl.ds(2 * index, 2)
            )
            for index in range(2)
        ]

    def middle_two(copies, source, received, target):
        return [
            scatter_middle(
                copies[index], source, received.at[2 * index : 2 * index + 2],
                target.at[2 * index : 2 * index + 2], index == 0, pl.ds(2 * index, 2),
            )
            for index in range(2)
        ]

    def end_two(copies, received, target):
        for index in range(2):
            scatter_end_lead(
                copies[index], received.at[2 * index : 2 * index + 2],
                target.at[2 * index : 2 * index + 2], index == 0, 2,
            )

    def hand_on(source, target):
        keep.append(local(source.at[at_z], target.at[at_z]))
        for k in range(1, LINE):
            hand.append(remote(source.at[z_of[k]], target.at[at_z], to_z[k]))

    def hand_all(source, target):
        mine = target(at_z)
        keep.append(local(source, mine))
        near = remote(source, mine, to_z[1])
        far = remote(source, mine, to_z[2])
        hand.append(near)
        return far, target

    def hand_further(started):
        far, target = started
        far.wait_recv()
        theirs = target(z_of[2])
        hand.append(remote(theirs, theirs, to_z[1]))

    left, right = slice(0, wide), slice(wide, half)

    def context_start(source, received):
        return (
            remote(source.at[:, left], received.at[:, left], to_x),
            remote(source.at[:, right], received.at[:, right], to_y),
        )

    def context_add(source, received, copies):
        for copy in copies:
            copy.wait_recv()
            sent(copy)
        source[...] = (source[...].astype(F32) + received[...].astype(F32)).astype(BF16)

    def context_middle(source, received, target, copies):
        context_add(source, received, copies)
        return (
            remote(source.at[:, left], target.at[:, left], to_y),
            remote(source.at[:, right], target.at[:, right], to_x),
        )

    x_copy.wait_recv()
    one_copy.wait_recv()
    whole = t_mm(xbuf[:, width : width + 128], gp1[:, low]) + t_mm(
        xother[:, width : width + 128], gp1o[...]
    )
    pc[...] = whole[0 : pc.shape[0]].astype(BF16)
    main_context = context_start(pc, pcx)
    next_copy.wait_recv()
    whole = t_mm(nxt[...], gp1[:, low]) + t_mm(nxto[...], gp1o[...])
    p1[...] = whole.astype(BF16).reshape(p1.shape)
    part = t_mm(h2[...], gl[...])
    p3[...] = part.astype(BF16).reshape(p3.shape)
    three_copy = remote(p3.at[pl.ds(2 * (1 - core), 2)], p3o, to_core)
    main_vec = finish_vectors(0, False)
    acc[...] = jnp.zeros_like(acc)
    table_sum(1, gp1, 0, rows_all)
    for copy in main_ready_other:
        sent(copy)
    pl.semaphore_signal(free_b, inc=1, device_id=to_core, device_id_type=mesh_id)
    dyn_again = load_weights(1, dyn_w1, dyn_wc, dyn_w2)
    for copy in factor_copies + [one_copy]:
        sent(copy)
    pl.semaphore_signal(free_f, inc=1, device_id=to_core, device_id_type=mesh_id)
    pl.semaphore_wait(free_b, 1)
    dyn_again_other = send_weights(1, dyn_w1, dyn_wc, dyn_w2)

    layers_forward(
        0, nxt, qv1.at[1], qv2.at[1], x1, x2, inv, h1, h2, 0, slot,
        ready_of(extra_ready, extra_ready_other),
    )
    extra_loss = value_rows(1, 0, slot)
    back_rows(upstream, x2, inv.at[1], qv2.at[1], gp2, 3, 0, slot, True)
    back_two_to_one(0, gp2, 0, slot)
    back_rows(upstream, x1, inv.at[0], qv1.at[1], gp1, 0, 0, slot, True)
    own_total = own_g[...] + mm_t(gp1[0:slot, :], w1[0])
    value = main_loss[0:slot] + extra_loss
    for index, copy in enumerate(dx_copies):
        copy.wait_recv()
        message = dxr[index].astype(F32)
        own_total = own_total + message[:, 0:width]
        value = value + (
            message[:, width : width + 1]
            + message[:, width + 1 : width + 2]
            + message[:, width + 2 : width + 3]
        )
    all_g[0:slot, :] = own_total.astype(BF16)
    grad_copies = [
        remote(all_g.at[pl.ds(0, slot)], all_g.at[pl.ds(slot * k, slot)], to_z[k])
        for k in range(1, LINE)
    ]
    lane_own = lax.broadcasted_iota(jnp.int32, (slot, 128), 1)
    lossbuf[...] = jnp.where(lane_own == 0, consistency, value)
    loss_copy = remote(lossbuf, out_losses.at[own_rows], to_core)
    keep += [local(lossbuf, out_losses.at[own_rows])]
    table_sum(0, gp1, 0, slot)
    rest = rows_all - slot
    stage = {}

    def between(step):
        if step == 0:
            return
        stage["context"] = context_middle(pc, pcx, pcy, main_context)
        stage["two"] = middle_two(main_two, p2, r2, t2)
        stage["one"] = start_two(p1, r1)
        three_copy.wait_recv()
        sent(three_copy)
        stage["three"] = []
        for index in range(2):
            p3h[index] = (
                p3[2 * core + index].astype(F32) + p3o[index].astype(F32)
            ).astype(BF16)
            stage["three"].append(scatter_start(p3h.at[index], r3.at[index], index == 0, None))
        stage["vec"] = join_vectors(0, main_vec)

    layers_forward(
        0, nxt, qv1.at[1], qv2.at[1], x1, x2, inv, h1, h2, slot, rest, between
    )
    first_two = main_two
    main_context, main_two, main_vec = stage["context"], stage["two"], stage["vec"]
    main_three_sum, main_one = stage["three"], stage["one"]
    value_rows(1, slot, rest)
    context_add(pc, pcy, main_context)
    context_hand = hand_all(pc, lambda at: out_qwc.at[at, pl.ds(0, pc.shape[0])])
    back_rows(upstream, x2, inv.at[1], qv2.at[1], gp2, 3, slot, rest, True)
    pl.semaphore_wait(free_f, 1)
    factor_copies = [remote(gp2, gp2o, to_core), remote(h1.at[:, high], h1o, to_core)]
    back_two_to_one(0, gp2, slot, rest)
    back_rows(upstream, x1, inv.at[0], qv1.at[1], gp1, 0, slot, rest, True)
    one_copy = remote(gp1.at[:, high], gp1o, to_core)
    extra_vec = finish_vectors(1, False)
    acc[...] = jnp.zeros_like(acc)

    end_two(main_two, r2, t2)
    hand_on(t2, out_qw2)

    def by_place(body):
        for index in range(LINE):
            @pl.when(at_z == index)
            def _(index=index):
                body(index)

    quarter = hidden // LINE
    quarter_w = width // LINE
    quarter_c = 128 // LINE

    def quarter_two(index, hid, target):
        cols = slice(index * quarter, (index + 1) * quarter)
        whole = t_mm(gp2[:, cols], hid[:, low]) + t_mm(gp2o[:, cols], h1o[...])
        target[...] = whole.astype(BF16).reshape(target.shape)

    def quarter_one(index, mine, others, target, at):
        cols = slice(index * quarter_w, (index + 1) * quarter_w)
        whole = t_mm(mine[:, cols], gp1[:, low]) + t_mm(others[:, cols], gp1o[...])
        target[...] = whole.astype(BF16).reshape(target.shape)
        cols = slice(width + index * quarter_c, width + (index + 1) * quarter_c)
        whole = t_mm(xbuf[:, cols], gp1[:, low]) + t_mm(xother[:, cols], gp1o[...])
        pq[at] = whole.astype(BF16)

    for copy in factor_copies + [one_copy]:
        copy.wait_recv()

    def extra_parts(index):
        part = t_mm(h2[:, index * quarter : (index + 1) * quarter], gl[...])
        e3[...] = part.astype(BF16).reshape(e3.shape)
        quarter_two(index, h1, e2)
        quarter_one(index, nxt, nxto, e1, 0)

    by_place(extra_parts)
    extra_three_sum = remote(e3, e3o, to_core)
    extra_two = scatter_start(e2, er2, True, None)
    extra_one = scatter_start(e1, er1, False, None)
    extra_context = context_start(pq.at[0], pqx.at[0])
    for copy in factor_copies + [one_copy]:
        sent(copy)
    pl.semaphore_signal(free_f, inc=1, device_id=to_core, device_id_type=mesh_id)
    for copy in grad_copies:
        copy.wait_recv()

    def simplex_back(rows):
        share = simplex[rows, :]
        weighted = all_g[rows, :].astype(F32) * share
        up = weighted - share * gather_sum(weighted, ones)
        upstream[rows, 0:width] = up

    over_rows(0, rows_all, simplex_back)
    back_rows(
        upstream.at[:, 0:width], x3, dyn_inv.at[2], dv3, dyn_gp3, 6, 0, rows_all, False
    )

    def dyn_third(index):
        left = dyn_h2[:, index * quarter : (index + 1) * quarter]
        d3s[...] = t_mm(left, dyn_gp3[:, other_cols]).astype(BF16).reshape(d3s.shape)
        d3[...] = t_mm(left, dyn_gp3[:, own_cols]).astype(BF16).reshape(d3.shape)

    by_place(dyn_third)
    d3_copy = remote(d3s, d3o, to_core)

    def three_tile(cols):
        upstream[:, cols] = mm_t(dyn_gp3[...], dw3[cols, :])

    two_tiles(three_tile)
    first_one = main_one
    main_one = middle_two(main_one, p1, r1, t1)
    back_rows(upstream, dyn_x2, dyn_inv.at[1], dyn_vec2, gp2, 3, 0, rows_all, True)
    pl.semaphore_wait(free_f, 1)
    factor_copies = [remote(gp2, gp2o, to_core), remote(dyn_h1.at[:, high], h1o, to_core)]
    d3_copy.wait_recv()
    sent(d3_copy)
    d3[...] = (d3[...].astype(F32) + d3o[...].astype(F32)).astype(BF16)
    dyn_three_sum = scatter_start(d3, er3b, False, None)
    extra_three_sum.wait_recv()
    sent(extra_three_sum)
    e3[...] = (e3[...].astype(F32) + e3o[...].astype(F32)).astype(BF16)
    extra_three_sum = scatter_start(e3, er3, False, None)
    extra_vec = join_vectors(1, extra_vec)
    dyn_again[2].wait()
    dyn_again_other[2].wait_recv()
    back_two_to_one(1, gp2, 0, rows_all)
    for copy in factor_copies:
        copy.wait_recv()
    for copy in first_two + first_one:
        sent(copy)
    d2, d1 = p2.at[0], p1.at[0]
    by_place(lambda index: quarter_two(index, dyn_h1, d2))
    back_rows(upstream, dyn_x1, dyn_inv.at[0], dv1, gp1, 0, 0, rows_all, True)
    one_copy = remote(gp1.at[:, high], gp1o, to_core)
    dyn_vec = finish_vectors(2, True)
    for index in (0, 1):
        dyn_again[index].wait()
        dyn_again_other[index].wait_recv()
    table_sum(1, gp1, 0, slot)
    table_copy = remote(tb, tbo, to_core)
    one_copy.wait_recv()
    by_place(lambda index: quarter_one(index, xbuf, xother, d1, 1))
    dyn_one_sum = scatter_start(d1, er1b, False, None)
    dyn_context = context_start(pq.at[1], pqx.at[1])
    lat_g = tgt
    lat_g[...] = mm_t(gp1[0:slot, :], w1[1])
    latent_copy = remote(lat_g.at[:, other_cols], out_latent.at[own_rows], to_core)
    keep += [local(lat_g.at[:, own_cols], out_latent.at[own_rows])]
    dyn_vec = join_vectors(2, dyn_vec)
    table_copy.wait_recv()
    sent(table_copy)
    tq[...] = tb[own_tasks, :] + tbo[own_tasks, :]
    table_copy = remote(tq, tqr.at[0], to_x)

    end_two(main_one, r1, t1)
    hand_on(t1, out_qw1)
    main_three_sum = [
        scatter_middle(main_three_sum[index], p3h.at[index], r3.at[index], t3.at[index],
                       index == 0, None)
        for index in range(2)
    ]
    main_vec = plane_vectors(0, main_vec)
    extra_context = context_middle(pq.at[0], pqx.at[0], pqy.at[0], extra_context)
    extra_one2 = scatter_middle(extra_one, e1, er1, et1, False, None)
    extra_two2 = scatter_middle(extra_two, e2, er2, et2, True, None)
    extra_vec = plane_vectors(1, extra_vec)
    hand_further(context_hand)
    dyn_context = context_middle(pq.at[1], pqx.at[1], pqy.at[1], dyn_context)
    table_copy.wait_recv()
    sent(table_copy)
    tq[...] = tq[...] + tqr[0]
    table_copy = remote(tq, tqr.at[1], to_y)
    dyn_vec = plane_vectors(2, dyn_vec)
    dyn_two_sum = (
        remote(d2.at[:, 1 - at_x, :, left], er2b.at[:, :, left], to_x),
        remote(d2.at[1 - at_y, :, :, right], er2b.at[:, :, right], to_y),
    )
    dyn_three2 = scatter_middle(dyn_three_sum, d3, er3b, et3b, False, None)
    extra_three2 = scatter_middle(extra_three_sum, e3, er3, et3, False, None)
    dyn_one2 = scatter_middle(dyn_one_sum, d1, er1b, et1b, False, None)
    def quarter_rows(at):
        return pl.ds(pl.multiple_of(quarter_c * at, quarter_c), quarter_c)

    context_add(pq.at[0], pqy.at[0], extra_context)
    extra_hand = hand_all(pq.at[0], lambda at: out_qwc.at[last, quarter_rows(at)])
    total_vectors(0, main_vec)
    vec_hand = hand_all(vp.at[0], lambda at: out_qvec.at[at, core])
    vec_near = hand.pop()
    vec_keep = [keep.pop()]
    for index in range(2):
        t3[index] = scatter_end(
            main_three_sum[index], r3.at[index], t3.at[index], index == 0
        ).astype(BF16)
    mine = at_z // 2 == core
    three_out = out_qw3.at[at_z]
    three_copies = []
    for k in range(1, LINE):
        theirs = z_of[k] // 2 == core
        copy = describe(t3.at[lax.rem(z_of[k], 2)], three_out, to_z[k])
        three_copies.append((theirs, copy))

        @pl.when(theirs)
        def _(copy=copy):
            copy.start()

    three_keep = describe_local(t3.at[lax.rem(at_z, 2)], three_out)

    @pl.when(mine)
    def _():
        three_keep.start()

    context_add(pq.at[1], pqy.at[1], dyn_context)
    dyn_hand = hand_all(pq.at[1], lambda at: out_dwc.at[quarter_rows(at)])
    table_copy.wait_recv()
    sent(table_copy)
    tq[...] = tq[...] + tqr[1]
    table_copies = [remote(tq, tqr.at[1 + k], to_z[k]) for k in range(1, LINE)]
    for copy in dyn_two_sum:
        copy.wait_recv()
    for other in range(2):
        for cols, kept in ((left, d2[other, at_x, :, left]), (right, d2[at_y, other, :, right])):
            er2b[other, :, cols] = (
                er2b[other, :, cols].astype(F32) + kept.astype(F32)
            ).astype(BF16)
    dyn_two2 = (
        remote(er2b.at[1 - at_y, :, left], et2b.at[:, left], to_y),
        remote(er2b.at[1 - at_x, :, right], et2b.at[:, right], to_x),
    )
    hand_further(extra_hand)
    hand_further(vec_hand)
    vec_further = hand.pop()
    total_vectors(1, extra_vec)
    vec_keep += [local(vp.at[1], out_qvec.at[last, core])]
    total_vectors(2, dyn_vec)
    keep += [local(vp.at[2], out_dvec.at[core])]
    hand += [remote(vp.at[2], out_dvec.at[core], to_core)]
    et2[...] = scatter_end(extra_two2, er2, et2, True).astype(BF16)
    keep += [local(et2, out_qw2.at[last])]
    et1[...] = scatter_end(extra_one2, er1, et1, False).astype(BF16)
    keep += [local(et1, out_qw1.at[last])]
    hand_further(dyn_hand)
    o2 = upstream.at[0:own_two, 0:half]
    o1 = upstream.at[own_two : own_two + own_one, 0:half]
    oc = upstream.at[0:own_two, half : half + half_w]
    oc[...] = scatter_end(dyn_three2, er3b, et3b, False)
    keep += [local(oc, out_dw3)]
    et3[...] = scatter_end(extra_three2, er3, et3, False).astype(BF16)
    keep += [local(et3, out_qw3.at[last])]
    o1[...] = scatter_end(dyn_one2, er1b, et1b, False)
    keep += [local(o1, out_dw1)]
    for copy in dyn_two2:
        copy.wait_recv()
    for cols, at in ((left, at_y), (right, at_x)):
        o2[:, cols] = er2b[at, :, cols].astype(F32) + et2b[:, cols].astype(F32)
    keep += [local(o2, out_dw2)]
    vec_near.wait_recv()
    vec_further.wait_recv()
    for copy in vec_keep:
        copy.wait()
    vec_cores = remote(out_qvec.at[:, core], out_qvec.at[:, core], to_core)
    for theirs, copy in three_copies:
        @pl.when(theirs)
        def _(copy=copy):
            copy.wait_send()

    three_further = describe(
        out_qw3.at[pl.ds(0, LINE)], out_qw3.at[pl.ds(0, LINE)], to_core
    )

    @pl.when(mine)
    def _():
        three_keep.wait()
        for _, copy in three_copies:
            copy.wait_recv()
        three_further.start()

    for copy in table_copies:
        copy.wait_recv()
        sent(copy)
    tq[...] = tq[...] + tqr[2] + tqr[3] + tqr[4]
    keep += [local(tq, out_table.at[own_tasks])]
    hand += [remote(tq, out_table.at[own_tasks], to_core)]
    for copy in hand + [loss_copy, latent_copy]:
        copy.wait_recv()
    for copy in keep:
        copy.wait()
    @pl.when(mine)
    def _():
        three_further.wait_send()

    @pl.when(jnp.logical_not(mine))
    def _():
        three_further.wait_recv()

    vec_cores.wait_recv()
    for copy in list(pending):
        sent(copy)


def line_shards(
    latent,
    action,
    task_ids,
    action_mask,
    task_table,
    target_latent,
    bin_lower,
    bin_frac,
    dyn_w1,
    dyn_wc,
    dyn_vec1,
    dyn_w2,
    dyn_vec2,
    dyn_w3,
    dyn_vec3,
    q_w1,
    q_wc,
    q_vec1,
    q_w2,
    q_vec2,
    q_w3,
    q_b3,
):
    local_rows, half_w = latent.shape
    slot = local_rows // 2
    rows = slot * LINE
    width = 2 * half_w
    half = dyn_w1.shape[1]
    hidden = 2 * half
    heads, bins = q_b3.shape
    tasks, acts = action_mask.shape
    context_width = dyn_wc.shape[0]
    pad_context = -(-context_width // 16) * 16
    own_two = hidden // BLOCK
    own_one = width // BLOCK
    scale = 1.0 / math.sqrt(local_rows * lax.axis_size("dp"))
    sizes = (slot, width, hidden, bins, tasks, acts, context_width, heads)

    def shape(*dims, kind=F32):
        return jax.ShapeDtypeStruct(dims, kind)

    out_shape = (
        shape(local_rows, 128),
        shape(local_rows, half_w),
        shape(tasks, 128),
        shape(own_one, half),
        shape(128, half, kind=BF16),
        shape(2, 8, half),
        shape(own_two, half),
        shape(own_two, half_w),
        shape(heads, own_one, half, kind=BF16),
        shape(heads, 128, half, kind=BF16),
        shape(heads, 2, 8, half),
        shape(heads, own_two, half, kind=BF16),
        shape(heads, own_two, bins, kind=BF16),
    )
    v = pltpu.VMEM
    scratch = [
        v((acts, local_rows), BF16),
        v((1, local_rows), jnp.int32),
        v((acts, tasks), jnp.int32),
        v((tasks, context_width - acts), BF16),
        v((1, local_rows), jnp.int32),
        v((1, local_rows), F32),
        v((3, hidden), F32),
        v((heads, bins), F32),
        v((2, width, hidden), BF16),
        v((2, context_width, hidden), BF16),
        v((2, hidden, hidden), BF16),
        v((hidden, width), BF16),
        v((2, bins, hidden), BF16),
        v((3, hidden), F32),
        v((3, width), F32),
        v((2, 3, hidden), F32),
        v((2, 3, hidden), F32),
        v((2, 1, bins), F32),
        v((rows, width + 128), BF16),
        v((rows, width + 128), BF16),
        v((slot, width), F32),
        v((rows, width), BF16),
        v((rows, width), BF16),
        v((rows, hidden), BF16),
        v((rows, hidden), BF16),
        v((rows, hidden), BF16),
        v((rows, hidden), BF16),
        v((rows, width), F32),
        v((rows, width), F32),
        v((3, rows, 1), F32),
        v((rows, hidden), F32),
        v((rows, hidden), F32),
        v((2, rows, 1), F32),
        v((rows, hidden), BF16),
        v((rows, hidden), BF16),
        v((rows, hidden), BF16),
        v((rows, hidden), BF16),
        v((rows, half), BF16),
        v((rows, hidden), BF16),
        v((rows, half), BF16),
        v((rows, hidden), F32),
        v((rows, bins), BF16),
        v((rows, width), BF16),
        v((9, 8, hidden), F32),
        v((rows, width + 128), BF16),
        v((LINE - 1, slot, width + 128), BF16),
        v((slot, width), F32),
        v((rows, width), BF16),
        v((slot, 128), F32),
        v((LINE, 2, 2, own_two, half), BF16),
        v((LINE, 2, own_two, half), BF16),
        v((LINE, own_two, half), BF16),
        v((LINE, 2, 2, own_one, half), BF16),
        v((LINE, 2, own_one, half), BF16),
        v((LINE, own_one, half), BF16),
        v((LINE, 2, 2, own_two, bins), BF16),
        v((2, 2, 2, own_two, bins), BF16),
        v((2, 2, own_two, bins), BF16),
        v((2, own_two, bins), BF16),
        v((2, 2, 2, own_two, bins), BF16),
        v((2, 2, own_two, half), BF16),
        v((2, own_two, half), BF16),
        v((own_two, half), BF16),
        v((2, 2, own_one, half), BF16),
        v((2, own_one, half), BF16),
        v((own_one, half), BF16),
        v((2, 2, own_two, bins), BF16),
        v((2, own_two, bins), BF16),
        v((own_two, bins), BF16),
        v((2, 2, own_two, bins), BF16),
        v((2, own_two, half), BF16),
        v((own_two, half), BF16),
        v((2, own_one, half), BF16),
        v((own_one, half), BF16),
        v((2, 2, own_two, half_w), BF16),
        v((2, 2, own_two, half_w), BF16),
        v((2, 2, own_two, half_w), BF16),
        v((2, own_two, half_w), BF16),
        v((own_two, half_w), BF16),
        v((pad_context, half), BF16),
        v((pad_context, half), BF16),
        v((pad_context, half), BF16),
        v((2, 128 // LINE, half), BF16),
        v((2, 128 // LINE, half), BF16),
        v((2, 128 // LINE, half), BF16),
        v((local_rows, 16), F32),
        v((LINE, 16, local_rows), F32),
        v((3, 8, hidden), F32),
        v((3, 8, hidden), F32),
        v((3, 8, half), F32),
        v((3, 8, half), F32),
        v((3, 8, half), F32),
        v((tasks, 128), F32),
        v((tasks, 128), F32),
        v((tasks // 2, 128), F32),
        v((5, tasks // 2, 128), F32),
        pltpu.SemaphoreType.DMA((REMOTE_COPIES,)),
        pltpu.SemaphoreType.DMA((REMOTE_COPIES,)),
        pltpu.SemaphoreType.DMA((LOCAL_COPIES,)),
        pltpu.SemaphoreType.REGULAR,
        pltpu.SemaphoreType.REGULAR,
        pltpu.SemaphoreType.REGULAR,
    ]
    outside = pl.BlockSpec(memory_space=pl.ANY)
    raw = pl.pallas_call(
        functools.partial(line_kernel, sizes, scale),
        out_shape=out_shape,
        in_specs=[outside] * 22,
        out_specs=[outside] * len(out_shape),
        scratch_shapes=scratch,
        compiler_params=pltpu.CompilerParams(
            collective_id=0, has_side_effects=True, vmem_limit_bytes=VMEM_BYTES
        ),
        cost_estimate=pl.CostEstimate(
            flops=2 * 10**10, bytes_accessed=6 * 10**7, transcendentals=10**7
        ),
        name="line_update",
    )(
        latent, action.T, task_ids[None], action_mask.T, task_table, target_latent,
        bin_lower[None], bin_frac[None], dyn_vec1, dyn_vec2, dyn_vec3, q_vec1, q_vec2, q_b3,
        dyn_w1, dyn_wc, dyn_w2, dyn_w3, q_w1, q_wc, q_w2, jnp.swapaxes(q_w3, 1, 2),
    )
    return finish(raw, (slot, width, hidden, bins, tasks, acts, context_width, heads))


def finish_kernel(sizes, *refs):
    (slot, width, hidden, bins, tasks, acts, context_width, heads) = sizes
    half, half_w = hidden // 2, width // 2
    raw, outs, held, made = refs[0:13], refs[13:30], refs[30:43], refs[43:56]
    in_sem, out_sem = refs[56:]
    (
        raw_losses, raw_latent, raw_table, raw_dw1, raw_dwc, raw_dvec, raw_dw2, raw_dw3,
        raw_qw1, raw_qwc, raw_qvec, raw_qw2, raw_qw3,
    ) = held
    (losses, table, dwc, dvec1, dvec2, dvec3, qw1, qwc, qvec1, qw2, qvec2, qw3, qb3) = made
    (
        out_losses, out_latent, out_table, out_dw1, out_dwc, out_dvec1, out_dw2, out_dvec2,
        out_dw3, out_dvec3, out_qw1, out_qwc, out_qvec1, out_qw2, out_qvec2, out_qw3, out_qb3,
    ) = outs
    core = lax.axis_index("tensor")
    loads = {}
    for index in (11, 9, 6, 8, 1, 7, 3, 4, 10, 12, 5, 0, 2):
        loads[index] = pltpu.make_async_copy(raw[index], held[index], in_sem.at[index])
        loads[index].start()
    stored = []

    def store(source, target):
        copy = pltpu.make_async_copy(source, target, out_sem.at[len(stored)])
        copy.start()
        stored.append(copy)

    loads[11].wait()
    for head in range(heads):
        qw2[head] = raw_qw2[head].astype(F32)
    store(qw2, out_qw2)
    loads[9].wait()
    for head in range(heads):
        qwc[head] = raw_qwc[head].astype(F32)[0:context_width]
    store(qwc, out_qwc)
    for index, source, target in (
        (6, raw_dw2, out_dw2), (1, raw_latent, out_latent), (7, raw_dw3, out_dw3),
        (3, raw_dw1, out_dw1),
    ):
        loads[index].wait()
        store(source, target)
    loads[8].wait()
    qw1[...] = raw_qw1[...].astype(F32)
    store(qw1, out_qw1)
    loads[4].wait()
    dwc[...] = raw_dwc[...].astype(F32)[0:context_width]
    store(dwc, out_dwc)
    loads[10].wait()
    loads[12].wait()
    for head in range(heads):
        qvec1[head] = raw_qvec[head, core, 0:3]
        for index in range(2):
            qvec2[head, :, index * half : (index + 1) * half] = raw_qvec[head, index, 3:6]
        qw3[head] = raw_qw3[head].astype(F32).T
        qb3[head : head + 1, :] = raw_qvec[head, 0, 6:7, 0:bins]
    store(qvec1, out_qvec1)
    store(qvec2, out_qvec2)
    store(qw3, out_qw3)
    store(qb3, out_qb3)
    loads[5].wait()
    dvec1[...] = raw_dvec[core, 0:3]
    line = jnp.concatenate([raw_dvec[0, 6:7], raw_dvec[1, 6:7]], 1)
    rows = jnp.concatenate(
        [line[:, 0:width], line[:, width : 2 * width], raw_dvec[0, 7:8, 0:width]], 0
    )
    dvec3[...] = jnp.where(core == 0, rows[:, 0:half_w], rows[:, half_w:])
    for index in range(2):
        dvec2[:, index * half : (index + 1) * half] = raw_dvec[index, 3:6]
    store(dvec1, out_dvec1)
    store(dvec2, out_dvec2)
    store(dvec3, out_dvec3)
    loads[0].wait()
    loads[2].wait()
    losses[...] = raw_losses[...].T[0:2]
    table[...] = raw_table[:, acts:context_width]
    store(losses, out_losses)
    store(table, out_table)
    for copy in stored:
        copy.wait()


def finish(raw, sizes):
    (slot, width, hidden, bins, tasks, acts, context_width, heads) = sizes
    half, half_w = hidden // 2, width // 2
    own_two, own_one = hidden // BLOCK, width // BLOCK
    dims = [
        (2, 2 * slot),
        (2 * slot, half_w),
        (tasks, context_width - acts),
        (own_one, half),
        (context_width, half),
        (3, half),
        (own_two, half),
        (3, hidden),
        (own_two, half_w),
        (3, half_w),
        (heads, own_one, half),
        (heads, context_width, half),
        (heads, 3, half),
        (heads, own_two, half),
        (heads, 3, hidden),
        (heads, bins, own_two),
        (heads, bins),
    ]
    outside = pl.BlockSpec(memory_space=pl.ANY)
    outs = pl.pallas_call(
        functools.partial(finish_kernel, sizes),
        in_specs=[outside] * len(raw),
        out_specs=[outside] * len(dims),
        out_shape=[jax.ShapeDtypeStruct(item, F32) for item in dims],
        scratch_shapes=[pltpu.VMEM(item.shape, item.dtype) for item in raw]
        + [pltpu.VMEM(item, F32) for index, item in enumerate(dims) if index not in (1, 3, 6, 8)]
        + [pltpu.SemaphoreType.DMA((len(raw),)), pltpu.SemaphoreType.DMA((len(dims),))],
        compiler_params=pltpu.CompilerParams(vmem_limit_bytes=VMEM_BYTES),
        name="finish",
    )(*raw)
    outs = list(outs)
    outs[0] = outs[0].T
    outs[6] = outs[6].T
    outs[13] = jnp.swapaxes(outs[13], 1, 2)
    outs[15] = jnp.swapaxes(outs[15], 1, 2)
    return tuple(outs)


def shards(*arrays):
    if lax.axis_size("dp") == BLOCK:
        return line_shards(*arrays)
    return general_shards(*arrays)


def solution(mesh):
    return jax.shard_map(
        shards,
        mesh=mesh,
        in_specs=(
            P("dp", "tensor"),
            P("dp", None),
            P("dp"),
            P(),
            P(),
            P("dp", "tensor"),
            P("dp"),
            P("dp"),
            P(None, "tensor"),
            P(None, "tensor"),
            P(None, "tensor"),
            P("tensor", None),
            P(),
            P(None, "tensor"),
            P(None, "tensor"),
            P(None, None, "tensor"),
            P(None, None, "tensor"),
            P(None, None, "tensor"),
            P(None, "tensor", None),
            P(),
            P(),
            P(),
        ),
        out_specs=(
            P("dp", None),
            P("dp", "tensor"),
            P(),
            P("dp", "tensor"),
            P(None, "tensor"),
            P(None, "tensor"),
            P("tensor", "dp"),
            P(),
            P("dp", "tensor"),
            P(None, "tensor"),
            P(None, "dp", "tensor"),
            P(None, None, "tensor"),
            P(None, None, "tensor"),
            P(None, "tensor", "dp"),
            P(),
            P(None, "dp", None),
            P(),
        ),
        check_vma=False,
    )
```

```python
import functools
import math

import jax
import jax.numpy as jnp
from jax import lax
from jax.experimental import pallas as pl
from jax.experimental.pallas import tpu as pltpu
from jax.sharding import PartitionSpec as P

GROUP = 8
LINE = 4
PLANE = 4
BLOCK = LINE * PLANE
EPSILON = 1e-05
HIGHEST = lax.Precision.HIGHEST
F32 = jnp.float32
BF16 = jnp.bfloat16
REMOTE_COPIES = 128
SENDS = 56
LOCAL_COPIES = 25
VMEM_BYTES = 63 << 20


def swap_core(values):
    return lax.ppermute(values, "tensor", [(0, 1), (1, 0)])


def swap_dp(values, bit):
    size = lax.axis_size("dp")
    return lax.ppermute(values, "dp", [(place, place ^ bit) for place in range(size)])


def pick(values, index, axis=0):
    return lax.dynamic_index_in_dim(values, index, axis, keepdims=False)


def own_then_other(values):
    return values, swap_core(values)


def mish_parts(values):
    grown = jnp.exp(jnp.minimum(values, 20.0))
    top = grown * (grown + 2.0)
    share = 1.0 / (top + 2.0)
    return grown, top * share, share


def mish(values):
    return values * mish_parts(values)[1]


def mish_slope(values):
    return mish_slope_of(values, *mish_parts(values))


def mish_slope_of(values, grown, ratio, share):
    return ratio + 4.0 * values * grown * (1.0 + grown) * share * share


def norm(before, gain, shift):
    centred = before - jnp.mean(before, -1, keepdims=True)
    inverse = lax.rsqrt(jnp.mean(centred * centred, -1, keepdims=True) + EPSILON)
    normed = centred * inverse
    return normed * gain + shift, normed, inverse


def norm_back(upstream, normed, inverse, gain):
    weighted = upstream * gain
    return inverse * (
        weighted
        - jnp.mean(weighted, -1, keepdims=True)
        - normed * jnp.mean(weighted * normed, -1, keepdims=True)
    )


def vector_sums(rounded, upstream, normed):
    return jnp.stack(
        [jnp.sum(rounded.astype(F32), 0), jnp.sum(upstream * normed, 0), jnp.sum(upstream, 0)]
    )


def mm(left, right):
    return jnp.dot(left, right, preferred_element_type=F32)


def mm_t(left, right):
    return lax.dot_general(left, right, (((1,), (1,)), ((), ())), preferred_element_type=F32)


def t_mm(left, right):
    return lax.dot_general(left, right, (((0,), (0,)), ((), ())), preferred_element_type=F32)


def block_forward(inputs, context, w_one, w_context, vec_one, w_two, vec_two):
    before = mm(inputs, w_one) + mm(context, w_context) + vec_one[0:1]
    out_one, normed_one, inverse_one = norm(before, vec_one[1:2], vec_one[2:3])
    hidden_one = mish(out_one).astype(BF16)
    second = mm(hidden_one, w_two) + vec_two[0:1]
    out_two, normed_two, inverse_two = norm(second, vec_two[1:2], vec_two[2:3])
    hidden_two = mish(out_two).astype(BF16)
    return hidden_one, hidden_two, (normed_one, inverse_one, normed_two, inverse_two)


def block_backward(grad_hidden, saved, vec_one, w_two, vec_two):
    normed_one, inverse_one, normed_two, inverse_two = saved
    upstream = mish_slope(normed_two * vec_two[1:2] + vec_two[2:3]) * grad_hidden
    grad_two = norm_back(upstream, normed_two, inverse_two, vec_two[1:2]).astype(BF16)
    sums_two = vector_sums(grad_two, upstream, normed_two)
    grad_one_hidden = mm_t(grad_two, w_two)
    upstream = mish_slope(normed_one * vec_one[1:2] + vec_one[2:3]) * grad_one_hidden
    grad_one = norm_back(upstream, normed_one, inverse_one, vec_one[1:2]).astype(BF16)
    sums_one = vector_sums(grad_one, upstream, normed_one)
    return grad_two, sums_two, grad_one, sums_one


def dynamics_forward(inputs, context, w_one, w_context, vec_one, w_two, vec_two, w_three, vec_three):
    hidden_one, hidden_two, saved = block_forward(
        inputs, context, w_one, w_context, vec_one, w_two, vec_two
    )
    before = mm(hidden_two, w_three) + vec_three[0:1]
    out, normed, inverse = norm(before, vec_three[1:2], vec_three[2:3])
    grouped = out.reshape(out.shape[0], -1, GROUP)
    simplex = jax.nn.softmax(grouped, axis=-1).reshape(out.shape)
    return hidden_one, hidden_two, saved, simplex, normed, inverse


def dynamics_backward(grad_next, simplex, normed, inverse, saved, w_three, vec_three, vec_one, w_two, vec_two):
    weighted = grad_next * simplex
    rows = weighted.shape[0]
    along = jnp.sum(weighted.reshape(rows, -1, GROUP), -1, keepdims=True)
    along = jnp.broadcast_to(along, (rows, along.shape[1], GROUP)).reshape(weighted.shape)
    upstream = weighted - simplex * along
    grad_three = norm_back(upstream, normed, inverse, vec_three[1:2]).astype(BF16)
    sums_three = vector_sums(grad_three, upstream, normed)
    grad_hidden = mm_t(grad_three, w_three)
    grad_two, sums_two, grad_one, sums_one = block_backward(
        grad_hidden, saved, vec_one, w_two, vec_two
    )
    return grad_three, sums_three, grad_two, sums_two, grad_one, sums_one


def value_head(hidden_two, w_three, bias, lower, fraction, scale, heads):
    logits = mm(hidden_two, w_three) + bias
    log_prob = jax.nn.log_softmax(logits, axis=-1)
    bins = jnp.arange(logits.shape[-1], dtype=jnp.int32)[None, :]
    target = jnp.where(bins == lower, 1.0 - fraction, 0.0) + jnp.where(
        bins == lower + 1, fraction, 0.0
    )
    loss = -jnp.sum(target * log_prob, -1) / heads
    grad_logits = (scale / heads * (jnp.exp(log_prob) - target)).astype(BF16)
    return loss, grad_logits


def spread(values, axis_len):
    blocks = lax.axis_size("dp") // BLOCK
    rows = values.shape[0] // (blocks * BLOCK)
    values = values.reshape((blocks, LINE, 2, 2, rows) + values.shape[1:])
    if blocks > 1:
        values = jnp.moveaxis(values, 0, 3)
    return values.reshape((LINE, 2, 2, blocks * rows) + values.shape[5:])


def across_blocks(values, axis):
    blocks = lax.axis_size("dp") // BLOCK
    if blocks == 1:
        return values
    groups = [[block * BLOCK + place for block in range(blocks)] for place in range(BLOCK)]
    return lax.psum_scatter(
        values, "dp", scatter_dimension=axis, axis_index_groups=groups, tiled=True
    )


def sum_across_blocks(values):
    blocks = lax.axis_size("dp") // BLOCK
    if blocks == 1:
        return values
    groups = [[block * BLOCK + place for block in range(blocks)] for place in range(BLOCK)]
    return lax.psum(values, "dp", axis_index_groups=groups)


def reduce_first(values, axis_x, bit_x, at_x, axis_y, bit_y, at_y):
    sent = pick(values, 1 - at_x, axis_x).astype(BF16)
    total = pick(values, at_x, axis_x) + swap_dp(sent, bit_x).astype(F32)
    if axis_y > axis_x:
        axis_y -= 1
    sent = pick(total, 1 - at_y, axis_y).astype(BF16)
    return pick(total, at_y, axis_y) + swap_dp(sent, bit_y).astype(F32)


def plane_scatter(values, at_x, at_y):
    half = LINE // 2
    first = reduce_first(values[:half], 2, 1, at_x, 1, 2, at_y)
    second = reduce_first(values[half:], 1, 2, at_y, 2, 1, at_x)
    return jnp.concatenate([first, second], 0)


def plane_scatter_one(values, at_x, at_y):
    half = values.shape[-1] // 256 * 128
    if half == 0:
        return reduce_first(values, 1, 1, at_x, 0, 2, at_y)
    first = reduce_first(values[..., :half], 1, 1, at_x, 0, 2, at_y)
    second = reduce_first(values[..., half:], 0, 2, at_y, 1, 1, at_x)
    return jnp.concatenate([first, second], -1)


def line_exchange(values, at_z, last):
    out = jnp.zeros((LINE + 1,) + values.shape[1:], F32)
    for step in range(LINE):
        part = pick(values, at_z ^ step)
        if step:
            part = swap_dp(part.astype(BF16), 4 * step).astype(F32)
        out = lax.dynamic_update_index_in_dim(out, part, at_z ^ step, 0)
    return lax.dynamic_update_index_in_dim(out, last, LINE, 0)


def plane_total(values, kind=F32):
    values = values + swap_dp(values.astype(kind), 1).astype(F32)
    return values + swap_dp(values.astype(kind), 2).astype(F32)


def line_collect(values, at_z, last, kind=F32):
    out = jnp.zeros((LINE + 1,) + values.shape, F32)
    sent = values.astype(kind)
    for step in range(LINE):
        part = swap_dp(sent, 4 * step).astype(F32) if step else values
        out = lax.dynamic_update_index_in_dim(out, part, at_z ^ step, 0)
    return lax.dynamic_update_index_in_dim(out, last, LINE, 0)


def line_total(values):
    total = values
    for step in range(1, LINE):
        total = total + swap_dp(values, 4 * step)
    return total


def in_core_order(core, own, other, axis):
    return jnp.where(
        core == 0, jnp.concatenate([own, other], axis), jnp.concatenate([other, own], axis)
    )


def general_shards(
    latent,
    action,
    task_ids,
    action_mask,
    task_table,
    target_latent,
    bin_lower,
    bin_frac,
    dyn_w1,
    dyn_wc,
    dyn_vec1,
    dyn_w2,
    dyn_vec2,
    dyn_w3,
    dyn_vec3,
    q_w1,
    q_wc,
    q_vec1,
    q_w2,
    q_vec2,
    q_w3,
    q_b3,
):
    place = lax.axis_index("dp")
    core = lax.axis_index("tensor")
    at_x, at_y, at_z = place % 2, place // 2 % 2, place // 4 % 4
    local_rows = latent.shape[0]
    half_rows = local_rows // 2
    half_latent = latent.shape[1]
    half_hidden = dyn_w1.shape[1]
    inv_root = 1.0 / math.sqrt(local_rows * lax.axis_size("dp"))
    task_count = task_table.shape[0]
    heads = q_w1.shape[0]
    head_places = (at_z, heads - 1)

    def both(values, axis):
        return jnp.concatenate(own_then_other(values), axis)

    dyn_w1_all, dyn_wc_all, dyn_vec1_all = both(dyn_w1, 1), both(dyn_wc, 1), both(dyn_vec1, 1)
    dyn_w2_all = both(dyn_w2, 0)
    dyn_w3_all = in_core_order(core, *own_then_other(dyn_w3), 1)
    dyn_vec3_all = in_core_order(core, *own_then_other(dyn_vec3), 1)
    head_weights = []
    for head in head_places:
        head_weights.append(
            (
                both(pick(q_w1, head), 1),
                both(pick(q_wc, head), 1),
                both(pick(q_vec1, head), 1),
                both(pick(q_w2, head), 0),
                pick(q_vec2, head),
                pick(q_w3, head),
                pick(q_b3, head),
            )
        )

    def my_rows(values):
        return lax.dynamic_slice_in_dim(values, core * half_rows, half_rows, 0)

    def their_rows(values):
        return lax.dynamic_slice_in_dim(values, (1 - core) * half_rows, half_rows, 0)

    def whole_columns(values):
        return in_core_order(core, my_rows(values), swap_core(their_rows(values)), 1)

    my_latent = whole_columns(latent)
    my_target = whole_columns(target_latent)
    my_ids = my_rows(task_ids)[:, None]
    onehot = (my_ids == jnp.arange(task_count, dtype=jnp.int32)[None, :]).astype(BF16)
    table = jnp.concatenate([action_mask.astype(BF16), task_table], 1)
    looked_up = mm(onehot, table)
    acts = action.shape[1]
    acted = my_rows(action).astype(F32) * looked_up[:, :acts]
    my_context = jnp.concatenate([acted, looked_up[:, acts:]], 1).astype(BF16)
    fraction = my_rows(bin_frac)[:, None]
    piece_one = lax.reduce_precision(fraction, 8, 7)
    piece_two = lax.reduce_precision(fraction - piece_one, 8, 7)
    piece_three = fraction - piece_one - piece_two
    meta = [my_ids, my_rows(bin_lower)[:, None], piece_one, piece_two, piece_three]
    meta = [item.astype(BF16) for item in meta]
    width = my_latent.shape[1]
    context_width = my_context.shape[1]
    packed = jnp.concatenate([my_latent, my_context] + meta, 1)
    packed = jnp.concatenate([packed] + [swap_dp(packed, 4 * step) for step in range(1, LINE)], 0)
    inputs = packed[:, :width]
    context = packed[:, width : width + context_width]
    meta = packed[:, width + context_width :].astype(F32)
    all_ids = meta[:, 0:1].astype(jnp.int32)
    lower = meta[:, 1:2].astype(jnp.int32)
    fraction = meta[:, 2:3] + meta[:, 3:4] + meta[:, 4:5]
    all_onehot = (all_ids == jnp.arange(task_count, dtype=jnp.int32)[None, :]).astype(F32)
    other_inputs, other_context = swap_core(inputs), swap_core(context)

    dyn_one, dyn_two, dyn_saved, simplex, normed_three, inverse_three = dynamics_forward(
        inputs, context, dyn_w1_all, dyn_wc_all, dyn_vec1_all, dyn_w2_all, dyn_vec2,
        dyn_w3_all, dyn_vec3_all,
    )
    next_low = simplex.astype(BF16)
    mismatch = next_low[:half_rows].astype(F32) - my_target
    consistency = jnp.sum(mismatch * mismatch, -1)
    other_next = swap_core(next_low)

    head_results = []
    for weights in head_weights:
        w_one, w_context, vec_one, w_two, vec_two, w_three, bias = weights
        hidden_one, hidden_two, saved = block_forward(
            next_low, context, w_one, w_context, vec_one, w_two, vec_two
        )
        loss, grad_logits = value_head(
            hidden_two, w_three, bias[None], lower, fraction, inv_root, heads
        )
        grad_hidden = mm_t(grad_logits, w_three)
        grad_two, sums_two, grad_one, sums_one = block_backward(
            grad_hidden, saved, vec_one, w_two, vec_two
        )
        head_results.append(
            (hidden_one, hidden_two, loss, grad_logits, grad_two, sums_two, grad_one, sums_one)
        )

    main, extra = head_results
    grad_in = mm_t(main[6], head_weights[0][0])
    own_grad = grad_in[:half_rows] + mm_t(extra[6][:half_rows], head_weights[1][0])
    own_loss = main[2][:half_rows] + extra[2][:half_rows]
    for step in range(1, LINE):
        part = slice(step * half_rows, (step + 1) * half_rows)
        own_grad = own_grad + swap_dp(grad_in[part].astype(BF16), 4 * step).astype(F32)
        own_loss = own_loss + swap_dp(main[2][part], 4 * step)
    own_grad = own_grad + 2.0 * inv_root * mismatch
    own_low = own_grad.astype(BF16)
    grad_next = jnp.concatenate(
        [own_low] + [swap_dp(own_low, 4 * step) for step in range(1, LINE)], 0
    ).astype(F32)
    my_losses = jnp.stack([consistency, own_loss], 1)
    losses = in_core_order(core, my_losses, swap_core(my_losses), 0)

    grad_three, sums_three, dyn_grad_two, dyn_sums_two, dyn_grad_one, dyn_sums_one = (
        dynamics_backward(
            grad_next, simplex, normed_three, inverse_three, dyn_saved, dyn_w3_all, dyn_vec3_all,
            dyn_vec1_all, dyn_w2_all, dyn_vec2,
        )
    )
    own_latent_grad = mm_t(dyn_grad_one[:half_rows], dyn_w1_all)
    left, right = own_latent_grad[:, :half_latent], own_latent_grad[:, half_latent:]
    kept = jnp.where(core == 0, left, right)
    received = swap_core(jnp.where(core == 0, right, left))
    latent_grad = in_core_order(core, kept, received, 0)

    def own_half(values):
        return jnp.concatenate([values[:, :half_hidden], swap_core(values[:, half_hidden:])], 0)

    def all_rows(values):
        return jnp.concatenate([values, swap_core(values)], 0)

    def quarter(values, size):
        blocks = lax.axis_size("dp") // BLOCK
        cut = values.reshape(values.shape[0], blocks, LINE, size // (blocks * LINE))
        return pick(cut, at_z, 2).reshape(values.shape[0], size // LINE)

    def spread_quarter(values):
        blocks = lax.axis_size("dp") // BLOCK
        rows = values.shape[0] // (blocks * PLANE)
        values = values.reshape((blocks, 2, 2, rows) + values.shape[1:])
        if blocks > 1:
            values = jnp.moveaxis(values, 0, 2)
        return values.reshape((2, 2, blocks * rows) + values.shape[4:])

    both_next = jnp.concatenate([next_low, other_next], 0)
    both_inputs = jnp.concatenate([inputs, other_inputs], 0)
    both_context = jnp.concatenate([context, other_context], 0)
    features = both_next.shape[1]
    hidden = 2 * half_hidden

    def quarter_grads(hidden_one, grad_two, grad_one, rows_in):
        first_factor, grad_factor = own_half(hidden_one), own_half(grad_one)
        w_two_part = t_mm(all_rows(quarter(grad_two, hidden)), first_factor)
        w_one_part = t_mm(quarter(rows_in, features), grad_factor)
        w_context_part = t_mm(both_context, grad_factor)
        return (
            plane_scatter_one(spread_quarter(w_two_part), at_x, at_y),
            plane_scatter_one(spread_quarter(w_one_part), at_x, at_y),
            plane_total(w_context_part, BF16),
        )

    def outer_quarter(left, right):
        part = t_mm(quarter(left, hidden), right)
        return plane_scatter_one(spread_quarter(part), at_x, at_y)

    first_factor, grad_factor = own_half(main[0]), own_half(main[6])
    main_two = plane_scatter(spread(t_mm(all_rows(main[4]), first_factor), 0), at_x, at_y)
    main_one = plane_scatter(spread(t_mm(both_next, grad_factor), 0), at_x, at_y)
    main_three = plane_scatter(spread(t_mm(main[1], main[3]), 0), at_x, at_y)
    main_context = plane_total(t_mm(both_context, grad_factor), BF16)
    extra_two, extra_one, extra_context = quarter_grads(extra[0], extra[4], extra[6], both_next)
    extra_three = outer_quarter(extra[1], extra[3])
    dyn_w2_part, dyn_w1_part, dyn_context = quarter_grads(
        dyn_one, dyn_grad_two, dyn_grad_one, both_inputs
    )
    dyn_w3_part = outer_quarter(
        all_rows(dyn_two),
        jnp.concatenate(
            [
                jnp.where(core == 0, grad_three[:, :half_latent], grad_three[:, half_latent:]),
                swap_core(
                    jnp.where(core == 0, grad_three[:, half_latent:], grad_three[:, :half_latent])
                ),
            ],
            0,
        ),
    )

    q_w2_out = across_blocks(line_exchange(main_two, at_z, extra_two), 1).transpose(0, 2, 1)
    q_w1_out = across_blocks(line_exchange(main_one, at_z, extra_one), 1)
    q_w3_out = line_exchange(main_three, at_z, extra_three)
    q_w3_out = across_blocks(q_w3_out + swap_core(q_w3_out), 1)
    dyn_w2_out = across_blocks(dyn_w2_part, 0).transpose(1, 0)
    dyn_w1_out = across_blocks(dyn_w1_part, 0)
    dyn_w3_out = across_blocks(dyn_w3_part, 0)
    q_wc_out = sum_across_blocks(line_collect(main_context, at_z, extra_context, BF16))
    dyn_wc_out = sum_across_blocks(dyn_context)

    def core_vec(values):
        own, other = values[:, :half_hidden], values[:, half_hidden:]
        return own + swap_core(other)

    def sums_of(result):
        return (
            core_vec(result[7]),
            result[5] + swap_core(result[5]),
            jnp.sum(result[3].astype(F32), 0)[None],
        )

    def pack(items):
        return jnp.concatenate([item.reshape(-1) for item in items])

    main_sums, extra_sums = sums_of(main), sums_of(extra)
    main_bias = main_sums[2] + swap_core(main_sums[2])
    extra_bias = extra_sums[2] + swap_core(extra_sums[2])
    main_sums, extra_sums = main_sums[:2] + (main_bias,), extra_sums[:2] + (extra_bias,)
    three_own = jnp.where(core == 0, sums_three[:, :half_latent], sums_three[:, half_latent:])
    three_other = jnp.where(core == 0, sums_three[:, half_latent:], sums_three[:, :half_latent])
    dyn_sums = (
        core_vec(dyn_sums_one),
        dyn_sums_two + swap_core(dyn_sums_two),
        three_own + swap_core(three_other),
    )
    def table_part(grad_one, w_context, rows):
        embed = mm_t(grad_one[:rows], w_context[acts:])
        return lax.dot_general(
            all_onehot[:rows], embed, (((0,), (0,)), ((), ())), precision=HIGHEST
        )

    table_grad = (
        table_part(main[6], head_weights[0][1], inputs.shape[0])
        + table_part(extra[6], head_weights[1][1], half_rows)
        + table_part(dyn_grad_one, dyn_wc_all, half_rows)
    )
    table_grad = line_total(table_grad + swap_core(table_grad))
    flat = sum_across_blocks(
        plane_total(pack((table_grad,) + dyn_sums + extra_sums + main_sums))
    )
    sizes = [table_grad] + list(dyn_sums)
    pieces = []
    start = 0
    for item in sizes:
        pieces.append(flat[start : start + item.size].reshape(item.shape))
        start += item.size
    head_size = sum(item.size for item in main_sums)
    extra_flat, main_flat = flat[start : start + head_size], flat[start + head_size :]
    head_flat = line_collect(main_flat, at_z, extra_flat)
    head_pieces = []
    start = 0
    for item in main_sums:
        head_pieces.append(
            head_flat[:, start : start + item.size].reshape((heads,) + item.shape)
        )
        start += item.size
    table_out, dyn_vec1_out, dyn_vec2_out, dyn_vec3_out = pieces
    q_vec1_out, q_vec2_out, q_b3_out = head_pieces
    return (
        losses,
        latent_grad,
        table_out,
        dyn_w1_out,
        dyn_wc_out,
        dyn_vec1_out,
        dyn_w2_out,
        dyn_vec2_out,
        dyn_w3_out,
        dyn_vec3_out,
        q_w1_out,
        q_wc_out,
        q_vec1_out,
        q_w2_out,
        q_vec2_out,
        q_w3_out,
        q_b3_out[:, 0],
    )


def gather_sum(values, ones):
    parts = []
    for start in range(0, values.shape[1], 128):
        piece = values[:, start : start + 128]
        high = piece.astype(BF16)
        rest = piece - high.astype(F32)
        middle = rest.astype(BF16)
        low = (rest - middle.astype(F32)).astype(BF16)
        parts.append(mm(high, ones) + mm(middle, ones) + mm(low, ones))
    return jnp.concatenate(parts, 1)


def line_kernel(sizes, scale, *refs):
    (slot, width, hidden, bins, tasks, acts, context_width, heads) = sizes
    (
        latent, raw_action, raw_ids, raw_mask, raw_table, target_latent, raw_lower, raw_frac,
        dyn_vec1, raw_dyn_vec2, dyn_vec3, q_vec1, q_vec2, raw_b3,
        dyn_w1, dyn_wc, dyn_w2, dyn_w3, q_w1, q_wc, q_w2, q_w3,
        out_losses, out_latent, out_table, out_dw1, out_dwc, out_dvec, out_dw2, out_dw3,
        out_qw1, out_qwc, out_qvec, out_qw2, out_qw3,
        action, task_ids, action_mask, task_table, bin_lower, bin_frac, dyn_vec2, q_b3,
        w1, wc, w2, dw3, qw3, dv1, dv3, qv1, qv2, qb3,
        xbuf, xother, tgt, nxt, nxto, dyn_x1, dyn_x2, dyn_h1, dyn_h2, simplex, x3,
        dyn_inv, x1, x2, inv, h1, h2, gp2, gp1, h1o, gp2o, gp1o, upstream, gl, dyn_gp3,
        acc, slope, dxm, dxr, own_g, all_g, lossbuf,
        p2, r2, t2, p1, r1, t1, p3, p3h, r3, t3, p3o,
        e2, er2, et2, e1, er1, et1, e3, er3, et3, e3o,
        er2b, et2b, er1b, et1b, d3, d3s, d3o, er3b, et3b,
        pc, pcx, pcy, pq, pqx, pqy, ctx, fr, vb, vbo, vp, vpx, vpy, tb, tbo, tq, tqr,
        send_sem, recv_sem, local_sem, free_a, free_b, free_f,
    ) = refs
    half = hidden // 2
    half_w = width // 2
    own_two, own_one = hidden // BLOCK, width // BLOCK
    rows_all = slot * LINE
    place = lax.axis_index("dp")
    core = lax.axis_index("tensor")
    at_x = lax.rem(place, 2)
    at_y = lax.rem(place // 2, 2)
    at_z = lax.rem(place // 4, 4)
    z_of = [
        at_z,
        at_z + 1 - 2 * lax.rem(at_z, 2),
        lax.rem(at_z + 2, 4),
        3 - at_z,
    ]
    to_core = (place, 1 - core)
    to_x = (place + 1 - 2 * at_x, core)
    to_y = (place + 2 - 4 * at_y, core)
    to_z = [None] + [(place + 4 * (z_of[k] - at_z), core) for k in range(1, LINE)]
    mesh_id = pl.DeviceIdType.MESH
    counter = [0, 0, 0]
    free = [[], []]
    held = {}
    pending = []

    def describe(source, target, device):
        at = counter[0]
        counter[0] += 1
        if free[0]:
            send_at = free[0].pop()
        else:
            send_at = counter[2]
            counter[2] += 1
        copy = pltpu.make_async_remote_copy(
            src_ref=source, dst_ref=target, send_sem=send_sem.at[send_at],
            recv_sem=recv_sem.at[at], device_id=device, device_id_type=mesh_id,
        )
        held[id(copy)] = send_at
        return copy

    def remote(source, target, device):
        copy = describe(source, target, device)
        copy.start()
        pending.append(copy)
        return copy

    def sent(copy):
        copy.wait_send()
        pending[:] = [item for item in pending if item is not copy]
        free[0].append(held[id(copy)])

    def all_sent():
        for copy in list(pending):
            sent(copy)

    def describe_local(source, target):
        if free[1]:
            at = free[1].pop()
        else:
            at = counter[1]
            counter[1] += 1
        copy = pltpu.make_async_copy(source, target, local_sem.at[at])
        held[id(copy)] = at
        return copy

    def done(copy):
        copy.wait()
        free[1].append(held[id(copy)])

    def local(source, target):
        copy = describe_local(source, target)
        copy.start()
        return copy

    barrier = pltpu.get_barrier_semaphore()
    peers = [to_core, to_x, to_y] + to_z[1:]
    for peer in peers:
        pl.semaphore_signal(barrier, inc=1, device_id=peer, device_id_type=mesh_id)


    low = slice(0, half)
    high = slice(half, hidden)
    own_cols = pl.ds(pl.multiple_of(half_w * core, 128), half_w)
    other_cols = pl.ds(pl.multiple_of(half_w * (1 - core), 128), half_w)
    own_rows = pl.ds(pl.multiple_of(slot * core, 64), slot)
    other_rows = pl.ds(pl.multiple_of(slot * (1 - core), 64), slot)

    def load_weights(to, one, context, two):
        mine = [
            local(one, w1.at[to, :, low]),
            local(context, wc.at[to, :, low]),
            local(two, w2.at[to, low, :]),
        ]
        return mine

    def send_weights(to, one, context, two):
        return [
            remote(one, w1.at[to, :, high], to_core),
            remote(context, wc.at[to, :, high], to_core),
            remote(two, w2.at[to, high, :], to_core),
        ]

    head_z = at_z
    last = heads - 1
    fact_copies = [
        local(source, target)
        for source, target in (
            (raw_ids, task_ids), (raw_frac, bin_frac), (raw_lower, bin_lower),
            (raw_action, action), (raw_mask, action_mask), (raw_table, task_table),
            (latent.at[own_rows], xbuf.at[pl.ds(0, slot), own_cols]),
        )
    ]
    vec_ready = [
        local(source, target)
        for source, target in (
            (dyn_vec1, dv1.at[:, low]), (raw_dyn_vec2, dyn_vec2), (dyn_vec3, dv3.at[:, own_cols]),
            (q_vec1.at[head_z], qv1.at[0, :, low]), (q_vec1.at[last], qv1.at[1, :, low]),
            (q_vec2.at[head_z], qv2.at[0]), (q_vec2.at[last], qv2.at[1]), (raw_b3, q_b3),
            (target_latent.at[own_rows], tgt.at[:, own_cols]),
        )
    ]
    dyn_ready = load_weights(0, dyn_w1, dyn_wc, dyn_w2)
    three_ready = local(dyn_w3, dw3.at[:, own_cols])
    main_ready = load_weights(1, q_w1.at[head_z], q_wc.at[head_z], q_w2.at[head_z])
    main_three = local(q_w3.at[head_z], qw3.at[0])
    extra_three = local(q_w3.at[last], qw3.at[1])

    vb[...] = jnp.zeros_like(vb)

    for copy in fact_copies:
        done(copy)
    fr[0] = jnp.zeros_like(fr[0])
    fr[0, 0:1, :] = task_ids[...].astype(F32)
    fr[0, 1:2, :] = bin_lower[...].astype(F32)
    fr[0, 2:3, :] = bin_frac[...]
    fr[0, 3 : 3 + acts, :] = action[...].astype(F32)

    def shift_matrix(count, start):
        near = lax.broadcasted_iota(jnp.int32, (count, 128), 0)
        far = lax.broadcasted_iota(jnp.int32, (count, 128), 1)
        return (near + start == far).astype(F32).astype(BF16)

    def context_rows(index):
        ctx[...] = fr[index].T
        columns = ctx[own_rows, :]
        ids, lower, fraction = columns[:, 0:1], columns[:, 1:2], columns[:, 2:3]
        task = lax.broadcasted_iota(jnp.int32, (slot, tasks), 1).astype(F32)
        onehot = (ids == task).astype(F32).astype(BF16)
        lane = lax.broadcasted_iota(jnp.int32, (slot, 128), 1)
        factor = mm(columns[:, 3 : 3 + acts].astype(BF16), to_acts) + (lane >= acts).astype(F32)
        piece_one = fraction.astype(BF16).astype(F32)
        piece_two = (fraction - piece_one).astype(BF16).astype(F32)
        facts = mm(onehot, lookup) * factor
        for at, item in enumerate(
            (ids, lower, piece_one, piece_two, fraction - piece_one - piece_two)
        ):
            facts = facts + jnp.where(lane == context_width + at, item, 0.0)
        rows = slice(index * slot, (index + 1) * slot)
        xbuf[rows, width : width + 128] = facts.astype(BF16)

    to_acts = shift_matrix(acts, 0)
    lookup = (
        t_mm(action_mask[...].astype(F32).astype(BF16), to_acts)
        + mm(task_table[...], shift_matrix(context_width - acts, acts))
    ).astype(BF16)
    pl.semaphore_wait(barrier, len(peers))
    facts_in = [remote(fr.at[0], fr.at[k], to_z[k]) for k in range(1, LINE)]
    lat_copy = remote(latent.at[other_rows], xbuf.at[pl.ds(0, slot), own_cols], to_core)
    tgt_copy = remote(target_latent.at[other_rows], tgt.at[:, own_cols], to_core)

    vec_copies = [
        remote(dyn_vec1, dv1.at[:, high], to_core),
        remote(dyn_vec3, dv3.at[:, own_cols], to_core),
        remote(q_vec1.at[head_z], qv1.at[0, :, high], to_core),
        remote(q_vec1.at[last], qv1.at[1, :, high], to_core),
    ]
    dyn_ready_other = send_weights(0, dyn_w1, dyn_wc, dyn_w2)
    three_ready_other = remote(dyn_w3, dw3.at[:, own_cols], to_core)
    main_ready_other = send_weights(1, q_w1.at[head_z], q_wc.at[head_z], q_w2.at[head_z])
    lat_copy.wait_recv()
    line_in = [
        remote(
            xbuf.at[pl.ds(0, slot), pl.ds(0, width)],
            xbuf.at[pl.ds(slot * k, slot), pl.ds(0, width)],
            to_z[k],
        )
        for k in range(1, LINE)
    ]
    context_rows(0)
    for index, copy in enumerate(facts_in):
        copy.wait_recv()
        context_rows(1 + index)
    for copy in vec_copies:
        copy.wait_recv()
    for copy in vec_ready:
        done(copy)
    qb3[0] = q_b3[pl.ds(head_z, 1), :]
    qb3[1] = q_b3[last : last + 1, :]

    CH = 64

    def over_rows(first, count, body):
        if count <= CH:
            body(pl.ds(first, count))
            return

        def step(index, carry):
            body(pl.ds(pl.multiple_of(first + index * CH, CH), CH))
            return carry

        lax.fori_loop(0, count // CH, step, 0)

    def norm_rows(pre, keep, inverse, vec, out, first, count, slope_to=None):
        features = pre.shape[1]

        def body(rows):
            values = pre[rows, :]
            centred = values - jnp.sum(values, -1, keepdims=True) * (1.0 / features)
            inv_rows = lax.rsqrt(
                jnp.sum(centred * centred, -1, keepdims=True) * (1.0 / features) + EPSILON
            )
            normed = centred * inv_rows
            keep[rows, :] = normed.astype(keep.dtype)
            inverse[rows, :] = inv_rows
            values = normed * vec[1:2, :] + vec[2:3, :]
            grown, ratio, share = mish_parts(values)
            out[rows, :] = (values * ratio).astype(BF16)
            if slope_to is not None:
                slope_to[rows, :] = mish_slope_of(values, grown, ratio, share)

        over_rows(first, count, body)

    def add_sums(at, rounded, along, shift):
        count, features = shift.shape
        for index, item in enumerate((rounded, along, shift)):
            acc[at + index, :, 0:features] += jnp.sum(item.reshape(count // 8, 8, features), 0)

    def back_rows(grad, normed_ref, inverse, vec, out, at, first, count, slope, kept=None):
        features = normed_ref.shape[1]

        def body(rows):
            normed = normed_ref[rows, :].astype(F32)
            gain = vec[1:2, :]
            up = grad[rows, :]
            if kept is not None:
                up = kept[rows, :] * up
            elif slope:
                up = mish_slope(normed * gain + vec[2:3, :]) * up
            weighted = up * gain
            along = up * normed
            mean_one = jnp.sum(weighted, -1, keepdims=True) * (1.0 / features)
            mean_two = jnp.sum(weighted * normed, -1, keepdims=True) * (1.0 / features)
            result = (inverse[rows, :] * (weighted - mean_one - normed * mean_two)).astype(BF16)
            out[rows, :] = result
            add_sums(at, result.astype(F32), along, up)

        over_rows(first, count, body)

    def two_tiles(body):
        def step(index, carry):
            body(pl.ds(pl.multiple_of(index * half, 128), half))
            return carry

        lax.fori_loop(0, 2, step, 0)

    def layers_forward(to, source, vec_one, vec_two, keep_one, keep_two, inverse, hid_one, hid_two,
                       first, count, ready, slope_to=None):
        rows = pl.ds(first, count)
        ready(0)

        def first_tile(cols):
            x1[rows, cols] = (
                mm(source[rows, 0:width], w1[to, :, cols])
                + mm(xbuf[rows, width : width + context_width], wc[to, :, cols])
                + vec_one[0:1, cols]
            )

        two_tiles(first_tile)
        norm_rows(x1, keep_one, inverse.at[0], vec_one, hid_one, first, count)
        ready(1)

        def second_tile(cols):
            x2[rows, cols] = mm(hid_one[rows, :], w2[to, :, cols]) + vec_two[0:1, cols]

        two_tiles(second_tile)
        norm_rows(x2, keep_two, inverse.at[1], vec_two, hid_two, first, count, slope_to)

    def back_two_to_one(to, grad, first, count, parts=(0, 1)):
        rows = pl.ds(first, count)

        def tile(cols):
            upstream[rows, cols] = mm_t(grad[rows, :], w2[to, cols, :])

        if len(parts) == 2:
            two_tiles(tile)
        else:
            tile(slice(parts[0] * half, (parts[0] + 1) * half))

    def ready_of(mine, others):
        def ready(stage):
            picked = (0, 1) if stage == 0 else (2,)
            for index in picked:
                done(mine[index])
                others[index].wait_recv()

        return ready

    def nothing(stage):
        return None

    line_in[0].wait_recv()
    layers_forward(
        0, xbuf, dv1, dyn_vec2, dyn_x1, dyn_x2, dyn_inv, dyn_h1, dyn_h2, 0, 2 * slot,
        ready_of(dyn_ready, dyn_ready_other),
    )
    for copy in line_in[1:]:
        copy.wait_recv()
    x_copy = remote(xbuf, xother, to_core)
    layers_forward(
        0, xbuf, dv1, dyn_vec2, dyn_x1, dyn_x2, dyn_inv, dyn_h1, dyn_h2, 2 * slot,
        rows_all - 2 * slot, nothing,
    )
    done(three_ready)
    three_ready_other.wait_recv()
    x3[...] = mm(dyn_h2[...], dw3[...]) + dv3[0:1, :]
    group_row = lax.broadcasted_iota(jnp.int32, (128, 128), 0) // GROUP
    group_col = lax.broadcasted_iota(jnp.int32, (128, 128), 1) // GROUP
    ones = (group_row == group_col).astype(F32).astype(BF16)

    def simplex_rows(rows):
        values = x3[rows, :]
        centred = values - jnp.sum(values, -1, keepdims=True) * (1.0 / width)
        inv_rows = lax.rsqrt(
            jnp.sum(centred * centred, -1, keepdims=True) * (1.0 / width) + EPSILON
        )
        normed = centred * inv_rows
        x3[rows, :] = normed
        dyn_inv[2, rows, :] = inv_rows
        grown = jnp.exp(normed * dv3[1:2, :] + dv3[2:3, :])
        share = grown / gather_sum(grown, ones)
        simplex[rows, :] = share
        nxt[rows, :] = share.astype(BF16)

    over_rows(0, rows_all, simplex_rows)
    for copy in dyn_ready_other:
        sent(copy)
    pl.semaphore_signal(free_a, inc=1, device_id=to_core, device_id_type=mesh_id)
    extra_ready = load_weights(0, q_w1.at[last], q_wc.at[last], q_w2.at[last])
    next_copy = remote(nxt, nxto, to_core)
    tgt_copy.wait_recv()
    gap = nxt[0:slot, :].astype(F32) - tgt[...]
    own_g[...] = gap * (2.0 * scale)
    consistency = jnp.sum(gap * gap, -1, keepdims=True)
    pl.semaphore_wait(free_a, 1)
    extra_ready_other = send_weights(0, q_w1.at[last], q_wc.at[last], q_w2.at[last])

    def value_rows(head, first, count):
        rows = pl.ds(first, count)
        logits = mm_t(h2[rows, :], qw3[head]) + qb3[head]
        logits = logits - jnp.max(logits, -1, keepdims=True)
        grown = jnp.exp(logits)
        total = jnp.sum(grown, -1, keepdims=True)
        lane = lax.broadcasted_iota(jnp.int32, (count, bins), 1).astype(F32)
        facts = xbuf[rows, width : width + 128].astype(F32)
        lower = facts[:, context_width + 1 : context_width + 2]
        fraction = (
            facts[:, context_width + 2 : context_width + 3]
            + facts[:, context_width + 3 : context_width + 4]
            + facts[:, context_width + 4 : context_width + 5]
        )
        target = jnp.where(lane == lower, 1.0 - fraction, 0.0) + jnp.where(
            lane == lower + 1.0, fraction, 0.0
        )
        loss = -jnp.sum(target * (logits - jnp.log(total)), -1, keepdims=True) * (1.0 / heads)
        grad = (scale / heads * (grown / total - target)).astype(BF16)
        gl[rows, :] = grad

        def tile(cols):
            upstream[rows, cols] = mm(grad, qw3[head, :, cols])

        two_tiles(tile)
        acc[6, 0, 0:bins] += jnp.sum(grad.astype(F32), 0)
        return loss

    def table_sum(to, grad, first, count):
        rows = pl.ds(first, count)
        embed = mm_t(grad[rows, :], wc[to])
        ids = xbuf[rows, width : width + 128].astype(F32)[:, context_width : context_width + 1]
        task = lax.broadcasted_iota(jnp.int32, (count, tasks), 1).astype(F32)
        onehot = (ids == task).astype(F32).astype(BF16)
        top = embed.astype(BF16)
        rest = embed - top.astype(F32)
        middle = rest.astype(BF16)
        lowest = (rest - middle.astype(F32)).astype(BF16)
        tb[:, 0:context_width] += (
            t_mm(onehot, top) + t_mm(onehot, middle) + t_mm(onehot, lowest)
        )

    def finish_vectors(slot_at, width_three):
        for index in range(3):
            vb[slot_at, index : index + 1, :] = jnp.sum(acc[index], 0, keepdims=True)
            vb[slot_at, 3 + index : 4 + index, :] = jnp.sum(acc[3 + index], 0, keepdims=True)
        if width_three:
            three = [jnp.sum(acc[6 + index, :, 0:width], 0, keepdims=True) for index in range(3)]
            vb[slot_at, 6:7, 0:width] = three[0]
            vb[slot_at, 6:7, width : 2 * width] = three[1]
            vb[slot_at, 7:8, 0:width] = three[2]
        else:
            vb[slot_at, 6:7, :] = jnp.sum(acc[6], 0, keepdims=True)
        return remote(vb.at[slot_at], vbo.at[slot_at], to_core)

    own_tasks = pl.ds(pl.multiple_of(tasks // 2 * core, 8), tasks // 2)
    half_cols = pl.ds(pl.multiple_of(half * core, 128), half)

    def join_vectors(slot_at, copy):
        copy.wait_recv()
        sent(copy)
        vp[slot_at, 0:3, :] = vb[slot_at, 0:3, low] + vbo[slot_at, 0:3, high]
        vp[slot_at, 3:8, :] = vb[slot_at, 3:8, half_cols] + vbo[slot_at, 3:8, half_cols]
        return remote(vp.at[slot_at], vpx.at[slot_at], to_x)

    def plane_vectors(slot_at, copy):
        copy.wait_recv()
        sent(copy)
        vp[slot_at] = vp[slot_at] + vpx[slot_at]
        return remote(vp.at[slot_at], vpy.at[slot_at], to_y)

    def total_vectors(slot_at, copy):
        copy.wait_recv()
        sent(copy)
        vp[slot_at] = vp[slot_at] + vpy[slot_at]

    def scatter_start(source, target, x_first, lead):
        if lead is None:
            piece = source.at[:, 1 - at_x] if x_first else source.at[1 - at_y]
        else:
            piece = source.at[lead, :, 1 - at_x] if x_first else source.at[lead, 1 - at_y]
        return remote(piece, target, to_x if x_first else to_y)

    def scatter_middle(copy, source, received, target, x_first, lead):
        copy.wait_recv()
        if lead is None:
            for other in range(2):
                kept = source[other, at_x] if x_first else source[at_y, other]
                received[other] = (received[other].astype(F32) + kept.astype(F32)).astype(BF16)
            piece = received.at[1 - at_y] if x_first else received.at[1 - at_x]
        else:
            for index in range(lead.size):
                for other in range(2):
                    kept = (
                        source[lead.start + index, other, at_x]
                        if x_first
                        else source[lead.start + index, at_y, other]
                    )
                    received[index, other] = (
                        received[index, other].astype(F32) + kept.astype(F32)
                    ).astype(BF16)
            piece = received.at[:, 1 - at_y] if x_first else received.at[:, 1 - at_x]
        return remote(piece, target, to_y if x_first else to_x)

    def scatter_end(copy, received, target, x_first):
        copy.wait_recv()
        mine = at_y if x_first else at_x
        return received[mine].astype(F32) + target[...].astype(F32)

    def scatter_end_lead(copy, received, target, x_first, count):
        copy.wait_recv()
        mine = at_y if x_first else at_x
        for index in range(count):
            target[index] = (
                received[index, mine].astype(F32) + target[index].astype(F32)
            ).astype(BF16)

    first_half, second_half = pl.ds(0, 2), pl.ds(2, 2)

    for copy in [lat_copy, tgt_copy] + facts_in + vec_copies + line_in:
        sent(copy)
    acc[...] = jnp.zeros_like(acc)
    tb[...] = jnp.zeros_like(tb)
    done(main_three)
    done(extra_three)
    layers_forward(
        1, nxt, qv1.at[0], qv2.at[0], x1, x2, inv, h1, h2, 0, rows_all,
        ready_of(main_ready, main_ready_other), slope,
    )
    factor_copies = [remote(h1.at[:, high], h1o, to_core)]
    main_loss = value_rows(0, 0, rows_all)
    for first in range(0, rows_all, 2 * slot):
        back_rows(upstream, x2, inv.at[1], qv2.at[0], gp2, 3, first, 2 * slot, True, slope)
        block = pl.ds(first, 2 * slot)
        factor_copies.append(remote(gp2.at[block], gp2o.at[block], to_core))
    back_two_to_one(1, gp2, 0, rows_all, (0,))
    for copy in factor_copies:
        copy.wait_recv()
    wide = half // 256 * 128 + 128
    main_two = [[], []]
    for part in (slice(0, wide), slice(wide, half)):
        for index in range(2):
            cols = slice(index * half, (index + 1) * half)
            whole = t_mm(gp2[:, cols], h1[:, part]) + t_mm(gp2o[:, cols], h1o[:, part])
            p2[2 * index : 2 * index + 2, :, :, :, part] = whole.astype(BF16).reshape(
                (2, 2, 2, own_two, part.stop - part.start)
            )
            lead = pl.ds(2 * index, 2)
            if index == 0:
                piece, device = p2.at[lead, :, 1 - at_x, :, part], to_x
            else:
                piece, device = p2.at[lead, 1 - at_y, :, :, part], to_y
            main_two[index].append(remote(piece, r2.at[lead, :, :, part], device))
    back_two_to_one(1, gp2, 0, rows_all, (1,))
    back_rows(upstream, x1, inv.at[0], qv1.at[0], gp1, 0, 0, rows_all, True)
    one_copy = remote(gp1.at[:, high], gp1o, to_core)
    dx = mm_t(gp1[...], w1[1])
    own_g[...] = own_g[...] + dx[0:slot]
    dxm[:, 0:width] = dx.astype(BF16)
    lane_all = lax.broadcasted_iota(jnp.int32, (rows_all, 128), 1)
    loss_high = main_loss.astype(BF16).astype(F32)
    loss_rest = main_loss - loss_high
    loss_middle = loss_rest.astype(BF16).astype(F32)
    loss_low = loss_rest - loss_middle
    dxm[:, width : width + 128] = jnp.where(
        lane_all == 0, loss_high, jnp.where(lane_all == 1, loss_middle, loss_low)
    ).astype(BF16)
    dx_copies = [
        remote(dxm.at[pl.ds(slot * k, slot)], dxr.at[k - 1], to_z[k]) for k in range(1, LINE)
    ]
    hand, keep = [], []

    def start_two(source, received):
        return [
            scatter_start(
                source, received.at[2 * index : 2 * index + 2], index == 0, pl.ds(2 * index, 2)
            )
            for index in range(2)
        ]

    def middle_two(copies, source, received, target):
        return [
            scatter_middle(
                copies[index], source, received.at[2 * index : 2 * index + 2],
                target.at[2 * index : 2 * index + 2], index == 0, pl.ds(2 * index, 2),
            )
            for index in range(2)
        ]

    def end_two(copies, received, target):
        for index in range(2):
            scatter_end_lead(
                copies[index], received.at[2 * index : 2 * index + 2],
                target.at[2 * index : 2 * index + 2], index == 0, 2,
            )

    def hand_on(source, target):
        keep.append(local(source.at[at_z], target.at[at_z]))
        for k in range(1, LINE):
            hand.append(remote(source.at[z_of[k]], target.at[at_z], to_z[k]))

    def hand_all(source, target):
        mine = target(at_z)
        keep.append(local(source, mine))
        near = remote(source, mine, to_z[1])
        far = remote(source, mine, to_z[2])
        hand.append(near)
        return far, target

    def hand_further(started):
        far, target = started
        far.wait_recv()
        theirs = target(z_of[2])
        hand.append(remote(theirs, theirs, to_z[1]))

    left, right = slice(0, wide), slice(wide, half)

    def context_start(source, received):
        return (
            remote(source.at[:, left], received.at[:, left], to_x),
            remote(source.at[:, right], received.at[:, right], to_y),
        )

    def context_add(source, received, copies):
        for copy in copies:
            copy.wait_recv()
            sent(copy)
        source[...] = (source[...].astype(F32) + received[...].astype(F32)).astype(BF16)

    def context_middle(source, received, target, copies):
        context_add(source, received, copies)
        return (
            remote(source.at[:, left], target.at[:, left], to_y),
            remote(source.at[:, right], target.at[:, right], to_x),
        )

    x_copy.wait_recv()
    one_copy.wait_recv()
    whole = t_mm(xbuf[:, width : width + 128], gp1[:, low]) + t_mm(
        xother[:, width : width + 128], gp1o[...]
    )
    pc[...] = whole[0 : pc.shape[0]].astype(BF16)
    main_context = context_start(pc, pcx)
    next_copy.wait_recv()
    whole = t_mm(nxt[...], gp1[:, low]) + t_mm(nxto[...], gp1o[...])
    p1[...] = whole.astype(BF16).reshape(p1.shape)
    part = t_mm(h2[...], gl[...])
    p3[...] = part.astype(BF16).reshape(p3.shape)
    three_copy = remote(p3.at[pl.ds(2 * (1 - core), 2)], p3o, to_core)
    main_vec = finish_vectors(0, False)
    acc[...] = jnp.zeros_like(acc)
    table_sum(1, gp1, 0, rows_all)
    for copy in main_ready_other:
        sent(copy)
    pl.semaphore_signal(free_b, inc=1, device_id=to_core, device_id_type=mesh_id)
    dyn_again = load_weights(1, dyn_w1, dyn_wc, dyn_w2)
    for copy in factor_copies + [one_copy]:
        sent(copy)
    pl.semaphore_signal(free_f, inc=1, device_id=to_core, device_id_type=mesh_id)
    pl.semaphore_wait(free_b, 1)
    dyn_again_other = send_weights(1, dyn_w1, dyn_wc, dyn_w2)

    for copy in [three_ready_other, x_copy, next_copy]:
        sent(copy)
    layers_forward(
        0, nxt, qv1.at[1], qv2.at[1], x1, x2, inv, h1, h2, 0, slot,
        ready_of(extra_ready, extra_ready_other), slope,
    )
    extra_loss = value_rows(1, 0, slot)
    back_rows(upstream, x2, inv.at[1], qv2.at[1], gp2, 3, 0, slot, True, slope)
    back_two_to_one(0, gp2, 0, slot)
    back_rows(upstream, x1, inv.at[0], qv1.at[1], gp1, 0, 0, slot, True)
    own_total = own_g[...] + mm_t(gp1[0:slot, :], w1[0])
    value = main_loss[0:slot] + extra_loss
    for index, copy in enumerate(dx_copies):
        copy.wait_recv()
        message = dxr[index].astype(F32)
        own_total = own_total + message[:, 0:width]
        value = value + (
            message[:, width : width + 1]
            + message[:, width + 1 : width + 2]
            + message[:, width + 2 : width + 3]
        )
    all_g[0:slot, :] = own_total.astype(BF16)
    grad_copies = [
        remote(all_g.at[pl.ds(0, slot)], all_g.at[pl.ds(slot * k, slot)], to_z[k])
        for k in range(1, LINE)
    ]
    lane_own = lax.broadcasted_iota(jnp.int32, (slot, 128), 1)
    lossbuf[...] = jnp.where(lane_own == 0, consistency, value)
    loss_copy = remote(lossbuf, out_losses.at[own_rows], to_core)
    keep += [local(lossbuf, out_losses.at[own_rows])]
    table_sum(0, gp1, 0, slot)
    rest = rows_all - slot
    stage = {}

    def between(step):
        if step == 0:
            return
        stage["context"] = context_middle(pc, pcx, pcy, main_context)
        for copies in main_two:
            copies[0].wait_recv()
        stage["two"] = middle_two([copies[1] for copies in main_two], p2, r2, t2)
        stage["one"] = start_two(p1, r1)
        three_copy.wait_recv()
        sent(three_copy)
        stage["three"] = []
        for index in range(2):
            p3h[index] = (
                p3[2 * core + index].astype(F32) + p3o[index].astype(F32)
            ).astype(BF16)
            stage["three"].append(scatter_start(p3h.at[index], r3.at[index], index == 0, None))
        stage["vec"] = join_vectors(0, main_vec)

    layers_forward(
        0, nxt, qv1.at[1], qv2.at[1], x1, x2, inv, h1, h2, slot, rest, between, slope
    )
    first_two = main_two[0] + main_two[1]
    main_context, main_two, main_vec = stage["context"], stage["two"], stage["vec"]
    main_three_sum, main_one = stage["three"], stage["one"]
    value_rows(1, slot, rest)
    context_add(pc, pcy, main_context)
    context_hand = hand_all(pc, lambda at: out_qwc.at[at, pl.ds(0, pc.shape[0])])
    back_rows(upstream, x2, inv.at[1], qv2.at[1], gp2, 3, slot, rest, True, slope)
    pl.semaphore_wait(free_f, 1)
    factor_copies = [remote(gp2, gp2o, to_core), remote(h1.at[:, high], h1o, to_core)]
    back_two_to_one(0, gp2, slot, rest)
    back_rows(upstream, x1, inv.at[0], qv1.at[1], gp1, 0, slot, rest, True)
    one_copy = remote(gp1.at[:, high], gp1o, to_core)
    extra_vec = finish_vectors(1, False)
    acc[...] = jnp.zeros_like(acc)

    for copy in extra_ready_other + dx_copies + grad_copies + [loss_copy]:
        sent(copy)
    end_two(main_two, r2, t2)
    hand_on(t2, out_qw2)

    def by_place(body):
        for index in range(LINE):
            @pl.when(at_z == index)
            def _(index=index):
                body(index)

    quarter = hidden // LINE
    quarter_w = width // LINE
    quarter_c = 128 // LINE

    def quarter_two(index, hid, target):
        cols = slice(index * quarter, (index + 1) * quarter)
        whole = t_mm(gp2[:, cols], hid[:, low]) + t_mm(gp2o[:, cols], h1o[...])
        target[...] = whole.astype(BF16).reshape(target.shape)

    def quarter_one(index, mine, others, target, at):
        cols = slice(index * quarter_w, (index + 1) * quarter_w)
        whole = t_mm(mine[:, cols], gp1[:, low]) + t_mm(others[:, cols], gp1o[...])
        target[...] = whole.astype(BF16).reshape(target.shape)
        cols = slice(width + index * quarter_c, width + (index + 1) * quarter_c)
        whole = t_mm(xbuf[:, cols], gp1[:, low]) + t_mm(xother[:, cols], gp1o[...])
        pq[at] = whole.astype(BF16)

    for copy in factor_copies + [one_copy]:
        copy.wait_recv()

    def extra_parts(index):
        part = t_mm(h2[:, index * quarter : (index + 1) * quarter], gl[...])
        e3[...] = part.astype(BF16).reshape(e3.shape)
        quarter_two(index, h1, e2)
        quarter_one(index, nxt, nxto, e1, 0)

    by_place(extra_parts)
    extra_three_sum = remote(e3, e3o, to_core)
    extra_two = scatter_start(e2, er2, True, None)
    extra_one = scatter_start(e1, er1, False, None)
    extra_context = context_start(pq.at[0], pqx.at[0])
    for copy in factor_copies + [one_copy]:
        sent(copy)
    pl.semaphore_signal(free_f, inc=1, device_id=to_core, device_id_type=mesh_id)
    for copy in grad_copies:
        copy.wait_recv()

    for copy in first_two:
        sent(copy)
    def simplex_back(rows):
        share = simplex[rows, :]
        weighted = all_g[rows, :].astype(F32) * share
        up = weighted - share * gather_sum(weighted, ones)
        upstream[rows, 0:width] = up

    over_rows(0, rows_all, simplex_back)
    back_rows(
        upstream.at[:, 0:width], x3, dyn_inv.at[2], dv3, dyn_gp3, 6, 0, rows_all, False
    )

    def dyn_third(index):
        left = dyn_h2[:, index * quarter : (index + 1) * quarter]
        d3s[...] = t_mm(left, dyn_gp3[:, other_cols]).astype(BF16).reshape(d3s.shape)
        d3[...] = t_mm(left, dyn_gp3[:, own_cols]).astype(BF16).reshape(d3.shape)

    by_place(dyn_third)
    d3_copy = remote(d3s, d3o, to_core)

    def three_tile(cols):
        upstream[:, cols] = mm_t(dyn_gp3[...], dw3[cols, :])

    two_tiles(three_tile)
    first_one = main_one
    main_one = middle_two(main_one, p1, r1, t1)
    hand_further(context_hand)
    back_rows(upstream, dyn_x2, dyn_inv.at[1], dyn_vec2, gp2, 3, 0, rows_all, True)
    pl.semaphore_wait(free_f, 1)
    factor_copies = [remote(gp2, gp2o, to_core), remote(dyn_h1.at[:, high], h1o, to_core)]
    d3_copy.wait_recv()
    sent(d3_copy)
    d3[...] = (d3[...].astype(F32) + d3o[...].astype(F32)).astype(BF16)
    dyn_three_sum = scatter_start(d3, er3b, False, None)
    extra_three_sum.wait_recv()
    sent(extra_three_sum)
    e3[...] = (e3[...].astype(F32) + e3o[...].astype(F32)).astype(BF16)
    extra_three_sum = scatter_start(e3, er3, False, None)
    extra_vec = join_vectors(1, extra_vec)
    done(dyn_again[2])
    dyn_again_other[2].wait_recv()
    back_two_to_one(1, gp2, 0, rows_all)
    for copy in factor_copies:
        copy.wait_recv()
    for copy in first_one:
        sent(copy)
    d2, d1 = p2.at[0], p1.at[0]
    by_place(lambda index: quarter_two(index, dyn_h1, d2))
    back_rows(upstream, dyn_x1, dyn_inv.at[0], dv1, gp1, 0, 0, rows_all, True)
    one_copy = remote(gp1.at[:, high], gp1o, to_core)
    dyn_vec = finish_vectors(2, True)
    for index in (0, 1):
        done(dyn_again[index])
        dyn_again_other[index].wait_recv()
    table_sum(1, gp1, 0, slot)
    table_copy = remote(tb, tbo, to_core)
    one_copy.wait_recv()
    by_place(lambda index: quarter_one(index, xbuf, xother, d1, 1))
    dyn_one_sum = scatter_start(d1, er1b, True, None)
    dyn_context = context_start(pq.at[1], pqx.at[1])
    lat_g = tgt
    lat_g[...] = mm_t(gp1[0:slot, :], w1[1])
    latent_copy = remote(lat_g.at[:, other_cols], out_latent.at[own_rows], to_core)
    keep += [local(lat_g.at[:, own_cols], out_latent.at[own_rows])]
    dyn_vec = join_vectors(2, dyn_vec)
    table_copy.wait_recv()
    sent(table_copy)
    tq[...] = tb[own_tasks, :] + tbo[own_tasks, :]
    table_copy = remote(tq, tqr.at[0], to_x)

    end_two(main_one, r1, t1)
    hand_on(t1, out_qw1)
    main_three_sum = [
        scatter_middle(main_three_sum[index], p3h.at[index], r3.at[index], t3.at[index],
                       index == 0, None)
        for index in range(2)
    ]
    main_vec = plane_vectors(0, main_vec)
    extra_context = context_middle(pq.at[0], pqx.at[0], pqy.at[0], extra_context)
    extra_one2 = scatter_middle(extra_one, e1, er1, et1, False, None)
    extra_two2 = scatter_middle(extra_two, e2, er2, et2, True, None)
    extra_vec = plane_vectors(1, extra_vec)
    dyn_context = context_middle(pq.at[1], pqx.at[1], pqy.at[1], dyn_context)
    table_copy.wait_recv()
    sent(table_copy)
    tq[...] = tq[...] + tqr[0]
    table_copy = remote(tq, tqr.at[1], to_y)
    dyn_vec = plane_vectors(2, dyn_vec)
    dyn_two_sum = (
        remote(d2.at[:, 1 - at_x, :, left], er2b.at[:, :, left], to_x),
        remote(d2.at[1 - at_y, :, :, right], er2b.at[:, :, right], to_y),
    )
    dyn_three2 = scatter_middle(dyn_three_sum, d3, er3b, et3b, False, None)
    extra_three2 = scatter_middle(extra_three_sum, e3, er3, et3, False, None)
    dyn_one2 = scatter_middle(dyn_one_sum, d1, er1b, et1b, True, None)
    def quarter_rows(at):
        return pl.ds(pl.multiple_of(quarter_c * at, quarter_c), quarter_c)

    context_add(pq.at[0], pqy.at[0], extra_context)
    extra_hand = hand_all(pq.at[0], lambda at: out_qwc.at[last, quarter_rows(at)])
    total_vectors(0, main_vec)
    vec_hand = hand_all(vp.at[0], lambda at: out_qvec.at[at, core])
    vec_near = hand.pop()
    vec_keep = [keep.pop()]
    for index in range(2):
        t3[index] = scatter_end(
            main_three_sum[index], r3.at[index], t3.at[index], index == 0
        ).astype(BF16)
    mine = at_z // 2 == core
    three_out = out_qw3.at[at_z]
    three_copies = []
    for k in range(1, LINE):
        theirs = z_of[k] // 2 == core
        copy = describe(t3.at[lax.rem(z_of[k], 2)], three_out, to_z[k])
        three_copies.append((theirs, copy))

        @pl.when(theirs)
        def _(copy=copy):
            copy.start()

    three_keep = describe_local(t3.at[lax.rem(at_z, 2)], three_out)

    @pl.when(mine)
    def _():
        three_keep.start()

    context_add(pq.at[1], pqy.at[1], dyn_context)
    dyn_rows = out_dwc.at[quarter_rows(at_z)]
    keep += [local(pq.at[1], dyn_rows)]
    hand += [remote(pq.at[1], dyn_rows, to_z[k]) for k in range(1, LINE)]
    table_copy.wait_recv()
    sent(table_copy)
    tq[...] = tq[...] + tqr[1]
    table_copies = [remote(tq, tqr.at[1 + k], to_z[k]) for k in range(1, LINE)]
    for copy in dyn_two_sum:
        copy.wait_recv()
    for other in range(2):
        for cols, kept in ((left, d2[other, at_x, :, left]), (right, d2[at_y, other, :, right])):
            er2b[other, :, cols] = (
                er2b[other, :, cols].astype(F32) + kept.astype(F32)
            ).astype(BF16)
    dyn_two2 = (
        remote(er2b.at[1 - at_y, :, left], et2b.at[:, left], to_y),
        remote(er2b.at[1 - at_x, :, right], et2b.at[:, right], to_x),
    )
    hand_further(extra_hand)
    hand_further(vec_hand)
    vec_further = hand.pop()
    total_vectors(1, extra_vec)
    vec_keep += [local(vp.at[1], out_qvec.at[last, core])]
    total_vectors(2, dyn_vec)
    keep += [local(vp.at[2], out_dvec.at[core])]
    hand += [remote(vp.at[2], out_dvec.at[core], to_core)]
    et2[...] = scatter_end(extra_two2, er2, et2, True).astype(BF16)
    keep += [local(et2, out_qw2.at[last])]
    et1[...] = scatter_end(extra_one2, er1, et1, False).astype(BF16)
    keep += [local(et1, out_qw1.at[last])]
    o2 = upstream.at[0:own_two, 0:half]
    o1 = upstream.at[own_two : own_two + own_one, 0:half]
    oc = upstream.at[0:own_two, half : half + half_w]
    oc[...] = scatter_end(dyn_three2, er3b, et3b, False)
    keep += [local(oc, out_dw3)]
    et3[...] = scatter_end(extra_three2, er3, et3, False).astype(BF16)
    keep += [local(et3, out_qw3.at[last])]
    o1[...] = scatter_end(dyn_one2, er1b, et1b, True)
    keep += [local(o1, out_dw1)]
    for copy in dyn_two2:
        copy.wait_recv()
    for cols, at in ((left, at_y), (right, at_x)):
        o2[:, cols] = er2b[at, :, cols].astype(F32) + et2b[:, cols].astype(F32)
    keep += [local(o2, out_dw2)]
    vec_near.wait_recv()
    vec_further.wait_recv()
    for copy in vec_keep:
        copy.wait()
    vec_cores = remote(out_qvec.at[:, core], out_qvec.at[:, core], to_core)
    for theirs, copy in three_copies:
        @pl.when(theirs)
        def _(copy=copy):
            copy.wait_send()

    three_further = describe(
        out_qw3.at[pl.ds(0, LINE)], out_qw3.at[pl.ds(0, LINE)], to_core
    )

    @pl.when(mine)
    def _():
        three_keep.wait()
        for _, copy in three_copies:
            copy.wait_recv()
        three_further.start()

    for copy in table_copies:
        copy.wait_recv()
        sent(copy)
    tq[...] = tq[...] + tqr[2] + tqr[3] + tqr[4]
    keep += [local(tq, out_table.at[own_tasks])]
    hand += [remote(tq, out_table.at[own_tasks], to_core)]
    for copy in hand + [loss_copy, latent_copy]:
        copy.wait_recv()
    for copy in keep:
        copy.wait()
    @pl.when(mine)
    def _():
        three_further.wait_send()

    @pl.when(jnp.logical_not(mine))
    def _():
        three_further.wait_recv()

    vec_cores.wait_recv()
    for copy in list(pending):
        sent(copy)


def line_shards(
    latent,
    action,
    task_ids,
    action_mask,
    task_table,
    target_latent,
    bin_lower,
    bin_frac,
    dyn_w1,
    dyn_wc,
    dyn_vec1,
    dyn_w2,
    dyn_vec2,
    dyn_w3,
    dyn_vec3,
    q_w1,
    q_wc,
    q_vec1,
    q_w2,
    q_vec2,
    q_w3,
    q_b3,
):
    local_rows, half_w = latent.shape
    slot = local_rows // 2
    rows = slot * LINE
    width = 2 * half_w
    half = dyn_w1.shape[1]
    hidden = 2 * half
    heads, bins = q_b3.shape
    tasks, acts = action_mask.shape
    context_width = dyn_wc.shape[0]
    pad_context = -(-context_width // 16) * 16
    own_two = hidden // BLOCK
    own_one = width // BLOCK
    scale = 1.0 / math.sqrt(local_rows * lax.axis_size("dp"))
    sizes = (slot, width, hidden, bins, tasks, acts, context_width, heads)

    def shape(*dims, kind=F32):
        return jax.ShapeDtypeStruct(dims, kind)

    out_shape = (
        shape(local_rows, 128),
        shape(local_rows, half_w),
        shape(tasks, 128),
        shape(own_one, half),
        shape(128, half, kind=BF16),
        shape(2, 8, half),
        shape(own_two, half),
        shape(own_two, half_w),
        shape(heads, own_one, half, kind=BF16),
        shape(heads, 128, half, kind=BF16),
        shape(heads, 2, 8, half),
        shape(heads, own_two, half, kind=BF16),
        shape(heads, own_two, bins, kind=BF16),
    )
    v = pltpu.VMEM
    scratch = [
        v((acts, local_rows), BF16),
        v((1, local_rows), jnp.int32),
        v((acts, tasks), jnp.int32),
        v((tasks, context_width - acts), BF16),
        v((1, local_rows), jnp.int32),
        v((1, local_rows), F32),
        v((3, hidden), F32),
        v((heads, bins), F32),
        v((2, width, hidden), BF16),
        v((2, context_width, hidden), BF16),
        v((2, hidden, hidden), BF16),
        v((hidden, width), BF16),
        v((2, bins, hidden), BF16),
        v((3, hidden), F32),
        v((3, width), F32),
        v((2, 3, hidden), F32),
        v((2, 3, hidden), F32),
        v((2, 1, bins), F32),
        v((rows, width + 128), BF16),
        v((rows, width + 128), BF16),
        v((slot, width), F32),
        v((rows, width), BF16),
        v((rows, width), BF16),
        v((rows, hidden), BF16),
        v((rows, hidden), BF16),
        v((rows, hidden), BF16),
        v((rows, hidden), BF16),
        v((rows, width), F32),
        v((rows, width), F32),
        v((3, rows, 1), F32),
        v((rows, hidden), F32),
        v((rows, hidden), F32),
        v((2, rows, 1), F32),
        v((rows, hidden), BF16),
        v((rows, hidden), BF16),
        v((rows, hidden), BF16),
        v((rows, hidden), BF16),
        v((rows, half), BF16),
        v((rows, hidden), BF16),
        v((rows, half), BF16),
        v((rows, hidden), F32),
        v((rows, bins), BF16),
        v((rows, width), BF16),
        v((9, 8, hidden), F32),
        v((rows, hidden), F32),
        v((rows, width + 128), BF16),
        v((LINE - 1, slot, width + 128), BF16),
        v((slot, width), F32),
        v((rows, width), BF16),
        v((slot, 128), F32),
        v((LINE, 2, 2, own_two, half), BF16),
        v((LINE, 2, own_two, half), BF16),
        v((LINE, own_two, half), BF16),
        v((LINE, 2, 2, own_one, half), BF16),
        v((LINE, 2, own_one, half), BF16),
        v((LINE, own_one, half), BF16),
        v((LINE, 2, 2, own_two, bins), BF16),
        v((2, 2, 2, own_two, bins), BF16),
        v((2, 2, own_two, bins), BF16),
        v((2, own_two, bins), BF16),
        v((2, 2, 2, own_two, bins), BF16),
        v((2, 2, own_two, half), BF16),
        v((2, own_two, half), BF16),
        v((own_two, half), BF16),
        v((2, 2, own_one, half), BF16),
        v((2, own_one, half), BF16),
        v((own_one, half), BF16),
        v((2, 2, own_two, bins), BF16),
        v((2, own_two, bins), BF16),
        v((own_two, bins), BF16),
        v((2, 2, own_two, bins), BF16),
        v((2, own_two, half), BF16),
        v((own_two, half), BF16),
        v((2, own_one, half), BF16),
        v((own_one, half), BF16),
        v((2, 2, own_two, half_w), BF16),
        v((2, 2, own_two, half_w), BF16),
        v((2, 2, own_two, half_w), BF16),
        v((2, own_two, half_w), BF16),
        v((own_two, half_w), BF16),
        v((pad_context, half), BF16),
        v((pad_context, half), BF16),
        v((pad_context, half), BF16),
        v((2, 128 // LINE, half), BF16),
        v((2, 128 // LINE, half), BF16),
        v((2, 128 // LINE, half), BF16),
        v((local_rows, 16), F32),
        v((LINE, 16, local_rows), F32),
        v((3, 8, hidden), F32),
        v((3, 8, hidden), F32),
        v((3, 8, half), F32),
        v((3, 8, half), F32),
        v((3, 8, half), F32),
        v((tasks, 128), F32),
        v((tasks, 128), F32),
        v((tasks // 2, 128), F32),
        v((5, tasks // 2, 128), F32),
        pltpu.SemaphoreType.DMA((SENDS,)),
        pltpu.SemaphoreType.DMA((REMOTE_COPIES,)),
        pltpu.SemaphoreType.DMA((LOCAL_COPIES,)),
        pltpu.SemaphoreType.REGULAR,
        pltpu.SemaphoreType.REGULAR,
        pltpu.SemaphoreType.REGULAR,
    ]
    outside = pl.BlockSpec(memory_space=pl.ANY)
    raw = pl.pallas_call(
        functools.partial(line_kernel, sizes, scale),
        out_shape=out_shape,
        in_specs=[outside] * 22,
        out_specs=[outside] * len(out_shape),
        scratch_shapes=scratch,
        compiler_params=pltpu.CompilerParams(
            collective_id=0, has_side_effects=True, vmem_limit_bytes=VMEM_BYTES
        ),
        cost_estimate=pl.CostEstimate(
            flops=2 * 10**10, bytes_accessed=6 * 10**7, transcendentals=10**7
        ),
        name="line_update",
    )(
        latent, action.T, task_ids[None], action_mask.T, task_table, target_latent,
        bin_lower[None], bin_frac[None], dyn_vec1, dyn_vec2, dyn_vec3, q_vec1, q_vec2, q_b3,
        dyn_w1, dyn_wc, dyn_w2, dyn_w3, q_w1, q_wc, q_w2, jnp.swapaxes(q_w3, 1, 2),
    )
    return finish(raw, (slot, width, hidden, bins, tasks, acts, context_width, heads))


def finish_kernel(sizes, *refs):
    (slot, width, hidden, bins, tasks, acts, context_width, heads) = sizes
    half, half_w = hidden // 2, width // 2
    raw, outs, held, made = refs[0:13], refs[13:30], refs[30:43], refs[43:56]
    in_sem, out_sem = refs[56:]
    (
        raw_losses, raw_latent, raw_table, raw_dw1, raw_dwc, raw_dvec, raw_dw2, raw_dw3,
        raw_qw1, raw_qwc, raw_qvec, raw_qw2, raw_qw3,
    ) = held
    (losses, table, dwc, dvec1, dvec2, dvec3, qw1, qwc, qvec1, qw2, qvec2, qw3, qb3) = made
    (
        out_losses, out_latent, out_table, out_dw1, out_dwc, out_dvec1, out_dw2, out_dvec2,
        out_dw3, out_dvec3, out_qw1, out_qwc, out_qvec1, out_qw2, out_qvec2, out_qw3, out_qb3,
    ) = outs
    core = lax.axis_index("tensor")
    loads = {}
    for index in (11, 9, 6, 8, 1, 7, 3, 4, 10, 12, 5, 0, 2):
        loads[index] = pltpu.make_async_copy(raw[index], held[index], in_sem.at[index])
        loads[index].start()
    stored = []

    def store(source, target):
        copy = pltpu.make_async_copy(source, target, out_sem.at[len(stored)])
        copy.start()
        stored.append(copy)

    loads[11].wait()
    for head in range(heads):
        qw2[head] = raw_qw2[head].astype(F32)
    store(qw2, out_qw2)
    loads[9].wait()
    for head in range(heads):
        qwc[head] = raw_qwc[head].astype(F32)[0:context_width]
    store(qwc, out_qwc)
    for index, source, target in (
        (6, raw_dw2, out_dw2), (1, raw_latent, out_latent), (7, raw_dw3, out_dw3),
        (3, raw_dw1, out_dw1),
    ):
        loads[index].wait()
        store(source, target)
    loads[8].wait()
    qw1[...] = raw_qw1[...].astype(F32)
    store(qw1, out_qw1)
    loads[4].wait()
    dwc[...] = raw_dwc[...].astype(F32)[0:context_width]
    store(dwc, out_dwc)
    loads[10].wait()
    loads[12].wait()
    for head in range(heads):
        qvec1[head] = raw_qvec[head, core, 0:3]
        for index in range(2):
            qvec2[head, :, index * half : (index + 1) * half] = raw_qvec[head, index, 3:6]
        qw3[head] = raw_qw3[head].astype(F32).T
        qb3[head : head + 1, :] = raw_qvec[head, 0, 6:7, 0:bins]
    store(qvec1, out_qvec1)
    store(qvec2, out_qvec2)
    store(qw3, out_qw3)
    store(qb3, out_qb3)
    loads[5].wait()
    dvec1[...] = raw_dvec[core, 0:3]
    line = jnp.concatenate([raw_dvec[0, 6:7], raw_dvec[1, 6:7]], 1)
    rows = jnp.concatenate(
        [line[:, 0:width], line[:, width : 2 * width], raw_dvec[0, 7:8, 0:width]], 0
    )
    dvec3[...] = jnp.where(core == 0, rows[:, 0:half_w], rows[:, half_w:])
    for index in range(2):
        dvec2[:, index * half : (index + 1) * half] = raw_dvec[index, 3:6]
    store(dvec1, out_dvec1)
    store(dvec2, out_dvec2)
    store(dvec3, out_dvec3)
    loads[0].wait()
    loads[2].wait()
    losses[...] = raw_losses[...].T[0:2]
    table[...] = raw_table[:, acts:context_width]
    store(losses, out_losses)
    store(table, out_table)
    for copy in stored:
        copy.wait()


def finish(raw, sizes):
    (slot, width, hidden, bins, tasks, acts, context_width, heads) = sizes
    half, half_w = hidden // 2, width // 2
    own_two, own_one = hidden // BLOCK, width // BLOCK
    dims = [
        (2, 2 * slot),
        (2 * slot, half_w),
        (tasks, context_width - acts),
        (own_one, half),
        (context_width, half),
        (3, half),
        (own_two, half),
        (3, hidden),
        (own_two, half_w),
        (3, half_w),
        (heads, own_one, half),
        (heads, context_width, half),
        (heads, 3, half),
        (heads, own_two, half),
        (heads, 3, hidden),
        (heads, bins, own_two),
        (heads, bins),
    ]
    outside = pl.BlockSpec(memory_space=pl.ANY)
    outs = pl.pallas_call(
        functools.partial(finish_kernel, sizes),
        in_specs=[outside] * len(raw),
        out_specs=[outside] * len(dims),
        out_shape=[jax.ShapeDtypeStruct(item, F32) for item in dims],
        scratch_shapes=[pltpu.VMEM(item.shape, item.dtype) for item in raw]
        + [pltpu.VMEM(item, F32) for index, item in enumerate(dims) if index not in (1, 3, 6, 8)]
        + [pltpu.SemaphoreType.DMA((len(raw),)), pltpu.SemaphoreType.DMA((len(dims),))],
        compiler_params=pltpu.CompilerParams(vmem_limit_bytes=VMEM_BYTES),
        name="finish",
    )(*raw)
    outs = list(outs)
    outs[0] = outs[0].T
    outs[6] = outs[6].T
    outs[13] = jnp.swapaxes(outs[13], 1, 2)
    outs[15] = jnp.swapaxes(outs[15], 1, 2)
    return tuple(outs)


def shards(*arrays):
    if lax.axis_size("dp") == BLOCK:
        return line_shards(*arrays)
    return general_shards(*arrays)


def solution(mesh):
    return jax.shard_map(
        shards,
        mesh=mesh,
        in_specs=(
            P("dp", "tensor"),
            P("dp", None),
            P("dp"),
            P(),
            P(),
            P("dp", "tensor"),
            P("dp"),
            P("dp"),
            P(None, "tensor"),
            P(None, "tensor"),
            P(None, "tensor"),
            P("tensor", None),
            P(),
            P(None, "tensor"),
            P(None, "tensor"),
            P(None, None, "tensor"),
            P(None, None, "tensor"),
            P(None, None, "tensor"),
            P(None, "tensor", None),
            P(),
            P(),
            P(),
        ),
        out_specs=(
            P("dp", None),
            P("dp", "tensor"),
            P(),
            P("dp", "tensor"),
            P(None, "tensor"),
            P(None, "tensor"),
            P("tensor", "dp"),
            P(),
            P("dp", "tensor"),
            P(None, "tensor"),
            P(None, "dp", "tensor"),
            P(None, None, "tensor"),
            P(None, None, "tensor"),
            P(None, "tensor", "dp"),
            P(),
            P(None, "dp", None),
            P(),
        ),
        check_vma=False,
    )
```

```python
import functools
import math

import jax
import jax.numpy as jnp
from jax import lax
from jax.experimental import pallas as pl
from jax.experimental.pallas import tpu as pltpu
from jax.sharding import PartitionSpec as P

GROUP = 8
LINE = 4
PLANE = 4
BLOCK = LINE * PLANE
EPSILON = 1e-05
HIGHEST = lax.Precision.HIGHEST
F32 = jnp.float32
BF16 = jnp.bfloat16
REMOTE_COPIES = 128
SENDS = 56
LOCAL_COPIES = 25
VMEM_BYTES = 63 << 20


def swap_core(values):
    return lax.ppermute(values, "tensor", [(0, 1), (1, 0)])


def swap_dp(values, bit):
    size = lax.axis_size("dp")
    return lax.ppermute(values, "dp", [(place, place ^ bit) for place in range(size)])


def pick(values, index, axis=0):
    return lax.dynamic_index_in_dim(values, index, axis, keepdims=False)


def own_then_other(values):
    return values, swap_core(values)


def mish_parts(values):
    grown = jnp.exp(jnp.minimum(values, 20.0))
    top = grown * (grown + 2.0)
    share = 1.0 / (top + 2.0)
    return grown, top * share, share


def mish(values):
    return values * mish_parts(values)[1]


def mish_slope(values):
    return mish_slope_of(values, *mish_parts(values))


def mish_slope_of(values, grown, ratio, share):
    return ratio + 4.0 * values * grown * (1.0 + grown) * share * share


def norm(before, gain, shift):
    centred = before - jnp.mean(before, -1, keepdims=True)
    inverse = lax.rsqrt(jnp.mean(centred * centred, -1, keepdims=True) + EPSILON)
    normed = centred * inverse
    return normed * gain + shift, normed, inverse


def norm_back(upstream, normed, inverse, gain):
    weighted = upstream * gain
    return inverse * (
        weighted
        - jnp.mean(weighted, -1, keepdims=True)
        - normed * jnp.mean(weighted * normed, -1, keepdims=True)
    )


def vector_sums(rounded, upstream, normed):
    return jnp.stack(
        [jnp.sum(rounded.astype(F32), 0), jnp.sum(upstream * normed, 0), jnp.sum(upstream, 0)]
    )


def mm(left, right):
    return jnp.dot(left, right, preferred_element_type=F32)


def mm_t(left, right):
    return lax.dot_general(left, right, (((1,), (1,)), ((), ())), preferred_element_type=F32)


def t_mm(left, right):
    return lax.dot_general(left, right, (((0,), (0,)), ((), ())), preferred_element_type=F32)


def block_forward(inputs, context, w_one, w_context, vec_one, w_two, vec_two):
    before = mm(inputs, w_one) + mm(context, w_context) + vec_one[0:1]
    out_one, normed_one, inverse_one = norm(before, vec_one[1:2], vec_one[2:3])
    hidden_one = mish(out_one).astype(BF16)
    second = mm(hidden_one, w_two) + vec_two[0:1]
    out_two, normed_two, inverse_two = norm(second, vec_two[1:2], vec_two[2:3])
    hidden_two = mish(out_two).astype(BF16)
    return hidden_one, hidden_two, (normed_one, inverse_one, normed_two, inverse_two)


def block_backward(grad_hidden, saved, vec_one, w_two, vec_two):
    normed_one, inverse_one, normed_two, inverse_two = saved
    upstream = mish_slope(normed_two * vec_two[1:2] + vec_two[2:3]) * grad_hidden
    grad_two = norm_back(upstream, normed_two, inverse_two, vec_two[1:2]).astype(BF16)
    sums_two = vector_sums(grad_two, upstream, normed_two)
    grad_one_hidden = mm_t(grad_two, w_two)
    upstream = mish_slope(normed_one * vec_one[1:2] + vec_one[2:3]) * grad_one_hidden
    grad_one = norm_back(upstream, normed_one, inverse_one, vec_one[1:2]).astype(BF16)
    sums_one = vector_sums(grad_one, upstream, normed_one)
    return grad_two, sums_two, grad_one, sums_one


def dynamics_forward(inputs, context, w_one, w_context, vec_one, w_two, vec_two, w_three, vec_three):
    hidden_one, hidden_two, saved = block_forward(
        inputs, context, w_one, w_context, vec_one, w_two, vec_two
    )
    before = mm(hidden_two, w_three) + vec_three[0:1]
    out, normed, inverse = norm(before, vec_three[1:2], vec_three[2:3])
    grouped = out.reshape(out.shape[0], -1, GROUP)
    simplex = jax.nn.softmax(grouped, axis=-1).reshape(out.shape)
    return hidden_one, hidden_two, saved, simplex, normed, inverse


def dynamics_backward(grad_next, simplex, normed, inverse, saved, w_three, vec_three, vec_one, w_two, vec_two):
    weighted = grad_next * simplex
    rows = weighted.shape[0]
    along = jnp.sum(weighted.reshape(rows, -1, GROUP), -1, keepdims=True)
    along = jnp.broadcast_to(along, (rows, along.shape[1], GROUP)).reshape(weighted.shape)
    upstream = weighted - simplex * along
    grad_three = norm_back(upstream, normed, inverse, vec_three[1:2]).astype(BF16)
    sums_three = vector_sums(grad_three, upstream, normed)
    grad_hidden = mm_t(grad_three, w_three)
    grad_two, sums_two, grad_one, sums_one = block_backward(
        grad_hidden, saved, vec_one, w_two, vec_two
    )
    return grad_three, sums_three, grad_two, sums_two, grad_one, sums_one


def value_head(hidden_two, w_three, bias, lower, fraction, scale, heads):
    logits = mm(hidden_two, w_three) + bias
    log_prob = jax.nn.log_softmax(logits, axis=-1)
    bins = jnp.arange(logits.shape[-1], dtype=jnp.int32)[None, :]
    target = jnp.where(bins == lower, 1.0 - fraction, 0.0) + jnp.where(
        bins == lower + 1, fraction, 0.0
    )
    loss = -jnp.sum(target * log_prob, -1) / heads
    grad_logits = (scale / heads * (jnp.exp(log_prob) - target)).astype(BF16)
    return loss, grad_logits


def spread(values, axis_len):
    blocks = lax.axis_size("dp") // BLOCK
    rows = values.shape[0] // (blocks * BLOCK)
    values = values.reshape((blocks, LINE, 2, 2, rows) + values.shape[1:])
    if blocks > 1:
        values = jnp.moveaxis(values, 0, 3)
    return values.reshape((LINE, 2, 2, blocks * rows) + values.shape[5:])


def across_blocks(values, axis):
    blocks = lax.axis_size("dp") // BLOCK
    if blocks == 1:
        return values
    groups = [[block * BLOCK + place for block in range(blocks)] for place in range(BLOCK)]
    return lax.psum_scatter(
        values, "dp", scatter_dimension=axis, axis_index_groups=groups, tiled=True
    )


def sum_across_blocks(values):
    blocks = lax.axis_size("dp") // BLOCK
    if blocks == 1:
        return values
    groups = [[block * BLOCK + place for block in range(blocks)] for place in range(BLOCK)]
    return lax.psum(values, "dp", axis_index_groups=groups)


def reduce_first(values, axis_x, bit_x, at_x, axis_y, bit_y, at_y):
    sent = pick(values, 1 - at_x, axis_x).astype(BF16)
    total = pick(values, at_x, axis_x) + swap_dp(sent, bit_x).astype(F32)
    if axis_y > axis_x:
        axis_y -= 1
    sent = pick(total, 1 - at_y, axis_y).astype(BF16)
    return pick(total, at_y, axis_y) + swap_dp(sent, bit_y).astype(F32)


def plane_scatter(values, at_x, at_y):
    half = LINE // 2
    first = reduce_first(values[:half], 2, 1, at_x, 1, 2, at_y)
    second = reduce_first(values[half:], 1, 2, at_y, 2, 1, at_x)
    return jnp.concatenate([first, second], 0)


def plane_scatter_one(values, at_x, at_y):
    half = values.shape[-1] // 256 * 128
    if half == 0:
        return reduce_first(values, 1, 1, at_x, 0, 2, at_y)
    first = reduce_first(values[..., :half], 1, 1, at_x, 0, 2, at_y)
    second = reduce_first(values[..., half:], 0, 2, at_y, 1, 1, at_x)
    return jnp.concatenate([first, second], -1)


def line_exchange(values, at_z, last):
    out = jnp.zeros((LINE + 1,) + values.shape[1:], F32)
    for step in range(LINE):
        part = pick(values, at_z ^ step)
        if step:
            part = swap_dp(part.astype(BF16), 4 * step).astype(F32)
        out = lax.dynamic_update_index_in_dim(out, part, at_z ^ step, 0)
    return lax.dynamic_update_index_in_dim(out, last, LINE, 0)


def plane_total(values, kind=F32):
    values = values + swap_dp(values.astype(kind), 1).astype(F32)
    return values + swap_dp(values.astype(kind), 2).astype(F32)


def line_collect(values, at_z, last, kind=F32):
    out = jnp.zeros((LINE + 1,) + values.shape, F32)
    sent = values.astype(kind)
    for step in range(LINE):
        part = swap_dp(sent, 4 * step).astype(F32) if step else values
        out = lax.dynamic_update_index_in_dim(out, part, at_z ^ step, 0)
    return lax.dynamic_update_index_in_dim(out, last, LINE, 0)


def line_total(values):
    total = values
    for step in range(1, LINE):
        total = total + swap_dp(values, 4 * step)
    return total


def in_core_order(core, own, other, axis):
    return jnp.where(
        core == 0, jnp.concatenate([own, other], axis), jnp.concatenate([other, own], axis)
    )


def general_shards(
    latent,
    action,
    task_ids,
    action_mask,
    task_table,
    target_latent,
    bin_lower,
    bin_frac,
    dyn_w1,
    dyn_wc,
    dyn_vec1,
    dyn_w2,
    dyn_vec2,
    dyn_w3,
    dyn_vec3,
    q_w1,
    q_wc,
    q_vec1,
    q_w2,
    q_vec2,
    q_w3,
    q_b3,
):
    place = lax.axis_index("dp")
    core = lax.axis_index("tensor")
    at_x, at_y, at_z = place % 2, place // 2 % 2, place // 4 % 4
    local_rows = latent.shape[0]
    half_rows = local_rows // 2
    half_latent = latent.shape[1]
    half_hidden = dyn_w1.shape[1]
    inv_root = 1.0 / math.sqrt(local_rows * lax.axis_size("dp"))
    task_count = task_table.shape[0]
    heads = q_w1.shape[0]
    head_places = (at_z, heads - 1)

    def both(values, axis):
        return jnp.concatenate(own_then_other(values), axis)

    dyn_w1_all, dyn_wc_all, dyn_vec1_all = both(dyn_w1, 1), both(dyn_wc, 1), both(dyn_vec1, 1)
    dyn_w2_all = both(dyn_w2, 0)
    dyn_w3_all = in_core_order(core, *own_then_other(dyn_w3), 1)
    dyn_vec3_all = in_core_order(core, *own_then_other(dyn_vec3), 1)
    head_weights = []
    for head in head_places:
        head_weights.append(
            (
                both(pick(q_w1, head), 1),
                both(pick(q_wc, head), 1),
                both(pick(q_vec1, head), 1),
                both(pick(q_w2, head), 0),
                pick(q_vec2, head),
                pick(q_w3, head),
                pick(q_b3, head),
            )
        )

    def my_rows(values):
        return lax.dynamic_slice_in_dim(values, core * half_rows, half_rows, 0)

    def their_rows(values):
        return lax.dynamic_slice_in_dim(values, (1 - core) * half_rows, half_rows, 0)

    def whole_columns(values):
        return in_core_order(core, my_rows(values), swap_core(their_rows(values)), 1)

    my_latent = whole_columns(latent)
    my_target = whole_columns(target_latent)
    my_ids = my_rows(task_ids)[:, None]
    onehot = (my_ids == jnp.arange(task_count, dtype=jnp.int32)[None, :]).astype(BF16)
    table = jnp.concatenate([action_mask.astype(BF16), task_table], 1)
    looked_up = mm(onehot, table)
    acts = action.shape[1]
    acted = my_rows(action).astype(F32) * looked_up[:, :acts]
    my_context = jnp.concatenate([acted, looked_up[:, acts:]], 1).astype(BF16)
    fraction = my_rows(bin_frac)[:, None]
    piece_one = lax.reduce_precision(fraction, 8, 7)
    piece_two = lax.reduce_precision(fraction - piece_one, 8, 7)
    piece_three = fraction - piece_one - piece_two
    meta = [my_ids, my_rows(bin_lower)[:, None], piece_one, piece_two, piece_three]
    meta = [item.astype(BF16) for item in meta]
    width = my_latent.shape[1]
    context_width = my_context.shape[1]
    packed = jnp.concatenate([my_latent, my_context] + meta, 1)
    packed = jnp.concatenate([packed] + [swap_dp(packed, 4 * step) for step in range(1, LINE)], 0)
    inputs = packed[:, :width]
    context = packed[:, width : width + context_width]
    meta = packed[:, width + context_width :].astype(F32)
    all_ids = meta[:, 0:1].astype(jnp.int32)
    lower = meta[:, 1:2].astype(jnp.int32)
    fraction = meta[:, 2:3] + meta[:, 3:4] + meta[:, 4:5]
    all_onehot = (all_ids == jnp.arange(task_count, dtype=jnp.int32)[None, :]).astype(F32)
    other_inputs, other_context = swap_core(inputs), swap_core(context)

    dyn_one, dyn_two, dyn_saved, simplex, normed_three, inverse_three = dynamics_forward(
        inputs, context, dyn_w1_all, dyn_wc_all, dyn_vec1_all, dyn_w2_all, dyn_vec2,
        dyn_w3_all, dyn_vec3_all,
    )
    next_low = simplex.astype(BF16)
    mismatch = next_low[:half_rows].astype(F32) - my_target
    consistency = jnp.sum(mismatch * mismatch, -1)
    other_next = swap_core(next_low)

    head_results = []
    for weights in head_weights:
        w_one, w_context, vec_one, w_two, vec_two, w_three, bias = weights
        hidden_one, hidden_two, saved = block_forward(
            next_low, context, w_one, w_context, vec_one, w_two, vec_two
        )
        loss, grad_logits = value_head(
            hidden_two, w_three, bias[None], lower, fraction, inv_root, heads
        )
        grad_hidden = mm_t(grad_logits, w_three)
        grad_two, sums_two, grad_one, sums_one = block_backward(
            grad_hidden, saved, vec_one, w_two, vec_two
        )
        head_results.append(
            (hidden_one, hidden_two, loss, grad_logits, grad_two, sums_two, grad_one, sums_one)
        )

    main, extra = head_results
    grad_in = mm_t(main[6], head_weights[0][0])
    own_grad = grad_in[:half_rows] + mm_t(extra[6][:half_rows], head_weights[1][0])
    own_loss = main[2][:half_rows] + extra[2][:half_rows]
    for step in range(1, LINE):
        part = slice(step * half_rows, (step + 1) * half_rows)
        own_grad = own_grad + swap_dp(grad_in[part].astype(BF16), 4 * step).astype(F32)
        own_loss = own_loss + swap_dp(main[2][part], 4 * step)
    own_grad = own_grad + 2.0 * inv_root * mismatch
    own_low = own_grad.astype(BF16)
    grad_next = jnp.concatenate(
        [own_low] + [swap_dp(own_low, 4 * step) for step in range(1, LINE)], 0
    ).astype(F32)
    my_losses = jnp.stack([consistency, own_loss], 1)
    losses = in_core_order(core, my_losses, swap_core(my_losses), 0)

    grad_three, sums_three, dyn_grad_two, dyn_sums_two, dyn_grad_one, dyn_sums_one = (
        dynamics_backward(
            grad_next, simplex, normed_three, inverse_three, dyn_saved, dyn_w3_all, dyn_vec3_all,
            dyn_vec1_all, dyn_w2_all, dyn_vec2,
        )
    )
    own_latent_grad = mm_t(dyn_grad_one[:half_rows], dyn_w1_all)
    left, right = own_latent_grad[:, :half_latent], own_latent_grad[:, half_latent:]
    kept = jnp.where(core == 0, left, right)
    received = swap_core(jnp.where(core == 0, right, left))
    latent_grad = in_core_order(core, kept, received, 0)

    def own_half(values):
        return jnp.concatenate([values[:, :half_hidden], swap_core(values[:, half_hidden:])], 0)

    def all_rows(values):
        return jnp.concatenate([values, swap_core(values)], 0)

    def quarter(values, size):
        blocks = lax.axis_size("dp") // BLOCK
        cut = values.reshape(values.shape[0], blocks, LINE, size // (blocks * LINE))
        return pick(cut, at_z, 2).reshape(values.shape[0], size // LINE)

    def spread_quarter(values):
        blocks = lax.axis_size("dp") // BLOCK
        rows = values.shape[0] // (blocks * PLANE)
        values = values.reshape((blocks, 2, 2, rows) + values.shape[1:])
        if blocks > 1:
            values = jnp.moveaxis(values, 0, 2)
        return values.reshape((2, 2, blocks * rows) + values.shape[4:])

    both_next = jnp.concatenate([next_low, other_next], 0)
    both_inputs = jnp.concatenate([inputs, other_inputs], 0)
    both_context = jnp.concatenate([context, other_context], 0)
    features = both_next.shape[1]
    hidden = 2 * half_hidden

    def quarter_grads(hidden_one, grad_two, grad_one, rows_in):
        first_factor, grad_factor = own_half(hidden_one), own_half(grad_one)
        w_two_part = t_mm(all_rows(quarter(grad_two, hidden)), first_factor)
        w_one_part = t_mm(quarter(rows_in, features), grad_factor)
        w_context_part = t_mm(both_context, grad_factor)
        return (
            plane_scatter_one(spread_quarter(w_two_part), at_x, at_y),
            plane_scatter_one(spread_quarter(w_one_part), at_x, at_y),
            plane_total(w_context_part, BF16),
        )

    def outer_quarter(left, right):
        part = t_mm(quarter(left, hidden), right)
        return plane_scatter_one(spread_quarter(part), at_x, at_y)

    first_factor, grad_factor = own_half(main[0]), own_half(main[6])
    main_two = plane_scatter(spread(t_mm(all_rows(main[4]), first_factor), 0), at_x, at_y)
    main_one = plane_scatter(spread(t_mm(both_next, grad_factor), 0), at_x, at_y)
    main_three = plane_scatter(spread(t_mm(main[1], main[3]), 0), at_x, at_y)
    main_context = plane_total(t_mm(both_context, grad_factor), BF16)
    extra_two, extra_one, extra_context = quarter_grads(extra[0], extra[4], extra[6], both_next)
    extra_three = outer_quarter(extra[1], extra[3])
    dyn_w2_part, dyn_w1_part, dyn_context = quarter_grads(
        dyn_one, dyn_grad_two, dyn_grad_one, both_inputs
    )
    dyn_w3_part = outer_quarter(
        all_rows(dyn_two),
        jnp.concatenate(
            [
                jnp.where(core == 0, grad_three[:, :half_latent], grad_three[:, half_latent:]),
                swap_core(
                    jnp.where(core == 0, grad_three[:, half_latent:], grad_three[:, :half_latent])
                ),
            ],
            0,
        ),
    )

    q_w2_out = across_blocks(line_exchange(main_two, at_z, extra_two), 1).transpose(0, 2, 1)
    q_w1_out = across_blocks(line_exchange(main_one, at_z, extra_one), 1)
    q_w3_out = line_exchange(main_three, at_z, extra_three)
    q_w3_out = across_blocks(q_w3_out + swap_core(q_w3_out), 1)
    dyn_w2_out = across_blocks(dyn_w2_part, 0).transpose(1, 0)
    dyn_w1_out = across_blocks(dyn_w1_part, 0)
    dyn_w3_out = across_blocks(dyn_w3_part, 0)
    q_wc_out = sum_across_blocks(line_collect(main_context, at_z, extra_context, BF16))
    dyn_wc_out = sum_across_blocks(dyn_context)

    def core_vec(values):
        own, other = values[:, :half_hidden], values[:, half_hidden:]
        return own + swap_core(other)

    def sums_of(result):
        return (
            core_vec(result[7]),
            result[5] + swap_core(result[5]),
            jnp.sum(result[3].astype(F32), 0)[None],
        )

    def pack(items):
        return jnp.concatenate([item.reshape(-1) for item in items])

    main_sums, extra_sums = sums_of(main), sums_of(extra)
    main_bias = main_sums[2] + swap_core(main_sums[2])
    extra_bias = extra_sums[2] + swap_core(extra_sums[2])
    main_sums, extra_sums = main_sums[:2] + (main_bias,), extra_sums[:2] + (extra_bias,)
    three_own = jnp.where(core == 0, sums_three[:, :half_latent], sums_three[:, half_latent:])
    three_other = jnp.where(core == 0, sums_three[:, half_latent:], sums_three[:, :half_latent])
    dyn_sums = (
        core_vec(dyn_sums_one),
        dyn_sums_two + swap_core(dyn_sums_two),
        three_own + swap_core(three_other),
    )
    def table_part(grad_one, w_context, rows):
        embed = mm_t(grad_one[:rows], w_context[acts:])
        return lax.dot_general(
            all_onehot[:rows], embed, (((0,), (0,)), ((), ())), precision=HIGHEST
        )

    table_grad = (
        table_part(main[6], head_weights[0][1], inputs.shape[0])
        + table_part(extra[6], head_weights[1][1], half_rows)
        + table_part(dyn_grad_one, dyn_wc_all, half_rows)
    )
    table_grad = line_total(table_grad + swap_core(table_grad))
    flat = sum_across_blocks(
        plane_total(pack((table_grad,) + dyn_sums + extra_sums + main_sums))
    )
    sizes = [table_grad] + list(dyn_sums)
    pieces = []
    start = 0
    for item in sizes:
        pieces.append(flat[start : start + item.size].reshape(item.shape))
        start += item.size
    head_size = sum(item.size for item in main_sums)
    extra_flat, main_flat = flat[start : start + head_size], flat[start + head_size :]
    head_flat = line_collect(main_flat, at_z, extra_flat)
    head_pieces = []
    start = 0
    for item in main_sums:
        head_pieces.append(
            head_flat[:, start : start + item.size].reshape((heads,) + item.shape)
        )
        start += item.size
    table_out, dyn_vec1_out, dyn_vec2_out, dyn_vec3_out = pieces
    q_vec1_out, q_vec2_out, q_b3_out = head_pieces
    return (
        losses,
        latent_grad,
        table_out,
        dyn_w1_out,
        dyn_wc_out,
        dyn_vec1_out,
        dyn_w2_out,
        dyn_vec2_out,
        dyn_w3_out,
        dyn_vec3_out,
        q_w1_out,
        q_wc_out,
        q_vec1_out,
        q_w2_out,
        q_vec2_out,
        q_w3_out,
        q_b3_out[:, 0],
    )


def gather_sum(values, ones):
    parts = []
    for start in range(0, values.shape[1], 128):
        piece = values[:, start : start + 128]
        high = piece.astype(BF16)
        rest = (piece - high.astype(F32)).astype(BF16)
        parts.append(mm(jnp.concatenate([high, rest], 1), ones))
    return jnp.concatenate(parts, 1)


def line_kernel(sizes, scale, *refs):
    (slot, width, hidden, bins, tasks, acts, context_width, heads) = sizes
    (
        latent, raw_action, raw_ids, raw_mask, raw_table, target_latent, raw_lower, raw_frac,
        dyn_vec1, raw_dyn_vec2, dyn_vec3, q_vec1, q_vec2, raw_b3,
        dyn_w1, dyn_wc, dyn_w2, dyn_w3, q_w1, q_wc, q_w2, q_w3,
        out_losses, out_latent, out_table, out_dw1, out_dwc, out_dvec, out_dw2, out_dw3,
        out_qw1, out_qwc, out_qvec, out_qw2, out_qw3,
        action, task_ids, action_mask, task_table, bin_lower, bin_frac, dyn_vec2, q_b3,
        w1, wc, w2, dw3, qw3, dv1, dv3, qv1, qv2, qb3,
        xbuf, xother, tgt, nxt, nxto, dyn_x1, dyn_x2, dyn_h1, dyn_h2, simplex, x3,
        dyn_inv, x1, x2, inv, h1, h2, gp2, gp1, h1o, gp2o, gp1o, upstream, gl, dyn_gp3,
        acc, slope, dxm, dxr, own_g, all_g, lossbuf,
        p2, r2, t2, p1, r1, t1, p3, p3h, r3, t3, p3o,
        e2, er2, et2, e1, er1, et1, e3, er3, et3, e3o,
        er2b, et2b, er1b, et1b, d3, d3s, d3o, er3b, et3b,
        pc, pcx, pcy, pq, pqx, pqy, ctx, fr, vb, vbo, vp, vpx, vpy, tb, tbo, tq, tqr,
        send_sem, recv_sem, local_sem, free_a, free_b, free_f,
    ) = refs
    half = hidden // 2
    half_w = width // 2
    own_two, own_one = hidden // BLOCK, width // BLOCK
    rows_all = slot * LINE
    place = lax.axis_index("dp")
    core = lax.axis_index("tensor")
    at_x = lax.rem(place, 2)
    at_y = lax.rem(place // 2, 2)
    at_z = lax.rem(place // 4, 4)
    z_of = [
        at_z,
        at_z + 1 - 2 * lax.rem(at_z, 2),
        lax.rem(at_z + 2, 4),
        3 - at_z,
    ]
    to_core = (place, 1 - core)
    to_x = (place + 1 - 2 * at_x, core)
    to_y = (place + 2 - 4 * at_y, core)
    to_z = [None] + [(place + 4 * (z_of[k] - at_z), core) for k in range(1, LINE)]
    mesh_id = pl.DeviceIdType.MESH
    counter = [0, 0, 0]
    free = [[], []]
    held = {}
    pending = []

    def describe(source, target, device):
        at = counter[0]
        counter[0] += 1
        if free[0]:
            send_at = free[0].pop()
        else:
            send_at = counter[2]
            counter[2] += 1
        copy = pltpu.make_async_remote_copy(
            src_ref=source, dst_ref=target, send_sem=send_sem.at[send_at],
            recv_sem=recv_sem.at[at], device_id=device, device_id_type=mesh_id,
        )
        held[id(copy)] = send_at
        return copy

    def remote(source, target, device):
        copy = describe(source, target, device)
        copy.start()
        pending.append(copy)
        return copy

    def sent(copy):
        copy.wait_send()
        pending[:] = [item for item in pending if item is not copy]
        free[0].append(held[id(copy)])

    def all_sent():
        for copy in list(pending):
            sent(copy)

    def describe_local(source, target):
        if free[1]:
            at = free[1].pop()
        else:
            at = counter[1]
            counter[1] += 1
        copy = pltpu.make_async_copy(source, target, local_sem.at[at])
        held[id(copy)] = at
        return copy

    def done(copy):
        copy.wait()
        free[1].append(held[id(copy)])

    def local(source, target):
        copy = describe_local(source, target)
        copy.start()
        return copy

    barrier = pltpu.get_barrier_semaphore()
    peers = [to_core, to_x, to_y] + to_z[1:]
    for peer in peers:
        pl.semaphore_signal(barrier, inc=1, device_id=peer, device_id_type=mesh_id)


    low = slice(0, half)
    high = slice(half, hidden)
    own_cols = pl.ds(pl.multiple_of(half_w * core, 128), half_w)
    other_cols = pl.ds(pl.multiple_of(half_w * (1 - core), 128), half_w)
    own_rows = pl.ds(pl.multiple_of(slot * core, 64), slot)
    other_rows = pl.ds(pl.multiple_of(slot * (1 - core), 64), slot)

    def load_weights(to, one, context, two):
        mine = [
            local(one, w1.at[to, :, low]),
            local(context, wc.at[to, :, low]),
            local(two, w2.at[to, low, :]),
        ]
        return mine

    def send_weights(to, one, context, two):
        return [
            remote(one, w1.at[to, :, high], to_core),
            remote(context, wc.at[to, :, high], to_core),
            remote(two, w2.at[to, high, :], to_core),
        ]

    head_z = at_z
    last = heads - 1
    fact_copies = [
        local(source, target)
        for source, target in (
            (raw_ids, task_ids), (raw_frac, bin_frac), (raw_lower, bin_lower),
            (raw_action, action), (raw_mask, action_mask), (raw_table, task_table),
            (latent.at[own_rows], xbuf.at[pl.ds(0, slot), own_cols]),
        )
    ]
    vec_ready = [
        local(source, target)
        for source, target in (
            (dyn_vec1, dv1.at[:, low]), (raw_dyn_vec2, dyn_vec2), (dyn_vec3, dv3.at[:, own_cols]),
            (q_vec1.at[head_z], qv1.at[0, :, low]), (q_vec1.at[last], qv1.at[1, :, low]),
            (q_vec2.at[head_z], qv2.at[0]), (q_vec2.at[last], qv2.at[1]), (raw_b3, q_b3),
            (target_latent.at[own_rows], tgt.at[:, own_cols]),
        )
    ]
    dyn_ready = load_weights(0, dyn_w1, dyn_wc, dyn_w2)
    three_ready = local(dyn_w3, dw3.at[:, own_cols])
    main_ready = load_weights(1, q_w1.at[head_z], q_wc.at[head_z], q_w2.at[head_z])
    main_three = local(q_w3.at[head_z], qw3.at[0])
    extra_three = local(q_w3.at[last], qw3.at[1])

    vb[...] = jnp.zeros_like(vb)

    for copy in fact_copies:
        done(copy)
    fr[0] = jnp.zeros_like(fr[0])
    fr[0, 0:1, :] = task_ids[...].astype(F32)
    fr[0, 1:2, :] = bin_lower[...].astype(F32)
    fr[0, 2:3, :] = bin_frac[...]
    fr[0, 3 : 3 + acts, :] = action[...].astype(F32)

    def shift_matrix(count, start):
        near = lax.broadcasted_iota(jnp.int32, (count, 128), 0)
        far = lax.broadcasted_iota(jnp.int32, (count, 128), 1)
        return (near + start == far).astype(F32).astype(BF16)

    def context_rows(index):
        ctx[...] = fr[index].T
        columns = ctx[own_rows, :]
        ids, lower, fraction = columns[:, 0:1], columns[:, 1:2], columns[:, 2:3]
        task = lax.broadcasted_iota(jnp.int32, (slot, tasks), 1).astype(F32)
        onehot = (ids == task).astype(F32).astype(BF16)
        lane = lax.broadcasted_iota(jnp.int32, (slot, 128), 1)
        factor = mm(columns[:, 3 : 3 + acts].astype(BF16), to_acts) + (lane >= acts).astype(F32)
        piece_one = fraction.astype(BF16).astype(F32)
        piece_two = (fraction - piece_one).astype(BF16).astype(F32)
        facts = mm(onehot, lookup) * factor
        for at, item in enumerate(
            (ids, lower, piece_one, piece_two, fraction - piece_one - piece_two)
        ):
            facts = facts + jnp.where(lane == context_width + at, item, 0.0)
        rows = slice(index * slot, (index + 1) * slot)
        xbuf[rows, width : width + 128] = facts.astype(BF16)

    to_acts = shift_matrix(acts, 0)
    lookup = (
        t_mm(action_mask[...].astype(F32).astype(BF16), to_acts)
        + mm(task_table[...], shift_matrix(context_width - acts, acts))
    ).astype(BF16)
    pl.semaphore_wait(barrier, len(peers))
    facts_in = [remote(fr.at[0], fr.at[k], to_z[k]) for k in range(1, LINE)]
    lat_copy = remote(latent.at[other_rows], xbuf.at[pl.ds(0, slot), own_cols], to_core)
    tgt_copy = remote(target_latent.at[other_rows], tgt.at[:, own_cols], to_core)

    vec_copies = [
        remote(dyn_vec1, dv1.at[:, high], to_core),
        remote(dyn_vec3, dv3.at[:, own_cols], to_core),
        remote(q_vec1.at[head_z], qv1.at[0, :, high], to_core),
        remote(q_vec1.at[last], qv1.at[1, :, high], to_core),
    ]
    dyn_ready_other = send_weights(0, dyn_w1, dyn_wc, dyn_w2)
    three_ready_other = remote(dyn_w3, dw3.at[:, own_cols], to_core)
    main_ready_other = send_weights(1, q_w1.at[head_z], q_wc.at[head_z], q_w2.at[head_z])
    lat_copy.wait_recv()
    line_in = [
        remote(
            xbuf.at[pl.ds(0, slot), pl.ds(0, width)],
            xbuf.at[pl.ds(slot * k, slot), pl.ds(0, width)],
            to_z[k],
        )
        for k in range(1, LINE)
    ]
    context_rows(0)
    for index, copy in enumerate(facts_in):
        copy.wait_recv()
        context_rows(1 + index)
    for copy in vec_copies:
        copy.wait_recv()
    for copy in vec_ready:
        done(copy)
    qb3[0] = q_b3[pl.ds(head_z, 1), :]
    qb3[1] = q_b3[last : last + 1, :]

    CH = 64

    def over_rows(first, count, body, CH=CH):
        if count <= CH:
            body(pl.ds(first, count))
            return

        def step(index, carry):
            body(pl.ds(pl.multiple_of(first + index * CH, CH), CH))
            return carry

        lax.fori_loop(0, count // CH, step, 0)

    def norm_rows(pre, keep, inverse, vec, out, first, count, slope_to=None):
        features = pre.shape[1]

        def body(rows):
            values = pre[rows, :]
            centred = values - jnp.sum(values, -1, keepdims=True) * (1.0 / features)
            inv_rows = lax.rsqrt(
                jnp.sum(centred * centred, -1, keepdims=True) * (1.0 / features) + EPSILON
            )
            normed = centred * inv_rows
            keep[rows, :] = normed.astype(keep.dtype)
            inverse[rows, :] = inv_rows
            values = normed * vec[1:2, :] + vec[2:3, :]
            grown, ratio, share = mish_parts(values)
            out[rows, :] = (values * ratio).astype(BF16)
            if slope_to is not None:
                slope_to[rows, :] = mish_slope_of(values, grown, ratio, share)

        over_rows(first, count, body)

    def add_sums(at, rounded, along, shift):
        count, features = shift.shape
        for index, item in enumerate((rounded, along, shift)):
            acc[at + index, :, 0:features] += jnp.sum(item.reshape(count // 8, 8, features), 0)

    def back_rows(grad, normed_ref, inverse, vec, out, at, first, count, slope, kept=None):
        features = normed_ref.shape[1]

        def body(rows):
            normed = normed_ref[rows, :].astype(F32)
            gain = vec[1:2, :]
            up = grad[rows, :]
            if kept is not None:
                up = kept[rows, :] * up
            elif slope:
                up = mish_slope(normed * gain + vec[2:3, :]) * up
            weighted = up * gain
            along = up * normed
            mean_one = jnp.sum(weighted, -1, keepdims=True) * (1.0 / features)
            mean_two = jnp.sum(weighted * normed, -1, keepdims=True) * (1.0 / features)
            result = (inverse[rows, :] * (weighted - mean_one - normed * mean_two)).astype(BF16)
            out[rows, :] = result
            add_sums(at, result.astype(F32), along, up)

        over_rows(first, count, body)

    def two_tiles(body):
        def step(index, carry):
            body(pl.ds(pl.multiple_of(index * half, 128), half))
            return carry

        lax.fori_loop(0, 2, step, 0)

    def layers_forward(to, source, vec_one, vec_two, keep_one, keep_two, inverse, hid_one, hid_two,
                       first, count, ready, slope_to=None):
        rows = pl.ds(first, count)
        ready(0)

        def first_tile(cols):
            x1[rows, cols] = (
                mm(source[rows, 0:width], w1[to, :, cols])
                + mm(xbuf[rows, width : width + context_width], wc[to, :, cols])
                + vec_one[0:1, cols]
            )

        two_tiles(first_tile)
        norm_rows(x1, keep_one, inverse.at[0], vec_one, hid_one, first, count)
        ready(1)

        def second_tile(cols):
            x2[rows, cols] = mm(hid_one[rows, :], w2[to, :, cols]) + vec_two[0:1, cols]

        two_tiles(second_tile)
        norm_rows(x2, keep_two, inverse.at[1], vec_two, hid_two, first, count, slope_to)

    def back_two_to_one(to, grad, first, count, parts=(0, 1)):
        rows = pl.ds(first, count)

        def tile(cols):
            upstream[rows, cols] = mm_t(grad[rows, :], w2[to, cols, :])

        if len(parts) == 2:
            two_tiles(tile)
        else:
            tile(slice(parts[0] * half, (parts[0] + 1) * half))

    def ready_of(mine, others):
        def ready(stage):
            picked = (0, 1) if stage == 0 else (2,)
            for index in picked:
                done(mine[index])
                others[index].wait_recv()

        return ready

    def nothing(stage):
        return None

    line_in[0].wait_recv()
    layers_forward(
        0, xbuf, dv1, dyn_vec2, dyn_x1, dyn_x2, dyn_inv, dyn_h1, dyn_h2, 0, 2 * slot,
        ready_of(dyn_ready, dyn_ready_other),
    )
    for copy in line_in[1:]:
        copy.wait_recv()
    x_copy = remote(xbuf, xother, to_core)
    layers_forward(
        0, xbuf, dv1, dyn_vec2, dyn_x1, dyn_x2, dyn_inv, dyn_h1, dyn_h2, 2 * slot,
        rows_all - 2 * slot, nothing,
    )
    done(three_ready)
    three_ready_other.wait_recv()
    x3[...] = mm(dyn_h2[...], dw3[...]) + dv3[0:1, :]
    group_row = lax.rem(lax.broadcasted_iota(jnp.int32, (256, 128), 0), 128) // GROUP
    group_col = lax.broadcasted_iota(jnp.int32, (256, 128), 1) // GROUP
    ones = (group_row == group_col).astype(F32).astype(BF16)

    def simplex_rows(rows):
        values = x3[rows, :]
        centred = values - jnp.sum(values, -1, keepdims=True) * (1.0 / width)
        inv_rows = lax.rsqrt(
            jnp.sum(centred * centred, -1, keepdims=True) * (1.0 / width) + EPSILON
        )
        normed = centred * inv_rows
        x3[rows, :] = normed
        dyn_inv[2, rows, :] = inv_rows
        grown = jnp.exp(normed * dv3[1:2, :] + dv3[2:3, :])
        share = grown / gather_sum(grown, ones)
        simplex[rows, :] = share
        nxt[rows, :] = share.astype(BF16)

    over_rows(0, rows_all, simplex_rows, 2 * CH)
    for copy in dyn_ready_other:
        sent(copy)
    pl.semaphore_signal(free_a, inc=1, device_id=to_core, device_id_type=mesh_id)
    extra_ready = load_weights(0, q_w1.at[last], q_wc.at[last], q_w2.at[last])
    next_copy = remote(nxt, nxto, to_core)
    tgt_copy.wait_recv()
    gap = nxt[0:slot, :].astype(F32) - tgt[...]
    own_g[...] = gap * (2.0 * scale)
    consistency = jnp.sum(gap * gap, -1, keepdims=True)
    pl.semaphore_wait(free_a, 1)
    extra_ready_other = send_weights(0, q_w1.at[last], q_wc.at[last], q_w2.at[last])

    def value_rows(head, first, count):
        rows = pl.ds(first, count)
        logits = mm_t(h2[rows, :], qw3[head]) + qb3[head]
        logits = logits - jnp.max(logits, -1, keepdims=True)
        grown = jnp.exp(logits)
        total = jnp.sum(grown, -1, keepdims=True)
        lane = lax.broadcasted_iota(jnp.int32, (count, bins), 1).astype(F32)
        facts = xbuf[rows, width : width + 128].astype(F32)
        lower = facts[:, context_width + 1 : context_width + 2]
        fraction = (
            facts[:, context_width + 2 : context_width + 3]
            + facts[:, context_width + 3 : context_width + 4]
            + facts[:, context_width + 4 : context_width + 5]
        )
        target = jnp.where(lane == lower, 1.0 - fraction, 0.0) + jnp.where(
            lane == lower + 1.0, fraction, 0.0
        )
        loss = -jnp.sum(target * (logits - jnp.log(total)), -1, keepdims=True) * (1.0 / heads)
        grad = (scale / heads * (grown / total - target)).astype(BF16)
        gl[rows, :] = grad

        def tile(cols):
            upstream[rows, cols] = mm(grad, qw3[head, :, cols])

        two_tiles(tile)
        acc[6, 0, 0:bins] += jnp.sum(grad.astype(F32), 0)
        return loss

    def table_sum(to, grad, first, count):
        rows = pl.ds(first, count)
        embed = mm_t(grad[rows, :], wc[to])
        ids = xbuf[rows, width : width + 128].astype(F32)[:, context_width : context_width + 1]
        task = lax.broadcasted_iota(jnp.int32, (count, tasks), 1).astype(F32)
        onehot = (ids == task).astype(F32).astype(BF16)
        top = embed.astype(BF16)
        rest = embed - top.astype(F32)
        middle = rest.astype(BF16)
        lowest = (rest - middle.astype(F32)).astype(BF16)
        tb[:, 0:context_width] += (
            t_mm(onehot, top) + t_mm(onehot, middle) + t_mm(onehot, lowest)
        )

    def finish_vectors(slot_at, width_three):
        for index in range(3):
            vb[slot_at, index : index + 1, :] = jnp.sum(acc[index], 0, keepdims=True)
            vb[slot_at, 3 + index : 4 + index, :] = jnp.sum(acc[3 + index], 0, keepdims=True)
        if width_three:
            three = [jnp.sum(acc[6 + index, :, 0:width], 0, keepdims=True) for index in range(3)]
            vb[slot_at, 6:7, 0:width] = three[0]
            vb[slot_at, 6:7, width : 2 * width] = three[1]
            vb[slot_at, 7:8, 0:width] = three[2]
        else:
            vb[slot_at, 6:7, :] = jnp.sum(acc[6], 0, keepdims=True)
        return remote(vb.at[slot_at], vbo.at[slot_at], to_core)

    own_tasks = pl.ds(pl.multiple_of(tasks // 2 * core, 8), tasks // 2)
    half_cols = pl.ds(pl.multiple_of(half * core, 128), half)

    def join_vectors(slot_at, copy):
        copy.wait_recv()
        sent(copy)
        vp[slot_at, 0:3, :] = vb[slot_at, 0:3, low] + vbo[slot_at, 0:3, high]
        vp[slot_at, 3:8, :] = vb[slot_at, 3:8, half_cols] + vbo[slot_at, 3:8, half_cols]
        return remote(vp.at[slot_at], vpx.at[slot_at], to_x)

    def plane_vectors(slot_at, copy):
        copy.wait_recv()
        sent(copy)
        vp[slot_at] = vp[slot_at] + vpx[slot_at]
        return remote(vp.at[slot_at], vpy.at[slot_at], to_y)

    def total_vectors(slot_at, copy):
        copy.wait_recv()
        sent(copy)
        vp[slot_at] = vp[slot_at] + vpy[slot_at]

    def scatter_start(source, target, x_first, lead):
        if lead is None:
            piece = source.at[:, 1 - at_x] if x_first else source.at[1 - at_y]
        else:
            piece = source.at[lead, :, 1 - at_x] if x_first else source.at[lead, 1 - at_y]
        return remote(piece, target, to_x if x_first else to_y)

    def scatter_middle(copy, source, received, target, x_first, lead):
        copy.wait_recv()
        if lead is None:
            for other in range(2):
                kept = source[other, at_x] if x_first else source[at_y, other]
                received[other] = (received[other].astype(F32) + kept.astype(F32)).astype(BF16)
            piece = received.at[1 - at_y] if x_first else received.at[1 - at_x]
        else:
            for index in range(lead.size):
                for other in range(2):
                    kept = (
                        source[lead.start + index, other, at_x]
                        if x_first
                        else source[lead.start + index, at_y, other]
                    )
                    received[index, other] = (
                        received[index, other].astype(F32) + kept.astype(F32)
                    ).astype(BF16)
            piece = received.at[:, 1 - at_y] if x_first else received.at[:, 1 - at_x]
        return remote(piece, target, to_y if x_first else to_x)

    def scatter_end(copy, received, target, x_first):
        copy.wait_recv()
        mine = at_y if x_first else at_x
        return received[mine].astype(F32) + target[...].astype(F32)

    def scatter_end_lead(copy, received, target, x_first, count):
        copy.wait_recv()
        mine = at_y if x_first else at_x
        for index in range(count):
            target[index] = (
                received[index, mine].astype(F32) + target[index].astype(F32)
            ).astype(BF16)

    first_half, second_half = pl.ds(0, 2), pl.ds(2, 2)

    for copy in [lat_copy, tgt_copy] + facts_in + vec_copies + line_in:
        sent(copy)
    acc[...] = jnp.zeros_like(acc)
    tb[...] = jnp.zeros_like(tb)
    done(main_three)
    done(extra_three)
    layers_forward(
        1, nxt, qv1.at[0], qv2.at[0], x1, x2, inv, h1, h2, 0, rows_all,
        ready_of(main_ready, main_ready_other), slope,
    )
    factor_copies = [remote(h1.at[:, high], h1o, to_core)]
    main_loss = value_rows(0, 0, rows_all)
    for first in range(0, rows_all, 2 * slot):
        back_rows(upstream, x2, inv.at[1], qv2.at[0], gp2, 3, first, 2 * slot, True, slope)
        block = pl.ds(first, 2 * slot)
        factor_copies.append(remote(gp2.at[block], gp2o.at[block], to_core))
    back_two_to_one(1, gp2, 0, rows_all, (0,))
    for copy in factor_copies:
        copy.wait_recv()
    wide = half // 256 * 128 + 128
    main_two = [[], []]
    for part in (slice(0, wide), slice(wide, half)):
        for index in range(2):
            cols = slice(index * half, (index + 1) * half)
            whole = t_mm(gp2[:, cols], h1[:, part]) + t_mm(gp2o[:, cols], h1o[:, part])
            p2[2 * index : 2 * index + 2, :, :, :, part] = whole.astype(BF16).reshape(
                (2, 2, 2, own_two, part.stop - part.start)
            )
            lead = pl.ds(2 * index, 2)
            if index == 0:
                piece, device = p2.at[lead, :, 1 - at_x, :, part], to_x
            else:
                piece, device = p2.at[lead, 1 - at_y, :, :, part], to_y
            main_two[index].append(remote(piece, r2.at[lead, :, :, part], device))
    back_two_to_one(1, gp2, 0, rows_all, (1,))
    back_rows(upstream, x1, inv.at[0], qv1.at[0], gp1, 0, 0, rows_all, True)
    one_copy = remote(gp1.at[:, high], gp1o, to_core)
    dx = mm_t(gp1[...], w1[1])
    own_g[...] = own_g[...] + dx[0:slot]
    dxm[:, 0:width] = dx.astype(BF16)
    lane_all = lax.broadcasted_iota(jnp.int32, (rows_all, 128), 1)
    loss_high = main_loss.astype(BF16).astype(F32)
    loss_rest = main_loss - loss_high
    loss_middle = loss_rest.astype(BF16).astype(F32)
    loss_low = loss_rest - loss_middle
    dxm[:, width : width + 128] = jnp.where(
        lane_all == 0, loss_high, jnp.where(lane_all == 1, loss_middle, loss_low)
    ).astype(BF16)
    dx_copies = [
        remote(dxm.at[pl.ds(slot * k, slot)], dxr.at[k - 1], to_z[k]) for k in range(1, LINE)
    ]
    hand, keep = [], []

    def start_two(source, received):
        return [
            scatter_start(
                source, received.at[2 * index : 2 * index + 2], index == 0, pl.ds(2 * index, 2)
            )
            for index in range(2)
        ]

    def middle_two(copies, source, received, target):
        return [
            scatter_middle(
                copies[index], source, received.at[2 * index : 2 * index + 2],
                target.at[2 * index : 2 * index + 2], index == 0, pl.ds(2 * index, 2),
            )
            for index in range(2)
        ]

    def end_two(copies, received, target):
        for index in range(2):
            scatter_end_lead(
                copies[index], received.at[2 * index : 2 * index + 2],
                target.at[2 * index : 2 * index + 2], index == 0, 2,
            )

    def hand_on(source, target):
        keep.append(local(source.at[at_z], target.at[at_z]))
        for k in range(1, LINE):
            hand.append(remote(source.at[z_of[k]], target.at[at_z], to_z[k]))

    def hand_all(source, target):
        mine = target(at_z)
        keep.append(local(source, mine))
        near = remote(source, mine, to_z[1])
        far = remote(source, mine, to_z[2])
        hand.append(near)
        return far, target

    def hand_further(started):
        far, target = started
        far.wait_recv()
        theirs = target(z_of[2])
        hand.append(remote(theirs, theirs, to_z[1]))

    left, right = slice(0, wide), slice(wide, half)

    def context_start(source, received):
        return (
            remote(source.at[:, left], received.at[:, left], to_x),
            remote(source.at[:, right], received.at[:, right], to_y),
        )

    def context_add(source, received, copies):
        for copy in copies:
            copy.wait_recv()
            sent(copy)
        source[...] = (source[...].astype(F32) + received[...].astype(F32)).astype(BF16)

    def context_middle(source, received, target, copies):
        context_add(source, received, copies)
        return (
            remote(source.at[:, left], target.at[:, left], to_y),
            remote(source.at[:, right], target.at[:, right], to_x),
        )

    x_copy.wait_recv()
    one_copy.wait_recv()
    whole = t_mm(xbuf[:, width : width + 128], gp1[:, low]) + t_mm(
        xother[:, width : width + 128], gp1o[...]
    )
    pc[...] = whole[0 : pc.shape[0]].astype(BF16)
    main_context = context_start(pc, pcx)
    next_copy.wait_recv()
    whole = t_mm(nxt[...], gp1[:, low]) + t_mm(nxto[...], gp1o[...])
    p1[...] = whole.astype(BF16).reshape(p1.shape)
    part = t_mm(h2[...], gl[...])
    p3[...] = part.astype(BF16).reshape(p3.shape)
    three_copy = remote(p3.at[pl.ds(2 * (1 - core), 2)], p3o, to_core)
    main_vec = finish_vectors(0, False)
    acc[...] = jnp.zeros_like(acc)
    table_sum(1, gp1, 0, rows_all)
    for copy in main_ready_other:
        sent(copy)
    pl.semaphore_signal(free_b, inc=1, device_id=to_core, device_id_type=mesh_id)
    dyn_again = load_weights(1, dyn_w1, dyn_wc, dyn_w2)
    for copy in factor_copies + [one_copy]:
        sent(copy)
    pl.semaphore_signal(free_f, inc=1, device_id=to_core, device_id_type=mesh_id)
    pl.semaphore_wait(free_b, 1)
    dyn_again_other = send_weights(1, dyn_w1, dyn_wc, dyn_w2)

    for copy in [three_ready_other, x_copy, next_copy]:
        sent(copy)
    layers_forward(
        0, nxt, qv1.at[1], qv2.at[1], x1, x2, inv, h1, h2, 0, slot,
        ready_of(extra_ready, extra_ready_other), slope,
    )
    extra_loss = value_rows(1, 0, slot)
    back_rows(upstream, x2, inv.at[1], qv2.at[1], gp2, 3, 0, slot, True, slope)
    back_two_to_one(0, gp2, 0, slot)
    back_rows(upstream, x1, inv.at[0], qv1.at[1], gp1, 0, 0, slot, True)
    own_total = own_g[...] + mm_t(gp1[0:slot, :], w1[0])
    value = main_loss[0:slot] + extra_loss
    for index, copy in enumerate(dx_copies):
        copy.wait_recv()
        message = dxr[index].astype(F32)
        own_total = own_total + message[:, 0:width]
        value = value + (
            message[:, width : width + 1]
            + message[:, width + 1 : width + 2]
            + message[:, width + 2 : width + 3]
        )
    all_g[0:slot, :] = own_total.astype(BF16)
    grad_copies = [
        remote(all_g.at[pl.ds(0, slot)], all_g.at[pl.ds(slot * k, slot)], to_z[k])
        for k in range(1, LINE)
    ]
    lane_own = lax.broadcasted_iota(jnp.int32, (slot, 128), 1)
    lossbuf[...] = jnp.where(lane_own == 0, consistency, value)
    loss_copy = remote(lossbuf, out_losses.at[own_rows], to_core)
    keep += [local(lossbuf, out_losses.at[own_rows])]
    table_sum(0, gp1, 0, slot)
    rest = rows_all - slot
    stage = {}

    def between(step):
        if step == 0:
            return
        stage["context"] = context_middle(pc, pcx, pcy, main_context)
        for copies in main_two:
            copies[0].wait_recv()
        stage["two"] = middle_two([copies[1] for copies in main_two], p2, r2, t2)
        stage["one"] = start_two(p1, r1)
        three_copy.wait_recv()
        sent(three_copy)
        stage["three"] = []
        for index in range(2):
            p3h[index] = (
                p3[2 * core + index].astype(F32) + p3o[index].astype(F32)
            ).astype(BF16)
            stage["three"].append(scatter_start(p3h.at[index], r3.at[index], index == 0, None))
        stage["vec"] = join_vectors(0, main_vec)

    layers_forward(
        0, nxt, qv1.at[1], qv2.at[1], x1, x2, inv, h1, h2, slot, rest, between, slope
    )
    first_two = main_two[0] + main_two[1]
    main_context, main_two, main_vec = stage["context"], stage["two"], stage["vec"]
    main_three_sum, main_one = stage["three"], stage["one"]
    value_rows(1, slot, rest)
    context_add(pc, pcy, main_context)
    context_hand = hand_all(pc, lambda at: out_qwc.at[at, pl.ds(0, pc.shape[0])])
    back_rows(upstream, x2, inv.at[1], qv2.at[1], gp2, 3, slot, rest, True, slope)
    pl.semaphore_wait(free_f, 1)
    factor_copies = [remote(gp2, gp2o, to_core), remote(h1.at[:, high], h1o, to_core)]
    back_two_to_one(0, gp2, slot, rest)
    back_rows(upstream, x1, inv.at[0], qv1.at[1], gp1, 0, slot, rest, True)
    one_copy = remote(gp1.at[:, high], gp1o, to_core)
    extra_vec = finish_vectors(1, False)
    acc[...] = jnp.zeros_like(acc)

    for copy in extra_ready_other + dx_copies + grad_copies + [loss_copy]:
        sent(copy)
    end_two(main_two, r2, t2)
    hand_on(t2, out_qw2)

    def by_place(body):
        for index in range(LINE):
            @pl.when(at_z == index)
            def _(index=index):
                body(index)

    quarter = hidden // LINE
    quarter_w = width // LINE
    quarter_c = 128 // LINE

    def quarter_two(index, hid, target):
        cols = slice(index * quarter, (index + 1) * quarter)
        whole = t_mm(gp2[:, cols], hid[:, low]) + t_mm(gp2o[:, cols], h1o[...])
        target[...] = whole.astype(BF16).reshape(target.shape)

    def quarter_one(index, mine, others, target, at):
        cols = slice(index * quarter_w, (index + 1) * quarter_w)
        whole = t_mm(mine[:, cols], gp1[:, low]) + t_mm(others[:, cols], gp1o[...])
        target[...] = whole.astype(BF16).reshape(target.shape)
        cols = slice(width + index * quarter_c, width + (index + 1) * quarter_c)
        whole = t_mm(xbuf[:, cols], gp1[:, low]) + t_mm(xother[:, cols], gp1o[...])
        pq[at] = whole.astype(BF16)

    for copy in factor_copies + [one_copy]:
        copy.wait_recv()

    def extra_parts(index):
        part = t_mm(h2[:, index * quarter : (index + 1) * quarter], gl[...])
        e3[...] = part.astype(BF16).reshape(e3.shape)
        quarter_two(index, h1, e2)
        quarter_one(index, nxt, nxto, e1, 0)

    by_place(extra_parts)
    extra_three_sum = remote(e3, e3o, to_core)
    extra_two = scatter_start(e2, er2, True, None)
    extra_one = scatter_start(e1, er1, False, None)
    extra_context = context_start(pq.at[0], pqx.at[0])
    for copy in factor_copies + [one_copy]:
        sent(copy)
    pl.semaphore_signal(free_f, inc=1, device_id=to_core, device_id_type=mesh_id)
    for copy in grad_copies:
        copy.wait_recv()

    for copy in first_two:
        sent(copy)
    def simplex_back(rows):
        share = simplex[rows, :]
        weighted = all_g[rows, :].astype(F32) * share
        up = weighted - share * gather_sum(weighted, ones)
        upstream[rows, 0:width] = up

    over_rows(0, rows_all, simplex_back, 2 * CH)
    back_rows(
        upstream.at[:, 0:width], x3, dyn_inv.at[2], dv3, dyn_gp3, 6, 0, rows_all, False
    )

    def dyn_third(index):
        left = dyn_h2[:, index * quarter : (index + 1) * quarter]
        d3s[...] = t_mm(left, dyn_gp3[:, other_cols]).astype(BF16).reshape(d3s.shape)
        d3[...] = t_mm(left, dyn_gp3[:, own_cols]).astype(BF16).reshape(d3.shape)

    by_place(dyn_third)
    d3_copy = remote(d3s, d3o, to_core)

    def three_tile(cols):
        upstream[:, cols] = mm_t(dyn_gp3[...], dw3[cols, :])

    two_tiles(three_tile)
    first_one = main_one
    main_one = middle_two(main_one, p1, r1, t1)
    hand_further(context_hand)
    back_rows(upstream, dyn_x2, dyn_inv.at[1], dyn_vec2, gp2, 3, 0, rows_all, True)
    pl.semaphore_wait(free_f, 1)
    factor_copies = [remote(gp2, gp2o, to_core), remote(dyn_h1.at[:, high], h1o, to_core)]
    d3_copy.wait_recv()
    sent(d3_copy)
    d3[...] = (d3[...].astype(F32) + d3o[...].astype(F32)).astype(BF16)
    dyn_three_sum = scatter_start(d3, er3b, False, None)
    extra_three_sum.wait_recv()
    sent(extra_three_sum)
    e3[...] = (e3[...].astype(F32) + e3o[...].astype(F32)).astype(BF16)
    extra_three_sum = scatter_start(e3, er3, False, None)
    extra_vec = join_vectors(1, extra_vec)
    done(dyn_again[2])
    dyn_again_other[2].wait_recv()
    back_two_to_one(1, gp2, 0, rows_all)
    for copy in factor_copies:
        copy.wait_recv()
    for copy in first_one:
        sent(copy)
    d2, d1 = p2.at[0], p1.at[0]
    by_place(lambda index: quarter_two(index, dyn_h1, d2))
    back_rows(upstream, dyn_x1, dyn_inv.at[0], dv1, gp1, 0, 0, rows_all, True)
    one_copy = remote(gp1.at[:, high], gp1o, to_core)
    dyn_vec = finish_vectors(2, True)
    for index in (0, 1):
        done(dyn_again[index])
        dyn_again_other[index].wait_recv()
    table_sum(1, gp1, 0, slot)
    table_copy = remote(tb, tbo, to_core)
    one_copy.wait_recv()
    by_place(lambda index: quarter_one(index, xbuf, xother, d1, 1))
    dyn_one_sum = scatter_start(d1, er1b, True, None)
    dyn_context = context_start(pq.at[1], pqx.at[1])
    lat_g = tgt
    lat_g[...] = mm_t(gp1[0:slot, :], w1[1])
    latent_copy = remote(lat_g.at[:, other_cols], out_latent.at[own_rows], to_core)
    keep += [local(lat_g.at[:, own_cols], out_latent.at[own_rows])]
    dyn_vec = join_vectors(2, dyn_vec)
    table_copy.wait_recv()
    sent(table_copy)
    tq[...] = tb[own_tasks, :] + tbo[own_tasks, :]
    table_copy = remote(tq, tqr.at[0], to_x)

    end_two(main_one, r1, t1)
    hand_on(t1, out_qw1)
    main_three_sum = [
        scatter_middle(main_three_sum[index], p3h.at[index], r3.at[index], t3.at[index],
                       index == 0, None)
        for index in range(2)
    ]
    main_vec = plane_vectors(0, main_vec)
    extra_context = context_middle(pq.at[0], pqx.at[0], pqy.at[0], extra_context)
    extra_one2 = scatter_middle(extra_one, e1, er1, et1, False, None)
    extra_two2 = scatter_middle(extra_two, e2, er2, et2, True, None)
    extra_vec = plane_vectors(1, extra_vec)
    dyn_context = context_middle(pq.at[1], pqx.at[1], pqy.at[1], dyn_context)
    table_copy.wait_recv()
    sent(table_copy)
    tq[...] = tq[...] + tqr[0]
    table_copy = remote(tq, tqr.at[1], to_y)
    dyn_vec = plane_vectors(2, dyn_vec)
    dyn_two_sum = (
        remote(d2.at[:, 1 - at_x, :, left], er2b.at[:, :, left], to_x),
        remote(d2.at[1 - at_y, :, :, right], er2b.at[:, :, right], to_y),
    )
    dyn_three2 = scatter_middle(dyn_three_sum, d3, er3b, et3b, False, None)
    extra_three2 = scatter_middle(extra_three_sum, e3, er3, et3, False, None)
    dyn_one2 = scatter_middle(dyn_one_sum, d1, er1b, et1b, True, None)
    def quarter_rows(at):
        return pl.ds(pl.multiple_of(quarter_c * at, quarter_c), quarter_c)

    context_add(pq.at[0], pqy.at[0], extra_context)
    extra_hand = hand_all(pq.at[0], lambda at: out_qwc.at[last, quarter_rows(at)])
    total_vectors(0, main_vec)
    vec_hand = hand_all(vp.at[0], lambda at: out_qvec.at[at, core])
    vec_near = hand.pop()
    vec_keep = [keep.pop()]
    for index in range(2):
        t3[index] = scatter_end(
            main_three_sum[index], r3.at[index], t3.at[index], index == 0
        ).astype(BF16)
    mine = at_z // 2 == core
    three_out = out_qw3.at[at_z]
    three_copies = []
    for k in range(1, LINE):
        theirs = z_of[k] // 2 == core
        copy = describe(t3.at[lax.rem(z_of[k], 2)], three_out, to_z[k])
        three_copies.append((theirs, copy))

        @pl.when(theirs)
        def _(copy=copy):
            copy.start()

    three_keep = describe_local(t3.at[lax.rem(at_z, 2)], three_out)

    @pl.when(mine)
    def _():
        three_keep.start()

    context_add(pq.at[1], pqy.at[1], dyn_context)
    dyn_rows = out_dwc.at[quarter_rows(at_z)]
    keep += [local(pq.at[1], dyn_rows)]
    hand += [remote(pq.at[1], dyn_rows, to_z[k]) for k in range(1, LINE)]
    table_copy.wait_recv()
    sent(table_copy)
    tq[...] = tq[...] + tqr[1]
    table_copies = [remote(tq, tqr.at[1 + k], to_z[k]) for k in range(1, LINE)]
    for copy in dyn_two_sum:
        copy.wait_recv()
    for other in range(2):
        for cols, kept in ((left, d2[other, at_x, :, left]), (right, d2[at_y, other, :, right])):
            er2b[other, :, cols] = (
                er2b[other, :, cols].astype(F32) + kept.astype(F32)
            ).astype(BF16)
    dyn_two2 = (
        remote(er2b.at[1 - at_y, :, left], et2b.at[:, left], to_y),
        remote(er2b.at[1 - at_x, :, right], et2b.at[:, right], to_x),
    )
    hand_further(extra_hand)
    hand_further(vec_hand)
    vec_further = hand.pop()
    total_vectors(1, extra_vec)
    vec_keep += [local(vp.at[1], out_qvec.at[last, core])]
    total_vectors(2, dyn_vec)
    keep += [local(vp.at[2], out_dvec.at[core])]
    hand += [remote(vp.at[2], out_dvec.at[core], to_core)]
    et2[...] = scatter_end(extra_two2, er2, et2, True).astype(BF16)
    keep += [local(et2, out_qw2.at[last])]
    et1[...] = scatter_end(extra_one2, er1, et1, False).astype(BF16)
    keep += [local(et1, out_qw1.at[last])]
    o2 = upstream.at[0:own_two, 0:half]
    o1 = upstream.at[own_two : own_two + own_one, 0:half]
    oc = upstream.at[0:own_two, half : half + half_w]
    oc[...] = scatter_end(dyn_three2, er3b, et3b, False)
    keep += [local(oc, out_dw3)]
    et3[...] = scatter_end(extra_three2, er3, et3, False).astype(BF16)
    keep += [local(et3, out_qw3.at[last])]
    o1[...] = scatter_end(dyn_one2, er1b, et1b, True)
    keep += [local(o1, out_dw1)]
    for copy in dyn_two2:
        copy.wait_recv()
    for cols, at in ((left, at_y), (right, at_x)):
        o2[:, cols] = er2b[at, :, cols].astype(F32) + et2b[:, cols].astype(F32)
    keep += [local(o2, out_dw2)]
    vec_near.wait_recv()
    vec_further.wait_recv()
    for copy in vec_keep:
        copy.wait()
    vec_cores = remote(out_qvec.at[:, core], out_qvec.at[:, core], to_core)
    for theirs, copy in three_copies:
        @pl.when(theirs)
        def _(copy=copy):
            copy.wait_send()

    three_further = describe(
        out_qw3.at[pl.ds(0, LINE)], out_qw3.at[pl.ds(0, LINE)], to_core
    )

    @pl.when(mine)
    def _():
        three_keep.wait()
        for _, copy in three_copies:
            copy.wait_recv()
        three_further.start()

    for copy in table_copies:
        copy.wait_recv()
        sent(copy)
    tq[...] = tq[...] + tqr[2] + tqr[3] + tqr[4]
    keep += [local(tq, out_table.at[own_tasks])]
    hand += [remote(tq, out_table.at[own_tasks], to_core)]
    for copy in hand + [loss_copy, latent_copy]:
        copy.wait_recv()
    for copy in keep:
        copy.wait()
    @pl.when(mine)
    def _():
        three_further.wait_send()

    @pl.when(jnp.logical_not(mine))
    def _():
        three_further.wait_recv()

    vec_cores.wait_recv()
    for copy in list(pending):
        sent(copy)


def line_shards(
    latent,
    action,
    task_ids,
    action_mask,
    task_table,
    target_latent,
    bin_lower,
    bin_frac,
    dyn_w1,
    dyn_wc,
    dyn_vec1,
    dyn_w2,
    dyn_vec2,
    dyn_w3,
    dyn_vec3,
    q_w1,
    q_wc,
    q_vec1,
    q_w2,
    q_vec2,
    q_w3,
    q_b3,
):
    local_rows, half_w = latent.shape
    slot = local_rows // 2
    rows = slot * LINE
    width = 2 * half_w
    half = dyn_w1.shape[1]
    hidden = 2 * half
    heads, bins = q_b3.shape
    tasks, acts = action_mask.shape
    context_width = dyn_wc.shape[0]
    pad_context = -(-context_width // 16) * 16
    own_two = hidden // BLOCK
    own_one = width // BLOCK
    scale = 1.0 / math.sqrt(local_rows * lax.axis_size("dp"))
    sizes = (slot, width, hidden, bins, tasks, acts, context_width, heads)

    def shape(*dims, kind=F32):
        return jax.ShapeDtypeStruct(dims, kind)

    out_shape = (
        shape(local_rows, 128),
        shape(local_rows, half_w),
        shape(tasks, 128),
        shape(own_one, half),
        shape(128, half, kind=BF16),
        shape(2, 8, half),
        shape(own_two, half),
        shape(own_two, half_w),
        shape(heads, own_one, half, kind=BF16),
        shape(heads, 128, half, kind=BF16),
        shape(heads, 2, 8, half),
        shape(heads, own_two, half, kind=BF16),
        shape(heads, own_two, bins, kind=BF16),
    )
    v = pltpu.VMEM
    scratch = [
        v((acts, local_rows), BF16),
        v((1, local_rows), jnp.int32),
        v((acts, tasks), jnp.int32),
        v((tasks, context_width - acts), BF16),
        v((1, local_rows), jnp.int32),
        v((1, local_rows), F32),
        v((3, hidden), F32),
        v((heads, bins), F32),
        v((2, width, hidden), BF16),
        v((2, context_width, hidden), BF16),
        v((2, hidden, hidden), BF16),
        v((hidden, width), BF16),
        v((2, bins, hidden), BF16),
        v((3, hidden), F32),
        v((3, width), F32),
        v((2, 3, hidden), F32),
        v((2, 3, hidden), F32),
        v((2, 1, bins), F32),
        v((rows, width + 128), BF16),
        v((rows, width + 128), BF16),
        v((slot, width), F32),
        v((rows, width), BF16),
        v((rows, width), BF16),
        v((rows, hidden), BF16),
        v((rows, hidden), BF16),
        v((rows, hidden), BF16),
        v((rows, hidden), BF16),
        v((rows, width), F32),
        v((rows, width), F32),
        v((3, rows, 1), F32),
        v((rows, hidden), F32),
        v((rows, hidden), F32),
        v((2, rows, 1), F32),
        v((rows, hidden), BF16),
        v((rows, hidden), BF16),
        v((rows, hidden), BF16),
        v((rows, hidden), BF16),
        v((rows, half), BF16),
        v((rows, hidden), BF16),
        v((rows, half), BF16),
        v((rows, hidden), F32),
        v((rows, bins), BF16),
        v((rows, width), BF16),
        v((9, 8, hidden), F32),
        v((rows, hidden), F32),
        v((rows, width + 128), BF16),
        v((LINE - 1, slot, width + 128), BF16),
        v((slot, width), F32),
        v((rows, width), BF16),
        v((slot, 128), F32),
        v((LINE, 2, 2, own_two, half), BF16),
        v((LINE, 2, own_two, half), BF16),
        v((LINE, own_two, half), BF16),
        v((LINE, 2, 2, own_one, half), BF16),
        v((LINE, 2, own_one, half), BF16),
        v((LINE, own_one, half), BF16),
        v((LINE, 2, 2, own_two, bins), BF16),
        v((2, 2, 2, own_two, bins), BF16),
        v((2, 2, own_two, bins), BF16),
        v((2, own_two, bins), BF16),
        v((2, 2, 2, own_two, bins), BF16),
        v((2, 2, own_two, half), BF16),
        v((2, own_two, half), BF16),
        v((own_two, half), BF16),
        v((2, 2, own_one, half), BF16),
        v((2, own_one, half), BF16),
        v((own_one, half), BF16),
        v((2, 2, own_two, bins), BF16),
        v((2, own_two, bins), BF16),
        v((own_two, bins), BF16),
        v((2, 2, own_two, bins), BF16),
        v((2, own_two, half), BF16),
        v((own_two, half), BF16),
        v((2, own_one, half), BF16),
        v((own_one, half), BF16),
        v((2, 2, own_two, half_w), BF16),
        v((2, 2, own_two, half_w), BF16),
        v((2, 2, own_two, half_w), BF16),
        v((2, own_two, half_w), BF16),
        v((own_two, half_w), BF16),
        v((pad_context, half), BF16),
        v((pad_context, half), BF16),
        v((pad_context, half), BF16),
        v((2, 128 // LINE, half), BF16),
        v((2, 128 // LINE, half), BF16),
        v((2, 128 // LINE, half), BF16),
        v((local_rows, 16), F32),
        v((LINE, 16, local_rows), F32),
        v((3, 8, hidden), F32),
        v((3, 8, hidden), F32),
        v((3, 8, half), F32),
        v((3, 8, half), F32),
        v((3, 8, half), F32),
        v((tasks, 128), F32),
        v((tasks, 128), F32),
        v((tasks // 2, 128), F32),
        v((5, tasks // 2, 128), F32),
        pltpu.SemaphoreType.DMA((SENDS,)),
        pltpu.SemaphoreType.DMA((REMOTE_COPIES,)),
        pltpu.SemaphoreType.DMA((LOCAL_COPIES,)),
        pltpu.SemaphoreType.REGULAR,
        pltpu.SemaphoreType.REGULAR,
        pltpu.SemaphoreType.REGULAR,
    ]
    outside = pl.BlockSpec(memory_space=pl.ANY)
    raw = pl.pallas_call(
        functools.partial(line_kernel, sizes, scale),
        out_shape=out_shape,
        in_specs=[outside] * 22,
        out_specs=[outside] * len(out_shape),
        scratch_shapes=scratch,
        compiler_params=pltpu.CompilerParams(
            collective_id=0, has_side_effects=True, vmem_limit_bytes=VMEM_BYTES
        ),
        cost_estimate=pl.CostEstimate(
            flops=2 * 10**10, bytes_accessed=6 * 10**7, transcendentals=10**7
        ),
        name="line_update",
    )(
        latent, action.T, task_ids[None], action_mask.T, task_table, target_latent,
        bin_lower[None], bin_frac[None], dyn_vec1, dyn_vec2, dyn_vec3, q_vec1, q_vec2, q_b3,
        dyn_w1, dyn_wc, dyn_w2, dyn_w3, q_w1, q_wc, q_w2, jnp.swapaxes(q_w3, 1, 2),
    )
    return finish(raw, (slot, width, hidden, bins, tasks, acts, context_width, heads))


def finish_kernel(sizes, *refs):
    (slot, width, hidden, bins, tasks, acts, context_width, heads) = sizes
    half, half_w = hidden // 2, width // 2
    raw, outs, held, made = refs[0:13], refs[13:30], refs[30:43], refs[43:56]
    in_sem, out_sem = refs[56:]
    (
        raw_losses, raw_latent, raw_table, raw_dw1, raw_dwc, raw_dvec, raw_dw2, raw_dw3,
        raw_qw1, raw_qwc, raw_qvec, raw_qw2, raw_qw3,
    ) = held
    (losses, table, dwc, dvec1, dvec2, dvec3, qw1, qwc, qvec1, qw2, qvec2, qw3, qb3) = made
    (
        out_losses, out_latent, out_table, out_dw1, out_dwc, out_dvec1, out_dw2, out_dvec2,
        out_dw3, out_dvec3, out_qw1, out_qwc, out_qvec1, out_qw2, out_qvec2, out_qw3, out_qb3,
    ) = outs
    core = lax.axis_index("tensor")
    loads = {}
    for index in (11, 9, 6, 8, 1, 7, 3, 4, 10, 12, 5, 0, 2):
        loads[index] = pltpu.make_async_copy(raw[index], held[index], in_sem.at[index])
        loads[index].start()
    stored = []

    def store(source, target):
        copy = pltpu.make_async_copy(source, target, out_sem.at[len(stored)])
        copy.start()
        stored.append(copy)

    loads[11].wait()
    for head in range(heads):
        qw2[head] = raw_qw2[head].astype(F32)
    store(qw2, out_qw2)
    loads[9].wait()
    for head in range(heads):
        qwc[head] = raw_qwc[head].astype(F32)[0:context_width]
    store(qwc, out_qwc)
    for index, source, target in (
        (6, raw_dw2, out_dw2), (1, raw_latent, out_latent), (7, raw_dw3, out_dw3),
        (3, raw_dw1, out_dw1),
    ):
        loads[index].wait()
        store(source, target)
    loads[8].wait()
    qw1[...] = raw_qw1[...].astype(F32)
    store(qw1, out_qw1)
    loads[4].wait()
    dwc[...] = raw_dwc[...].astype(F32)[0:context_width]
    store(dwc, out_dwc)
    loads[10].wait()
    loads[12].wait()
    for head in range(heads):
        qvec1[head] = raw_qvec[head, core, 0:3]
        for index in range(2):
            qvec2[head, :, index * half : (index + 1) * half] = raw_qvec[head, index, 3:6]
        qw3[head] = raw_qw3[head].astype(F32).T
        qb3[head : head + 1, :] = raw_qvec[head, 0, 6:7, 0:bins]
    store(qvec1, out_qvec1)
    store(qvec2, out_qvec2)
    store(qw3, out_qw3)
    store(qb3, out_qb3)
    loads[5].wait()
    dvec1[...] = raw_dvec[core, 0:3]
    line = jnp.concatenate([raw_dvec[0, 6:7], raw_dvec[1, 6:7]], 1)
    rows = jnp.concatenate(
        [line[:, 0:width], line[:, width : 2 * width], raw_dvec[0, 7:8, 0:width]], 0
    )
    dvec3[...] = jnp.where(core == 0, rows[:, 0:half_w], rows[:, half_w:])
    for index in range(2):
        dvec2[:, index * half : (index + 1) * half] = raw_dvec[index, 3:6]
    store(dvec1, out_dvec1)
    store(dvec2, out_dvec2)
    store(dvec3, out_dvec3)
    loads[0].wait()
    loads[2].wait()
    losses[...] = raw_losses[...].T[0:2]
    table[...] = raw_table[:, acts:context_width]
    store(losses, out_losses)
    store(table, out_table)
    for copy in stored:
        copy.wait()


def finish(raw, sizes):
    (slot, width, hidden, bins, tasks, acts, context_width, heads) = sizes
    half, half_w = hidden // 2, width // 2
    own_two, own_one = hidden // BLOCK, width // BLOCK
    dims = [
        (2, 2 * slot),
        (2 * slot, half_w),
        (tasks, context_width - acts),
        (own_one, half),
        (context_width, half),
        (3, half),
        (own_two, half),
        (3, hidden),
        (own_two, half_w),
        (3, half_w),
        (heads, own_one, half),
        (heads, context_width, half),
        (heads, 3, half),
        (heads, own_two, half),
        (heads, 3, hidden),
        (heads, bins, own_two),
        (heads, bins),
    ]
    outside = pl.BlockSpec(memory_space=pl.ANY)
    outs = pl.pallas_call(
        functools.partial(finish_kernel, sizes),
        in_specs=[outside] * len(raw),
        out_specs=[outside] * len(dims),
        out_shape=[jax.ShapeDtypeStruct(item, F32) for item in dims],
        scratch_shapes=[pltpu.VMEM(item.shape, item.dtype) for item in raw]
        + [pltpu.VMEM(item, F32) for index, item in enumerate(dims) if index not in (1, 3, 6, 8)]
        + [pltpu.SemaphoreType.DMA((len(raw),)), pltpu.SemaphoreType.DMA((len(dims),))],
        compiler_params=pltpu.CompilerParams(vmem_limit_bytes=VMEM_BYTES),
        name="finish",
    )(*raw)
    outs = list(outs)
    outs[0] = outs[0].T
    outs[6] = outs[6].T
    outs[13] = jnp.swapaxes(outs[13], 1, 2)
    outs[15] = jnp.swapaxes(outs[15], 1, 2)
    return tuple(outs)


def shards(*arrays):
    if lax.axis_size("dp") == BLOCK:
        return line_shards(*arrays)
    return general_shards(*arrays)


def solution(mesh):
    return jax.shard_map(
        shards,
        mesh=mesh,
        in_specs=(
            P("dp", "tensor"),
            P("dp", None),
            P("dp"),
            P(),
            P(),
            P("dp", "tensor"),
            P("dp"),
            P("dp"),
            P(None, "tensor"),
            P(None, "tensor"),
            P(None, "tensor"),
            P("tensor", None),
            P(),
            P(None, "tensor"),
            P(None, "tensor"),
            P(None, None, "tensor"),
            P(None, None, "tensor"),
            P(None, None, "tensor"),
            P(None, "tensor", None),
            P(),
            P(),
            P(),
        ),
        out_specs=(
            P("dp", None),
            P("dp", "tensor"),
            P(),
            P("dp", "tensor"),
            P(None, "tensor"),
            P(None, "tensor"),
            P("tensor", "dp"),
            P(),
            P("dp", "tensor"),
            P(None, "tensor"),
            P(None, "dp", "tensor"),
            P(None, None, "tensor"),
            P(None, None, "tensor"),
            P(None, "tensor", "dp"),
            P(),
            P(None, "dp", None),
            P(),
        ),
        check_vma=False,
    )
```

```python
import functools
import math

import jax
import jax.numpy as jnp
from jax import lax
from jax.experimental import pallas as pl
from jax.experimental.pallas import tpu as pltpu
from jax.sharding import PartitionSpec as P

GROUP = 8
LINE = 4
PLANE = 4
BLOCK = LINE * PLANE
EPSILON = 1e-05
HIGHEST = lax.Precision.HIGHEST
F32 = jnp.float32
BF16 = jnp.bfloat16
REMOTE_COPIES = 128
SENDS = 56
LOCAL_COPIES = 25
VMEM_BYTES = 63 << 20


def swap_core(values):
    return lax.ppermute(values, "tensor", [(0, 1), (1, 0)])


def swap_dp(values, bit):
    size = lax.axis_size("dp")
    return lax.ppermute(values, "dp", [(place, place ^ bit) for place in range(size)])


def pick(values, index, axis=0):
    return lax.dynamic_index_in_dim(values, index, axis, keepdims=False)


def own_then_other(values):
    return values, swap_core(values)


def mish_parts(values):
    grown = jnp.exp(jnp.minimum(values, 20.0))
    top = grown * (grown + 2.0)
    share = 1.0 / (top + 2.0)
    return grown, top * share, share


def mish(values):
    return values * mish_parts(values)[1]


def mish_slope(values):
    return mish_slope_of(values, *mish_parts(values))


def mish_slope_of(values, grown, ratio, share):
    return ratio + 4.0 * values * grown * (1.0 + grown) * share * share


def norm(before, gain, shift):
    centred = before - jnp.mean(before, -1, keepdims=True)
    inverse = lax.rsqrt(jnp.mean(centred * centred, -1, keepdims=True) + EPSILON)
    normed = centred * inverse
    return normed * gain + shift, normed, inverse


def norm_back(upstream, normed, inverse, gain):
    weighted = upstream * gain
    return inverse * (
        weighted
        - jnp.mean(weighted, -1, keepdims=True)
        - normed * jnp.mean(weighted * normed, -1, keepdims=True)
    )


def vector_sums(rounded, upstream, normed):
    return jnp.stack(
        [jnp.sum(rounded.astype(F32), 0), jnp.sum(upstream * normed, 0), jnp.sum(upstream, 0)]
    )


def mm(left, right):
    return jnp.dot(left, right, preferred_element_type=F32)


def mm_t(left, right):
    return lax.dot_general(left, right, (((1,), (1,)), ((), ())), preferred_element_type=F32)


def t_mm(left, right):
    return lax.dot_general(left, right, (((0,), (0,)), ((), ())), preferred_element_type=F32)


def block_forward(inputs, context, w_one, w_context, vec_one, w_two, vec_two):
    before = mm(inputs, w_one) + mm(context, w_context) + vec_one[0:1]
    out_one, normed_one, inverse_one = norm(before, vec_one[1:2], vec_one[2:3])
    hidden_one = mish(out_one).astype(BF16)
    second = mm(hidden_one, w_two) + vec_two[0:1]
    out_two, normed_two, inverse_two = norm(second, vec_two[1:2], vec_two[2:3])
    hidden_two = mish(out_two).astype(BF16)
    return hidden_one, hidden_two, (normed_one, inverse_one, normed_two, inverse_two)


def block_backward(grad_hidden, saved, vec_one, w_two, vec_two):
    normed_one, inverse_one, normed_two, inverse_two = saved
    upstream = mish_slope(normed_two * vec_two[1:2] + vec_two[2:3]) * grad_hidden
    grad_two = norm_back(upstream, normed_two, inverse_two, vec_two[1:2]).astype(BF16)
    sums_two = vector_sums(grad_two, upstream, normed_two)
    grad_one_hidden = mm_t(grad_two, w_two)
    upstream = mish_slope(normed_one * vec_one[1:2] + vec_one[2:3]) * grad_one_hidden
    grad_one = norm_back(upstream, normed_one, inverse_one, vec_one[1:2]).astype(BF16)
    sums_one = vector_sums(grad_one, upstream, normed_one)
    return grad_two, sums_two, grad_one, sums_one


def dynamics_forward(inputs, context, w_one, w_context, vec_one, w_two, vec_two, w_three, vec_three):
    hidden_one, hidden_two, saved = block_forward(
        inputs, context, w_one, w_context, vec_one, w_two, vec_two
    )
    before = mm(hidden_two, w_three) + vec_three[0:1]
    out, normed, inverse = norm(before, vec_three[1:2], vec_three[2:3])
    grouped = out.reshape(out.shape[0], -1, GROUP)
    simplex = jax.nn.softmax(grouped, axis=-1).reshape(out.shape)
    return hidden_one, hidden_two, saved, simplex, normed, inverse


def dynamics_backward(grad_next, simplex, normed, inverse, saved, w_three, vec_three, vec_one, w_two, vec_two):
    weighted = grad_next * simplex
    rows = weighted.shape[0]
    along = jnp.sum(weighted.reshape(rows, -1, GROUP), -1, keepdims=True)
    along = jnp.broadcast_to(along, (rows, along.shape[1], GROUP)).reshape(weighted.shape)
    upstream = weighted - simplex * along
    grad_three = norm_back(upstream, normed, inverse, vec_three[1:2]).astype(BF16)
    sums_three = vector_sums(grad_three, upstream, normed)
    grad_hidden = mm_t(grad_three, w_three)
    grad_two, sums_two, grad_one, sums_one = block_backward(
        grad_hidden, saved, vec_one, w_two, vec_two
    )
    return grad_three, sums_three, grad_two, sums_two, grad_one, sums_one


def value_head(hidden_two, w_three, bias, lower, fraction, scale, heads):
    logits = mm(hidden_two, w_three) + bias
    log_prob = jax.nn.log_softmax(logits, axis=-1)
    bins = jnp.arange(logits.shape[-1], dtype=jnp.int32)[None, :]
    target = jnp.where(bins == lower, 1.0 - fraction, 0.0) + jnp.where(
        bins == lower + 1, fraction, 0.0
    )
    loss = -jnp.sum(target * log_prob, -1) / heads
    grad_logits = (scale / heads * (jnp.exp(log_prob) - target)).astype(BF16)
    return loss, grad_logits


def spread(values, axis_len):
    blocks = lax.axis_size("dp") // BLOCK
    rows = values.shape[0] // (blocks * BLOCK)
    values = values.reshape((blocks, LINE, 2, 2, rows) + values.shape[1:])
    if blocks > 1:
        values = jnp.moveaxis(values, 0, 3)
    return values.reshape((LINE, 2, 2, blocks * rows) + values.shape[5:])


def across_blocks(values, axis):
    blocks = lax.axis_size("dp") // BLOCK
    if blocks == 1:
        return values
    groups = [[block * BLOCK + place for block in range(blocks)] for place in range(BLOCK)]
    return lax.psum_scatter(
        values, "dp", scatter_dimension=axis, axis_index_groups=groups, tiled=True
    )


def sum_across_blocks(values):
    blocks = lax.axis_size("dp") // BLOCK
    if blocks == 1:
        return values
    groups = [[block * BLOCK + place for block in range(blocks)] for place in range(BLOCK)]
    return lax.psum(values, "dp", axis_index_groups=groups)


def reduce_first(values, axis_x, bit_x, at_x, axis_y, bit_y, at_y):
    sent = pick(values, 1 - at_x, axis_x).astype(BF16)
    total = pick(values, at_x, axis_x) + swap_dp(sent, bit_x).astype(F32)
    if axis_y > axis_x:
        axis_y -= 1
    sent = pick(total, 1 - at_y, axis_y).astype(BF16)
    return pick(total, at_y, axis_y) + swap_dp(sent, bit_y).astype(F32)


def plane_scatter(values, at_x, at_y):
    half = LINE // 2
    first = reduce_first(values[:half], 2, 1, at_x, 1, 2, at_y)
    second = reduce_first(values[half:], 1, 2, at_y, 2, 1, at_x)
    return jnp.concatenate([first, second], 0)


def plane_scatter_one(values, at_x, at_y):
    half = values.shape[-1] // 256 * 128
    if half == 0:
        return reduce_first(values, 1, 1, at_x, 0, 2, at_y)
    first = reduce_first(values[..., :half], 1, 1, at_x, 0, 2, at_y)
    second = reduce_first(values[..., half:], 0, 2, at_y, 1, 1, at_x)
    return jnp.concatenate([first, second], -1)


def line_exchange(values, at_z, last):
    out = jnp.zeros((LINE + 1,) + values.shape[1:], F32)
    for step in range(LINE):
        part = pick(values, at_z ^ step)
        if step:
            part = swap_dp(part.astype(BF16), 4 * step).astype(F32)
        out = lax.dynamic_update_index_in_dim(out, part, at_z ^ step, 0)
    return lax.dynamic_update_index_in_dim(out, last, LINE, 0)


def plane_total(values, kind=F32):
    values = values + swap_dp(values.astype(kind), 1).astype(F32)
    return values + swap_dp(values.astype(kind), 2).astype(F32)


def line_collect(values, at_z, last, kind=F32):
    out = jnp.zeros((LINE + 1,) + values.shape, F32)
    sent = values.astype(kind)
    for step in range(LINE):
        part = swap_dp(sent, 4 * step).astype(F32) if step else values
        out = lax.dynamic_update_index_in_dim(out, part, at_z ^ step, 0)
    return lax.dynamic_update_index_in_dim(out, last, LINE, 0)


def line_total(values):
    total = values
    for step in range(1, LINE):
        total = total + swap_dp(values, 4 * step)
    return total


def in_core_order(core, own, other, axis):
    return jnp.where(
        core == 0, jnp.concatenate([own, other], axis), jnp.concatenate([other, own], axis)
    )


def general_shards(
    latent,
    action,
    task_ids,
    action_mask,
    task_table,
    target_latent,
    bin_lower,
    bin_frac,
    dyn_w1,
    dyn_wc,
    dyn_vec1,
    dyn_w2,
    dyn_vec2,
    dyn_w3,
    dyn_vec3,
    q_w1,
    q_wc,
    q_vec1,
    q_w2,
    q_vec2,
    q_w3,
    q_b3,
):
    place = lax.axis_index("dp")
    core = lax.axis_index("tensor")
    at_x, at_y, at_z = place % 2, place // 2 % 2, place // 4 % 4
    local_rows = latent.shape[0]
    half_rows = local_rows // 2
    half_latent = latent.shape[1]
    half_hidden = dyn_w1.shape[1]
    inv_root = 1.0 / math.sqrt(local_rows * lax.axis_size("dp"))
    task_count = task_table.shape[0]
    heads = q_w1.shape[0]
    head_places = (at_z, heads - 1)

    def both(values, axis):
        return jnp.concatenate(own_then_other(values), axis)

    dyn_w1_all, dyn_wc_all, dyn_vec1_all = both(dyn_w1, 1), both(dyn_wc, 1), both(dyn_vec1, 1)
    dyn_w2_all = both(dyn_w2, 0)
    dyn_w3_all = in_core_order(core, *own_then_other(dyn_w3), 1)
    dyn_vec3_all = in_core_order(core, *own_then_other(dyn_vec3), 1)
    head_weights = []
    for head in head_places:
        head_weights.append(
            (
                both(pick(q_w1, head), 1),
                both(pick(q_wc, head), 1),
                both(pick(q_vec1, head), 1),
                both(pick(q_w2, head), 0),
                pick(q_vec2, head),
                pick(q_w3, head),
                pick(q_b3, head),
            )
        )

    def my_rows(values):
        return lax.dynamic_slice_in_dim(values, core * half_rows, half_rows, 0)

    def their_rows(values):
        return lax.dynamic_slice_in_dim(values, (1 - core) * half_rows, half_rows, 0)

    def whole_columns(values):
        return in_core_order(core, my_rows(values), swap_core(their_rows(values)), 1)

    my_latent = whole_columns(latent)
    my_target = whole_columns(target_latent)
    my_ids = my_rows(task_ids)[:, None]
    onehot = (my_ids == jnp.arange(task_count, dtype=jnp.int32)[None, :]).astype(BF16)
    table = jnp.concatenate([action_mask.astype(BF16), task_table], 1)
    looked_up = mm(onehot, table)
    acts = action.shape[1]
    acted = my_rows(action).astype(F32) * looked_up[:, :acts]
    my_context = jnp.concatenate([acted, looked_up[:, acts:]], 1).astype(BF16)
    fraction = my_rows(bin_frac)[:, None]
    piece_one = lax.reduce_precision(fraction, 8, 7)
    piece_two = lax.reduce_precision(fraction - piece_one, 8, 7)
    piece_three = fraction - piece_one - piece_two
    meta = [my_ids, my_rows(bin_lower)[:, None], piece_one, piece_two, piece_three]
    meta = [item.astype(BF16) for item in meta]
    width = my_latent.shape[1]
    context_width = my_context.shape[1]
    packed = jnp.concatenate([my_latent, my_context] + meta, 1)
    packed = jnp.concatenate([packed] + [swap_dp(packed, 4 * step) for step in range(1, LINE)], 0)
    inputs = packed[:, :width]
    context = packed[:, width : width + context_width]
    meta = packed[:, width + context_width :].astype(F32)
    all_ids = meta[:, 0:1].astype(jnp.int32)
    lower = meta[:, 1:2].astype(jnp.int32)
    fraction = meta[:, 2:3] + meta[:, 3:4] + meta[:, 4:5]
    all_onehot = (all_ids == jnp.arange(task_count, dtype=jnp.int32)[None, :]).astype(F32)
    other_inputs, other_context = swap_core(inputs), swap_core(context)

    dyn_one, dyn_two, dyn_saved, simplex, normed_three, inverse_three = dynamics_forward(
        inputs, context, dyn_w1_all, dyn_wc_all, dyn_vec1_all, dyn_w2_all, dyn_vec2,
        dyn_w3_all, dyn_vec3_all,
    )
    next_low = simplex.astype(BF16)
    mismatch = next_low[:half_rows].astype(F32) - my_target
    consistency = jnp.sum(mismatch * mismatch, -1)
    other_next = swap_core(next_low)

    head_results = []
    for weights in head_weights:
        w_one, w_context, vec_one, w_two, vec_two, w_three, bias = weights
        hidden_one, hidden_two, saved = block_forward(
            next_low, context, w_one, w_context, vec_one, w_two, vec_two
        )
        loss, grad_logits = value_head(
            hidden_two, w_three, bias[None], lower, fraction, inv_root, heads
        )
        grad_hidden = mm_t(grad_logits, w_three)
        grad_two, sums_two, grad_one, sums_one = block_backward(
            grad_hidden, saved, vec_one, w_two, vec_two
        )
        head_results.append(
            (hidden_one, hidden_two, loss, grad_logits, grad_two, sums_two, grad_one, sums_one)
        )

    main, extra = head_results
    grad_in = mm_t(main[6], head_weights[0][0])
    own_grad = grad_in[:half_rows] + mm_t(extra[6][:half_rows], head_weights[1][0])
    own_loss = main[2][:half_rows] + extra[2][:half_rows]
    for step in range(1, LINE):
        part = slice(step * half_rows, (step + 1) * half_rows)
        own_grad = own_grad + swap_dp(grad_in[part].astype(BF16), 4 * step).astype(F32)
        own_loss = own_loss + swap_dp(main[2][part], 4 * step)
    own_grad = own_grad + 2.0 * inv_root * mismatch
    own_low = own_grad.astype(BF16)
    grad_next = jnp.concatenate(
        [own_low] + [swap_dp(own_low, 4 * step) for step in range(1, LINE)], 0
    ).astype(F32)
    my_losses = jnp.stack([consistency, own_loss], 1)
    losses = in_core_order(core, my_losses, swap_core(my_losses), 0)

    grad_three, sums_three, dyn_grad_two, dyn_sums_two, dyn_grad_one, dyn_sums_one = (
        dynamics_backward(
            grad_next, simplex, normed_three, inverse_three, dyn_saved, dyn_w3_all, dyn_vec3_all,
            dyn_vec1_all, dyn_w2_all, dyn_vec2,
        )
    )
    own_latent_grad = mm_t(dyn_grad_one[:half_rows], dyn_w1_all)
    left, right = own_latent_grad[:, :half_latent], own_latent_grad[:, half_latent:]
    kept = jnp.where(core == 0, left, right)
    received = swap_core(jnp.where(core == 0, right, left))
    latent_grad = in_core_order(core, kept, received, 0)

    def own_half(values):
        return jnp.concatenate([values[:, :half_hidden], swap_core(values[:, half_hidden:])], 0)

    def all_rows(values):
        return jnp.concatenate([values, swap_core(values)], 0)

    def quarter(values, size):
        blocks = lax.axis_size("dp") // BLOCK
        cut = values.reshape(values.shape[0], blocks, LINE, size // (blocks * LINE))
        return pick(cut, at_z, 2).reshape(values.shape[0], size // LINE)

    def spread_quarter(values):
        blocks = lax.axis_size("dp") // BLOCK
        rows = values.shape[0] // (blocks * PLANE)
        values = values.reshape((blocks, 2, 2, rows) + values.shape[1:])
        if blocks > 1:
            values = jnp.moveaxis(values, 0, 2)
        return values.reshape((2, 2, blocks * rows) + values.shape[4:])

    both_next = jnp.concatenate([next_low, other_next], 0)
    both_inputs = jnp.concatenate([inputs, other_inputs], 0)
    both_context = jnp.concatenate([context, other_context], 0)
    features = both_next.shape[1]
    hidden = 2 * half_hidden

    def quarter_grads(hidden_one, grad_two, grad_one, rows_in):
        first_factor, grad_factor = own_half(hidden_one), own_half(grad_one)
        w_two_part = t_mm(all_rows(quarter(grad_two, hidden)), first_factor)
        w_one_part = t_mm(quarter(rows_in, features), grad_factor)
        w_context_part = t_mm(both_context, grad_factor)
        return (
            plane_scatter_one(spread_quarter(w_two_part), at_x, at_y),
            plane_scatter_one(spread_quarter(w_one_part), at_x, at_y),
            plane_total(w_context_part, BF16),
        )

    def outer_quarter(left, right):
        part = t_mm(quarter(left, hidden), right)
        return plane_scatter_one(spread_quarter(part), at_x, at_y)

    first_factor, grad_factor = own_half(main[0]), own_half(main[6])
    main_two = plane_scatter(spread(t_mm(all_rows(main[4]), first_factor), 0), at_x, at_y)
    main_one = plane_scatter(spread(t_mm(both_next, grad_factor), 0), at_x, at_y)
    main_three = plane_scatter(spread(t_mm(main[1], main[3]), 0), at_x, at_y)
    main_context = plane_total(t_mm(both_context, grad_factor), BF16)
    extra_two, extra_one, extra_context = quarter_grads(extra[0], extra[4], extra[6], both_next)
    extra_three = outer_quarter(extra[1], extra[3])
    dyn_w2_part, dyn_w1_part, dyn_context = quarter_grads(
        dyn_one, dyn_grad_two, dyn_grad_one, both_inputs
    )
    dyn_w3_part = outer_quarter(
        all_rows(dyn_two),
        jnp.concatenate(
            [
                jnp.where(core == 0, grad_three[:, :half_latent], grad_three[:, half_latent:]),
                swap_core(
                    jnp.where(core == 0, grad_three[:, half_latent:], grad_three[:, :half_latent])
                ),
            ],
            0,
        ),
    )

    q_w2_out = across_blocks(line_exchange(main_two, at_z, extra_two), 1).transpose(0, 2, 1)
    q_w1_out = across_blocks(line_exchange(main_one, at_z, extra_one), 1)
    q_w3_out = line_exchange(main_three, at_z, extra_three)
    q_w3_out = across_blocks(q_w3_out + swap_core(q_w3_out), 1)
    dyn_w2_out = across_blocks(dyn_w2_part, 0).transpose(1, 0)
    dyn_w1_out = across_blocks(dyn_w1_part, 0)
    dyn_w3_out = across_blocks(dyn_w3_part, 0)
    q_wc_out = sum_across_blocks(line_collect(main_context, at_z, extra_context, BF16))
    dyn_wc_out = sum_across_blocks(dyn_context)

    def core_vec(values):
        own, other = values[:, :half_hidden], values[:, half_hidden:]
        return own + swap_core(other)

    def sums_of(result):
        return (
            core_vec(result[7]),
            result[5] + swap_core(result[5]),
            jnp.sum(result[3].astype(F32), 0)[None],
        )

    def pack(items):
        return jnp.concatenate([item.reshape(-1) for item in items])

    main_sums, extra_sums = sums_of(main), sums_of(extra)
    main_bias = main_sums[2] + swap_core(main_sums[2])
    extra_bias = extra_sums[2] + swap_core(extra_sums[2])
    main_sums, extra_sums = main_sums[:2] + (main_bias,), extra_sums[:2] + (extra_bias,)
    three_own = jnp.where(core == 0, sums_three[:, :half_latent], sums_three[:, half_latent:])
    three_other = jnp.where(core == 0, sums_three[:, half_latent:], sums_three[:, :half_latent])
    dyn_sums = (
        core_vec(dyn_sums_one),
        dyn_sums_two + swap_core(dyn_sums_two),
        three_own + swap_core(three_other),
    )
    def table_part(grad_one, w_context, rows):
        embed = mm_t(grad_one[:rows], w_context[acts:])
        return lax.dot_general(
            all_onehot[:rows], embed, (((0,), (0,)), ((), ())), precision=HIGHEST
        )

    table_grad = (
        table_part(main[6], head_weights[0][1], inputs.shape[0])
        + table_part(extra[6], head_weights[1][1], half_rows)
        + table_part(dyn_grad_one, dyn_wc_all, half_rows)
    )
    table_grad = line_total(table_grad + swap_core(table_grad))
    flat = sum_across_blocks(
        plane_total(pack((table_grad,) + dyn_sums + extra_sums + main_sums))
    )
    sizes = [table_grad] + list(dyn_sums)
    pieces = []
    start = 0
    for item in sizes:
        pieces.append(flat[start : start + item.size].reshape(item.shape))
        start += item.size
    head_size = sum(item.size for item in main_sums)
    extra_flat, main_flat = flat[start : start + head_size], flat[start + head_size :]
    head_flat = line_collect(main_flat, at_z, extra_flat)
    head_pieces = []
    start = 0
    for item in main_sums:
        head_pieces.append(
            head_flat[:, start : start + item.size].reshape((heads,) + item.shape)
        )
        start += item.size
    table_out, dyn_vec1_out, dyn_vec2_out, dyn_vec3_out = pieces
    q_vec1_out, q_vec2_out, q_b3_out = head_pieces
    return (
        losses,
        latent_grad,
        table_out,
        dyn_w1_out,
        dyn_wc_out,
        dyn_vec1_out,
        dyn_w2_out,
        dyn_vec2_out,
        dyn_w3_out,
        dyn_vec3_out,
        q_w1_out,
        q_wc_out,
        q_vec1_out,
        q_w2_out,
        q_vec2_out,
        q_w3_out,
        q_b3_out[:, 0],
    )


def gather_sum(values, ones):
    parts = []
    for start in range(0, values.shape[1], 128):
        piece = values[:, start : start + 128]
        high = piece.astype(BF16)
        rest = (piece - high.astype(F32)).astype(BF16)
        parts.append(mm(jnp.concatenate([high, rest], 1), ones))
    return jnp.concatenate(parts, 1)


def line_kernel(sizes, scale, *refs):
    (slot, width, hidden, bins, tasks, acts, context_width, heads) = sizes
    (
        latent, raw_action, raw_ids, raw_mask, raw_table, target_latent, raw_lower, raw_frac,
        dyn_vec1, raw_dyn_vec2, dyn_vec3, q_vec1, q_vec2, raw_b3,
        dyn_w1, dyn_wc, dyn_w2, dyn_w3, q_w1, q_wc, q_w2, q_w3,
        out_losses, out_latent, out_table, out_dw1, out_dwc, out_dvec, out_dw2, out_dw3,
        out_qw1, out_qwc, out_qvec, out_qw2, out_qw3,
        action, task_ids, action_mask, task_table, bin_lower, bin_frac, dyn_vec2, q_b3,
        w1, wc, w2, dw3, qw3, dv1, dv3, qv1, qv2, qb3,
        xbuf, xother, tgt, nxt, nxto, dyn_x1, dyn_x2, dyn_h1, dyn_h2, simplex, x3,
        dyn_inv, x1, x2, inv, h1, h2, gp2, gp1, h1o, gp2o, gp1o, upstream, gl, dyn_gp3,
        acc, slope, dxm, dxr, own_g, all_g, lossbuf,
        p2, r2, t2, p1, r1, t1, p3, p3h, r3, t3, p3o,
        e2, er2, et2, e1, er1, et1, e3, er3, et3, e3o,
        er2b, et2b, er1b, et1b, d3, d3s, d3o, er3b, et3b,
        pc, pcx, pcy, pq, pqx, pqy, ctx, fr, vb, vbo, vp, vpx, vpy, tb, tbo, tq, tqr,
        send_sem, recv_sem, local_sem, free_a, free_b, free_f,
    ) = refs
    half = hidden // 2
    half_w = width // 2
    own_two, own_one = hidden // BLOCK, width // BLOCK
    rows_all = slot * LINE
    place = lax.axis_index("dp")
    core = lax.axis_index("tensor")
    at_x = lax.rem(place, 2)
    at_y = lax.rem(place // 2, 2)
    at_z = lax.rem(place // 4, 4)
    z_of = [
        at_z,
        at_z + 1 - 2 * lax.rem(at_z, 2),
        lax.rem(at_z + 2, 4),
        3 - at_z,
    ]
    to_core = (place, 1 - core)
    to_x = (place + 1 - 2 * at_x, core)
    to_y = (place + 2 - 4 * at_y, core)
    to_z = [None] + [(place + 4 * (z_of[k] - at_z), core) for k in range(1, LINE)]
    mesh_id = pl.DeviceIdType.MESH
    counter = [0, 0, 0]
    free = [[], []]
    held = {}
    pending = []

    def describe(source, target, device):
        at = counter[0]
        counter[0] += 1
        if free[0]:
            send_at = free[0].pop()
        else:
            send_at = counter[2]
            counter[2] += 1
        copy = pltpu.make_async_remote_copy(
            src_ref=source, dst_ref=target, send_sem=send_sem.at[send_at],
            recv_sem=recv_sem.at[at], device_id=device, device_id_type=mesh_id,
        )
        held[id(copy)] = send_at
        return copy

    def remote(source, target, device):
        copy = describe(source, target, device)
        copy.start()
        pending.append(copy)
        return copy

    def sent(copy):
        copy.wait_send()
        pending[:] = [item for item in pending if item is not copy]
        free[0].append(held[id(copy)])

    def all_sent():
        for copy in list(pending):
            sent(copy)

    def describe_local(source, target):
        if free[1]:
            at = free[1].pop()
        else:
            at = counter[1]
            counter[1] += 1
        copy = pltpu.make_async_copy(source, target, local_sem.at[at])
        held[id(copy)] = at
        return copy

    def done(copy):
        copy.wait()
        free[1].append(held[id(copy)])

    def local(source, target):
        copy = describe_local(source, target)
        copy.start()
        return copy

    barrier = pltpu.get_barrier_semaphore()
    peers = [to_core, to_x, to_y] + to_z[1:]
    for peer in peers:
        pl.semaphore_signal(barrier, inc=1, device_id=peer, device_id_type=mesh_id)


    low = slice(0, half)
    high = slice(half, hidden)
    own_cols = pl.ds(pl.multiple_of(half_w * core, 128), half_w)
    other_cols = pl.ds(pl.multiple_of(half_w * (1 - core), 128), half_w)
    own_rows = pl.ds(pl.multiple_of(slot * core, 64), slot)
    other_rows = pl.ds(pl.multiple_of(slot * (1 - core), 64), slot)

    def load_weights(to, one, context, two):
        mine = [
            local(one, w1.at[to, :, low]),
            local(context, wc.at[to, :, low]),
            local(two, w2.at[to, low, :]),
        ]
        return mine

    def send_weights(to, one, context, two):
        return [
            remote(one, w1.at[to, :, high], to_core),
            remote(context, wc.at[to, :, high], to_core),
            remote(two, w2.at[to, high, :], to_core),
        ]

    head_z = at_z
    last = heads - 1
    fact_copies = [
        local(source, target)
        for source, target in (
            (raw_ids, task_ids), (raw_frac, bin_frac), (raw_lower, bin_lower),
            (raw_action, action), (raw_mask, action_mask), (raw_table, task_table),
            (latent.at[own_rows], xbuf.at[pl.ds(0, slot), own_cols]),
        )
    ]
    vec_ready = [
        local(source, target)
        for source, target in (
            (dyn_vec1, dv1.at[:, low]), (raw_dyn_vec2, dyn_vec2), (dyn_vec3, dv3.at[:, own_cols]),
            (q_vec1.at[head_z], qv1.at[0, :, low]), (q_vec1.at[last], qv1.at[1, :, low]),
            (q_vec2.at[head_z], qv2.at[0]), (q_vec2.at[last], qv2.at[1]), (raw_b3, q_b3),
            (target_latent.at[own_rows], tgt.at[:, own_cols]),
        )
    ]
    dyn_ready = load_weights(0, dyn_w1, dyn_wc, dyn_w2)
    three_ready = local(dyn_w3, dw3.at[:, own_cols])
    main_ready = load_weights(1, q_w1.at[head_z], q_wc.at[head_z], q_w2.at[head_z])
    main_three = local(q_w3.at[head_z], qw3.at[0])
    extra_three = local(q_w3.at[last], qw3.at[1])

    vb[...] = jnp.zeros_like(vb)

    for copy in fact_copies:
        done(copy)
    fr[0] = jnp.zeros_like(fr[0])
    fr[0, 0:1, :] = task_ids[...].astype(F32)
    fr[0, 1:2, :] = bin_lower[...].astype(F32)
    fr[0, 2:3, :] = bin_frac[...]
    fr[0, 3 : 3 + acts, :] = action[...].astype(F32)

    def shift_matrix(count, start):
        near = lax.broadcasted_iota(jnp.int32, (count, 128), 0)
        far = lax.broadcasted_iota(jnp.int32, (count, 128), 1)
        return (near + start == far).astype(F32).astype(BF16)

    def context_rows(index):
        ctx[...] = fr[index].T
        columns = ctx[own_rows, :]
        ids, lower, fraction = columns[:, 0:1], columns[:, 1:2], columns[:, 2:3]
        task = lax.broadcasted_iota(jnp.int32, (slot, tasks), 1).astype(F32)
        onehot = (ids == task).astype(F32).astype(BF16)
        lane = lax.broadcasted_iota(jnp.int32, (slot, 128), 1)
        factor = mm(columns[:, 3 : 3 + acts].astype(BF16), to_acts) + (lane >= acts).astype(F32)
        piece_one = fraction.astype(BF16).astype(F32)
        piece_two = (fraction - piece_one).astype(BF16).astype(F32)
        facts = mm(onehot, lookup) * factor
        for at, item in enumerate(
            (ids, lower, piece_one, piece_two, fraction - piece_one - piece_two)
        ):
            facts = facts + jnp.where(lane == context_width + at, item, 0.0)
        rows = slice(index * slot, (index + 1) * slot)
        xbuf[rows, width : width + 128] = facts.astype(BF16)

    to_acts = shift_matrix(acts, 0)
    lookup = (
        t_mm(action_mask[...].astype(F32).astype(BF16), to_acts)
        + mm(task_table[...], shift_matrix(context_width - acts, acts))
    ).astype(BF16)
    pl.semaphore_wait(barrier, len(peers))
    facts_in = [remote(fr.at[0], fr.at[k], to_z[k]) for k in range(1, LINE)]
    lat_copy = remote(latent.at[other_rows], xbuf.at[pl.ds(0, slot), own_cols], to_core)
    tgt_copy = remote(target_latent.at[other_rows], tgt.at[:, own_cols], to_core)

    vec_copies = [
        remote(dyn_vec1, dv1.at[:, high], to_core),
        remote(dyn_vec3, dv3.at[:, own_cols], to_core),
        remote(q_vec1.at[head_z], qv1.at[0, :, high], to_core),
        remote(q_vec1.at[last], qv1.at[1, :, high], to_core),
    ]
    dyn_ready_other = send_weights(0, dyn_w1, dyn_wc, dyn_w2)
    three_ready_other = remote(dyn_w3, dw3.at[:, own_cols], to_core)
    main_ready_other = send_weights(1, q_w1.at[head_z], q_wc.at[head_z], q_w2.at[head_z])
    lat_copy.wait_recv()
    line_in = [
        remote(
            xbuf.at[pl.ds(0, slot), pl.ds(0, width)],
            xbuf.at[pl.ds(slot * k, slot), pl.ds(0, width)],
            to_z[k],
        )
        for k in range(1, LINE)
    ]
    context_rows(0)
    for index, copy in enumerate(facts_in):
        copy.wait_recv()
        context_rows(1 + index)
    for copy in vec_copies:
        copy.wait_recv()
    for copy in vec_ready:
        done(copy)
    qb3[0] = q_b3[pl.ds(head_z, 1), :]
    qb3[1] = q_b3[last : last + 1, :]

    CH = 64

    def over_rows(first, count, body, CH=CH):
        if count <= CH:
            body(pl.ds(first, count))
            return

        def step(index, carry):
            body(pl.ds(pl.multiple_of(first + index * CH, CH), CH))
            return carry

        lax.fori_loop(0, count // CH, step, 0)

    def norm_rows(pre, keep, inverse, vec, out, first, count, slope_to=None):
        features = pre.shape[1]

        def body(rows):
            values = pre[rows, :]
            centred = values - jnp.sum(values, -1, keepdims=True) * (1.0 / features)
            inv_rows = lax.rsqrt(
                jnp.sum(centred * centred, -1, keepdims=True) * (1.0 / features) + EPSILON
            )
            normed = centred * inv_rows
            keep[rows, :] = normed.astype(keep.dtype)
            inverse[rows, :] = inv_rows
            values = normed * vec[1:2, :] + vec[2:3, :]
            grown, ratio, share = mish_parts(values)
            out[rows, :] = (values * ratio).astype(BF16)
            if slope_to is not None:
                slope_to[rows, :] = mish_slope_of(values, grown, ratio, share)

        over_rows(first, count, body)

    def add_sums(at, rounded, along, shift):
        count, features = shift.shape
        for index, item in enumerate((rounded, along, shift)):
            acc[at + index, :, 0:features] += jnp.sum(item.reshape(count // 8, 8, features), 0)

    def back_rows(grad, normed_ref, inverse, vec, out, at, first, count, slope, kept=None):
        features = normed_ref.shape[1]

        def body(rows):
            normed = normed_ref[rows, :].astype(F32)
            gain = vec[1:2, :]
            up = grad[rows, :]
            if kept is not None:
                up = kept[rows, :] * up
            elif slope:
                up = mish_slope(normed * gain + vec[2:3, :]) * up
            weighted = up * gain
            along = up * normed
            mean_one = jnp.sum(weighted, -1, keepdims=True) * (1.0 / features)
            mean_two = jnp.sum(weighted * normed, -1, keepdims=True) * (1.0 / features)
            result = (inverse[rows, :] * (weighted - mean_one - normed * mean_two)).astype(BF16)
            out[rows, :] = result
            add_sums(at, result.astype(F32), along, up)

        over_rows(first, count, body)

    def two_tiles(body):
        for index in range(2):
            body(slice(index * half, (index + 1) * half))

    def layers_forward(to, source, vec_one, vec_two, keep_one, keep_two, inverse, hid_one, hid_two,
                       first, count, ready, slope_to=None):
        rows = pl.ds(first, count)
        ready(0)

        def first_tile(cols):
            x1[rows, cols] = (
                mm(source[rows, 0:width], w1[to, :, cols])
                + mm(xbuf[rows, width : width + context_width], wc[to, :, cols])
                + vec_one[0:1, cols]
            )

        two_tiles(first_tile)
        norm_rows(x1, keep_one, inverse.at[0], vec_one, hid_one, first, count)
        ready(1)

        def second_tile(cols):
            x2[rows, cols] = mm(hid_one[rows, :], w2[to, :, cols]) + vec_two[0:1, cols]

        two_tiles(second_tile)
        norm_rows(x2, keep_two, inverse.at[1], vec_two, hid_two, first, count, slope_to)

    def back_two_to_one(to, grad, first, count, parts=(0, 1)):
        rows = pl.ds(first, count)

        def tile(cols):
            upstream[rows, cols] = mm_t(grad[rows, :], w2[to, cols, :])

        if len(parts) == 2:
            two_tiles(tile)
        else:
            tile(slice(parts[0] * half, (parts[0] + 1) * half))

    def ready_of(mine, others):
        def ready(stage):
            picked = (0, 1) if stage == 0 else (2,)
            for index in picked:
                done(mine[index])
                others[index].wait_recv()

        return ready

    def nothing(stage):
        return None

    line_in[0].wait_recv()
    layers_forward(
        0, xbuf, dv1, dyn_vec2, dyn_x1, dyn_x2, dyn_inv, dyn_h1, dyn_h2, 0, 2 * slot,
        ready_of(dyn_ready, dyn_ready_other),
    )
    for copy in line_in[1:]:
        copy.wait_recv()
    x_copy = remote(xbuf, xother, to_core)
    layers_forward(
        0, xbuf, dv1, dyn_vec2, dyn_x1, dyn_x2, dyn_inv, dyn_h1, dyn_h2, 2 * slot,
        rows_all - 2 * slot, nothing,
    )
    done(three_ready)
    three_ready_other.wait_recv()
    x3[...] = mm(dyn_h2[...], dw3[...]) + dv3[0:1, :]
    group_row = lax.rem(lax.broadcasted_iota(jnp.int32, (256, 128), 0), 128) // GROUP
    group_col = lax.broadcasted_iota(jnp.int32, (256, 128), 1) // GROUP
    ones = (group_row == group_col).astype(F32).astype(BF16)

    def simplex_rows(rows):
        values = x3[rows, :]
        centred = values - jnp.sum(values, -1, keepdims=True) * (1.0 / width)
        inv_rows = lax.rsqrt(
            jnp.sum(centred * centred, -1, keepdims=True) * (1.0 / width) + EPSILON
        )
        normed = centred * inv_rows
        x3[rows, :] = normed
        dyn_inv[2, rows, :] = inv_rows
        grown = jnp.exp(normed * dv3[1:2, :] + dv3[2:3, :])
        share = grown / gather_sum(grown, ones)
        simplex[rows, :] = share
        nxt[rows, :] = share.astype(BF16)

    over_rows(0, rows_all, simplex_rows, 2 * CH)
    for copy in dyn_ready_other:
        sent(copy)
    pl.semaphore_signal(free_a, inc=1, device_id=to_core, device_id_type=mesh_id)
    extra_ready = load_weights(0, q_w1.at[last], q_wc.at[last], q_w2.at[last])
    next_copy = remote(nxt, nxto, to_core)
    tgt_copy.wait_recv()
    gap = nxt[0:slot, :].astype(F32) - tgt[...]
    own_g[...] = gap * (2.0 * scale)
    consistency = jnp.sum(gap * gap, -1, keepdims=True)
    pl.semaphore_wait(free_a, 1)
    extra_ready_other = send_weights(0, q_w1.at[last], q_wc.at[last], q_w2.at[last])

    def value_rows(head, first, count):
        rows = pl.ds(first, count)
        logits = mm_t(h2[rows, :], qw3[head]) + qb3[head]
        logits = logits - jnp.max(logits, -1, keepdims=True)
        grown = jnp.exp(logits)
        total = jnp.sum(grown, -1, keepdims=True)
        lane = lax.broadcasted_iota(jnp.int32, (count, bins), 1).astype(F32)
        facts = xbuf[rows, width : width + 128].astype(F32)
        lower = facts[:, context_width + 1 : context_width + 2]
        fraction = (
            facts[:, context_width + 2 : context_width + 3]
            + facts[:, context_width + 3 : context_width + 4]
            + facts[:, context_width + 4 : context_width + 5]
        )
        target = jnp.where(lane == lower, 1.0 - fraction, 0.0) + jnp.where(
            lane == lower + 1.0, fraction, 0.0
        )
        loss = -jnp.sum(target * (logits - jnp.log(total)), -1, keepdims=True) * (1.0 / heads)
        grad = (scale / heads * (grown / total - target)).astype(BF16)
        gl[rows, :] = grad

        def tile(cols):
            upstream[rows, cols] = mm(grad, qw3[head, :, cols])

        two_tiles(tile)
        acc[6, 0, 0:bins] += jnp.sum(grad.astype(F32), 0)
        return loss

    def table_sum(to, grad, first, count):
        rows = pl.ds(first, count)
        embed = mm_t(grad[rows, :], wc[to])
        ids = xbuf[rows, width : width + 128].astype(F32)[:, context_width : context_width + 1]
        task = lax.broadcasted_iota(jnp.int32, (count, tasks), 1).astype(F32)
        onehot = (ids == task).astype(F32).astype(BF16)
        top = embed.astype(BF16)
        rest = embed - top.astype(F32)
        middle = rest.astype(BF16)
        lowest = (rest - middle.astype(F32)).astype(BF16)
        tb[:, 0:context_width] += (
            t_mm(onehot, top) + t_mm(onehot, middle) + t_mm(onehot, lowest)
        )

    def finish_vectors(slot_at, width_three):
        for index in range(3):
            vb[slot_at, index : index + 1, :] = jnp.sum(acc[index], 0, keepdims=True)
            vb[slot_at, 3 + index : 4 + index, :] = jnp.sum(acc[3 + index], 0, keepdims=True)
        if width_three:
            three = [jnp.sum(acc[6 + index, :, 0:width], 0, keepdims=True) for index in range(3)]
            vb[slot_at, 6:7, 0:width] = three[0]
            vb[slot_at, 6:7, width : 2 * width] = three[1]
            vb[slot_at, 7:8, 0:width] = three[2]
        else:
            vb[slot_at, 6:7, :] = jnp.sum(acc[6], 0, keepdims=True)
        return remote(vb.at[slot_at], vbo.at[slot_at], to_core)

    own_tasks = pl.ds(pl.multiple_of(tasks // 2 * core, 8), tasks // 2)
    half_cols = pl.ds(pl.multiple_of(half * core, 128), half)

    def join_vectors(slot_at, copy):
        copy.wait_recv()
        sent(copy)
        vp[slot_at, 0:3, :] = vb[slot_at, 0:3, low] + vbo[slot_at, 0:3, high]
        vp[slot_at, 3:8, :] = vb[slot_at, 3:8, half_cols] + vbo[slot_at, 3:8, half_cols]
        return remote(vp.at[slot_at], vpx.at[slot_at], to_x)

    def plane_vectors(slot_at, copy):
        copy.wait_recv()
        sent(copy)
        vp[slot_at] = vp[slot_at] + vpx[slot_at]
        return remote(vp.at[slot_at], vpy.at[slot_at], to_y)

    def total_vectors(slot_at, copy):
        copy.wait_recv()
        sent(copy)
        vp[slot_at] = vp[slot_at] + vpy[slot_at]

    def scatter_start(source, target, x_first, lead):
        if lead is None:
            piece = source.at[:, 1 - at_x] if x_first else source.at[1 - at_y]
        else:
            piece = source.at[lead, :, 1 - at_x] if x_first else source.at[lead, 1 - at_y]
        return remote(piece, target, to_x if x_first else to_y)

    def scatter_middle(copy, source, received, target, x_first, lead):
        copy.wait_recv()
        if lead is None:
            for other in range(2):
                kept = source[other, at_x] if x_first else source[at_y, other]
                received[other] = (received[other].astype(F32) + kept.astype(F32)).astype(BF16)
            piece = received.at[1 - at_y] if x_first else received.at[1 - at_x]
        else:
            for index in range(lead.size):
                for other in range(2):
                    kept = (
                        source[lead.start + index, other, at_x]
                        if x_first
                        else source[lead.start + index, at_y, other]
                    )
                    received[index, other] = (
                        received[index, other].astype(F32) + kept.astype(F32)
                    ).astype(BF16)
            piece = received.at[:, 1 - at_y] if x_first else received.at[:, 1 - at_x]
        return remote(piece, target, to_y if x_first else to_x)

    def scatter_end(copy, received, target, x_first):
        copy.wait_recv()
        mine = at_y if x_first else at_x
        return received[mine].astype(F32) + target[...].astype(F32)

    def scatter_end_lead(copy, received, target, x_first, count):
        copy.wait_recv()
        mine = at_y if x_first else at_x
        for index in range(count):
            target[index] = (
                received[index, mine].astype(F32) + target[index].astype(F32)
            ).astype(BF16)

    first_half, second_half = pl.ds(0, 2), pl.ds(2, 2)

    for copy in [lat_copy, tgt_copy] + facts_in + vec_copies + line_in:
        sent(copy)
    acc[...] = jnp.zeros_like(acc)
    tb[...] = jnp.zeros_like(tb)
    done(main_three)
    done(extra_three)
    layers_forward(
        1, nxt, qv1.at[0], qv2.at[0], x1, x2, inv, h1, h2, 0, rows_all,
        ready_of(main_ready, main_ready_other), slope,
    )
    factor_copies = [remote(h1.at[:, high], h1o, to_core)]
    main_loss = value_rows(0, 0, rows_all)
    for first in range(0, rows_all, 2 * slot):
        back_rows(upstream, x2, inv.at[1], qv2.at[0], gp2, 3, first, 2 * slot, True, slope)
        block = pl.ds(first, 2 * slot)
        factor_copies.append(remote(gp2.at[block], gp2o.at[block], to_core))
    back_two_to_one(1, gp2, 0, rows_all, (0,))
    for copy in factor_copies:
        copy.wait_recv()
    wide = half // 256 * 128 + 128
    main_two = [[], []]
    for part in (slice(0, wide), slice(wide, half)):
        for index in range(2):
            cols = slice(index * half, (index + 1) * half)
            whole = t_mm(gp2[:, cols], h1[:, part]) + t_mm(gp2o[:, cols], h1o[:, part])
            p2[2 * index : 2 * index + 2, :, :, :, part] = whole.astype(BF16).reshape(
                (2, 2, 2, own_two, part.stop - part.start)
            )
            lead = pl.ds(2 * index, 2)
            if index == 0:
                piece, device = p2.at[lead, :, 1 - at_x, :, part], to_x
            else:
                piece, device = p2.at[lead, 1 - at_y, :, :, part], to_y
            main_two[index].append(remote(piece, r2.at[lead, :, :, part], device))
    back_two_to_one(1, gp2, 0, rows_all, (1,))
    back_rows(upstream, x1, inv.at[0], qv1.at[0], gp1, 0, 0, rows_all, True)
    one_copy = remote(gp1.at[:, high], gp1o, to_core)
    dx = mm_t(gp1[...], w1[1])
    own_g[...] = own_g[...] + dx[0:slot]
    dxm[:, 0:width] = dx.astype(BF16)
    lane_all = lax.broadcasted_iota(jnp.int32, (rows_all, 128), 1)
    loss_high = main_loss.astype(BF16).astype(F32)
    loss_rest = main_loss - loss_high
    loss_middle = loss_rest.astype(BF16).astype(F32)
    loss_low = loss_rest - loss_middle
    dxm[:, width : width + 128] = jnp.where(
        lane_all == 0, loss_high, jnp.where(lane_all == 1, loss_middle, loss_low)
    ).astype(BF16)
    dx_copies = [
        remote(dxm.at[pl.ds(slot * k, slot)], dxr.at[k - 1], to_z[k]) for k in range(1, LINE)
    ]
    hand, keep = [], []

    def start_two(source, received):
        return [
            scatter_start(
                source, received.at[2 * index : 2 * index + 2], index == 0, pl.ds(2 * index, 2)
            )
            for index in range(2)
        ]

    def middle_two(copies, source, received, target):
        return [
            scatter_middle(
                copies[index], source, received.at[2 * index : 2 * index + 2],
                target.at[2 * index : 2 * index + 2], index == 0, pl.ds(2 * index, 2),
            )
            for index in range(2)
        ]

    def end_two(copies, received, target):
        for index in range(2):
            scatter_end_lead(
                copies[index], received.at[2 * index : 2 * index + 2],
                target.at[2 * index : 2 * index + 2], index == 0, 2,
            )

    def hand_on(source, target):
        keep.append(local(source.at[at_z], target.at[at_z]))
        for k in range(1, LINE):
            hand.append(remote(source.at[z_of[k]], target.at[at_z], to_z[k]))

    def hand_all(source, target):
        mine = target(at_z)
        keep.append(local(source, mine))
        near = remote(source, mine, to_z[1])
        far = remote(source, mine, to_z[2])
        hand.append(near)
        return far, target

    def hand_further(started):
        far, target = started
        far.wait_recv()
        theirs = target(z_of[2])
        hand.append(remote(theirs, theirs, to_z[1]))

    left, right = slice(0, wide), slice(wide, half)

    def context_start(source, received):
        return (
            remote(source.at[:, left], received.at[:, left], to_x),
            remote(source.at[:, right], received.at[:, right], to_y),
        )

    def context_add(source, received, copies):
        for copy in copies:
            copy.wait_recv()
            sent(copy)
        source[...] = (source[...].astype(F32) + received[...].astype(F32)).astype(BF16)

    def context_middle(source, received, target, copies):
        context_add(source, received, copies)
        return (
            remote(source.at[:, left], target.at[:, left], to_y),
            remote(source.at[:, right], target.at[:, right], to_x),
        )

    x_copy.wait_recv()
    one_copy.wait_recv()
    whole = t_mm(xbuf[:, width : width + 128], gp1[:, low]) + t_mm(
        xother[:, width : width + 128], gp1o[...]
    )
    pc[...] = whole[0 : pc.shape[0]].astype(BF16)
    main_context = context_start(pc, pcx)
    next_copy.wait_recv()
    whole = t_mm(nxt[...], gp1[:, low]) + t_mm(nxto[...], gp1o[...])
    p1[...] = whole.astype(BF16).reshape(p1.shape)
    part = t_mm(h2[...], gl[...])
    p3[...] = part.astype(BF16).reshape(p3.shape)
    three_copy = remote(p3.at[pl.ds(2 * (1 - core), 2)], p3o, to_core)
    main_vec = finish_vectors(0, False)
    acc[...] = jnp.zeros_like(acc)
    table_sum(1, gp1, 0, rows_all)
    for copy in main_ready_other:
        sent(copy)
    pl.semaphore_signal(free_b, inc=1, device_id=to_core, device_id_type=mesh_id)
    dyn_again = load_weights(1, dyn_w1, dyn_wc, dyn_w2)
    for copy in factor_copies + [one_copy]:
        sent(copy)
    pl.semaphore_signal(free_f, inc=1, device_id=to_core, device_id_type=mesh_id)
    pl.semaphore_wait(free_b, 1)
    dyn_again_other = send_weights(1, dyn_w1, dyn_wc, dyn_w2)

    for copy in [three_ready_other, x_copy, next_copy]:
        sent(copy)
    layers_forward(
        0, nxt, qv1.at[1], qv2.at[1], x1, x2, inv, h1, h2, 0, slot,
        ready_of(extra_ready, extra_ready_other), slope,
    )
    extra_loss = value_rows(1, 0, slot)
    back_rows(upstream, x2, inv.at[1], qv2.at[1], gp2, 3, 0, slot, True, slope)
    back_two_to_one(0, gp2, 0, slot)
    back_rows(upstream, x1, inv.at[0], qv1.at[1], gp1, 0, 0, slot, True)
    own_total = own_g[...] + mm_t(gp1[0:slot, :], w1[0])
    value = main_loss[0:slot] + extra_loss
    for index, copy in enumerate(dx_copies):
        copy.wait_recv()
        message = dxr[index].astype(F32)
        own_total = own_total + message[:, 0:width]
        value = value + (
            message[:, width : width + 1]
            + message[:, width + 1 : width + 2]
            + message[:, width + 2 : width + 3]
        )
    all_g[0:slot, :] = own_total.astype(BF16)
    grad_copies = [
        remote(all_g.at[pl.ds(0, slot)], all_g.at[pl.ds(slot * k, slot)], to_z[k])
        for k in range(1, LINE)
    ]
    lane_own = lax.broadcasted_iota(jnp.int32, (slot, 128), 1)
    lossbuf[...] = jnp.where(lane_own == 0, consistency, value)
    loss_copy = remote(lossbuf, out_losses.at[own_rows], to_core)
    keep += [local(lossbuf, out_losses.at[own_rows])]
    table_sum(0, gp1, 0, slot)
    rest = rows_all - slot
    stage = {}

    def between(step):
        if step == 0:
            return
        stage["context"] = context_middle(pc, pcx, pcy, main_context)
        for copies in main_two:
            copies[0].wait_recv()
        stage["two"] = middle_two([copies[1] for copies in main_two], p2, r2, t2)
        stage["one"] = start_two(p1, r1)
        three_copy.wait_recv()
        sent(three_copy)
        stage["three"] = []
        for index in range(2):
            p3h[index] = (
                p3[2 * core + index].astype(F32) + p3o[index].astype(F32)
            ).astype(BF16)
            stage["three"].append(scatter_start(p3h.at[index], r3.at[index], index == 0, None))
        stage["vec"] = join_vectors(0, main_vec)

    layers_forward(
        0, nxt, qv1.at[1], qv2.at[1], x1, x2, inv, h1, h2, slot, rest, between, slope
    )
    first_two = main_two[0] + main_two[1]
    main_context, main_two, main_vec = stage["context"], stage["two"], stage["vec"]
    main_three_sum, main_one = stage["three"], stage["one"]
    value_rows(1, slot, rest)
    context_add(pc, pcy, main_context)
    context_hand = hand_all(pc, lambda at: out_qwc.at[at, pl.ds(0, pc.shape[0])])
    back_rows(upstream, x2, inv.at[1], qv2.at[1], gp2, 3, slot, rest, True, slope)
    pl.semaphore_wait(free_f, 1)
    factor_copies = [remote(gp2, gp2o, to_core), remote(h1.at[:, high], h1o, to_core)]
    back_two_to_one(0, gp2, slot, rest)
    back_rows(upstream, x1, inv.at[0], qv1.at[1], gp1, 0, slot, rest, True)
    one_copy = remote(gp1.at[:, high], gp1o, to_core)
    extra_vec = finish_vectors(1, False)
    acc[...] = jnp.zeros_like(acc)

    for copy in extra_ready_other + dx_copies + grad_copies + [loss_copy]:
        sent(copy)
    end_two(main_two, r2, t2)
    hand_on(t2, out_qw2)

    def by_place(body):
        for index in range(LINE):
            @pl.when(at_z == index)
            def _(index=index):
                body(index)

    quarter = hidden // LINE
    quarter_w = width // LINE
    quarter_c = 128 // LINE

    def quarter_two(index, hid, target):
        cols = slice(index * quarter, (index + 1) * quarter)
        whole = t_mm(gp2[:, cols], hid[:, low]) + t_mm(gp2o[:, cols], h1o[...])
        target[...] = whole.astype(BF16).reshape(target.shape)

    def quarter_one(index, mine, others, target, at):
        cols = slice(index * quarter_w, (index + 1) * quarter_w)
        whole = t_mm(mine[:, cols], gp1[:, low]) + t_mm(others[:, cols], gp1o[...])
        target[...] = whole.astype(BF16).reshape(target.shape)
        cols = slice(width + index * quarter_c, width + (index + 1) * quarter_c)
        whole = t_mm(xbuf[:, cols], gp1[:, low]) + t_mm(xother[:, cols], gp1o[...])
        pq[at] = whole.astype(BF16)

    for copy in factor_copies + [one_copy]:
        copy.wait_recv()

    def extra_parts(index):
        part = t_mm(h2[:, index * quarter : (index + 1) * quarter], gl[...])
        e3[...] = part.astype(BF16).reshape(e3.shape)
        quarter_two(index, h1, e2)
        quarter_one(index, nxt, nxto, e1, 0)

    by_place(extra_parts)
    extra_three_sum = remote(e3, e3o, to_core)
    extra_two = scatter_start(e2, er2, True, None)
    extra_one = scatter_start(e1, er1, False, None)
    extra_context = context_start(pq.at[0], pqx.at[0])
    for copy in factor_copies + [one_copy]:
        sent(copy)
    pl.semaphore_signal(free_f, inc=1, device_id=to_core, device_id_type=mesh_id)
    for copy in grad_copies:
        copy.wait_recv()

    for copy in first_two:
        sent(copy)
    def simplex_back(rows):
        share = simplex[rows, :]
        weighted = all_g[rows, :].astype(F32) * share
        up = weighted - share * gather_sum(weighted, ones)
        upstream[rows, 0:width] = up

    over_rows(0, rows_all, simplex_back, 2 * CH)
    back_rows(
        upstream.at[:, 0:width], x3, dyn_inv.at[2], dv3, dyn_gp3, 6, 0, rows_all, False
    )

    def dyn_third(index):
        left = dyn_h2[:, index * quarter : (index + 1) * quarter]
        d3s[...] = t_mm(left, dyn_gp3[:, other_cols]).astype(BF16).reshape(d3s.shape)
        d3[...] = t_mm(left, dyn_gp3[:, own_cols]).astype(BF16).reshape(d3.shape)

    by_place(dyn_third)
    d3_copy = remote(d3s, d3o, to_core)

    def three_tile(cols):
        upstream[:, cols] = mm_t(dyn_gp3[...], dw3[cols, :])

    two_tiles(three_tile)
    first_one = main_one
    main_one = middle_two(main_one, p1, r1, t1)
    hand_further(context_hand)
    back_rows(upstream, dyn_x2, dyn_inv.at[1], dyn_vec2, gp2, 3, 0, rows_all, True)
    pl.semaphore_wait(free_f, 1)
    factor_copies = [remote(gp2, gp2o, to_core), remote(dyn_h1.at[:, high], h1o, to_core)]
    d3_copy.wait_recv()
    sent(d3_copy)
    d3[...] = (d3[...].astype(F32) + d3o[...].astype(F32)).astype(BF16)
    dyn_three_sum = scatter_start(d3, er3b, False, None)
    extra_three_sum.wait_recv()
    sent(extra_three_sum)
    e3[...] = (e3[...].astype(F32) + e3o[...].astype(F32)).astype(BF16)
    extra_three_sum = scatter_start(e3, er3, False, None)
    extra_vec = join_vectors(1, extra_vec)
    done(dyn_again[2])
    dyn_again_other[2].wait_recv()
    back_two_to_one(1, gp2, 0, rows_all)
    for copy in factor_copies:
        copy.wait_recv()
    for copy in first_one:
        sent(copy)
    d2, d1 = p2.at[0], p1.at[0]
    by_place(lambda index: quarter_two(index, dyn_h1, d2))
    back_rows(upstream, dyn_x1, dyn_inv.at[0], dv1, gp1, 0, 0, rows_all, True)
    one_copy = remote(gp1.at[:, high], gp1o, to_core)
    dyn_vec = finish_vectors(2, True)
    for index in (0, 1):
        done(dyn_again[index])
        dyn_again_other[index].wait_recv()
    table_sum(1, gp1, 0, slot)
    table_copy = remote(tb, tbo, to_core)
    one_copy.wait_recv()
    by_place(lambda index: quarter_one(index, xbuf, xother, d1, 1))
    dyn_one_sum = scatter_start(d1, er1b, True, None)
    dyn_context = context_start(pq.at[1], pqx.at[1])
    end_two(main_one, r1, t1)
    hand_on(t1, out_qw1)
    lat_g = tgt
    lat_g[...] = mm_t(gp1[0:slot, :], w1[1])
    latent_copy = remote(lat_g.at[:, other_cols], out_latent.at[own_rows], to_core)
    keep += [local(lat_g.at[:, own_cols], out_latent.at[own_rows])]
    dyn_vec = join_vectors(2, dyn_vec)
    table_copy.wait_recv()
    sent(table_copy)
    tq[...] = tb[own_tasks, :] + tbo[own_tasks, :]
    table_copy = remote(tq, tqr.at[0], to_x)

    main_three_sum = [
        scatter_middle(main_three_sum[index], p3h.at[index], r3.at[index], t3.at[index],
                       index == 0, None)
        for index in range(2)
    ]
    main_vec = plane_vectors(0, main_vec)
    extra_context = context_middle(pq.at[0], pqx.at[0], pqy.at[0], extra_context)
    extra_one2 = scatter_middle(extra_one, e1, er1, et1, False, None)
    extra_two2 = scatter_middle(extra_two, e2, er2, et2, True, None)
    extra_vec = plane_vectors(1, extra_vec)
    dyn_context = context_middle(pq.at[1], pqx.at[1], pqy.at[1], dyn_context)
    table_copy.wait_recv()
    sent(table_copy)
    tq[...] = tq[...] + tqr[0]
    table_copy = remote(tq, tqr.at[1], to_y)
    dyn_vec = plane_vectors(2, dyn_vec)
    dyn_two_sum = (
        remote(d2.at[:, 1 - at_x, :, left], er2b.at[:, :, left], to_x),
        remote(d2.at[1 - at_y, :, :, right], er2b.at[:, :, right], to_y),
    )
    dyn_three2 = scatter_middle(dyn_three_sum, d3, er3b, et3b, False, None)
    extra_three2 = scatter_middle(extra_three_sum, e3, er3, et3, False, None)
    dyn_one2 = scatter_middle(dyn_one_sum, d1, er1b, et1b, True, None)
    def quarter_rows(at):
        return pl.ds(pl.multiple_of(quarter_c * at, quarter_c), quarter_c)

    context_add(pq.at[0], pqy.at[0], extra_context)
    extra_hand = hand_all(pq.at[0], lambda at: out_qwc.at[last, quarter_rows(at)])
    total_vectors(0, main_vec)
    vec_hand = hand_all(vp.at[0], lambda at: out_qvec.at[at, core])
    vec_near = hand.pop()
    vec_keep = [keep.pop()]
    for index in range(2):
        t3[index] = scatter_end(
            main_three_sum[index], r3.at[index], t3.at[index], index == 0
        ).astype(BF16)
    mine = at_z // 2 == core
    three_out = out_qw3.at[at_z]
    three_copies = []
    for k in range(1, LINE):
        theirs = z_of[k] // 2 == core
        copy = describe(t3.at[lax.rem(z_of[k], 2)], three_out, to_z[k])
        three_copies.append((theirs, copy))

        @pl.when(theirs)
        def _(copy=copy):
            copy.start()

    three_keep = describe_local(t3.at[lax.rem(at_z, 2)], three_out)

    @pl.when(mine)
    def _():
        three_keep.start()

    context_add(pq.at[1], pqy.at[1], dyn_context)
    dyn_rows = out_dwc.at[quarter_rows(at_z)]
    keep += [local(pq.at[1], dyn_rows)]
    hand += [remote(pq.at[1], dyn_rows, to_z[k]) for k in range(1, LINE)]
    table_copy.wait_recv()
    sent(table_copy)
    tq[...] = tq[...] + tqr[1]
    table_copies = [remote(tq, tqr.at[1 + k], to_z[k]) for k in range(1, LINE)]
    for copy in dyn_two_sum:
        copy.wait_recv()
    for other in range(2):
        for cols, kept in ((left, d2[other, at_x, :, left]), (right, d2[at_y, other, :, right])):
            er2b[other, :, cols] = (
                er2b[other, :, cols].astype(F32) + kept.astype(F32)
            ).astype(BF16)
    dyn_two2 = (
        remote(er2b.at[1 - at_y, :, left], et2b.at[:, left], to_y),
        remote(er2b.at[1 - at_x, :, right], et2b.at[:, right], to_x),
    )
    hand_further(extra_hand)
    hand_further(vec_hand)
    vec_further = hand.pop()
    total_vectors(1, extra_vec)
    vec_keep += [local(vp.at[1], out_qvec.at[last, core])]
    total_vectors(2, dyn_vec)
    keep += [local(vp.at[2], out_dvec.at[core])]
    hand += [remote(vp.at[2], out_dvec.at[core], to_core)]
    et2[...] = scatter_end(extra_two2, er2, et2, True).astype(BF16)
    keep += [local(et2, out_qw2.at[last])]
    et1[...] = scatter_end(extra_one2, er1, et1, False).astype(BF16)
    keep += [local(et1, out_qw1.at[last])]
    o2 = upstream.at[0:own_two, 0:half]
    o1 = upstream.at[own_two : own_two + own_one, 0:half]
    oc = upstream.at[0:own_two, half : half + half_w]
    oc[...] = scatter_end(dyn_three2, er3b, et3b, False)
    keep += [local(oc, out_dw3)]
    et3[...] = scatter_end(extra_three2, er3, et3, False).astype(BF16)
    keep += [local(et3, out_qw3.at[last])]
    o1[...] = scatter_end(dyn_one2, er1b, et1b, True)
    keep += [local(o1, out_dw1)]
    for copy in dyn_two2:
        copy.wait_recv()
    for cols, at in ((left, at_y), (right, at_x)):
        o2[:, cols] = er2b[at, :, cols].astype(F32) + et2b[:, cols].astype(F32)
    keep += [local(o2, out_dw2)]
    vec_near.wait_recv()
    vec_further.wait_recv()
    for copy in vec_keep:
        copy.wait()
    vec_cores = remote(out_qvec.at[:, core], out_qvec.at[:, core], to_core)
    for theirs, copy in three_copies:
        @pl.when(theirs)
        def _(copy=copy):
            copy.wait_send()

    three_further = describe(
        out_qw3.at[pl.ds(0, LINE)], out_qw3.at[pl.ds(0, LINE)], to_core
    )

    @pl.when(mine)
    def _():
        three_keep.wait()
        for _, copy in three_copies:
            copy.wait_recv()
        three_further.start()

    for copy in table_copies:
        copy.wait_recv()
        sent(copy)
    tq[...] = tq[...] + tqr[2] + tqr[3] + tqr[4]
    keep += [local(tq, out_table.at[own_tasks])]
    hand += [remote(tq, out_table.at[own_tasks], to_core)]
    for copy in hand + [loss_copy, latent_copy]:
        copy.wait_recv()
    for copy in keep:
        copy.wait()
    @pl.when(mine)
    def _():
        three_further.wait_send()

    @pl.when(jnp.logical_not(mine))
    def _():
        three_further.wait_recv()

    vec_cores.wait_recv()
    for copy in list(pending):
        sent(copy)


def line_shards(
    latent,
    action,
    task_ids,
    action_mask,
    task_table,
    target_latent,
    bin_lower,
    bin_frac,
    dyn_w1,
    dyn_wc,
    dyn_vec1,
    dyn_w2,
    dyn_vec2,
    dyn_w3,
    dyn_vec3,
    q_w1,
    q_wc,
    q_vec1,
    q_w2,
    q_vec2,
    q_w3,
    q_b3,
):
    local_rows, half_w = latent.shape
    slot = local_rows // 2
    rows = slot * LINE
    width = 2 * half_w
    half = dyn_w1.shape[1]
    hidden = 2 * half
    heads, bins = q_b3.shape
    tasks, acts = action_mask.shape
    context_width = dyn_wc.shape[0]
    pad_context = -(-context_width // 16) * 16
    own_two = hidden // BLOCK
    own_one = width // BLOCK
    scale = 1.0 / math.sqrt(local_rows * lax.axis_size("dp"))
    sizes = (slot, width, hidden, bins, tasks, acts, context_width, heads)

    def shape(*dims, kind=F32):
        return jax.ShapeDtypeStruct(dims, kind)

    out_shape = (
        shape(local_rows, 128),
        shape(local_rows, half_w),
        shape(tasks, 128),
        shape(own_one, half),
        shape(128, half, kind=BF16),
        shape(2, 8, half),
        shape(own_two, half),
        shape(own_two, half_w),
        shape(heads, own_one, half, kind=BF16),
        shape(heads, 128, half, kind=BF16),
        shape(heads, 2, 8, half),
        shape(heads, own_two, half, kind=BF16),
        shape(heads, own_two, bins, kind=BF16),
    )
    v = pltpu.VMEM
    scratch = [
        v((acts, local_rows), BF16),
        v((1, local_rows), jnp.int32),
        v((acts, tasks), jnp.int32),
        v((tasks, context_width - acts), BF16),
        v((1, local_rows), jnp.int32),
        v((1, local_rows), F32),
        v((3, hidden), F32),
        v((heads, bins), F32),
        v((2, width, hidden), BF16),
        v((2, context_width, hidden), BF16),
        v((2, hidden, hidden), BF16),
        v((hidden, width), BF16),
        v((2, bins, hidden), BF16),
        v((3, hidden), F32),
        v((3, width), F32),
        v((2, 3, hidden), F32),
        v((2, 3, hidden), F32),
        v((2, 1, bins), F32),
        v((rows, width + 128), BF16),
        v((rows, width + 128), BF16),
        v((slot, width), F32),
        v((rows, width), BF16),
        v((rows, width), BF16),
        v((rows, hidden), BF16),
        v((rows, hidden), BF16),
        v((rows, hidden), BF16),
        v((rows, hidden), BF16),
        v((rows, width), F32),
        v((rows, width), F32),
        v((3, rows, 1), F32),
        v((rows, hidden), F32),
        v((rows, hidden), F32),
        v((2, rows, 1), F32),
        v((rows, hidden), BF16),
        v((rows, hidden), BF16),
        v((rows, hidden), BF16),
        v((rows, hidden), BF16),
        v((rows, half), BF16),
        v((rows, hidden), BF16),
        v((rows, half), BF16),
        v((rows, hidden), F32),
        v((rows, bins), BF16),
        v((rows, width), BF16),
        v((9, 8, hidden), F32),
        v((rows, hidden), F32),
        v((rows, width + 128), BF16),
        v((LINE - 1, slot, width + 128), BF16),
        v((slot, width), F32),
        v((rows, width), BF16),
        v((slot, 128), F32),
        v((LINE, 2, 2, own_two, half), BF16),
        v((LINE, 2, own_two, half), BF16),
        v((LINE, own_two, half), BF16),
        v((LINE, 2, 2, own_one, half), BF16),
        v((LINE, 2, own_one, half), BF16),
        v((LINE, own_one, half), BF16),
        v((LINE, 2, 2, own_two, bins), BF16),
        v((2, 2, 2, own_two, bins), BF16),
        v((2, 2, own_two, bins), BF16),
        v((2, own_two, bins), BF16),
        v((2, 2, 2, own_two, bins), BF16),
        v((2, 2, own_two, half), BF16),
        v((2, own_two, half), BF16),
        v((own_two, half), BF16),
        v((2, 2, own_one, half), BF16),
        v((2, own_one, half), BF16),
        v((own_one, half), BF16),
        v((2, 2, own_two, bins), BF16),
        v((2, own_two, bins), BF16),
        v((own_two, bins), BF16),
        v((2, 2, own_two, bins), BF16),
        v((2, own_two, half), BF16),
        v((own_two, half), BF16),
        v((2, own_one, half), BF16),
        v((own_one, half), BF16),
        v((2, 2, own_two, half_w), BF16),
        v((2, 2, own_two, half_w), BF16),
        v((2, 2, own_two, half_w), BF16),
        v((2, own_two, half_w), BF16),
        v((own_two, half_w), BF16),
        v((pad_context, half), BF16),
        v((pad_context, half), BF16),
        v((pad_context, half), BF16),
        v((2, 128 // LINE, half), BF16),
        v((2, 128 // LINE, half), BF16),
        v((2, 128 // LINE, half), BF16),
        v((local_rows, 16), F32),
        v((LINE, 16, local_rows), F32),
        v((3, 8, hidden), F32),
        v((3, 8, hidden), F32),
        v((3, 8, half), F32),
        v((3, 8, half), F32),
        v((3, 8, half), F32),
        v((tasks, 128), F32),
        v((tasks, 128), F32),
        v((tasks // 2, 128), F32),
        v((5, tasks // 2, 128), F32),
        pltpu.SemaphoreType.DMA((SENDS,)),
        pltpu.SemaphoreType.DMA((REMOTE_COPIES,)),
        pltpu.SemaphoreType.DMA((LOCAL_COPIES,)),
        pltpu.SemaphoreType.REGULAR,
        pltpu.SemaphoreType.REGULAR,
        pltpu.SemaphoreType.REGULAR,
    ]
    outside = pl.BlockSpec(memory_space=pl.ANY)
    raw = pl.pallas_call(
        functools.partial(line_kernel, sizes, scale),
        out_shape=out_shape,
        in_specs=[outside] * 22,
        out_specs=[outside] * len(out_shape),
        scratch_shapes=scratch,
        compiler_params=pltpu.CompilerParams(
            collective_id=0, has_side_effects=True, vmem_limit_bytes=VMEM_BYTES
        ),
        cost_estimate=pl.CostEstimate(
            flops=2 * 10**10, bytes_accessed=6 * 10**7, transcendentals=10**7
        ),
        name="line_update",
    )(
        latent, action.T, task_ids[None], action_mask.T, task_table, target_latent,
        bin_lower[None], bin_frac[None], dyn_vec1, dyn_vec2, dyn_vec3, q_vec1, q_vec2, q_b3,
        dyn_w1, dyn_wc, dyn_w2, dyn_w3, q_w1, q_wc, q_w2, jnp.swapaxes(q_w3, 1, 2),
    )
    return finish(raw, (slot, width, hidden, bins, tasks, acts, context_width, heads))


def finish_kernel(sizes, *refs):
    (slot, width, hidden, bins, tasks, acts, context_width, heads) = sizes
    half, half_w = hidden // 2, width // 2
    raw, outs, held, made = refs[0:13], refs[13:30], refs[30:43], refs[43:56]
    in_sem, out_sem = refs[56:]
    (
        raw_losses, raw_latent, raw_table, raw_dw1, raw_dwc, raw_dvec, raw_dw2, raw_dw3,
        raw_qw1, raw_qwc, raw_qvec, raw_qw2, raw_qw3,
    ) = held
    (losses, table, dwc, dvec1, dvec2, dvec3, qw1, qwc, qvec1, qw2, qvec2, qw3, qb3) = made
    (
        out_losses, out_latent, out_table, out_dw1, out_dwc, out_dvec1, out_dw2, out_dvec2,
        out_dw3, out_dvec3, out_qw1, out_qwc, out_qvec1, out_qw2, out_qvec2, out_qw3, out_qb3,
    ) = outs
    core = lax.axis_index("tensor")
    loads = {}
    for index in (11, 9, 6, 8, 1, 7, 3, 4, 10, 12, 5, 0, 2):
        loads[index] = pltpu.make_async_copy(raw[index], held[index], in_sem.at[index])
        loads[index].start()
    stored = []

    def store(source, target):
        copy = pltpu.make_async_copy(source, target, out_sem.at[len(stored)])
        copy.start()
        stored.append(copy)

    loads[11].wait()
    for head in range(heads):
        qw2[head] = raw_qw2[head].astype(F32)
    store(qw2, out_qw2)
    loads[9].wait()
    for head in range(heads):
        qwc[head] = raw_qwc[head].astype(F32)[0:context_width]
    store(qwc, out_qwc)
    for index, source, target in (
        (6, raw_dw2, out_dw2), (1, raw_latent, out_latent), (7, raw_dw3, out_dw3),
        (3, raw_dw1, out_dw1),
    ):
        loads[index].wait()
        store(source, target)
    loads[8].wait()
    qw1[...] = raw_qw1[...].astype(F32)
    store(qw1, out_qw1)
    loads[4].wait()
    dwc[...] = raw_dwc[...].astype(F32)[0:context_width]
    store(dwc, out_dwc)
    loads[10].wait()
    loads[12].wait()
    for head in range(heads):
        qvec1[head] = raw_qvec[head, core, 0:3]
        for index in range(2):
            qvec2[head, :, index * half : (index + 1) * half] = raw_qvec[head, index, 3:6]
        qw3[head] = raw_qw3[head].astype(F32).T
        qb3[head : head + 1, :] = raw_qvec[head, 0, 6:7, 0:bins]
    store(qvec1, out_qvec1)
    store(qvec2, out_qvec2)
    store(qw3, out_qw3)
    store(qb3, out_qb3)
    loads[5].wait()
    dvec1[...] = raw_dvec[core, 0:3]
    line = jnp.concatenate([raw_dvec[0, 6:7], raw_dvec[1, 6:7]], 1)
    rows = jnp.concatenate(
        [line[:, 0:width], line[:, width : 2 * width], raw_dvec[0, 7:8, 0:width]], 0
    )
    dvec3[...] = jnp.where(core == 0, rows[:, 0:half_w], rows[:, half_w:])
    for index in range(2):
        dvec2[:, index * half : (index + 1) * half] = raw_dvec[index, 3:6]
    store(dvec1, out_dvec1)
    store(dvec2, out_dvec2)
    store(dvec3, out_dvec3)
    loads[0].wait()
    loads[2].wait()
    losses[...] = raw_losses[...].T[0:2]
    table[...] = raw_table[:, acts:context_width]
    store(losses, out_losses)
    store(table, out_table)
    for copy in stored:
        copy.wait()


def finish(raw, sizes):
    (slot, width, hidden, bins, tasks, acts, context_width, heads) = sizes
    half, half_w = hidden // 2, width // 2
    own_two, own_one = hidden // BLOCK, width // BLOCK
    dims = [
        (2, 2 * slot),
        (2 * slot, half_w),
        (tasks, context_width - acts),
        (own_one, half),
        (context_width, half),
        (3, half),
        (own_two, half),
        (3, hidden),
        (own_two, half_w),
        (3, half_w),
        (heads, own_one, half),
        (heads, context_width, half),
        (heads, 3, half),
        (heads, own_two, half),
        (heads, 3, hidden),
        (heads, bins, own_two),
        (heads, bins),
    ]
    outside = pl.BlockSpec(memory_space=pl.ANY)
    outs = pl.pallas_call(
        functools.partial(finish_kernel, sizes),
        in_specs=[outside] * len(raw),
        out_specs=[outside] * len(dims),
        out_shape=[jax.ShapeDtypeStruct(item, F32) for item in dims],
        scratch_shapes=[pltpu.VMEM(item.shape, item.dtype) for item in raw]
        + [pltpu.VMEM(item, F32) for index, item in enumerate(dims) if index not in (1, 3, 6, 8)]
        + [pltpu.SemaphoreType.DMA((len(raw),)), pltpu.SemaphoreType.DMA((len(dims),))],
        compiler_params=pltpu.CompilerParams(vmem_limit_bytes=VMEM_BYTES),
        name="finish",
    )(*raw)
    outs = list(outs)
    outs[0] = outs[0].T
    outs[6] = outs[6].T
    outs[13] = jnp.swapaxes(outs[13], 1, 2)
    outs[15] = jnp.swapaxes(outs[15], 1, 2)
    return tuple(outs)


def shards(*arrays):
    if lax.axis_size("dp") == BLOCK:
        return line_shards(*arrays)
    return general_shards(*arrays)


def solution(mesh):
    return jax.shard_map(
        shards,
        mesh=mesh,
        in_specs=(
            P("dp", "tensor"),
            P("dp", None),
            P("dp"),
            P(),
            P(),
            P("dp", "tensor"),
            P("dp"),
            P("dp"),
            P(None, "tensor"),
            P(None, "tensor"),
            P(None, "tensor"),
            P("tensor", None),
            P(),
            P(None, "tensor"),
            P(None, "tensor"),
            P(None, None, "tensor"),
            P(None, None, "tensor"),
            P(None, None, "tensor"),
            P(None, "tensor", None),
            P(),
            P(),
            P(),
        ),
        out_specs=(
            P("dp", None),
            P("dp", "tensor"),
            P(),
            P("dp", "tensor"),
            P(None, "tensor"),
            P(None, "tensor"),
            P("tensor", "dp"),
            P(),
            P("dp", "tensor"),
            P(None, "tensor"),
            P(None, "dp", "tensor"),
            P(None, None, "tensor"),
            P(None, None, "tensor"),
            P(None, "tensor", "dp"),
            P(),
            P(None, "dp", None),
            P(),
        ),
        check_vma=False,
    )
```
